32 devices in a mesh: dp: 8 (over z, x), tensor: 4 (over y, core).
Axes of the slice: x: 2, y: 2, z: 4, core: 2. Of those that a mesh axis runs over, the one named last changes fastest.
Arguments:
- inputs: bfloat16 [1024, 8192], P('dp', 'tensor')
- cotangent: bfloat16 [1024, 8192], P('dp', 'tensor'), may hold values from -6 to 6
- norm_gain: bfloat16 [8192], P('tensor'), may hold values from 0.5 to 12
- w_query: bfloat16 [8192, 512], P(None, 'tensor')
- w_key: bfloat16 [8192, 512], P(None, 'tensor')
- w_value: bfloat16 [8192, 512], P(None, 'tensor'), may hold values from -0.0625 to 0.0625
- w_output: bfloat16 [512, 8192], P('tensor'), may hold values from -0.25 to 0.25
- send_rows: int32 [8, 128], P('dp'), may hold values from 0 to 128, as said below
- receive_slots: int32 [1024], P('dp'), may hold values from 0 to 127, as said below
- owner_segments: int32 [1024], P('dp'), may hold values from 0 to 1, as said below
Outputs:
- layer_out: bfloat16 [1024, 8192], P('dp', 'tensor')
- input_grad: bfloat16 [1024, 8192], P('dp', 'tensor')
The draws below stay inside these ranges and needn't reach their ends.
Inputs may be any that keep to these rules, and one draw needn't show every extreme that they name: `send_rows`: entry o * 16 + c of device p's list is the local row that p sends to device o in slot c, or 128 for an empty slot; every local row is sent exactly once, and a device sends either 16 rows or none to each device. `receive_slots`: entry i of device o is the slot p * 16 + c received from device p in slot c; the entries of one device are distinct and match send_rows, so each device ends with 128 rows. `owner_segments`: starts at 0 on each device, never falls along its rows and rises by at most one from row to row; a device holds at most 2 stays.
All inputs are finite; a program needn't handle non-finite values.
Results may differ from the reference program's by a relative error of at most 0.017.
The reference program's roundings to bfloat16 on the way (of `normed`, `head_grad`, `low_weights`, `attended`, `grad_value` and `grad_scores`) count: a program that leaves them out, or rounds other values in their place, can miss the bound.
Values may be sent and summed in bfloat16 or wider, within the bound.
No kernel may reach another device: no remote copies, remote signals or barrier semaphores. Data moves between devices by JAX's collectives and lax.ppermute only.
A program may use at most 64 MiB of HBM per device.

```python
import math
import jax
import jax.numpy as jnp
from jax import lax

D = 8192
HEAD_DIM = 128
HEADS_DEV = 1
TOK_DEV = 128
BLOCKS = 8
CAP = 16
STAYS = 2
TOKENS = 1024
HEADS = 4
QDIM = 512
N_DP = 8
N_TENSOR = 4


def shuffled_rows(one_key):
    return jax.random.permutation(one_key, TOK_DEV).astype(jnp.int32)


def inverse_order(order):
    count = order.shape[0]
    return jnp.zeros((count,), jnp.int32).at[order].set(jnp.arange(count, dtype=jnp.int32))


def layout_plan(key):
    offsets = jax.random.permutation(jax.random.fold_in(key, 101), N_DP)[:BLOCKS].astype(jnp.int32)
    labels = jax.random.permutation(jax.random.fold_in(key, 104), N_DP).astype(jnp.int32)
    places = jax.random.permutation(jax.random.fold_in(key, 105), N_DP).astype(jnp.int32)
    row_order = jax.vmap(shuffled_rows)(jax.random.split(jax.random.fold_in(key, 106), N_DP))
    slot_order = jax.vmap(shuffled_rows)(jax.random.split(jax.random.fold_in(key, 107), N_DP))
    return (offsets, labels, places, row_order, slot_order)


def draw_send_rows(key, part):
    offsets, labels, places, row_order, slot_order = layout_plan(key)
    owners = places[(labels[:, None] + offsets[None, :]) % N_DP]
    senders = jnp.broadcast_to(jnp.arange(N_DP, dtype=jnp.int32)[:, None], (N_DP, BLOCKS))
    local = row_order.reshape(N_DP, BLOCKS, CAP)
    listed = jnp.full((N_DP, N_DP, CAP), TOK_DEV, jnp.int32).at[senders, owners].set(local)
    return listed.reshape(N_DP, N_DP * CAP).astype(jnp.int32)


def draw_receive_slots(key, part):
    offsets, labels, places, row_order, slot_order = layout_plan(key)
    label_of_owner = inverse_order(places)
    sender_of_label = inverse_order(labels)
    senders = sender_of_label[(label_of_owner[:, None] - offsets[None, :]) % N_DP]
    natural = senders[:, :, None] * CAP + jnp.arange(CAP, dtype=jnp.int32)[None, None, :]
    natural = natural.reshape(N_DP, TOK_DEV)
    arranged = jnp.take_along_axis(natural, slot_order, axis=1)
    return arranged.reshape(-1).astype(jnp.int32)


def draw_owner_segments(key, part):
    key = jax.random.fold_in(key, 3)
    key_count, key_most, key_least, key_rank = jax.random.split(key, 4)
    device = jnp.arange(N_DP, dtype=jnp.int32)
    counts = jax.random.randint(key_count, (N_DP,), 1, STAYS + 1).astype(jnp.int32)
    busiest = jax.random.randint(key_most, (), 0, N_DP).astype(jnp.int32)
    single = (busiest + 1 + jax.random.randint(key_least, (), 0, N_DP - 1).astype(jnp.int32)) % N_DP
    counts = jnp.where(device == busiest, STAYS, jnp.where(device == single, 1, counts))
    position = jnp.arange(TOK_DEV, dtype=jnp.int32)[None, :]
    raw = jax.random.randint(key_rank, (N_DP, TOK_DEV), 0, 1048576).astype(jnp.int32)
    scores = jnp.where(position == 0, 1073741824, raw * TOK_DEV + position)
    ranks = jnp.sum((scores[:, None, :] < scores[:, :, None]).astype(jnp.int32), axis=-1)
    starts = (ranks < counts[:, None] - 1).astype(jnp.int32)
    stays = jnp.cumsum(starts, axis=1)
    return stays.reshape(-1).astype(jnp.int32)


def draw_inputs(key, part):
    key = jax.random.fold_in(key, 7)
    key_base, key_rows, key_cols = jax.random.split(key, 3)
    row_scale = jnp.exp(jax.random.uniform(key_rows, (TOKENS, 1), jnp.float32, math.log(0.4), math.log(4.0)))
    rising = 10.0 ** (jnp.arange(D, dtype=jnp.float32) / D)
    col_scale = rising[None, :] * jnp.exp(jax.random.uniform(key_cols, (1, D), jnp.float32, math.log(0.7), math.log(1.4)))
    base = jax.random.normal(key_base, (TOKENS, D), jnp.float32)
    return (base * row_scale * col_scale).astype(jnp.bfloat16)


def draw_norm_gain(key, part):
    key = jax.random.fold_in(key, 31)
    feature = jnp.arange(D, dtype=jnp.float32) / D
    rough = jnp.exp(jax.random.uniform(key, (D,), jnp.float32, math.log(0.8), math.log(1.25)))
    gain = 4.0 ** feature * rough
    return gain.astype(jnp.bfloat16)


def draw_w_query(key, part):
    key = jax.random.fold_in(key, 21)
    own = jax.random.normal(key, (D, QDIM), jnp.float32)
    mixed = own
    return (mixed / math.sqrt(D)).astype(jnp.bfloat16)


def draw_w_key(key, part):
    key = jax.random.fold_in(key, 22)
    own = jax.random.normal(key, (D, QDIM), jnp.float32)
    mixed = own
    return (mixed / math.sqrt(D)).astype(jnp.bfloat16)


def block_levels(stream_key, shape, cuts, least, top_value):
    def one(axis_at, shards_of):
        steps = jax.random.uniform(jax.random.fold_in(jax.random.fold_in(stream_key, 6), axis_at), (shards_of,), jnp.float32, least / len(cuts), top_value / len(cuts))
        return jnp.repeat(jnp.exp(steps), shape[axis_at] // shards_of).reshape((-1,) + (1,) * (len(shape) - axis_at - 1))

    factor_of = one(*cuts[0])
    for cut in cuts[1:]:
        factor_of = factor_of * one(*cut)
    return factor_of


def centred(stream_key, shape, spread, bound, shards=(), kind=jnp.bfloat16):
    drawn = jax.random.normal(stream_key, shape, jnp.float32) * spread
    if len(shards) > 0:
        drawn = block_levels(stream_key, shape, shards, -0.22, 0.18) * drawn
    return jnp.clip(drawn, min=-bound, max=bound).astype(kind)


def setup_inputs(seed: int = 0) -> dict:
    keys = jax.random.split(jax.random.key(seed), 11)
    inputs = draw_inputs(jax.random.fold_in(keys[10], 71), 0)
    cotangent = centred(keys[1], (TOKENS, D), 1.0, 6.0, ((0, 8), (1, 4)))
    norm_gain = draw_norm_gain(jax.random.fold_in(keys[10], 71), 0)
    w_query = draw_w_query(jax.random.fold_in(keys[10], 71), 0)
    w_key = draw_w_key(jax.random.fold_in(keys[10], 71), 0)
    w_value = centred(keys[5], (D, QDIM), D ** -0.5, 0.0625, ((1, 4),))
    w_output = centred(keys[6], (QDIM, D), QDIM ** -0.5, 0.25, ((0, 4),))
    send_rows = draw_send_rows(jax.random.fold_in(keys[10], 71), 0)
    receive_slots = draw_receive_slots(jax.random.fold_in(keys[10], 71), 0)
    owner_segments = draw_owner_segments(jax.random.fold_in(keys[10], 71), 0)
    return dict(inputs=inputs, cotangent=cotangent, norm_gain=norm_gain, w_query=w_query, w_key=w_key, w_value=w_value, w_output=w_output, send_rows=send_rows, receive_slots=receive_slots, owner_segments=owner_segments)


def source_rows(send_rows, receive_slots):
    slots = receive_slots.reshape(N_DP, TOK_DEV).astype(jnp.int32)
    sender = slots // CAP
    within = slots % CAP
    owner = jnp.arange(N_DP, dtype=jnp.int32)[:, None]
    column = owner * CAP + within
    local_row = send_rows[sender, column].astype(jnp.int32)
    return (sender * TOK_DEV + local_row).reshape(-1).astype(jnp.int32)

def held(array):
    return lax.optimization_barrier(array)

def attention_pair(queries, key_rows, value_rows, head_grad, segments):
    scaling = 1.0 / math.sqrt(HEAD_DIM)
    query_wide = queries.astype(jnp.float32)
    key_wide = key_rows.astype(jnp.float32)
    value_wide = value_rows.astype(jnp.float32)
    grad_wide = head_grad.astype(jnp.float32)
    scores = jnp.einsum('qhe,khe->hqk', query_wide, key_wide) * scaling
    position = jnp.arange(TOK_DEV, dtype=jnp.int32)
    allowed = (segments[:, None] == segments[None, :]) & (position[None, :] <= position[:, None])
    scores = jnp.where(allowed[None], scores, -1e+30)
    largest = lax.optimization_barrier(jnp.max(scores, axis=-1, keepdims=True))
    raised = jnp.exp(scores - largest)
    softmax_out = raised / lax.optimization_barrier(jnp.sum(raised, axis=-1, keepdims=True))
    low_weights = held(softmax_out.astype(jnp.bfloat16)).astype(jnp.float32)
    attended = jnp.einsum('hqk,khe->qhe', low_weights, value_wide).astype(jnp.bfloat16)
    grad_value = jnp.einsum('hqk,qhe->khe', low_weights, grad_wide).astype(jnp.bfloat16)
    grad_probs = jnp.einsum('qhe,khe->hqk', grad_wide, value_wide)
    grad_scores = softmax_out * (grad_probs - lax.optimization_barrier(jnp.sum(softmax_out * grad_probs, axis=-1, keepdims=True))) * scaling
    grad_scores = held(grad_scores.astype(jnp.bfloat16)).astype(jnp.float32)
    grad_query = jnp.einsum('hqk,khe->qhe', grad_scores, key_wide).astype(jnp.bfloat16)
    grad_key = jnp.einsum('hqk,qhe->khe', grad_scores, query_wide).astype(jnp.bfloat16)
    return (attended, grad_query, grad_key, grad_value)

def reference(inputs, cotangent, norm_gain, w_query, w_key, w_value, w_output, send_rows, receive_slots, owner_segments):
    source = source_rows(send_rows, receive_slots)
    wide_in = inputs.astype(jnp.float32)
    inverse_rms = lax.rsqrt(lax.optimization_barrier(jnp.mean(wide_in * wide_in, axis=-1, keepdims=True)) + 1e-05)
    scaled = wide_in * inverse_rms
    normed = (scaled * norm_gain.astype(jnp.float32)).astype(jnp.bfloat16)
    queries = jnp.dot(normed, w_query, preferred_element_type=jnp.float32).astype(jnp.bfloat16)
    key_rows = jnp.dot(normed, w_key, preferred_element_type=jnp.float32).astype(jnp.bfloat16)
    value_rows = jnp.dot(normed, w_value, preferred_element_type=jnp.float32).astype(jnp.bfloat16)
    head_grad = jnp.dot(cotangent, w_output.T, preferred_element_type=jnp.float32).astype(jnp.bfloat16)

    def regroup(array):
        return array[source].reshape(N_DP, TOK_DEV, HEADS, HEAD_DIM)

    def restore(array):
        flat = array.reshape(TOKENS, QDIM)
        return jnp.zeros((TOKENS, QDIM), jnp.bfloat16).at[source].set(flat)
    segments = owner_segments.reshape(N_DP, TOK_DEV)
    results = jax.vmap(attention_pair)(regroup(queries), regroup(key_rows), regroup(value_rows), regroup(head_grad), segments)
    attended = restore(results[0])
    grad_query = restore(results[1])
    grad_key = restore(results[2])
    grad_value = restore(results[3])
    group_width = HEADS_DEV * HEAD_DIM
    total = jnp.zeros((TOKENS, D), jnp.float32)
    grad_total = jnp.zeros((TOKENS, D), jnp.float32)
    for group_index in range(N_TENSOR):
        lower = group_index * group_width
        upper = lower + group_width
        part = jnp.dot(attended[:, lower:upper], w_output[lower:upper], preferred_element_type=jnp.float32)
        total = total + held(part.astype(jnp.bfloat16)).astype(jnp.float32)
        grad_part = jnp.dot(grad_query[:, lower:upper], w_query[:, lower:upper].T, preferred_element_type=jnp.float32)
        grad_part = grad_part + jnp.dot(grad_key[:, lower:upper], w_key[:, lower:upper].T, preferred_element_type=jnp.float32)
        grad_part = grad_part + jnp.dot(grad_value[:, lower:upper], w_value[:, lower:upper].T, preferred_element_type=jnp.float32)
        grad_total = grad_total + held(grad_part.astype(jnp.bfloat16)).astype(jnp.float32)
    layer_out = (wide_in + total).astype(jnp.bfloat16)
    grad_hat = grad_total * norm_gain.astype(jnp.float32)
    mean_dot = lax.optimization_barrier(jnp.mean(grad_hat * scaled, axis=-1, keepdims=True))
    input_grad = (cotangent.astype(jnp.float32) + inverse_rms * (grad_hat - scaled * mean_dot)).astype(jnp.bfloat16)
    return (layer_out, input_grad)
```

```python
import functools
import math

import jax
import jax.numpy as jnp
from jax import lax
from jax.experimental import pallas as pl
from jax.experimental.pallas import tpu as pltpu
from jax.sharding import PartitionSpec as P

HEAD_DIM = 128
EPSILON = 1e-05
SCALING = 1.0 / math.sqrt(HEAD_DIM)
CONTRACT_LAST = (((1,), (1,)), ((), ()))
CONTRACT_FIRST = (((0,), (0,)), ((), ()))
VMEM_LIMIT = 48 * 1024 * 1024


def dot(left, right, dims=(((1,), (0,)), ((), ()))):
    return lax.dot_general(left, right, dims, preferred_element_type=jnp.float32)


def params():
    return pltpu.CompilerParams(vmem_limit_bytes=VMEM_LIMIT)


def whole(array):
    zeros = (0,) * array.ndim
    return pl.BlockSpec(array.shape, lambda *_: zeros)


def swap(array, mask, count):
    return lax.ppermute(array, "tensor", [(i, i ^ mask) for i in range(count)])


def project_rows_kernel(
    order, x0, x1, x2, x3, gain, w_query, w_key, w_value, send, home, bucket, inverse, total
):
    step = pl.program_id(0)
    blocks = (x0, x1, x2, x3)
    features = sum(block.shape[1] for block in blocks)

    @pl.when(step == 0)
    def _():
        squares = 0.0
        for block in blocks:
            wide = block[...].astype(jnp.float32)
            squares = squares + jnp.sum(wide * wide, axis=-1, keepdims=True)
        inverse[...] = lax.rsqrt(squares / features + EPSILON)
        total[...] = jnp.zeros_like(total)

    for index, block in enumerate(blocks):

        @pl.when(step == index)
        def _():
            scaled = block[...].astype(jnp.float32) * inverse[...]
            normed = (scaled * gain[index : index + 1, :].astype(jnp.float32)).astype(jnp.bfloat16)
            for place, weight in enumerate((w_query, w_key, w_value)):
                part = slice(place * HEAD_DIM, (place + 1) * HEAD_DIM)
                total[:, part] += dot(normed, weight[...])

    @pl.when(step == len(blocks) - 1)
    def _():
        rounded = total[...].astype(jnp.bfloat16)
        home[...] = rounded
        rows = lax.broadcasted_iota(jnp.int32, (send.shape[0], rounded.shape[0]), 1)
        chosen = jnp.where(send[...] == rows, 1.0, 0.0).astype(jnp.bfloat16)
        bucket[...] = dot(chosen, rounded).astype(jnp.bfloat16)


def project_rows(order, blocks, gain, w_query, w_key, w_value, send):
    rows, width = blocks[0].shape
    slots = send.shape[0]
    weight_spec = pl.BlockSpec((width, HEAD_DIM), lambda s, order: (order[s], 0))
    return pl.pallas_call(
        project_rows_kernel,
        out_shape=(
            jax.ShapeDtypeStruct((rows, 3 * HEAD_DIM), jnp.bfloat16),
            jax.ShapeDtypeStruct((slots, 3 * HEAD_DIM), jnp.bfloat16),
            jax.ShapeDtypeStruct((rows, 1), jnp.float32),
        ),
        grid_spec=pltpu.PrefetchScalarGridSpec(
            num_scalar_prefetch=1,
            grid=(4,),
            in_specs=[whole(b) for b in blocks] + [whole(gain)] + [weight_spec] * 3 + [whole(send)],
            out_specs=[
                pl.BlockSpec((rows, 3 * HEAD_DIM), lambda *_: (0, 0)),
                pl.BlockSpec((slots, 3 * HEAD_DIM), lambda *_: (0, 0)),
                pl.BlockSpec((rows, 1), lambda *_: (0, 0)),
            ],
            scratch_shapes=[pltpu.VMEM((rows, 3 * HEAD_DIM), jnp.float32)],
        ),
        compiler_params=params(),
        name="project_rows",
    )(order, *blocks, gain, w_query, w_key, w_value, send)


def project_grad_kernel(order, c0, c1, c2, c3, w_output, send, home, bucket, total):
    step = pl.program_id(0)
    blocks = (c0, c1, c2, c3)

    @pl.when(step == 0)
    def _():
        total[...] = jnp.zeros_like(total)

    for index, block in enumerate(blocks):

        @pl.when(step == index)
        def _():
            total[...] += dot(block[...], w_output[...], CONTRACT_LAST)

    @pl.when(step == len(blocks) - 1)
    def _():
        rounded = total[...].astype(jnp.bfloat16)
        home[...] = rounded
        rows = lax.broadcasted_iota(jnp.int32, (send.shape[0], rounded.shape[0]), 1)
        chosen = jnp.where(send[...] == rows, 1.0, 0.0).astype(jnp.bfloat16)
        bucket[...] = dot(chosen, rounded).astype(jnp.bfloat16)


def project_grad(order, blocks, w_output, send):
    rows, width = blocks[0].shape
    slots = send.shape[0]
    return pl.pallas_call(
        project_grad_kernel,
        out_shape=(
            jax.ShapeDtypeStruct((rows, HEAD_DIM), jnp.bfloat16),
            jax.ShapeDtypeStruct((slots, HEAD_DIM), jnp.bfloat16),
        ),
        grid_spec=pltpu.PrefetchScalarGridSpec(
            num_scalar_prefetch=1,
            grid=(4,),
            in_specs=[whole(b) for b in blocks]
            + [pl.BlockSpec((HEAD_DIM, width), lambda s, order: (0, order[s])), whole(send)],
            out_specs=[
                pl.BlockSpec((rows, HEAD_DIM), lambda *_: (0, 0)),
                pl.BlockSpec((slots, HEAD_DIM), lambda *_: (0, 0)),
            ],
            scratch_shapes=[pltpu.VMEM((rows, HEAD_DIM), jnp.float32)],
        ),
        compiler_params=params(),
        name="project_grad",
    )(order, *blocks, w_output, send)


def one_owner(queries, key_rows, value_rows, head_grad, allowed):
    scores = jnp.where(allowed, dot(queries, key_rows, CONTRACT_LAST) * SCALING, -1e30)
    raised = jnp.exp(scores - jnp.max(scores, axis=-1, keepdims=True))
    softmax_out = raised / jnp.sum(raised, axis=-1, keepdims=True)
    low_weights = softmax_out.astype(jnp.bfloat16)
    attended = dot(low_weights, value_rows).astype(jnp.bfloat16)
    grad_value = dot(low_weights, head_grad, CONTRACT_FIRST).astype(jnp.bfloat16)
    grad_probs = dot(head_grad, value_rows, CONTRACT_LAST)
    inner = jnp.sum(softmax_out * grad_probs, axis=-1, keepdims=True)
    grad_scores = (softmax_out * (grad_probs - inner) * SCALING).astype(jnp.bfloat16)
    grad_query = dot(grad_scores, key_rows).astype(jnp.bfloat16)
    grad_key = dot(grad_scores, queries, CONTRACT_FIRST).astype(jnp.bfloat16)
    return attended, grad_query, grad_key, grad_value


def attend_kernel(me, qkv, grad, code_down, code_across, send, out, held, picked):
    devices, owners, cap, _ = qkv.shape
    slots = devices * cap
    mine = pl.ds(pl.multiple_of(me[0] * cap, cap), cap)
    for owner in range(owners):
        rows = qkv[:, owner].reshape(slots, 3 * HEAD_DIM)
        head_grad = grad[:, owner].reshape(slots, HEAD_DIM)
        down = code_down[:, owner : owner + 1]
        across = code_across[owner : owner + 1, :]
        allowed = (across <= down) & (across >= (down // slots) * slots)
        results = one_owner(
            rows[:, :HEAD_DIM],
            rows[:, HEAD_DIM : 2 * HEAD_DIM],
            rows[:, 2 * HEAD_DIM :],
            head_grad,
            allowed,
        )
        for place, result in enumerate(results):
            held[owner, :, place * HEAD_DIM : (place + 1) * HEAD_DIM] = result
    for owner in range(owners):
        picked[owner * cap : (owner + 1) * cap, :] = held[owner, mine, :]
    rows = lax.broadcasted_iota(jnp.int32, (out.shape[0], slots), 0)
    chosen = jnp.where(send[...] == rows, 1.0, 0.0).astype(jnp.bfloat16)
    out[...] = dot(chosen, picked[...]).astype(jnp.bfloat16)


def attend_all(me, qkv, grad, code_down, code_across, send, rows):
    devices, owners, cap, _ = qkv.shape
    slots = devices * cap
    vmem = pl.BlockSpec(memory_space=pltpu.VMEM)
    return pl.pallas_call(
        attend_kernel,
        out_shape=jax.ShapeDtypeStruct((rows, 4 * HEAD_DIM), jnp.bfloat16),
        in_specs=[pl.BlockSpec(memory_space=pltpu.SMEM)] + [vmem] * 5,
        out_specs=vmem,
        scratch_shapes=[
            pltpu.VMEM((owners, slots, 4 * HEAD_DIM), jnp.bfloat16),
            pltpu.VMEM((slots, 4 * HEAD_DIM), jnp.bfloat16),
        ],
        compiler_params=params(),
        name="attend_all",
    )(me, qkv, grad, code_down, code_across, send)


def spread_kernel(order, own, near, wq, wk, wv, wo, nq, nk, nv, no, grad_part, out_part):
    grad = 0.0
    for place, weight in ((1, wq), (2, wk), (3, wv)):
        grad += dot(own[:, place * HEAD_DIM : (place + 1) * HEAD_DIM], weight[...], CONTRACT_LAST)
    for place, weight in ((1, nq), (2, nk), (3, nv)):
        grad += dot(near[:, place * HEAD_DIM : (place + 1) * HEAD_DIM], weight[...], CONTRACT_LAST)
    grad_part[...] = grad.astype(grad_part.dtype)
    out = dot(own[:, :HEAD_DIM], wo[...]) + dot(near[:, :HEAD_DIM], no[...])
    out_part[...] = out.astype(out_part.dtype)


def spread(order, slot, own, near, own_weights, near_weights, width, dtype, tile=512):
    rows = own.shape[0]
    steps = width // tile
    here = lambda j, order: (order[slot] * steps + j, 0)
    here_across = lambda j, order: (0, order[slot] * steps + j)
    flat = lambda j, order: (j, 0)
    flat_across = lambda j, order: (0, j)
    return pl.pallas_call(
        spread_kernel,
        out_shape=(
            jax.ShapeDtypeStruct((rows, width), dtype),
            jax.ShapeDtypeStruct((rows, width), dtype),
        ),
        grid_spec=pltpu.PrefetchScalarGridSpec(
            num_scalar_prefetch=1,
            grid=(steps,),
            in_specs=[whole(own), whole(near)]
            + [pl.BlockSpec((tile, HEAD_DIM), here)] * 3
            + [pl.BlockSpec((HEAD_DIM, tile), here_across)]
            + [pl.BlockSpec((tile, HEAD_DIM), flat)] * 3
            + [pl.BlockSpec((HEAD_DIM, tile), flat_across)],
            out_specs=[pl.BlockSpec((rows, tile), flat_across)] * 2,
        ),
        compiler_params=params(),
        name="spread",
    )(order, own, near, *own_weights, *near_weights)


def balanced_codes(receive_slots, owner_segments, slots):
    rows = receive_slots.shape[0]
    taken = receive_slots[:, None] == jnp.arange(slots, dtype=jnp.int32)[None, :]
    code = owner_segments * slots + jnp.arange(rows, dtype=jnp.int32)
    return jnp.sum(jnp.where(taken, code[:, None], 0), axis=0)


def attend_gathered(bucket_qkv, bucket_grad, send_rows, receive_slots, owner_segments, rows):
    devices = lax.axis_size("dp")
    slots = send_rows.shape[1]
    cap = slots // devices
    code = balanced_codes(receive_slots, owner_segments, slots)
    codes = lax.all_gather(code, "dp")
    qkv = lax.all_gather(bucket_qkv, "dp").reshape(devices, devices, cap, 3 * HEAD_DIM)
    grad = lax.all_gather(bucket_grad, "dp").reshape(devices, devices, cap, HEAD_DIM)
    me = lax.axis_index("dp").astype(jnp.int32).reshape(1)
    return attend_all(me, qkv, grad, codes.T, codes, send_rows, rows)


def attend_exchanged(bucket_qkv, bucket_grad, send_rows, receive_slots, owner_segments, rows):
    slots = send_rows.shape[1]
    bucket = jnp.concatenate([bucket_qkv, bucket_grad], axis=1)
    moved = lax.all_to_all(bucket, "dp", split_axis=0, concat_axis=0, tiled=True)
    parts = jnp.split(moved[receive_slots], 4, axis=1)
    position = jnp.arange(rows, dtype=jnp.int32)
    same = owner_segments[:, None] == owner_segments[None, :]
    allowed = same & (position[None, :] <= position[:, None])
    results = jnp.concatenate(one_owner(*parts, allowed), axis=1)
    back = jnp.zeros((slots, 4 * HEAD_DIM), jnp.bfloat16).at[receive_slots].set(results)
    back = lax.all_to_all(back, "dp", split_axis=0, concat_axis=0, tiled=True)
    return jnp.zeros((rows, 4 * HEAD_DIM), jnp.bfloat16).at[send_rows[0]].set(back, mode="drop")


def on_device(
    inputs,
    cotangent,
    norm_gain,
    w_query,
    w_key,
    w_value,
    w_output,
    send_rows,
    receive_slots,
    owner_segments,
):
    rows, width = inputs.shape
    slots = send_rows.shape[1]
    tensor = lax.axis_size("tensor")
    features = width * tensor
    order = lax.axis_index("tensor").astype(jnp.int32) ^ jnp.arange(4, dtype=jnp.int32)
    send_down = send_rows.reshape(slots, 1)

    x2 = swap(inputs, 2, tensor)
    c2 = swap(cotangent, 2, tensor)
    x1 = swap(inputs, 1, tensor)
    c1 = swap(cotangent, 1, tensor)
    x3 = swap(x2, 1, tensor)
    c3 = swap(c2, 1, tensor)
    gain_row = norm_gain.reshape(1, width)
    gain2 = jnp.concatenate([gain_row, swap(gain_row, 1, tensor)], axis=0)
    gain = jnp.concatenate([gain2, swap(gain2, 2, tensor)], axis=0)

    near = []
    for weight in (w_query, w_key, w_value):
        pieces = [
            lax.dynamic_slice_in_dim(weight, order[slot] * width, width, axis=0) for slot in (1, 3)
        ]
        near.append(swap(jnp.concatenate(pieces, axis=0), 1, tensor))
    pieces = [
        lax.dynamic_slice_in_dim(w_output, order[slot] * width, width, axis=1) for slot in (1, 3)
    ]
    near.append(swap(jnp.concatenate(pieces, axis=1), 1, tensor))

    home, bucket_qkv, inverse_rms = project_rows(
        order, (inputs, x1, x2, x3), gain, w_query, w_key, w_value, send_down
    )
    _, bucket_grad = project_grad(order, (cotangent, c1, c2, c3), w_output, send_down)
    dense = slots == rows
    attend = attend_gathered if dense else attend_exchanged
    results = attend(bucket_qkv, bucket_grad, send_rows, receive_slots, owner_segments, rows)
    results_near = swap(results, 1, tensor)

    own_weights = (w_query, w_key, w_value, w_output)
    far_near = [n[width:] for n in near[:3]] + [near[3][:, width:]]
    grad_far, out_far = spread(
        order, 2, results, results_near, own_weights, far_near, width, jnp.bfloat16
    )
    grad_got = swap(grad_far, 2, tensor)
    out_got = swap(out_far, 2, tensor)
    grad_own, out_own = spread(
        order, 0, results, results_near, own_weights, near, width, jnp.float32
    )
    row_dot = jnp.sum(
        results[:, HEAD_DIM:].astype(jnp.float32) * home.astype(jnp.float32),
        axis=-1,
        keepdims=True,
    )
    row_dot = row_dot + swap(row_dot, 1, tensor)
    row_dot = row_dot + swap(row_dot, 2, tensor)

    wide_in = inputs.astype(jnp.float32)
    layer_out = (wide_in + out_own + out_got.astype(jnp.float32)).astype(jnp.bfloat16)
    scaled = wide_in * inverse_rms
    grad_hat = (grad_own + grad_got.astype(jnp.float32)) * norm_gain.astype(jnp.float32)
    input_grad = (
        cotangent.astype(jnp.float32) + inverse_rms * (grad_hat - scaled * (row_dot / features))
    ).astype(jnp.bfloat16)
    return (layer_out, input_grad)


def solution(mesh):
    return jax.shard_map(
        on_device,
        mesh=mesh,
        in_specs=(
            P("dp", "tensor"),
            P("dp", "tensor"),
            P("tensor"),
            P(None, "tensor"),
            P(None, "tensor"),
            P(None, "tensor"),
            P("tensor", None),
            P("dp", None),
            P("dp"),
            P("dp"),
        ),
        out_specs=(P("dp", "tensor"), P("dp", "tensor")),
        check_vma=False,
    )
```

```python
import functools
import math

import jax
import jax.numpy as jnp
from jax import lax
from jax.experimental import pallas as pl
from jax.experimental.pallas import tpu as pltpu
from jax.sharding import PartitionSpec as P

HEAD_DIM = 128
EPSILON = 1e-05
SCALING = 1.0 / math.sqrt(HEAD_DIM)
CONTRACT_LAST = (((1,), (1,)), ((), ()))
CONTRACT_FIRST = (((0,), (0,)), ((), ()))
VMEM_LIMIT = 24 * 1024 * 1024


def dot(left, right, dims=(((1,), (0,)), ((), ()))):
    return lax.dot_general(left, right, dims, preferred_element_type=jnp.float32)


def params():
    return pltpu.CompilerParams(vmem_limit_bytes=VMEM_LIMIT)


def whole(array):
    zeros = (0,) * len(array.shape)
    return pl.BlockSpec(array.shape, lambda *_: zeros)


def swap(array, mask, count):
    return lax.ppermute(array, "tensor", [(i, i ^ mask) for i in range(count)])


def one_hot(places, shape, dimension):
    rows = lax.broadcasted_iota(jnp.int32, shape, dimension)
    return jnp.where(places == rows, 1.0, 0.0).astype(jnp.bfloat16)


def write_buckets(rounded, send, buckets):
    chosen = one_hot(send[...], (send.shape[0], rounded.shape[0]), 1)
    sorted_rows = dot(chosen, rounded).astype(jnp.bfloat16)
    cap = buckets[0].shape[0]
    for index, bucket in enumerate(buckets):
        bucket[...] = sorted_rows[index * cap : (index + 1) * cap, :]


def bucket_shapes(count, slots, width):
    return [jax.ShapeDtypeStruct((slots // max(count, 1), width), jnp.bfloat16)] * count


def project_rows_kernel(
    order, x0, x1, x2, x3, g0, g1, g2, g3, weights, send, home, inverse, *rest
):
    *buckets, total = rest
    step = pl.program_id(0)
    blocks = (x0, x1, x2, x3)
    features = sum(block.shape[1] for block in blocks)

    @pl.when(step == 0)
    def _():
        squares = 0.0
        for block in blocks:
            wide = block[...].astype(jnp.float32)
            squares = squares + jnp.sum(wide * wide, axis=-1, keepdims=True)
        inverse[...] = lax.rsqrt(squares / features + EPSILON)
        total[...] = jnp.zeros_like(total)

    for index, (block, gain) in enumerate(zip(blocks, (g0, g1, g2, g3))):

        @pl.when(step == index)
        def _():
            scaled = block[...].astype(jnp.float32) * inverse[...]
            normed = (scaled * gain[...].astype(jnp.float32)).astype(jnp.bfloat16)
            total[...] += dot(normed, weights[...])

    @pl.when(step == len(blocks) - 1)
    def _():
        rounded = total[...].astype(jnp.bfloat16)
        home[...] = rounded
        if buckets:
            write_buckets(rounded, send, buckets)


def project_rows(order, blocks, gains, weights, send, count):
    rows, width = blocks[0].shape
    columns = weights.shape[1]
    shapes = [
        jax.ShapeDtypeStruct((rows, columns), jnp.bfloat16),
        jax.ShapeDtypeStruct((rows, 1), jnp.float32),
    ] + bucket_shapes(count, send.shape[0], columns)
    return pl.pallas_call(
        project_rows_kernel,
        out_shape=shapes,
        grid_spec=pltpu.PrefetchScalarGridSpec(
            num_scalar_prefetch=1,
            grid=(4,),
            in_specs=[whole(b) for b in blocks + gains]
            + [pl.BlockSpec((width, columns), lambda s, order: (order[s], 0)), whole(send)],
            out_specs=[whole(shape) for shape in shapes],
            scratch_shapes=[pltpu.VMEM((rows, columns), jnp.float32)],
        ),
        compiler_params=params(),
        name="project_rows",
    )(order, *blocks, *gains, weights, send)


def grad_part_kernel(order, block, own, near, *rest):
    *before, total, other = rest
    weights = jnp.concatenate([own[...], near[...]], axis=0)
    part = dot(block[...], weights, CONTRACT_LAST)
    heads = own.shape[0]
    for place, out in enumerate((total, other)):
        value = part[:, place * heads : (place + 1) * heads]
        out[...] = value + before[place][...] if before else value


def grad_part(order, slot, half, block, w_output, near, before):
    rows, width = block.shape
    heads = w_output.shape[0]
    shapes = [jax.ShapeDtypeStruct((rows, heads), jnp.float32)] * 2
    return pl.pallas_call(
        grad_part_kernel,
        out_shape=shapes,
        grid_spec=pltpu.PrefetchScalarGridSpec(
            num_scalar_prefetch=1,
            grid=(1,),
            in_specs=[
                whole(block),
                pl.BlockSpec((heads, width), lambda s, order: (0, order[slot])),
                pl.BlockSpec((heads, width), lambda s, order: (0, half)),
            ]
            + [whole(b) for b in before],
            out_specs=[whole(shape) for shape in shapes],
        ),
        compiler_params=params(),
        name="grad_part",
    )(order, block, w_output, near, *before)


def grad_buckets_kernel(total, other, send, *buckets):
    write_buckets((total[...] + other[...]).astype(jnp.bfloat16), send, buckets)


def grad_buckets(total, other, send, count):
    return pl.pallas_call(
        grad_buckets_kernel,
        out_shape=bucket_shapes(count, send.shape[0], total.shape[1]),
        compiler_params=params(),
        name="grad_buckets",
    )(total, other, send)


def softmax_rows(queries, key_rows, allowed):
    scores = jnp.where(allowed, dot(queries, key_rows, CONTRACT_LAST) * SCALING, -1e30)
    raised = jnp.exp(scores - jnp.max(scores, axis=-1, keepdims=True))
    return raised / jnp.sum(raised, axis=-1, keepdims=True)


def attended_rows(softmax_out, value_rows):
    return dot(softmax_out.astype(jnp.bfloat16), value_rows).astype(jnp.bfloat16)


def attention_grads(softmax_out, queries, key_rows, value_rows, head_grad):
    low_weights = softmax_out.astype(jnp.bfloat16)
    grad_value = dot(low_weights, head_grad, CONTRACT_FIRST).astype(jnp.bfloat16)
    grad_probs = dot(head_grad, value_rows, CONTRACT_LAST)
    inner = jnp.sum(softmax_out * grad_probs, axis=-1, keepdims=True)
    grad_scores = (softmax_out * (grad_probs - inner) * SCALING).astype(jnp.bfloat16)
    grad_query = dot(grad_scores, key_rows).astype(jnp.bfloat16)
    grad_key = dot(grad_scores, queries, CONTRACT_FIRST).astype(jnp.bfloat16)
    return jnp.concatenate([grad_query, grad_key, grad_value], axis=1)


def thirds(rows):
    return (rows[:, :HEAD_DIM], rows[:, HEAD_DIM : 2 * HEAD_DIM], rows[:, 2 * HEAD_DIM :])


def attend_kernel(count, code_down, code_across, *refs):
    pieces, (softmax, qkv), backs = refs[:count], refs[count : count + 2], refs[count + 2 :]
    rows = jnp.concatenate([piece[...] for piece in pieces], axis=0)
    qkv[...] = rows
    queries, key_rows, value_rows = thirds(rows)
    slots = rows.shape[0]
    down, across = code_down[...], code_across[...]
    allowed = (across <= down) & (across >= (down // slots) * slots)
    softmax_out = softmax_rows(queries, key_rows, allowed)
    softmax[...] = softmax_out
    attended = attended_rows(softmax_out, value_rows)
    cap = pieces[0].shape[0]
    for index, back in enumerate(backs):
        back[...] = attended[index * cap : (index + 1) * cap, :]


def attend(code, pieces):
    count = len(pieces)
    cap, columns = pieces[0].shape
    slots = count * cap
    return pl.pallas_call(
        functools.partial(attend_kernel, count),
        out_shape=[
            jax.ShapeDtypeStruct((slots, slots), jnp.float32),
            jax.ShapeDtypeStruct((slots, columns), jnp.bfloat16),
        ]
        + bucket_shapes(count, slots, HEAD_DIM),
        compiler_params=params(),
        name="attend",
    )(code.reshape(slots, 1), code.reshape(1, slots), *pieces)


def attend_back_kernel(softmax, qkv, *refs):
    count = len(refs) // 2
    pieces, backs = refs[:count], refs[count:]
    head_grad = jnp.concatenate([piece[...] for piece in pieces], axis=0)
    grads = attention_grads(softmax[...], *thirds(qkv[...]), head_grad)
    cap = pieces[0].shape[0]
    for index, back in enumerate(backs):
        back[...] = grads[index * cap : (index + 1) * cap, :]


def attend_back(softmax, qkv, pieces):
    return pl.pallas_call(
        attend_back_kernel,
        out_shape=bucket_shapes(len(pieces), qkv.shape[0], qkv.shape[1]),
        compiler_params=params(),
        name="attend_back",
    )(softmax, qkv, *pieces)


def bring_home_kernel(send, *refs):
    *pieces, out = refs
    rows = jnp.concatenate([piece[...] for piece in pieces], axis=0)
    chosen = one_hot(send[...], (out.shape[0], rows.shape[0]), 0)
    out[...] = dot(chosen, rows).astype(jnp.bfloat16)


def bring_home(send, pieces, rows):
    return pl.pallas_call(
        bring_home_kernel,
        out_shape=jax.ShapeDtypeStruct((rows, pieces[0].shape[1]), jnp.bfloat16),
        compiler_params=params(),
        name="bring_home",
    )(send, *pieces)


def spread_kernel(dims, order, own, near, own_weights, near_weights, out):
    total = dot(own[...], own_weights[...], dims) + dot(near[...], near_weights[...], dims)
    out[...] = total.astype(out.dtype)


def spread_grad(order, slot, half, own, near, weights, near_weights, start, span, dtype, tile=512):
    rows, columns = own.shape
    width = near_weights.shape[0] // 2
    steps, first = width // tile, start // tile
    return pl.pallas_call(
        functools.partial(spread_kernel, CONTRACT_LAST),
        out_shape=jax.ShapeDtypeStruct((rows, span), dtype),
        grid_spec=pltpu.PrefetchScalarGridSpec(
            num_scalar_prefetch=1,
            grid=(span // tile,),
            in_specs=[
                whole(own),
                whole(near),
                pl.BlockSpec((tile, columns), lambda j, order: (order[slot] * steps + first + j, 0)),
                pl.BlockSpec((tile, columns), lambda j, order: (half * steps + first + j, 0)),
            ],
            out_specs=pl.BlockSpec((rows, tile), lambda j, order: (0, j)),
        ),
        compiler_params=params(),
        name="spread_grad",
    )(order, own, near, weights, near_weights)


def spread_out(order, slot, half, own, near, weights, near_weights, dtype, tile=1024):
    rows, heads = own.shape
    width = near_weights.shape[1] // 2
    steps = width // tile
    return pl.pallas_call(
        functools.partial(spread_kernel, (((1,), (0,)), ((), ()))),
        out_shape=jax.ShapeDtypeStruct((rows, width), dtype),
        grid_spec=pltpu.PrefetchScalarGridSpec(
            num_scalar_prefetch=1,
            grid=(steps,),
            in_specs=[
                whole(own),
                whole(near),
                pl.BlockSpec((heads, tile), lambda j, order: (0, order[slot] * steps + j)),
                pl.BlockSpec((heads, tile), lambda j, order: (0, half * steps + j)),
            ],
            out_specs=pl.BlockSpec((rows, tile), lambda j, order: (0, j)),
        ),
        compiler_params=params(),
        name="spread_out",
    )(order, own, near, weights, near_weights)


def exchange(pieces):
    count = len(pieces)
    return [pieces[0]] + [
        lax.ppermute(piece, "dp", [(i, i ^ k) for i in range(count)])
        for k, piece in enumerate(pieces)
        if k
    ]


def balanced_codes(receive_slots, owner_segments, slots):
    rows = receive_slots.shape[0]
    taken = receive_slots[:, None] == jnp.arange(slots, dtype=jnp.int32)[None, :]
    code = owner_segments * slots + jnp.arange(rows, dtype=jnp.int32)
    return jnp.sum(jnp.where(taken, code[:, None], 0), axis=0)


def attend_sparse(qkv, head_grad, send_rows, receive_slots, owner_segments):
    rows = qkv.shape[0]
    slots = send_rows.shape[1]
    both = jnp.concatenate([qkv, head_grad], axis=1)
    padded = jnp.concatenate([both, jnp.zeros((1, 4 * HEAD_DIM), both.dtype)], axis=0)
    moved = lax.all_to_all(padded[send_rows[0]], "dp", split_axis=0, concat_axis=0, tiled=True)
    queries, key_rows, value_rows, grads = jnp.split(moved[receive_slots], 4, axis=1)
    position = jnp.arange(rows, dtype=jnp.int32)
    same = owner_segments[:, None] == owner_segments[None, :]
    allowed = same & (position[None, :] <= position[:, None])
    softmax_out = softmax_rows(queries, key_rows, allowed)
    attended = attended_rows(softmax_out, value_rows)
    grads = attention_grads(softmax_out, queries, key_rows, value_rows, grads)
    results = jnp.concatenate([attended, grads], axis=1)
    back = jnp.zeros((slots, 4 * HEAD_DIM), jnp.bfloat16).at[receive_slots].set(results)
    back = lax.all_to_all(back, "dp", split_axis=0, concat_axis=0, tiled=True)
    home = jnp.zeros((rows, 4 * HEAD_DIM), jnp.bfloat16).at[send_rows[0]].set(back, mode="drop")
    return home[:, :HEAD_DIM], home[:, HEAD_DIM:]


def on_device(
    inputs,
    cotangent,
    norm_gain,
    w_query,
    w_key,
    w_value,
    w_output,
    send_rows,
    receive_slots,
    owner_segments,
):
    rows, width = inputs.shape
    slots = send_rows.shape[1]
    tensor = lax.axis_size("tensor")
    owners = lax.axis_size("dp")
    features = width * tensor
    order = lax.axis_index("tensor").astype(jnp.int32) ^ jnp.arange(4, dtype=jnp.int32)
    dense = slots == rows and owners & (owners - 1) == 0
    count = owners if dense else 0
    gain_row = norm_gain.reshape(1, width)

    gain2 = swap(gain_row, 2, tensor)
    gain1 = swap(gain_row, 1, tensor)
    x2 = swap(inputs, 2, tensor)
    x1 = swap(inputs, 1, tensor)
    later, x2 = lax.optimization_barrier((cotangent, x2))
    c2 = swap(later, 2, tensor)
    x3 = swap(x2, 1, tensor)
    gain3 = swap(gain2, 1, tensor)

    weights = jnp.concatenate([w_query, w_key, w_value], axis=1)
    near_weights = swap(
        jnp.concatenate(
            [lax.dynamic_slice_in_dim(weights, order[s] * width, width, axis=0) for s in (1, 3)],
            axis=0,
        ),
        1,
        tensor,
    )
    near_output = swap(
        jnp.concatenate(
            [lax.dynamic_slice_in_dim(w_output, order[s] * width, width, axis=1) for s in (1, 3)],
            axis=1,
        ),
        1,
        tensor,
    )
    if dense:
        turned = lax.axis_index("dp").astype(jnp.int32) ^ jnp.arange(owners, dtype=jnp.int32)
        code = balanced_codes(receive_slots, owner_segments, slots)
        code = code.reshape(owners, -1)[turned].reshape(-1)
        send = send_rows.reshape(owners, -1)[turned].reshape(-1)
    else:
        send = send_rows.reshape(-1)
    send_down = send.reshape(slots, 1)
    send_across = send.reshape(1, slots)

    first = grad_part(order, 0, 0, cotangent, w_output, near_output, ())
    home, inverse_rms, *buckets = project_rows(
        order, [inputs, x1, x2, x3], [gain_row, gain1, gain2, gain3], weights, send_down, count
    )
    if dense:
        softmax, qkv, *backs = attend(code, exchange(buckets))
        attended = bring_home(send_across, exchange(backs), rows)
    own_grad, near_grad = grad_part(order, 2, 1, c2, w_output, near_output, first)
    got_grad = swap(near_grad, 1, tensor)
    if dense:
        grad_pieces = exchange(grad_buckets(own_grad, got_grad, send_down, count))
        backs = attend_back(softmax, qkv, grad_pieces)
        grads = bring_home(send_across, exchange(backs), rows)
    else:
        head_grad = (own_grad + got_grad).astype(jnp.bfloat16)
        attended, grads = attend_sparse(home, head_grad, send_rows, receive_slots, owner_segments)

    attended_near = swap(attended, 1, tensor)
    out_far = spread_out(
        order, 2, 1, attended, attended_near, w_output, near_output, jnp.bfloat16
    )
    out_got = swap(out_far, 2, tensor)
    out_own = spread_out(
        order, 0, 0, attended, attended_near, w_output, near_output, jnp.float32
    )

    grads_near = swap(grads, 1, tensor)
    span = width // 2
    grad_got = []
    for start in (0, span):
        part = spread_grad(
            order, 2, 1, grads, grads_near, weights, near_weights, start, span, jnp.bfloat16
        )
        grad_got.append(swap(part, 2, tensor))
    grad_own = spread_grad(
        order, 0, 0, grads, grads_near, weights, near_weights, 0, width, jnp.float32
    )
    row_dot = jnp.sum(
        grads.astype(jnp.float32) * home.astype(jnp.float32), axis=-1, keepdims=True
    )
    row_dot = row_dot + swap(row_dot, 1, tensor)
    row_dot, grad_own = lax.optimization_barrier((row_dot, grad_own))
    row_dot = row_dot + swap(row_dot, 2, tensor)

    wide_in = inputs.astype(jnp.float32)
    layer_out = (wide_in + out_own + out_got.astype(jnp.float32)).astype(jnp.bfloat16)
    scaled = wide_in * inverse_rms
    grad_sum = grad_own + jnp.concatenate(grad_got, axis=1).astype(jnp.float32)
    grad_hat = grad_sum * norm_gain.astype(jnp.float32)
    input_grad = (
        cotangent.astype(jnp.float32) + inverse_rms * (grad_hat - scaled * (row_dot / features))
    ).astype(jnp.bfloat16)
    return (layer_out, input_grad)


def solution(mesh):
    return jax.shard_map(
        on_device,
        mesh=mesh,
        in_specs=(
            P("dp", "tensor"),
            P("dp", "tensor"),
            P("tensor"),
            P(None, "tensor"),
            P(None, "tensor"),
            P(None, "tensor"),
            P("tensor", None),
            P("dp", None),
            P("dp"),
            P("dp"),
        ),
        out_specs=(P("dp", "tensor"), P("dp", "tensor")),
        check_vma=False,
    )
```

```python
import math

import jax
import jax.numpy as jnp
from jax import lax
from jax.experimental import pallas as pl
from jax.experimental.pallas import tpu as pltpu
from jax.sharding import PartitionSpec as P

HEAD_DIM = 128
EPSILON = 1e-05
SCALING = 1.0 / math.sqrt(HEAD_DIM)
CONTRACT_LAST = (((1,), (1,)), ((), ()))
CONTRACT_FIRST = (((0,), (0,)), ((), ()))
VMEM_LIMIT = 24 * 1024 * 1024
VMEM = pl.BlockSpec(memory_space=pltpu.VMEM)
SMEM = pl.BlockSpec(memory_space=pltpu.SMEM)
ANY = pl.BlockSpec(memory_space=pl.ANY)
TILE = 512


def dot(left, right, dims=(((1,), (0,)), ((), ()))):
    return lax.dot_general(left, right, dims, preferred_element_type=jnp.float32)


def call(kernel, name, out_shape, operands, scratch=(), first=SMEM, rest=VMEM):
    single = not isinstance(out_shape, (list, tuple))
    shapes = [out_shape] if single else list(out_shape)
    results = pl.pallas_call(
        kernel,
        out_shape=shapes,
        in_specs=[first] + [rest] * (len(operands) - 1),
        out_specs=[VMEM] * len(shapes),
        scratch_shapes=list(scratch),
        compiler_params=pltpu.CompilerParams(vmem_limit_bytes=VMEM_LIMIT),
        cost_estimate=pl.CostEstimate(flops=1000, bytes_accessed=1000, transcendentals=0),
        name=name,
    )(*operands)
    return results[0] if single else results


def shape(dtype, *sizes):
    return jax.ShapeDtypeStruct(sizes, dtype)


def swap(array, mask, count):
    return lax.ppermute(array, "tensor", [(i, i ^ mask) for i in range(count)])


def block_start(order, slot, width):
    return pl.multiple_of(order[slot] * width, width)


def one_hot(places, rows):
    row = lax.broadcasted_iota(jnp.int32, (rows, places.shape[1]), 0)
    return jnp.where(places == row, 1.0, 0.0).astype(jnp.bfloat16)


def into_slots(send, values):
    chosen = one_hot(send, values.shape[0])
    return dot(chosen, values, CONTRACT_FIRST).astype(jnp.bfloat16)


def prepare_kernel(
    order, w_query, w_key, w_value, w_output, joined, near_joined, near_output, far_output, sems
):
    width = near_joined.shape[0] // 2
    copies = []

    def copy(source, target):
        copies.append(pltpu.make_async_copy(source, target, sems.at[len(copies)]))

    for place, weight in enumerate((w_query, w_key, w_value)):
        columns = pl.ds(place * HEAD_DIM, HEAD_DIM)
        copy(weight, joined.at[:, columns])
        for part, slot in enumerate((1, 3)):
            rows = pl.ds(block_start(order, slot, width), width)
            copy(weight.at[rows, :], near_joined.at[pl.ds(part * width, width), columns])
    for target, slots in ((near_output, (1, 3)), (far_output, (2, 3))):
        for part, slot in enumerate(slots):
            columns = pl.ds(block_start(order, slot, width), width)
            copy(w_output.at[:, columns], target.at[:, pl.ds(part * width, width)])
    for one in copies:
        one.start()
    for one in copies:
        one.wait()


def prepare(order, w_query, w_key, w_value, w_output, width):
    depth, heads = w_query.shape
    low = jnp.bfloat16
    return call(
        prepare_kernel,
        "prepare",
        [
            shape(low, depth, 3 * heads),
            shape(low, 2 * width, 3 * heads),
            shape(low, heads, 2 * width),
            shape(low, heads, 2 * width),
        ],
        (order, w_query, w_key, w_value, w_output),
        scratch=[pltpu.SemaphoreType.DMA((13,))],
        rest=ANY,
    )


def project_rows_kernel(
    order, x0, x1, x2, x3, gain_own, gain_near, weights, send, home, inverse, bucket, total
):
    blocks = (x0, x1, x2, x3)
    width = x0.shape[1]
    squares = 0.0
    for block in blocks:
        wide = block[...].astype(jnp.float32)
        squares = squares + jnp.sum(wide * wide, axis=-1, keepdims=True)
    inverse_rms = lax.rsqrt(squares / (width * len(blocks)) + EPSILON)
    inverse[...] = inverse_rms
    for index, block in enumerate(blocks):
        gain = (gain_own, gain_near)[index % 2][index // 2 : index // 2 + 1, :]
        scaled = block[...].astype(jnp.float32) * inverse_rms
        normed = (scaled * gain.astype(jnp.float32)).astype(jnp.bfloat16)
        part = dot(normed, weights[pl.ds(block_start(order, index, width), width), :])
        total[...] = total[...] + part if index else part
    rounded = total[...].astype(jnp.bfloat16)
    home[...] = rounded
    bucket[...] = into_slots(send[...], rounded)


def project_rows(order, blocks, gains, weights, send):
    rows = blocks[0].shape[0]
    columns = weights.shape[1]
    return call(
        project_rows_kernel,
        "project_rows",
        [
            shape(jnp.bfloat16, rows, columns),
            shape(jnp.float32, rows, 1),
            shape(jnp.bfloat16, send.shape[1], columns),
        ],
        (order, *blocks, *gains, weights, send),
        scratch=[pltpu.VMEM((rows, columns), jnp.float32)],
    )


def grad_part_kernel(slot, half):
    def kernel(order, block, own, near, *rest):
        *before, total, other = rest
        width = block.shape[1]
        here = own[:, pl.ds(block_start(order, slot, width), width)]
        weights = jnp.concatenate([here, near[:, half * width : (half + 1) * width]], axis=0)
        part = dot(block[...], weights, CONTRACT_LAST)
        heads = own.shape[0]
        for place, out in enumerate((total, other)):
            value = part[:, place * heads : (place + 1) * heads]
            out[...] = value + before[place][...] if before else value

    return kernel


def grad_part(order, slot, half, block, w_output, near, before):
    shapes = [shape(jnp.float32, block.shape[0], w_output.shape[0])] * 2
    return call(
        grad_part_kernel(slot, half), "grad_part", shapes, (order, block, w_output, near, *before)
    )


def grad_bucket_kernel(total, other, send, bucket):
    bucket[...] = into_slots(send[...], (total[...] + other[...]).astype(jnp.bfloat16))


def grad_bucket(total, other, send):
    out = shape(jnp.bfloat16, send.shape[1], total.shape[1])
    return call(grad_bucket_kernel, "grad_bucket", out, (total, other, send), first=VMEM)


def balanced(receive, moved):
    chosen = one_hot(receive, moved.shape[0])
    return dot(chosen, moved, CONTRACT_FIRST).astype(jnp.bfloat16)


def thirds(rows):
    return (rows[:, :HEAD_DIM], rows[:, HEAD_DIM : 2 * HEAD_DIM], rows[:, 2 * HEAD_DIM :])


def attend_kernel(moved, receive, segments, softmax, attended, qkv):
    rows = balanced(receive[...], moved[...])
    qkv[...] = rows
    queries, key_rows, value_rows = thirds(rows)
    count = rows.shape[0]
    down = lax.broadcasted_iota(jnp.int32, (count, count), 0)
    across = lax.broadcasted_iota(jnp.int32, (count, count), 1)
    stays = segments[...]
    own_stay = jnp.sum(jnp.where(down == across, stays, 0), axis=1, keepdims=True)
    allowed = (own_stay == stays) & (across <= down)
    scores = jnp.where(allowed, dot(queries, key_rows, CONTRACT_LAST) * SCALING, -1e30)
    raised = jnp.exp(scores - jnp.max(scores, axis=-1, keepdims=True))
    softmax_out = raised / jnp.sum(raised, axis=-1, keepdims=True)
    softmax[...] = softmax_out
    attended[...] = dot(softmax_out.astype(jnp.bfloat16), value_rows).astype(jnp.bfloat16)


def attend(moved, receive, segments):
    rows = receive.shape[1]
    return call(
        attend_kernel,
        "attend",
        [
            shape(jnp.float32, rows, rows),
            shape(jnp.bfloat16, rows, HEAD_DIM),
            shape(jnp.bfloat16, rows, moved.shape[1]),
        ],
        (moved, receive, segments),
        first=VMEM,
    )


def attend_back_kernel(softmax, attended, qkv, moved, receive, back):
    queries, key_rows, value_rows = thirds(qkv[...])
    head_grad = balanced(receive[...], moved[...])
    softmax_out = softmax[...]
    low_weights = softmax_out.astype(jnp.bfloat16)
    grad_value = dot(low_weights, head_grad, CONTRACT_FIRST).astype(jnp.bfloat16)
    grad_probs = dot(head_grad, value_rows, CONTRACT_LAST)
    inner = jnp.sum(softmax_out * grad_probs, axis=-1, keepdims=True)
    grad_scores = (softmax_out * (grad_probs - inner) * SCALING).astype(jnp.bfloat16)
    grad_query = dot(grad_scores, key_rows).astype(jnp.bfloat16)
    grad_key = dot(grad_scores, queries, CONTRACT_FIRST).astype(jnp.bfloat16)
    results = jnp.concatenate([grad_query, grad_key, grad_value, attended[...]], axis=1)
    chosen = one_hot(receive[...], back.shape[0])
    back[...] = dot(chosen, results).astype(jnp.bfloat16)


def attend_back(softmax, attended, qkv, moved, receive):
    out = shape(jnp.bfloat16, moved.shape[0], 4 * HEAD_DIM)
    operands = (softmax, attended, qkv, moved, receive)
    return call(attend_back_kernel, "attend_back", out, operands, first=VMEM)


def bring_home_kernel(moved, send, home, results, row_dot):
    chosen = one_hot(send[...], results.shape[0])
    rows = dot(chosen, moved[...])
    results[...] = rows.astype(jnp.bfloat16)
    product = rows[:, : 3 * HEAD_DIM] * home[...].astype(jnp.float32)
    row_dot[...] = jnp.sum(product, axis=-1, keepdims=True)


def bring_home(moved, send, home):
    rows = home.shape[0]
    shapes = [shape(jnp.bfloat16, rows, 4 * HEAD_DIM), shape(jnp.float32, rows, 1)]
    return call(bring_home_kernel, "bring_home", shapes, (moved, send, home), first=VMEM)


def spread_kernel(slot, half):
    def kernel(order, own, near, weights, near_weights, out):
        width = out.shape[1]
        first = block_start(order, slot, width)
        own_grads = own[:, : 3 * HEAD_DIM]
        near_grads = near[:, : 3 * HEAD_DIM]
        for start in range(0, width, TILE):
            total = dot(own_grads, weights[pl.ds(first + start, TILE), :], CONTRACT_LAST)
            here = near_weights[half * width + start : half * width + start + TILE, :]
            total = total + dot(near_grads, here, CONTRACT_LAST)
            out[:, start : start + TILE] = total.astype(out.dtype)

    return kernel


def spread(order, slot, half, own, near, weights, near_weights, dtype):
    out = shape(dtype, own.shape[0], near_weights.shape[0] // 2)
    operands = (order, own, near, weights, near_weights)
    return call(spread_kernel(slot, half), "spread", out, operands)


def finish_out_kernel(order, inputs, own, near, far, w_own, w_near, w_far, w_last, out):
    width = inputs.shape[1]
    first = block_start(order, 0, width)
    last = slice(3 * HEAD_DIM, None)
    rows = (own[:, last], near[:, last], far[:, :HEAD_DIM], far[:, HEAD_DIM:])
    for start in range(0, width, TILE):
        tile = slice(start, start + TILE)
        total = dot(rows[0], w_own[:, pl.ds(first + start, TILE)])
        for left, weight in zip(rows[1:], (w_near, w_far, w_last)):
            total = total + dot(left, weight[:, tile])
        out[:, tile] = (inputs[:, tile].astype(jnp.float32) + total).astype(jnp.bfloat16)


def finish_grad_kernel(
    inputs, cotangent, gain, inverse, own, got, dot_own, dot_far, out
):
    features = 4 * inputs.shape[1]
    mean_dot = (dot_own[...] + dot_far[...]) / features
    inverse_rms = inverse[...]
    for start in range(0, inputs.shape[1], TILE):
        tile = slice(start, start + TILE)
        grad_normed = own[:, tile] + got[:, tile].astype(jnp.float32)
        grad_hat = grad_normed * gain[:, tile].astype(jnp.float32)
        scaled = inputs[:, tile].astype(jnp.float32) * inverse_rms
        change = inverse_rms * (grad_hat - scaled * mean_dot)
        out[:, tile] = (cotangent[:, tile].astype(jnp.float32) + change).astype(jnp.bfloat16)


def move(bucket):
    return lax.all_to_all(bucket, "dp", split_axis=0, concat_axis=0, tiled=True)


def after(array, *others):
    return lax.optimization_barrier((array, *others))[0]


def on_device(
    inputs,
    cotangent,
    norm_gain,
    w_query,
    w_key,
    w_value,
    w_output,
    send_rows,
    receive_slots,
    owner_segments,
):
    rows, width = inputs.shape
    tensor = lax.axis_size("tensor")
    order = lax.axis_index("tensor").astype(jnp.int32) ^ jnp.arange(4, dtype=jnp.int32)
    receive = receive_slots.reshape(1, rows)
    segments = owner_segments.reshape(1, rows)
    gain = norm_gain.reshape(1, width)

    gain2 = swap(gain, 2, tensor)
    x2 = swap(inputs, 2, tensor)
    x1 = swap(inputs, 1, tensor)
    c2 = swap(after(cotangent, gain2), 2, tensor)
    gain_own = jnp.concatenate([gain, gain2], axis=0)
    gain_near = swap(gain_own, 1, tensor)
    joined, near_joined, near_output, far_output = prepare(
        order, w_query, w_key, w_value, w_output, width
    )
    x3 = swap(x2, 1, tensor)
    near_output = swap(after(near_output, x2), 1, tensor)
    near_joined = swap(after(near_joined, x2), 1, tensor)

    home, inverse_rms, bucket = project_rows(
        order, (inputs, x1, x2, x3), (gain_own, gain_near), joined, send_rows
    )
    far_output = swap(after(far_output, home), 2, tensor)
    softmax, attended, qkv = attend(move(bucket), receive, segments)

    first = grad_part(order, 0, 0, cotangent, w_output, near_output, ())
    own_grad, near_grad = grad_part(order, 2, 1, c2, w_output, near_output, first)
    got_grad = swap(near_grad, 1, tensor)
    bucket = grad_bucket(own_grad, got_grad, send_rows)
    back = attend_back(softmax, attended, qkv, move(bucket), receive)
    own, row_dot = bring_home(move(back), send_rows, home)

    near = swap(own, 1, tensor)
    far_part = spread(order, 2, 1, own, near, joined, near_joined, jnp.bfloat16)
    grad_got = swap(far_part, 2, tensor)
    grad_own = spread(order, 0, 0, own, near, joined, near_joined, jnp.float32)

    last = slice(3 * HEAD_DIM, None)
    far = swap(jnp.concatenate([own[:, last], near[:, last]], axis=1), 2, tensor)
    last_output = swap(far_output[:, width:], 1, tensor)
    layer_out = call(
        finish_out_kernel,
        "finish_out",
        shape(jnp.bfloat16, rows, width),
        (order, inputs, own, near, far, w_output, near_output, far_output, last_output),
    )
    row_dot = row_dot + swap(row_dot, 1, tensor)
    row_dot_far = swap(row_dot, 2, tensor)
    input_grad = call(
        finish_grad_kernel,
        "finish_grad",
        shape(jnp.bfloat16, rows, width),
        (inputs, cotangent, gain, inverse_rms, grad_own, grad_got, row_dot, row_dot_far),
        first=VMEM,
    )
    return (layer_out, input_grad)


def solution(mesh):
    return jax.shard_map(
        on_device,
        mesh=mesh,
        in_specs=(
            P("dp", "tensor"),
            P("dp", "tensor"),
            P("tensor"),
            P(None, "tensor"),
            P(None, "tensor"),
            P(None, "tensor"),
            P("tensor", None),
            P("dp", None),
            P("dp"),
            P("dp"),
        ),
        out_specs=(P("dp", "tensor"), P("dp", "tensor")),
        check_vma=False,
    )
```

```python
import math

import jax
import jax.numpy as jnp
from jax import lax
from jax.experimental import pallas as pl
from jax.experimental.pallas import tpu as pltpu
from jax.sharding import PartitionSpec as P

HEAD_DIM = 128
EPSILON = 1e-05
SCALING = 1.0 / math.sqrt(HEAD_DIM)
CONTRACT_LAST = (((1,), (1,)), ((), ()))
CONTRACT_FIRST = (((0,), (0,)), ((), ()))
VMEM_LIMIT = 12 * 1024 * 1024
VMEM = pl.BlockSpec(memory_space=pltpu.VMEM)
SMEM = pl.BlockSpec(memory_space=pltpu.SMEM)
TILE = 512


def dot(left, right, dims=(((1,), (0,)), ((), ()))):
    return lax.dot_general(left, right, dims, preferred_element_type=jnp.float32)


def call(kernel, name, out_shape, operands, scratch=(), first=SMEM, rest=VMEM):
    single = not isinstance(out_shape, (list, tuple))
    shapes = [out_shape] if single else list(out_shape)
    results = pl.pallas_call(
        kernel,
        out_shape=shapes,
        in_specs=[first] + [rest] * (len(operands) - 1),
        out_specs=[VMEM] * len(shapes),
        scratch_shapes=list(scratch),
        compiler_params=pltpu.CompilerParams(vmem_limit_bytes=VMEM_LIMIT),
        cost_estimate=pl.CostEstimate(flops=1000, bytes_accessed=1000, transcendentals=0),
        name=name,
    )(*operands)
    return results[0] if single else results


def shape(dtype, *sizes):
    return jax.ShapeDtypeStruct(sizes, dtype)


def swap(array, mask, count):
    return lax.ppermute(array, "tensor", [(i, i ^ mask) for i in range(count)])


def block_start(order, slot, width):
    return pl.multiple_of(order[slot] * width, width)


def one_hot(places, rows):
    row = lax.broadcasted_iota(jnp.int32, (rows, places.shape[1]), 0)
    return jnp.where(places == row, 1.0, 0.0).astype(jnp.bfloat16)


def prepare_kernel(
    order,
    w_query,
    w_key,
    w_value,
    w_output,
    send,
    receive,
    segments,
    own_turned,
    near_turned,
    output_turned,
    near_output,
    far_output,
    send_out,
    receive_out,
    segments_out,
):
    width = near_output.shape[1]
    for target, slots in ((near_output, (1,)), (far_output, (2, 3))):
        for part, slot in enumerate(slots):
            columns = pl.ds(block_start(order, slot, width), width)
            target[:, part * width : (part + 1) * width] = w_output[:, columns]
    for start in range(0, w_output.shape[1], TILE):
        output_turned[start : start + TILE, :] = w_output[:, start : start + TILE].T
    for source, target in ((send, send_out), (receive, receive_out), (segments, segments_out)):
        target[...] = source[...]
    for out, slots in ((own_turned, (0, 2)), (near_turned, (1, 3))):
        for part, slot in enumerate(slots):
            first = block_start(order, slot, width)
            for start in range(0, width, TILE):
                columns = slice(part * width + start, part * width + start + TILE)
                for place, weight in enumerate((w_query, w_key, w_value)):
                    rows = slice(place * HEAD_DIM, (place + 1) * HEAD_DIM)
                    out[rows, columns] = weight[pl.ds(first + start, TILE), :].T


def prepare(order, w_query, w_key, w_value, w_output, send, receive, segments, width):
    heads = w_query.shape[1]
    low = jnp.bfloat16
    return call(
        prepare_kernel,
        "prepare",
        [
            shape(low, 3 * heads, 2 * width),
            shape(low, 3 * heads, 2 * width),
            shape(low, w_output.shape[1], heads),
            shape(low, heads, width),
            shape(low, heads, 2 * width),
            shape(jnp.int32, *send.shape),
            shape(jnp.int32, *receive.shape),
            shape(jnp.int32, *segments.shape),
        ],
        (order, w_query, w_key, w_value, w_output, send, receive, segments),
    )


def sum_squares(block):
    wide = block[...].astype(jnp.float32)
    return jnp.sum(wide * wide, axis=-1, keepdims=True)


def begin_kernel(order, x0, x1, x2, c0, c1, c2, output_turned, squares, part):
    width = x0.shape[1]
    squares[...] = sum_squares(x0) + sum_squares(x1) + sum_squares(x2)
    total = 0.0
    for index, block in enumerate((c0, c1, c2)):
        here = pl.ds(block_start(order, index, width), width)
        total = total + dot(block[...], output_turned[here, :])
    part[...] = total


def begin(order, blocks, output_turned):
    rows = blocks[0].shape[0]
    shapes = [shape(jnp.float32, rows, 1), shape(jnp.float32, rows, HEAD_DIM)]
    return call(begin_kernel, "begin", shapes, (order, *blocks, output_turned))


def project_kernel(
    order,
    x0,
    x1,
    x2,
    x3,
    c3,
    gain_own,
    gain_near,
    w_query,
    w_key,
    w_value,
    output_turned,
    squares,
    part,
    send,
    home,
    inverse,
    bucket,
    total,
):
    blocks = (x0, x1, x2, x3)
    width = x0.shape[1]
    mean = (squares[...] + sum_squares(x3)) / (width * len(blocks))
    inverse_rms = lax.rsqrt(mean + EPSILON)
    inverse[...] = inverse_rms
    here = pl.ds(block_start(order, 3, width), width)
    head_grad = (part[...] + dot(c3[...], output_turned[here, :])).astype(jnp.bfloat16)
    for index, block in enumerate(blocks):
        gain = (gain_own, gain_near)[index % 2][index // 2 : index // 2 + 1, :]
        scaled = block[...].astype(jnp.float32) * inverse_rms
        normed = (scaled * gain.astype(jnp.float32)).astype(jnp.bfloat16)
        here = pl.ds(block_start(order, index, width), width)
        weights = jnp.concatenate([w_query[here, :], w_key[here, :], w_value[here, :]], axis=1)
        product = dot(normed, weights)
        total[...] = total[...] + product if index else product
    rounded = total[...].astype(jnp.bfloat16)
    home[...] = rounded
    chosen = one_hot(send[...], rounded.shape[0])
    split = rounded.shape[1]
    bucket[:, :split] = dot(chosen, rounded, CONTRACT_FIRST).astype(jnp.bfloat16)
    bucket[:, split:] = dot(chosen, head_grad, CONTRACT_FIRST).astype(jnp.bfloat16)


def project(order, blocks, gains, weights, squares, part, send):
    rows = blocks[0].shape[0]
    columns = 3 * HEAD_DIM
    return call(
        project_kernel,
        "project",
        [
            shape(jnp.bfloat16, rows, columns),
            shape(jnp.float32, rows, 1),
            shape(jnp.bfloat16, send.shape[1], columns + HEAD_DIM),
        ],
        (order, *blocks, *gains, *weights, squares, part, send),
        scratch=[pltpu.VMEM((rows, columns), jnp.float32)],
    )


def attend_kernel(moved, receive, segments, back):
    place = one_hot(receive[...], moved.shape[0])
    rows = dot(place, moved[...], CONTRACT_FIRST).astype(jnp.bfloat16)
    queries, key_rows, value_rows, head_grad = (
        rows[:, index * HEAD_DIM : (index + 1) * HEAD_DIM] for index in range(4)
    )
    count = rows.shape[0]
    down = lax.broadcasted_iota(jnp.int32, (count, count), 0)
    across = lax.broadcasted_iota(jnp.int32, (count, count), 1)
    stays = segments[...]
    own_stay = jnp.sum(jnp.where(down == across, stays, 0), axis=1, keepdims=True)
    allowed = (own_stay == stays) & (across <= down)
    scores = jnp.where(allowed, dot(queries, key_rows, CONTRACT_LAST) * SCALING, -1e30)
    raised = jnp.exp(scores - jnp.max(scores, axis=-1, keepdims=True))
    softmax_out = raised / jnp.sum(raised, axis=-1, keepdims=True)
    low_weights = softmax_out.astype(jnp.bfloat16)
    attended = dot(low_weights, value_rows).astype(jnp.bfloat16)
    grad_value = dot(low_weights, head_grad, CONTRACT_FIRST).astype(jnp.bfloat16)
    grad_probs = dot(head_grad, value_rows, CONTRACT_LAST)
    inner = jnp.sum(softmax_out * grad_probs, axis=-1, keepdims=True)
    grad_scores = (softmax_out * (grad_probs - inner) * SCALING).astype(jnp.bfloat16)
    grad_query = dot(grad_scores, key_rows).astype(jnp.bfloat16)
    grad_key = dot(grad_scores, queries, CONTRACT_FIRST).astype(jnp.bfloat16)
    results = jnp.concatenate([grad_query, grad_key, grad_value, attended], axis=1)
    back[...] = dot(place, results).astype(jnp.bfloat16)


def attend(moved, receive, segments):
    out = shape(jnp.bfloat16, *moved.shape)
    return call(attend_kernel, "attend", out, (moved, receive, segments), first=VMEM)


def write_parts(value, out):
    out[...] = jnp.zeros_like(out)
    for place in range(3):
        low = value.astype(jnp.bfloat16)
        out[:, place : place + 1] = low
        value = value - low.astype(jnp.float32)


def read_parts(parts):
    return sum(parts[:, place : place + 1].astype(jnp.float32) for place in (2, 1, 0))


def bring_home_kernel(moved, send, home, results):
    chosen = one_hot(send[...], results.shape[0])
    rows = dot(chosen, moved[...])
    results[:, : 4 * HEAD_DIM] = rows.astype(jnp.bfloat16)
    product = rows[:, : 3 * HEAD_DIM] * home[...].astype(jnp.float32)
    row_dot = jnp.sum(product, axis=-1, keepdims=True)
    write_parts(row_dot, results.at[:, 4 * HEAD_DIM :])


def bring_home(moved, send, home):
    out = shape(jnp.bfloat16, home.shape[0], 5 * HEAD_DIM)
    return call(bring_home_kernel, "bring_home", out, (moved, send, home), first=VMEM)


def spread_into(own, near, weights, near_weights, first, out, place):
    own_grads = own[:, : 3 * HEAD_DIM]
    near_grads = near[:, : 3 * HEAD_DIM]
    for start in range(0, out.shape[1] - place, TILE):
        columns = slice(first + start, first + start + TILE)
        total = dot(own_grads, weights[:, columns]) + dot(near_grads, near_weights[:, columns])
        out[:, place + start : place + start + TILE] = total.astype(out.dtype)


def spread_far_kernel(own, near, weights, near_weights, out):
    width = weights.shape[1] // 2
    write_parts(
        read_parts(own[:, 4 * HEAD_DIM :]) + read_parts(near[:, 4 * HEAD_DIM :]),
        out.at[:, :HEAD_DIM],
    )
    attended = slice(3 * HEAD_DIM, 4 * HEAD_DIM)
    out[:, HEAD_DIM : 2 * HEAD_DIM] = own[:, attended]
    out[:, 2 * HEAD_DIM : 3 * HEAD_DIM] = near[:, attended]
    spread_into(own, near, weights, near_weights, width, out, 3 * HEAD_DIM)


def spread_rest_kernel(own, near, weights, near_weights, out):
    width = weights.shape[1] // 2
    spread_into(own, near, weights, near_weights, width + width // 2, out, 0)


def spread_own_kernel(own, near, weights, near_weights, out):
    spread_into(own, near, weights, near_weights, 0, out, 0)


def finish_out_kernel(order, inputs, own, near, far, w_own, w_near, w_far, w_last, out):
    width = inputs.shape[1]
    first = block_start(order, 0, width)
    attended = slice(3 * HEAD_DIM, 4 * HEAD_DIM)
    rows = (
        own[:, attended],
        near[:, attended],
        far[:, HEAD_DIM : 2 * HEAD_DIM],
        far[:, 2 * HEAD_DIM : 3 * HEAD_DIM],
    )
    for start in range(0, width, TILE):
        tile = slice(start, start + TILE)
        total = dot(rows[0], w_own[:, pl.ds(first + start, TILE)])
        for left, weight in zip(rows[1:], (w_near, w_far, w_last)):
            total = total + dot(left, weight[:, tile])
        out[:, tile] = (inputs[:, tile].astype(jnp.float32) + total).astype(jnp.bfloat16)


def finish_grad_kernel(inputs, cotangent, gain, inverse, own, near, grad_own, far, rest, out):
    width = inputs.shape[1]
    row_dot = read_parts(own[:, 4 * HEAD_DIM :]) + read_parts(near[:, 4 * HEAD_DIM :])
    mean_dot = (row_dot + read_parts(far[:, :HEAD_DIM])) / (4 * width)
    inverse_rms = inverse[...]
    for start in range(0, width, TILE):
        tile = slice(start, start + TILE)
        if start < width // 2:
            got = far[:, 3 * HEAD_DIM + start : 3 * HEAD_DIM + start + TILE]
        else:
            got = rest[:, start - width // 2 : start - width // 2 + TILE]
        grad_normed = grad_own[:, tile] + got.astype(jnp.float32)
        grad_hat = grad_normed * gain[:, tile].astype(jnp.float32)
        scaled = inputs[:, tile].astype(jnp.float32) * inverse_rms
        change = inverse_rms * (grad_hat - scaled * mean_dot)
        out[:, tile] = (cotangent[:, tile].astype(jnp.float32) + change).astype(jnp.bfloat16)


def move(bucket):
    return lax.all_to_all(bucket, "dp", split_axis=0, concat_axis=0, tiled=True)


def after(array, *others):
    return lax.optimization_barrier((array, *others))[0]


def on_device(
    inputs,
    cotangent,
    norm_gain,
    w_query,
    w_key,
    w_value,
    w_output,
    send_rows,
    receive_slots,
    owner_segments,
):
    rows, width = inputs.shape
    tensor = lax.axis_size("tensor")
    low = jnp.bfloat16
    order = lax.axis_index("tensor").astype(jnp.int32) ^ jnp.arange(4, dtype=jnp.int32)
    gain = norm_gain.reshape(1, width)

    x2 = swap(inputs, 2, tensor)
    c2 = swap(cotangent, 2, tensor)
    gain2 = swap(gain, 2, tensor)
    x1 = swap(inputs, 1, tensor)
    c1 = swap(cotangent, 1, tensor)
    weights = (w_query, w_key, w_value)
    own_turned, near_turned, output_turned, near_output, far_output, send, receive, segments = (
        prepare(
            order,
            *weights,
            w_output,
            send_rows,
            receive_slots.reshape(1, rows),
            owner_segments.reshape(1, rows),
            width,
        )
    )
    x2, c2, gain2, segments = lax.optimization_barrier((x2, c2, gain2, segments))
    x3 = swap(x2, 1, tensor)
    c3 = swap(c2, 1, tensor)
    gain_own = jnp.concatenate([gain, gain2], axis=0)
    gain_near = swap(gain_own, 1, tensor)

    squares, part = begin(order, (inputs, x1, x2, cotangent, c1, c2), output_turned)
    home, inverse_rms, bucket = project(
        order,
        (inputs, x1, x2, x3, c3),
        (gain_own, gain_near),
        (*weights, output_turned),
        squares,
        part,
        send,
    )
    near_output = swap(after(near_output, home), 1, tensor)
    near_turned = swap(after(near_turned, home), 1, tensor)
    far_output = swap(after(far_output, home), 2, tensor)
    last_output = swap(far_output[:, width:], 1, tensor)
    own = bring_home(move(attend(move(bucket), receive, segments)), send, home)

    near = swap(own, 1, tensor)
    sides = (own, near, own_turned, near_turned)
    half = width // 2
    far = call(
        spread_far_kernel,
        "spread_far",
        shape(low, rows, 3 * HEAD_DIM + half),
        sides,
        first=VMEM,
    )
    far = swap(far, 2, tensor)
    rest = call(spread_rest_kernel, "spread_rest", shape(low, rows, half), sides, first=VMEM)
    rest = swap(rest, 2, tensor)
    grad_own = call(
        spread_own_kernel, "spread_own", shape(jnp.float32, rows, width), sides, first=VMEM
    )
    layer_out = call(
        finish_out_kernel,
        "finish_out",
        shape(low, rows, width),
        (order, inputs, own, near, far, w_output, near_output, far_output, last_output),
    )
    input_grad = call(
        finish_grad_kernel,
        "finish_grad",
        shape(low, rows, width),
        (inputs, cotangent, gain, inverse_rms, own, near, grad_own, far, rest),
        first=VMEM,
    )
    return (layer_out, input_grad)


def solution(mesh):
    return jax.shard_map(
        on_device,
        mesh=mesh,
        in_specs=(
            P("dp", "tensor"),
            P("dp", "tensor"),
            P("tensor"),
            P(None, "tensor"),
            P(None, "tensor"),
            P(None, "tensor"),
            P("tensor", None),
            P("dp", None),
            P("dp"),
            P("dp"),
        ),
        out_specs=(P("dp", "tensor"), P("dp", "tensor")),
        check_vma=False,
    )
```

```python
import math

import jax
import jax.numpy as jnp
from jax import lax
from jax.experimental import pallas as pl
from jax.experimental.pallas import tpu as pltpu
from jax.sharding import PartitionSpec as P

HEAD_DIM = 128
EPSILON = 1e-05
SCALING = 1.0 / math.sqrt(HEAD_DIM)
CONTRACT_LAST = (((1,), (1,)), ((), ()))
CONTRACT_FIRST = (((0,), (0,)), ((), ()))
VMEM_LIMIT = 12 * 1024 * 1024
VMEM = pl.BlockSpec(memory_space=pltpu.VMEM)
SMEM = pl.BlockSpec(memory_space=pltpu.SMEM)
TILE = 512


def dot(left, right, dims=(((1,), (0,)), ((), ()))):
    return lax.dot_general(left, right, dims, preferred_element_type=jnp.float32)


def call(kernel, name, out_shape, operands, scratch=(), first=SMEM, rest=VMEM):
    single = not isinstance(out_shape, (list, tuple))
    shapes = [out_shape] if single else list(out_shape)
    results = pl.pallas_call(
        kernel,
        out_shape=shapes,
        in_specs=[first] + [rest] * (len(operands) - 1),
        out_specs=[VMEM] * len(shapes),
        scratch_shapes=list(scratch),
        compiler_params=pltpu.CompilerParams(vmem_limit_bytes=VMEM_LIMIT),
        cost_estimate=pl.CostEstimate(flops=1000, bytes_accessed=1000, transcendentals=0),
        name=name,
    )(*operands)
    return results[0] if single else results


def shape(dtype, *sizes):
    return jax.ShapeDtypeStruct(sizes, dtype)


def swap(array, mask, count):
    return lax.ppermute(array, "tensor", [(i, i ^ mask) for i in range(count)])


def block_start(order, slot, width):
    return pl.multiple_of(order[slot] * width, width)


def one_hot(places, rows):
    row = lax.broadcasted_iota(jnp.int32, (rows, places.shape[1]), 0)
    return jnp.where(places == row, 1.0, 0.0).astype(jnp.bfloat16)


def prepare_kernel(
    order,
    w_query,
    w_key,
    w_value,
    w_output,
    send,
    receive,
    segments,
    own_turned,
    near_turned,
    output_turned,
    own_here,
    near_here,
    far_output,
    send_out,
    receive_out,
    segments_out,
):
    width = near_here.shape[1]
    far_left, far_right = far_output.at[:, :width], far_output.at[:, width:]
    for slot, target in enumerate((own_here, near_here, far_left, far_right)):
        target[...] = w_output[:, pl.ds(block_start(order, slot, width), width)]
    for start in range(0, w_output.shape[1], TILE):
        output_turned[start : start + TILE, :] = w_output[:, start : start + TILE].T
    for source, target in ((send, send_out), (receive, receive_out), (segments, segments_out)):
        target[...] = source[...]
    for out, slots in ((own_turned, (0, 2)), (near_turned, (1, 3))):
        for part, slot in enumerate(slots):
            first = block_start(order, slot, width)
            for start in range(0, width, TILE):
                columns = slice(part * width + start, part * width + start + TILE)
                for place, weight in enumerate((w_query, w_key, w_value)):
                    rows = slice(place * HEAD_DIM, (place + 1) * HEAD_DIM)
                    out[rows, columns] = weight[pl.ds(first + start, TILE), :].T


def prepare(order, w_query, w_key, w_value, w_output, send, receive, segments, width):
    heads = w_query.shape[1]
    low = jnp.bfloat16
    return call(
        prepare_kernel,
        "prepare",
        [
            shape(low, 3 * heads, 2 * width),
            shape(low, 3 * heads, 2 * width),
            shape(low, w_output.shape[1], heads),
            shape(low, heads, width),
            shape(low, heads, width),
            shape(low, heads, 2 * width),
            shape(jnp.int32, *send.shape),
            shape(jnp.int32, *receive.shape),
            shape(jnp.int32, *segments.shape),
        ],
        (order, w_query, w_key, w_value, w_output, send, receive, segments),
    )


def sum_squares(block):
    wide = block[...].astype(jnp.float32)
    return jnp.sum(wide * wide, axis=-1, keepdims=True)


def begin_kernel(order, x0, x1, c0, c1, output_turned, squares, part):
    width = x0.shape[1]
    squares[...] = sum_squares(x0) + sum_squares(x1)
    total = 0.0
    for index, block in enumerate((c0, c1)):
        here = pl.ds(block_start(order, index, width), width)
        total = total + dot(block[...], output_turned[here, :])
    part[...] = total


def go_on_kernel(order, x2, c2, output_turned, squares_in, part_in, squares, part):
    width = x2.shape[1]
    here = pl.ds(block_start(order, 2, width), width)
    part[...] = part_in[...] + dot(c2[...], output_turned[here, :])
    squares[...] = squares_in[...] + sum_squares(x2)


def begin(kernel, name, *operands):
    rows = operands[1].shape[0]
    shapes = [shape(jnp.float32, rows, 1), shape(jnp.float32, rows, HEAD_DIM)]
    return call(kernel, name, shapes, operands)


def project_kernel(
    order,
    x0,
    x1,
    x2,
    x3,
    c3,
    gain_own,
    gain_near,
    w_query,
    w_key,
    w_value,
    output_turned,
    squares,
    part,
    send,
    home,
    inverse,
    bucket,
    total,
):
    blocks = (x0, x1, x2, x3)
    width = x0.shape[1]
    mean = (squares[...] + sum_squares(x3)) / (width * len(blocks))
    inverse_rms = lax.rsqrt(mean + EPSILON)
    inverse[...] = inverse_rms
    here = pl.ds(block_start(order, 3, width), width)
    head_grad = (part[...] + dot(c3[...], output_turned[here, :])).astype(jnp.bfloat16)
    for index, block in enumerate(blocks):
        gain = (gain_own, gain_near)[index % 2][index // 2 : index // 2 + 1, :]
        scaled = block[...].astype(jnp.float32) * inverse_rms
        normed = (scaled * gain.astype(jnp.float32)).astype(jnp.bfloat16)
        here = pl.ds(block_start(order, index, width), width)
        weights = jnp.concatenate([w_query[here, :], w_key[here, :], w_value[here, :]], axis=1)
        product = dot(normed, weights)
        total[...] = total[...] + product if index else product
    rounded = total[...].astype(jnp.bfloat16)
    home[...] = rounded
    chosen = one_hot(send[...], rounded.shape[0])
    split = rounded.shape[1]
    bucket[:, :split] = dot(chosen, rounded, CONTRACT_FIRST).astype(jnp.bfloat16)
    bucket[:, split:] = dot(chosen, head_grad, CONTRACT_FIRST).astype(jnp.bfloat16)


def project(order, blocks, gains, weights, squares, part, send):
    rows = blocks[0].shape[0]
    columns = 3 * HEAD_DIM
    return call(
        project_kernel,
        "project",
        [
            shape(jnp.bfloat16, rows, columns),
            shape(jnp.float32, rows, 1),
            shape(jnp.bfloat16, send.shape[1], columns + HEAD_DIM),
        ],
        (order, *blocks, *gains, *weights, squares, part, send),
        scratch=[pltpu.VMEM((rows, columns), jnp.float32)],
    )


def attend_kernel(moved, receive, segments, back):
    place = one_hot(receive[...], moved.shape[0])
    rows = dot(place, moved[...], CONTRACT_FIRST).astype(jnp.bfloat16)
    queries, key_rows, value_rows, head_grad = (
        rows[:, index * HEAD_DIM : (index + 1) * HEAD_DIM] for index in range(4)
    )
    count = rows.shape[0]
    down = lax.broadcasted_iota(jnp.int32, (count, count), 0)
    across = lax.broadcasted_iota(jnp.int32, (count, count), 1)
    stays = segments[...]
    own_stay = jnp.sum(jnp.where(down == across, stays, 0), axis=1, keepdims=True)
    allowed = (own_stay == stays) & (across <= down)
    scores = jnp.where(allowed, dot(queries, key_rows, CONTRACT_LAST) * SCALING, -1e30)
    raised = jnp.exp(scores - jnp.max(scores, axis=-1, keepdims=True))
    softmax_out = raised / jnp.sum(raised, axis=-1, keepdims=True)
    low_weights = softmax_out.astype(jnp.bfloat16)
    attended = dot(low_weights, value_rows).astype(jnp.bfloat16)
    grad_value = dot(low_weights, head_grad, CONTRACT_FIRST).astype(jnp.bfloat16)
    grad_probs = dot(head_grad, value_rows, CONTRACT_LAST)
    inner = jnp.sum(softmax_out * grad_probs, axis=-1, keepdims=True)
    grad_scores = (softmax_out * (grad_probs - inner) * SCALING).astype(jnp.bfloat16)
    grad_query = dot(grad_scores, key_rows).astype(jnp.bfloat16)
    grad_key = dot(grad_scores, queries, CONTRACT_FIRST).astype(jnp.bfloat16)
    results = jnp.concatenate([grad_query, grad_key, grad_value, attended], axis=1)
    back[...] = dot(place, results).astype(jnp.bfloat16)


def attend(moved, receive, segments):
    out = shape(jnp.bfloat16, *moved.shape)
    return call(attend_kernel, "attend", out, (moved, receive, segments), first=VMEM)


def write_parts(value, out):
    out[...] = jnp.zeros_like(out)
    for place in range(3):
        low = value.astype(jnp.bfloat16)
        out[:, place : place + 1] = low
        value = value - low.astype(jnp.float32)


def read_parts(parts):
    return sum(parts[:, place : place + 1].astype(jnp.float32) for place in (2, 1, 0))


def bring_home_kernel(moved, send, home, results):
    chosen = one_hot(send[...], results.shape[0])
    rows = dot(chosen, moved[...])
    results[:, : 4 * HEAD_DIM] = rows.astype(jnp.bfloat16)
    product = rows[:, : 3 * HEAD_DIM] * home[...].astype(jnp.float32)
    row_dot = jnp.sum(product, axis=-1, keepdims=True)
    write_parts(row_dot, results.at[:, 4 * HEAD_DIM :])


def bring_home(moved, send, home):
    out = shape(jnp.bfloat16, home.shape[0], 5 * HEAD_DIM)
    return call(bring_home_kernel, "bring_home", out, (moved, send, home), first=VMEM)


def spread_into(own, near, weights, near_weights, first, out, place, held, total, sem):
    span = held.shape[1]
    copy = pltpu.make_async_copy(near_weights.at[:, pl.ds(first, span)], held, sem)
    copy.start()
    own_grads = own[:, : 3 * HEAD_DIM]
    near_grads = near[:, : 3 * HEAD_DIM]
    for start in range(0, span, TILE):
        columns = slice(first + start, first + start + TILE)
        total[:, start : start + TILE] = dot(own_grads, weights[:, columns])
    copy.wait()
    for start in range(0, span, TILE):
        tile = slice(start, start + TILE)
        result = total[:, tile] + dot(near_grads, held[:, tile])
        out[:, place + start : place + start + TILE] = result.astype(out.dtype)


def spread_far_kernel(own, near, weights, near_weights, out, *scratch):
    width = weights.shape[1] // 2
    write_parts(
        read_parts(own[:, 4 * HEAD_DIM :]) + read_parts(near[:, 4 * HEAD_DIM :]),
        out.at[:, :HEAD_DIM],
    )
    attended = slice(3 * HEAD_DIM, 4 * HEAD_DIM)
    out[:, HEAD_DIM : 2 * HEAD_DIM] = own[:, attended]
    out[:, 2 * HEAD_DIM : 3 * HEAD_DIM] = near[:, attended]
    spread_into(own, near, weights, near_weights, width, out, 3 * HEAD_DIM, *scratch)


def spread_rest_kernel(own, near, weights, near_weights, out, *scratch):
    width = weights.shape[1] // 2
    spread_into(own, near, weights, near_weights, width + width // 2, out, 0, *scratch)


def spread_own_kernel(own, near, weights, near_weights, out, *scratch):
    spread_into(own, near, weights, near_weights, 0, out, 0, *scratch)


def spread(kernel, name, out, span, operands):
    rows, depth = operands[0].shape[0], operands[2].shape[0]
    return pl.pallas_call(
        kernel,
        out_shape=out,
        in_specs=[VMEM] * 3 + [pl.BlockSpec(memory_space=pl.ANY)],
        out_specs=VMEM,
        scratch_shapes=[
            pltpu.VMEM((depth, span), jnp.bfloat16),
            pltpu.VMEM((rows, span), jnp.float32),
            pltpu.SemaphoreType.DMA,
        ],
        compiler_params=pltpu.CompilerParams(vmem_limit_bytes=VMEM_LIMIT),
        cost_estimate=pl.CostEstimate(flops=1000, bytes_accessed=1000, transcendentals=0),
        name=name,
    )(*operands)


def finish_out_kernel(inputs, own, near, far, w_own, w_near, w_far, w_last, out):
    width = inputs.shape[1]
    attended = slice(3 * HEAD_DIM, 4 * HEAD_DIM)
    rows = jnp.concatenate(
        [own[:, attended], near[:, attended], far[:, HEAD_DIM : 3 * HEAD_DIM]], axis=1
    )
    for start in range(0, width, TILE):
        tile = slice(start, start + TILE)
        second = slice(width + start, width + start + TILE)
        stacked = [w_own[:, tile], w_near[:, tile], w_far[:, tile], w_last[:, second]]
        total = dot(rows, jnp.concatenate(stacked, axis=0))
        out[:, tile] = (inputs[:, tile].astype(jnp.float32) + total).astype(jnp.bfloat16)


def finish_grad_kernel(inputs, cotangent, gain, inverse, own, near, grad_own, far, rest, out):
    width = inputs.shape[1]
    row_dot = read_parts(own[:, 4 * HEAD_DIM :]) + read_parts(near[:, 4 * HEAD_DIM :])
    mean_dot = (row_dot + read_parts(far[:, :HEAD_DIM])) / (4 * width)
    inverse_rms = inverse[...]
    for start in range(0, width, TILE):
        tile = slice(start, start + TILE)
        if start < width // 2:
            got = far[:, 3 * HEAD_DIM + start : 3 * HEAD_DIM + start + TILE]
        else:
            got = rest[:, start - width // 2 : start - width // 2 + TILE]
        grad_normed = grad_own[:, tile] + got.astype(jnp.float32)
        grad_hat = grad_normed * gain[:, tile].astype(jnp.float32)
        scaled = inputs[:, tile].astype(jnp.float32) * inverse_rms
        change = inverse_rms * (grad_hat - scaled * mean_dot)
        out[:, tile] = (cotangent[:, tile].astype(jnp.float32) + change).astype(jnp.bfloat16)


def move(bucket):
    return lax.all_to_all(bucket, "dp", split_axis=0, concat_axis=0, tiled=True)


def after(array, *others):
    return lax.optimization_barrier((array, *others))[0]


def on_device(
    inputs,
    cotangent,
    norm_gain,
    w_query,
    w_key,
    w_value,
    w_output,
    send_rows,
    receive_slots,
    owner_segments,
):
    rows, width = inputs.shape
    tensor = lax.axis_size("tensor")
    low = jnp.bfloat16
    order = lax.axis_index("tensor").astype(jnp.int32) ^ jnp.arange(4, dtype=jnp.int32)
    gain = norm_gain.reshape(1, width)

    x2 = swap(inputs, 2, tensor)
    c2 = swap(cotangent, 2, tensor)
    gain2 = swap(gain, 2, tensor)
    x1 = swap(inputs, 1, tensor)
    c1 = swap(cotangent, 1, tensor)
    weights = (w_query, w_key, w_value)
    (own_turned, near_turned, output_turned, own_here, near_here, far_output, *indices) = prepare(
        order,
        *weights,
        w_output,
        send_rows,
        receive_slots.reshape(1, rows),
        owner_segments.reshape(1, rows),
        width,
    )
    send, receive, segments = indices
    squares, part = begin(
        begin_kernel, "begin", order, inputs, x1, cotangent, c1, output_turned
    )
    x2, c2, gain2, squares, part = lax.optimization_barrier((x2, c2, gain2, squares, part))
    x3 = swap(x2, 1, tensor)
    c3 = swap(c2, 1, tensor)
    gain_own = jnp.concatenate([gain, gain2], axis=0)
    gain_near = swap(gain_own, 1, tensor)
    squares, part = begin(go_on_kernel, "go_on", order, x2, c2, output_turned, squares, part)
    home, inverse_rms, bucket = project(
        order,
        (inputs, x1, x2, x3, c3),
        (gain_own, gain_near),
        (*weights, output_turned),
        squares,
        part,
        send,
    )
    near_turned = swap(after(near_turned, home), 1, tensor)
    far_output = swap(after(far_output, home), 2, tensor)
    back = attend(move(bucket), receive, segments)
    own = bring_home(move(back), send, home)

    near = swap(own, 1, tensor)
    sides = (own, near, own_turned, near_turned)
    half = width // 2
    far_shape = shape(low, rows, 3 * HEAD_DIM + half)
    far_part = spread(spread_far_kernel, "spread_far", far_shape, half, sides)
    far = swap(far_part, 2, tensor)
    sides = (after(own, far_part), *sides[1:])
    rest_part = spread(spread_rest_kernel, "spread_rest", shape(low, rows, half), half, sides)
    rest = swap(rest_part, 2, tensor)
    sides = (after(own, rest_part), *sides[1:])
    own_shape = shape(jnp.float32, rows, width)
    grad_own = spread(spread_own_kernel, "spread_own", own_shape, width, sides)
    near_here = swap(after(near_here, home), 1, tensor)
    last_output = swap(after(far_output, near), 1, tensor)
    layer_out = call(
        finish_out_kernel,
        "finish_out",
        shape(low, rows, width),
        (inputs, own, near, far, own_here, near_here, far_output, last_output),
        first=VMEM,
    )
    rest = after(rest, layer_out)
    input_grad = call(
        finish_grad_kernel,
        "finish_grad",
        shape(low, rows, width),
        (inputs, cotangent, gain, inverse_rms, own, near, grad_own, far, rest),
        first=VMEM,
    )
    return (layer_out, input_grad)


def solution(mesh):
    return jax.shard_map(
        on_device,
        mesh=mesh,
        in_specs=(
            P("dp", "tensor"),
            P("dp", "tensor"),
            P("tensor"),
            P(None, "tensor"),
            P(None, "tensor"),
            P(None, "tensor"),
            P("tensor", None),
            P("dp", None),
            P("dp"),
            P("dp"),
        ),
        out_specs=(P("dp", "tensor"), P("dp", "tensor")),
        check_vma=False,
    )
```

```python
import math

import jax
import jax.numpy as jnp
from jax import lax
from jax.experimental import pallas as pl
from jax.experimental.pallas import tpu as pltpu
from jax.sharding import PartitionSpec as P

HEAD_DIM = 128
EPSILON = 1e-05
SCALING = 1.0 / math.sqrt(HEAD_DIM)
CONTRACT_LAST = (((1,), (1,)), ((), ()))
CONTRACT_FIRST = (((0,), (0,)), ((), ()))
VMEM_LIMIT = 12 * 1024 * 1024
VMEM = pl.BlockSpec(memory_space=pltpu.VMEM)
SMEM = pl.BlockSpec(memory_space=pltpu.SMEM)
TILE = 512
GAIN_ROWS = 16


def dot(left, right, dims=(((1,), (0,)), ((), ()))):
    return lax.dot_general(left, right, dims, preferred_element_type=jnp.float32)


def call(kernel, name, out_shape, operands, scratch=(), first=SMEM, rest=VMEM):
    single = not isinstance(out_shape, (list, tuple))
    shapes = [out_shape] if single else list(out_shape)
    results = pl.pallas_call(
        kernel,
        out_shape=shapes,
        in_specs=[first] + [rest] * (len(operands) - 1),
        out_specs=[VMEM] * len(shapes),
        scratch_shapes=list(scratch),
        compiler_params=pltpu.CompilerParams(vmem_limit_bytes=VMEM_LIMIT),
        cost_estimate=pl.CostEstimate(flops=1000, bytes_accessed=1000, transcendentals=0),
        name=name,
    )(*operands)
    return results[0] if single else results


def shape(dtype, *sizes):
    return jax.ShapeDtypeStruct(sizes, dtype)


def swap(array, mask, count):
    return lax.ppermute(array, "tensor", [(i, i ^ mask) for i in range(count)])


def block_start(order, slot, width):
    return pl.multiple_of(order[slot] * width, width)


def one_hot(places, rows):
    row = lax.broadcasted_iota(jnp.int32, (rows, places.shape[1]), 0)
    return jnp.where(places == row, 1.0, 0.0).astype(jnp.bfloat16)


def prepare_kernel(
    order,
    w_query,
    w_key,
    w_value,
    w_output,
    send,
    receive,
    segments,
    own_turned,
    near_first,
    near_second,
    near_third,
    near_last,
    output_turned,
    own_here,
    far_output,
    send_out,
    receive_out,
    segments_out,
):
    width = own_here.shape[1]
    far_left, far_right = far_output.at[:, :width], far_output.at[:, width:]
    for slot, target in ((0, own_here), (2, far_left), (3, far_right)):
        target[...] = w_output[:, pl.ds(block_start(order, slot, width), width)]
    for index, target in enumerate((near_first, near_second)):
        first = order[1] * width + index * (width // 2)
        columns = pl.ds(pl.multiple_of(first, width // 2), width // 2)
        target[3 * HEAD_DIM :, :] = w_output[:, columns]
    for start in range(0, w_output.shape[1], TILE):
        output_turned[start : start + TILE, :] = w_output[:, start : start + TILE].T
    for source, target in ((send, send_out), (receive, receive_out), (segments, segments_out)):
        target[...] = source[...]
    half = width // 2
    near_parts = ((near_first, near_second), (near_third, near_last))
    for part in range(2):
        own_first = block_start(order, 2 * part, width)
        near_start = block_start(order, 2 * part + 1, width)
        for start in range(0, width, TILE):
            there = near_parts[part][start // half]
            columns = slice(start % half, start % half + TILE)
            for place, weight in enumerate((w_query, w_key, w_value)):
                rows = slice(place * HEAD_DIM, (place + 1) * HEAD_DIM)
                own_columns = slice(part * width + start, part * width + start + TILE)
                own_turned[rows, own_columns] = weight[pl.ds(own_first + start, TILE), :].T
                there[rows, columns] = weight[pl.ds(near_start + start, TILE), :].T


def prepare(order, w_query, w_key, w_value, w_output, send, receive, segments, width):
    heads = w_query.shape[1]
    low = jnp.bfloat16
    return call(
        prepare_kernel,
        "prepare",
        [
            shape(low, 3 * heads, 2 * width),
            *[shape(low, 4 * heads, width // 2)] * 2,
            *[shape(low, 3 * heads, width // 2)] * 2,
            shape(low, w_output.shape[1], heads),
            shape(low, heads, width),
            shape(low, heads, 2 * width),
            shape(jnp.int32, *send.shape),
            shape(jnp.int32, *receive.shape),
            shape(jnp.int32, *segments.shape),
        ],
        (order, w_query, w_key, w_value, w_output, send, receive, segments),
    )


def sum_squares(block):
    wide = block.astype(jnp.float32)
    return jnp.sum(wide * wide, axis=-1, keepdims=True)


def pack_kernel(gain, inputs, out, sem):
    rows = inputs.shape[0]
    copy = pltpu.make_async_copy(inputs, out.at[pl.ds(0, rows), :], sem)
    copy.start()
    out[rows:, :] = jnp.broadcast_to(gain[...], (out.shape[0] - rows, out.shape[1]))
    copy.wait()


def pack(gain, inputs):
    rows, width = inputs.shape
    return call(
        pack_kernel,
        "pack",
        shape(jnp.bfloat16, rows + GAIN_ROWS, width),
        (gain, inputs),
        scratch=[pltpu.SemaphoreType.DMA],
        first=VMEM,
        rest=pl.BlockSpec(memory_space=pl.ANY),
    )


def begin_kernel(order, x0, x1, c0, c1, output_turned, squares, part):
    rows, width = c0.shape
    squares[...] = sum_squares(x0[:rows, :]) + sum_squares(x1[:rows, :])
    total = 0.0
    for index, block in enumerate((c0, c1)):
        here = pl.ds(block_start(order, index, width), width)
        total = total + dot(block[...], output_turned[here, :])
    part[...] = total


def begin(order, x0, x1, c0, c1, output_turned):
    rows = c0.shape[0]
    shapes = [shape(jnp.float32, rows, 1), shape(jnp.float32, rows, HEAD_DIM)]
    operands = (order, x0, x1, c0, c1, output_turned)
    return call(begin_kernel, "begin", shapes, operands)


def go_on_kernel(x2, squares_in, squares, upper, lower):
    rows = squares.shape[0]
    half = upper.shape[0]
    squares[...] = squares_in[...] + sum_squares(x2[:rows, :])
    upper[...] = x2[:half, :]
    lower[...] = x2[half:, :]


def go_on(x2, squares):
    rows, width = squares.shape[0], x2.shape[1]
    shapes = [
        shape(jnp.float32, rows, 1),
        shape(jnp.bfloat16, rows // 2, width),
        shape(jnp.bfloat16, rows // 2 + GAIN_ROWS, width),
    ]
    return call(go_on_kernel, "go_on", shapes, (x2, squares), first=VMEM)


def project_kernel(
    order,
    x0,
    x1,
    x2,
    upper,
    lower,
    w_query,
    w_key,
    w_value,
    squares,
    send,
    home,
    inverse,
    bucket,
    total,
):
    rows, width = home.shape[0], x0.shape[1]
    x3 = jnp.concatenate([upper[...], lower[...]], axis=0)
    mean = (squares[...] + sum_squares(x3[:rows, :])) / (4 * width)
    inverse_rms = lax.rsqrt(mean + EPSILON)
    inverse[...] = inverse_rms
    for index, block in enumerate((x0[...], x1[...], x2[...], x3)):
        scaled = block[:rows, :].astype(jnp.float32) * inverse_rms
        gain = block[rows : rows + 1, :].astype(jnp.float32)
        normed = (scaled * gain).astype(jnp.bfloat16)
        here = pl.ds(block_start(order, index, width), width)
        weights = jnp.concatenate([w_query[here, :], w_key[here, :], w_value[here, :]], axis=1)
        product = dot(normed, weights)
        total[...] = total[...] + product if index else product
    rounded = total[...].astype(jnp.bfloat16)
    home[...] = rounded
    bucket[...] = dot(one_hot(send[...], rows), rounded, CONTRACT_FIRST).astype(jnp.bfloat16)


def project(order, blocks, weights, squares, send):
    rows = squares.shape[0]
    columns = 3 * HEAD_DIM
    return call(
        project_kernel,
        "project",
        [
            shape(jnp.bfloat16, rows, columns),
            shape(jnp.float32, rows, 1),
            shape(jnp.bfloat16, send.shape[1], columns),
        ],
        (order, *blocks, *weights, squares, send),
        scratch=[pltpu.VMEM((rows, columns), jnp.float32)],
    )


def add_grad_kernel(order, c2, output_turned, part_in, part):
    width = c2.shape[1]
    here = pl.ds(block_start(order, 2, width), width)
    part[...] = part_in[...] + dot(c2[...], output_turned[here, :])


def add_grad(order, c2, output_turned, part):
    out = shape(jnp.float32, *part.shape)
    return call(add_grad_kernel, "add_grad", out, (order, c2, output_turned, part))


def fill_kernel(order, c3, output_turned, part, send, attended, bucket):
    rows, width = c3.shape
    here = pl.ds(block_start(order, 3, width), width)
    head_grad = (part[...] + dot(c3[...], output_turned[here, :])).astype(jnp.bfloat16)
    sorted_grad = dot(one_hot(send[...], rows), head_grad, CONTRACT_FIRST)
    bucket[:, :HEAD_DIM] = sorted_grad.astype(jnp.bfloat16)
    bucket[:, HEAD_DIM:] = attended[...]


def fill(order, c3, output_turned, part, send, attended):
    out = shape(jnp.bfloat16, send.shape[1], 2 * HEAD_DIM)
    return call(fill_kernel, "fill", out, (order, c3, output_turned, part, send, attended))


def attend_kernel(moved, receive, segments, softmax, qkv, back):
    place = one_hot(receive[...], moved.shape[0])
    rows = dot(place, moved[...], CONTRACT_FIRST).astype(jnp.bfloat16)
    qkv[...] = rows
    queries, key_rows, value_rows = (
        rows[:, index * HEAD_DIM : (index + 1) * HEAD_DIM] for index in range(3)
    )
    count = rows.shape[0]
    down = lax.broadcasted_iota(jnp.int32, (count, count), 0)
    across = lax.broadcasted_iota(jnp.int32, (count, count), 1)
    stays = segments[...]
    own_stay = jnp.sum(jnp.where(down == across, stays, 0), axis=1, keepdims=True)
    allowed = (own_stay == stays) & (across <= down)
    scores = jnp.where(allowed, dot(queries, key_rows, CONTRACT_LAST) * SCALING, -1e30)
    raised = jnp.exp(scores - jnp.max(scores, axis=-1, keepdims=True))
    softmax_out = raised / jnp.sum(raised, axis=-1, keepdims=True)
    softmax[...] = softmax_out
    attended = dot(softmax_out.astype(jnp.bfloat16), value_rows).astype(jnp.bfloat16)
    back[...] = dot(place, attended).astype(jnp.bfloat16)


def attend(moved, receive, segments):
    rows = receive.shape[1]
    shapes = [
        shape(jnp.float32, rows, rows),
        shape(jnp.bfloat16, rows, moved.shape[1]),
        shape(jnp.bfloat16, moved.shape[0], HEAD_DIM),
    ]
    return call(attend_kernel, "attend", shapes, (moved, receive, segments), first=VMEM)


def attend_back_kernel(softmax, qkv, moved, receive, back):
    place = one_hot(receive[...], moved.shape[0])
    head_grad = dot(place, moved[:, :HEAD_DIM], CONTRACT_FIRST).astype(jnp.bfloat16)
    queries, key_rows, value_rows = (
        qkv[:, index * HEAD_DIM : (index + 1) * HEAD_DIM] for index in range(3)
    )
    softmax_out = softmax[...]
    low_weights = softmax_out.astype(jnp.bfloat16)
    grad_value = dot(low_weights, head_grad, CONTRACT_FIRST).astype(jnp.bfloat16)
    grad_probs = dot(head_grad, value_rows, CONTRACT_LAST)
    inner = jnp.sum(softmax_out * grad_probs, axis=-1, keepdims=True)
    grad_scores = (softmax_out * (grad_probs - inner) * SCALING).astype(jnp.bfloat16)
    grad_query = dot(grad_scores, key_rows).astype(jnp.bfloat16)
    grad_key = dot(grad_scores, queries, CONTRACT_FIRST).astype(jnp.bfloat16)
    results = jnp.concatenate([grad_query, grad_key, grad_value], axis=1)
    back[...] = dot(place, results).astype(jnp.bfloat16)


def attend_back(softmax, qkv, moved, receive):
    out = shape(jnp.bfloat16, moved.shape[0], qkv.shape[1])
    return call(attend_back_kernel, "attend_back", out, (softmax, qkv, moved, receive), first=VMEM)


def write_parts(value, out):
    out[...] = jnp.zeros_like(out)
    for place in range(3):
        low = value.astype(jnp.bfloat16)
        out[:, place : place + 1] = low
        value = value - low.astype(jnp.float32)


def read_parts(parts):
    return sum(parts[:, place : place + 1].astype(jnp.float32) for place in (2, 1, 0))


def bring_home_kernel(moved, moved_attended, send, home, results):
    chosen = one_hot(send[...], results.shape[0])
    grads = dot(chosen, moved[...])
    attended = dot(chosen, moved_attended[:, HEAD_DIM:])
    results[:, : 3 * HEAD_DIM] = grads.astype(jnp.bfloat16)
    results[:, 3 * HEAD_DIM : 4 * HEAD_DIM] = attended.astype(jnp.bfloat16)
    product = grads * home[...].astype(jnp.float32)
    row_dot = jnp.sum(product, axis=-1, keepdims=True)
    write_parts(row_dot, results.at[:, 4 * HEAD_DIM :])


def bring_home(moved, moved_attended, send, home):
    out = shape(jnp.bfloat16, home.shape[0], 5 * HEAD_DIM)
    operands = (moved, moved_attended, send, home)
    return call(bring_home_kernel, "bring_home", out, operands, first=VMEM)


def spread_into(own, near, weights, near_weights, first, out, place, held, total, sems):
    half = near_weights[0].shape[1]
    copies = [
        pltpu.make_async_copy(
            part.at[pl.ds(0, held.shape[0]), :],
            held.at[:, pl.ds(index * half, half)],
            sems.at[index],
        )
        for index, part in enumerate(near_weights)
    ]
    for copy in copies:
        copy.start()
    span = half * len(copies)
    own_grads = own[:, : 3 * HEAD_DIM]
    near_grads = near[:, : 3 * HEAD_DIM]
    for start in range(0, span, TILE):
        columns = slice(first + start, first + start + TILE)
        total[:, start : start + TILE] = dot(own_grads, weights[:, columns])
    for start in range(0, span, TILE):
        if start % half == 0:
            copies[start // half].wait()
        tile = slice(start, start + TILE)
        result = total[:, tile] + dot(near_grads, held[:, tile])
        out[:, place + start : place + start + TILE] = result.astype(out.dtype)


def spread_far_kernel(own, near, weights, near_weights, out, *scratch):
    width = weights.shape[1] // 2
    write_parts(
        read_parts(own[:, 4 * HEAD_DIM :]) + read_parts(near[:, 4 * HEAD_DIM :]),
        out.at[:, :HEAD_DIM],
    )
    attended = slice(3 * HEAD_DIM, 4 * HEAD_DIM)
    out[:, HEAD_DIM : 2 * HEAD_DIM] = own[:, attended]
    out[:, 2 * HEAD_DIM : 3 * HEAD_DIM] = near[:, attended]
    spread_into(own, near, weights, (near_weights,), width, out, 3 * HEAD_DIM, *scratch)


def spread_rest_kernel(own, near, weights, near_weights, out, *scratch):
    width = weights.shape[1] // 2
    first = width + width // 2
    spread_into(own, near, weights, (near_weights,), first, out, 0, *scratch)


def spread_own_kernel(own, near, weights, near_left, near_right, out, *scratch):
    spread_into(own, near, weights, (near_left, near_right), 0, out, 0, *scratch)


def spread(kernel, name, out, operands):
    rows, depth = operands[0].shape[0], operands[2].shape[0]
    parts = len(operands) - 3
    span = parts * operands[3].shape[1]
    return pl.pallas_call(
        kernel,
        out_shape=out,
        in_specs=[VMEM] * 3 + [pl.BlockSpec(memory_space=pl.ANY)] * parts,
        out_specs=VMEM,
        scratch_shapes=[
            pltpu.VMEM((depth, span), jnp.bfloat16),
            pltpu.VMEM((rows, span), jnp.float32),
            pltpu.SemaphoreType.DMA((parts,)),
        ],
        compiler_params=pltpu.CompilerParams(vmem_limit_bytes=VMEM_LIMIT),
        cost_estimate=pl.CostEstimate(flops=1000, bytes_accessed=1000, transcendentals=0),
        name=name,
    )(*operands)


def split_kernel(far_output, *pieces):
    width = far_output.shape[1] // 2
    span = width // len(pieces)
    for index, piece in enumerate(pieces):
        piece[...] = far_output[:, width + index * span : width + (index + 1) * span]


def split(far_output):
    heads, width = far_output.shape
    pieces = [shape(jnp.bfloat16, heads, width // 8)] * 4
    return call(split_kernel, "split", pieces, (far_output,), first=VMEM)


def finish_out_kernel(inputs, own, near, far, w_own, w_left, w_right, w_far, *rest):
    *w_last, out = rest
    width = inputs.shape[1]
    half = width // 2
    attended = slice(3 * HEAD_DIM, 4 * HEAD_DIM)
    rows = jnp.concatenate(
        [own[:, attended], near[:, attended], far[:, HEAD_DIM : 3 * HEAD_DIM]], axis=1
    )
    for start in range(0, width, TILE):
        tile = slice(start, start + TILE)
        w_near = (w_left, w_right)[start // half]
        w_near = w_near[3 * HEAD_DIM :, start % half : start % half + TILE]
        stacked = [w_own[:, tile], w_near, w_far[:, tile], w_last[start // TILE][...]]
        total = dot(rows, jnp.concatenate(stacked, axis=0))
        out[:, tile] = (inputs[:, tile].astype(jnp.float32) + total).astype(jnp.bfloat16)


def finish_grad_kernel(inputs, cotangent, gain, inverse, own, near, grad_own, far, rest, out):
    width = inputs.shape[1]
    row_dot = read_parts(own[:, 4 * HEAD_DIM :]) + read_parts(near[:, 4 * HEAD_DIM :])
    mean_dot = (row_dot + read_parts(far[:, :HEAD_DIM])) / (4 * width)
    inverse_rms = inverse[...]
    for start in range(0, width, TILE):
        tile = slice(start, start + TILE)
        if start < width // 2:
            got = far[:, 3 * HEAD_DIM + start : 3 * HEAD_DIM + start + TILE]
        else:
            got = rest[:, start - width // 2 : start - width // 2 + TILE]
        grad_normed = grad_own[:, tile] + got.astype(jnp.float32)
        grad_hat = grad_normed * gain[:, tile].astype(jnp.float32)
        scaled = inputs[:, tile].astype(jnp.float32) * inverse_rms
        change = inverse_rms * (grad_hat - scaled * mean_dot)
        out[:, tile] = (cotangent[:, tile].astype(jnp.float32) + change).astype(jnp.bfloat16)


def move(bucket):
    return lax.all_to_all(bucket, "dp", split_axis=0, concat_axis=0, tiled=True)


def after(array, *others):
    return lax.optimization_barrier((array, *others))[0]


def on_device(
    inputs,
    cotangent,
    norm_gain,
    w_query,
    w_key,
    w_value,
    w_output,
    send_rows,
    receive_slots,
    owner_segments,
):
    rows, width = inputs.shape
    tensor = lax.axis_size("tensor")
    low = jnp.bfloat16
    order = lax.axis_index("tensor").astype(jnp.int32) ^ jnp.arange(4, dtype=jnp.int32)
    gain = norm_gain.reshape(1, width)

    packed = pack(gain, inputs)
    x2 = swap(packed, 2, tensor)
    c2 = swap(cotangent, 2, tensor)
    x1 = swap(packed, 1, tensor)
    c1 = swap(cotangent, 1, tensor)
    weights = (w_query, w_key, w_value)
    own_turned, *prepared = prepare(
        order,
        *weights,
        w_output,
        send_rows,
        receive_slots.reshape(1, rows),
        owner_segments.reshape(1, rows),
        width,
    )
    near_turned, prepared = prepared[:4], prepared[4:]
    output_turned, own_here, far_output, send, receive, segments = prepared
    squares, part = begin(order, packed, x1, cotangent, c1, output_turned)

    x2, squares, part = lax.optimization_barrier((x2, squares, part))
    squares, upper, lower = go_on(x2, squares)
    home, inverse_rms, bucket = project(
        order,
        (packed, x1, x2, swap(upper, 1, tensor), swap(lower, 1, tensor)),
        weights,
        squares,
        send,
    )
    softmax, qkv, attended = attend(move(bucket), receive, segments)

    c2 = after(c2, softmax)
    c3 = swap(c2, 1, tensor)
    part = add_grad(order, c2, output_turned, part)
    c3, part = lax.optimization_barrier((c3, part))
    moved = move(fill(order, c3, output_turned, part, send, attended))
    far_output = swap(after(far_output, c3), 2, tensor)
    near_turned = [swap(after(piece, c3), 1, tensor) for piece in near_turned]
    back = attend_back(softmax, qkv, moved, receive)
    back, *near_turned = lax.optimization_barrier((back, *near_turned))
    own = bring_home(move(back), moved, send, home)

    near = swap(own, 1, tensor)
    half = width // 2
    far_shape = shape(low, rows, 3 * HEAD_DIM + half)
    rest_shape = shape(low, rows, half)
    own_shape = shape(jnp.float32, rows, width)
    sides = (own, near, own_turned, near_turned[2])
    far_part = spread(spread_far_kernel, "spread_far", far_shape, sides)
    far = swap(far_part, 2, tensor)
    sides = (after(own, far_part), near, own_turned, near_turned[3])
    rest_part = spread(spread_rest_kernel, "spread_rest", rest_shape, sides)
    rest = swap(rest_part, 2, tensor)
    sides = (after(own, rest_part), near, own_turned, *near_turned[:2])
    grad_own = spread(spread_own_kernel, "spread_own", own_shape, sides)
    last = [swap(piece, 1, tensor) for piece in split(after(far_output, grad_own))]
    layer_out = call(
        finish_out_kernel,
        "finish_out",
        shape(low, rows, width),
        (inputs, own, near, far, own_here, *near_turned[:2], far_output, *last),
        first=VMEM,
    )
    rest = after(rest, layer_out)
    input_grad = call(
        finish_grad_kernel,
        "finish_grad",
        shape(low, rows, width),
        (inputs, cotangent, gain, inverse_rms, own, near, grad_own, far, rest),
        first=VMEM,
    )
    return (layer_out, input_grad)


def solution(mesh):
    return jax.shard_map(
        on_device,
        mesh=mesh,
        in_specs=(
            P("dp", "tensor"),
            P("dp", "tensor"),
            P("tensor"),
            P(None, "tensor"),
            P(None, "tensor"),
            P(None, "tensor"),
            P("tensor", None),
            P("dp", None),
            P("dp"),
            P("dp"),
        ),
        out_specs=(P("dp", "tensor"), P("dp", "tensor")),
        check_vma=False,
    )
```

```python
import math

import jax
import jax.numpy as jnp
from jax import lax
from jax.experimental import pallas as pl
from jax.experimental.pallas import tpu as pltpu
from jax.sharding import PartitionSpec as P

HEAD_DIM = 128
EPSILON = 1e-05
SCALING = 1.0 / math.sqrt(HEAD_DIM)
CONTRACT_LAST = (((1,), (1,)), ((), ()))
CONTRACT_FIRST = (((0,), (0,)), ((), ()))
VMEM_LIMIT = 12 * 1024 * 1024
VMEM = pl.BlockSpec(memory_space=pltpu.VMEM)
SMEM = pl.BlockSpec(memory_space=pltpu.SMEM)
TILE = 512
EXTRA = 3 * HEAD_DIM


def dot(left, right, dims=(((1,), (0,)), ((), ()))):
    return lax.dot_general(left, right, dims, preferred_element_type=jnp.float32)


def call(kernel, name, out_shape, operands, scratch=(), first=SMEM, rest=VMEM):
    single = not isinstance(out_shape, (list, tuple))
    shapes = [out_shape] if single else list(out_shape)
    results = pl.pallas_call(
        kernel,
        out_shape=shapes,
        in_specs=[first] + [rest] * (len(operands) - 1),
        out_specs=[VMEM] * len(shapes),
        scratch_shapes=list(scratch),
        compiler_params=pltpu.CompilerParams(vmem_limit_bytes=VMEM_LIMIT),
        cost_estimate=pl.CostEstimate(flops=1000, bytes_accessed=1000, transcendentals=0),
        name=name,
    )(*operands)
    return results[0] if single else results


def shape(dtype, *sizes):
    return jax.ShapeDtypeStruct(sizes, dtype)


def swap(array, mask, count):
    return lax.ppermute(array, "tensor", [(i, i ^ mask) for i in range(count)])


def block_start(order, slot, width):
    return pl.multiple_of(order[slot] * width, width)


def one_hot(places, rows):
    row = lax.broadcasted_iota(jnp.int32, (rows, places.shape[1]), 0)
    return jnp.where(places == row, 1.0, 0.0).astype(jnp.bfloat16)


def prepare_kernel(
    order,
    w_query,
    w_key,
    w_value,
    w_output,
    send,
    receive,
    segments,
    own_turned,
    near_turned,
    output_turned,
    own_here,
    far_output,
    send_out,
    receive_out,
    segments_out,
):
    width = own_here.shape[1]
    blocks = [w_output[:, pl.ds(block_start(order, slot, width), width)] for slot in range(4)]
    own_here[...] = blocks[0]
    for target, left, right in (
        (far_output, blocks[2], blocks[3]),
        (near_turned.at[3 * HEAD_DIM :, :], blocks[1], blocks[3]),
    ):
        target[:, :width] = left
        target[:, width:] = right
    for start in range(0, w_output.shape[1], TILE):
        output_turned[start : start + TILE, :] = w_output[:, start : start + TILE].T
    for source, target in ((send, send_out), (receive, receive_out), (segments, segments_out)):
        target[...] = source[...]
    for out, slots in ((own_turned, (0, 2)), (near_turned, (1, 3))):
        for part, slot in enumerate(slots):
            first = block_start(order, slot, width)
            for start in range(0, width, TILE):
                columns = slice(part * width + start, part * width + start + TILE)
                for place, weight in enumerate((w_query, w_key, w_value)):
                    rows = slice(place * HEAD_DIM, (place + 1) * HEAD_DIM)
                    out[rows, columns] = weight[pl.ds(first + start, TILE), :].T


def prepare(order, w_query, w_key, w_value, w_output, send, receive, segments, width):
    heads = w_query.shape[1]
    low = jnp.bfloat16
    return call(
        prepare_kernel,
        "prepare",
        [
            shape(low, 3 * heads, 2 * width),
            shape(low, 4 * heads, 2 * width),
            shape(low, w_output.shape[1], heads),
            shape(low, heads, width),
            shape(low, heads, 2 * width),
            shape(jnp.int32, *send.shape),
            shape(jnp.int32, *receive.shape),
            shape(jnp.int32, *segments.shape),
        ],
        (order, w_query, w_key, w_value, w_output, send, receive, segments),
    )


def sum_squares(block):
    wide = block[...].astype(jnp.float32)
    return jnp.sum(wide * wide, axis=-1, keepdims=True)


def begin_kernel(order, x0, x1, c0, c1, output_turned, squares, part):
    width = x0.shape[1]
    squares[...] = sum_squares(x0) + sum_squares(x1)
    total = 0.0
    for index, block in enumerate((c0, c1)):
        here = pl.ds(block_start(order, index, width), width)
        total = total + dot(block[...], output_turned[here, :])
    part[...] = total


def go_on_kernel(order, x2, c2, output_turned, squares_in, part_in, squares, part):
    width = x2.shape[1]
    here = pl.ds(block_start(order, 2, width), width)
    part[...] = part_in[...] + dot(c2[...], output_turned[here, :])
    squares[...] = squares_in[...] + sum_squares(x2)


def begin(kernel, name, *operands):
    rows = operands[1].shape[0]
    shapes = [shape(jnp.float32, rows, 1), shape(jnp.float32, rows, HEAD_DIM)]
    return call(kernel, name, shapes, operands)


def project_kernel(
    order,
    x0,
    x1,
    x2,
    x3,
    c3,
    gain_own,
    gain_near,
    w_query,
    w_key,
    w_value,
    output_turned,
    squares,
    part,
    send,
    home,
    inverse,
    bucket,
    total,
):
    blocks = (x0, x1, x2, x3)
    width = x0.shape[1]
    mean = (squares[...] + sum_squares(x3)) / (width * len(blocks))
    inverse_rms = lax.rsqrt(mean + EPSILON)
    inverse[...] = inverse_rms
    here = pl.ds(block_start(order, 3, width), width)
    head_grad = (part[...] + dot(c3[...], output_turned[here, :])).astype(jnp.bfloat16)
    for index, block in enumerate(blocks):
        gain = (gain_own, gain_near)[index % 2][index // 2 : index // 2 + 1, :]
        scaled = block[...].astype(jnp.float32) * inverse_rms
        normed = (scaled * gain.astype(jnp.float32)).astype(jnp.bfloat16)
        here = pl.ds(block_start(order, index, width), width)
        weights = jnp.concatenate([w_query[here, :], w_key[here, :], w_value[here, :]], axis=1)
        product = dot(normed, weights)
        total[...] = total[...] + product if index else product
    rounded = total[...].astype(jnp.bfloat16)
    home[...] = rounded
    chosen = one_hot(send[...], rounded.shape[0])
    split = rounded.shape[1]
    bucket[:, :split] = dot(chosen, rounded, CONTRACT_FIRST).astype(jnp.bfloat16)
    bucket[:, split:] = dot(chosen, head_grad, CONTRACT_FIRST).astype(jnp.bfloat16)


def project(order, blocks, gains, weights, squares, part, send):
    rows = blocks[0].shape[0]
    columns = 3 * HEAD_DIM
    return call(
        project_kernel,
        "project",
        [
            shape(jnp.bfloat16, rows, columns),
            shape(jnp.float32, rows, 1),
            shape(jnp.bfloat16, send.shape[1], columns + HEAD_DIM),
        ],
        (order, *blocks, *gains, *weights, squares, part, send),
        scratch=[pltpu.VMEM((rows, columns), jnp.float32)],
    )


def attend_kernel(moved, receive, segments, back):
    place = one_hot(receive[...], moved.shape[0])
    rows = dot(place, moved[...], CONTRACT_FIRST).astype(jnp.bfloat16)
    queries, key_rows, value_rows, head_grad = (
        rows[:, index * HEAD_DIM : (index + 1) * HEAD_DIM] for index in range(4)
    )
    count = rows.shape[0]
    down = lax.broadcasted_iota(jnp.int32, (count, count), 0)
    across = lax.broadcasted_iota(jnp.int32, (count, count), 1)
    stays = segments[...]
    own_stay = jnp.sum(jnp.where(down == across, stays, 0), axis=1, keepdims=True)
    allowed = (own_stay == stays) & (across <= down)
    scores = jnp.where(allowed, dot(queries, key_rows, CONTRACT_LAST) * SCALING, -1e30)
    raised = jnp.exp(scores - jnp.max(scores, axis=-1, keepdims=True))
    softmax_out = raised / jnp.sum(raised, axis=-1, keepdims=True)
    low_weights = softmax_out.astype(jnp.bfloat16)
    attended = dot(low_weights, value_rows).astype(jnp.bfloat16)
    grad_value = dot(low_weights, head_grad, CONTRACT_FIRST).astype(jnp.bfloat16)
    grad_probs = dot(head_grad, value_rows, CONTRACT_LAST)
    inner = jnp.sum(softmax_out * grad_probs, axis=-1, keepdims=True)
    grad_scores = (softmax_out * (grad_probs - inner) * SCALING).astype(jnp.bfloat16)
    grad_query = dot(grad_scores, key_rows).astype(jnp.bfloat16)
    grad_key = dot(grad_scores, queries, CONTRACT_FIRST).astype(jnp.bfloat16)
    results = jnp.concatenate([grad_query, grad_key, grad_value, attended], axis=1)
    back[...] = dot(place, results).astype(jnp.bfloat16)


def attend(moved, receive, segments):
    out = shape(jnp.bfloat16, *moved.shape)
    return call(attend_kernel, "attend", out, (moved, receive, segments), first=VMEM)


def write_parts(value, out):
    out[...] = jnp.zeros_like(out)
    for place in range(3):
        low = value.astype(jnp.bfloat16)
        out[:, place : place + 1] = low
        value = value - low.astype(jnp.float32)


def read_parts(parts):
    return sum(parts[:, place : place + 1].astype(jnp.float32) for place in (2, 1, 0))


def bring_home_kernel(moved, send, home, results):
    chosen = one_hot(send[...], results.shape[0])
    rows = dot(chosen, moved[...])
    results[:, : 4 * HEAD_DIM] = rows.astype(jnp.bfloat16)
    product = rows[:, : 3 * HEAD_DIM] * home[...].astype(jnp.float32)
    row_dot = jnp.sum(product, axis=-1, keepdims=True)
    write_parts(row_dot, results.at[:, 4 * HEAD_DIM :])


def bring_home(moved, send, home):
    out = shape(jnp.bfloat16, home.shape[0], 5 * HEAD_DIM)
    return call(bring_home_kernel, "bring_home", out, (moved, send, home), first=VMEM)


def spread_kernel(first, place):
    def kernel(own, near, weights, near_weights, out, held, total, sems):
        depth, span = held.shape
        copies = []
        for index, start in enumerate(range(0, span, TILE)):
            source = near_weights.at[pl.ds(0, depth), pl.ds(first + start, TILE)]
            target = held.at[:, pl.ds(start, TILE)]
            copies.append(pltpu.make_async_copy(source, target, sems.at[index]))
            copies[-1].start()
        if place:
            attended = slice(depth, depth + HEAD_DIM)
            out[:, :HEAD_DIM] = own[:, attended]
            out[:, HEAD_DIM : 2 * HEAD_DIM] = near[:, attended]
            row_dot = read_parts(own[:, depth + HEAD_DIM :]) + read_parts(near[:, depth + HEAD_DIM :])
            write_parts(row_dot, out.at[:, 2 * HEAD_DIM : place])
        own_rows, near_rows = own[:, :depth], near[:, :depth]
        for start in range(0, span, TILE):
            columns = slice(first + start, first + start + TILE)
            total[:, start : start + TILE] = dot(own_rows, weights[:, columns])
        for index, start in enumerate(range(0, span, TILE)):
            copies[index].wait()
            result = total[:, start : start + TILE] + dot(near_rows, held[:, start : start + TILE])
            out[:, place + start : place + start + TILE] = result.astype(out.dtype)

    return kernel


def spread(name, first, span, place, dtype, own, near, weights, near_weights):
    rows, depth = own.shape[0], weights.shape[0]
    return pl.pallas_call(
        spread_kernel(first, place),
        out_shape=shape(dtype, rows, place + span),
        in_specs=[VMEM] * 3 + [pl.BlockSpec(memory_space=pl.ANY)],
        out_specs=VMEM,
        scratch_shapes=[
            pltpu.VMEM((depth, span), jnp.bfloat16),
            pltpu.VMEM((rows, span), jnp.float32),
            pltpu.SemaphoreType.DMA((span // TILE,)),
        ],
        compiler_params=pltpu.CompilerParams(vmem_limit_bytes=VMEM_LIMIT),
        cost_estimate=pl.CostEstimate(flops=1000, bytes_accessed=1000, transcendentals=0),
        name=name,
    )(own, near, weights, near_weights)


def finish_out_kernel(
    near_weights, inputs, own, near, far, w_own, w_far, w_last, out, w_near, sem
):
    width = inputs.shape[1]
    rows = pl.ds(3 * HEAD_DIM, HEAD_DIM)
    copy = pltpu.make_async_copy(near_weights.at[rows, pl.ds(0, width)], w_near, sem)
    copy.start()
    there = slice(3 * HEAD_DIM, 4 * HEAD_DIM)
    attended = [own[:, there], near[:, there], far[:, : 2 * HEAD_DIM]]
    attended = jnp.concatenate(attended, axis=1)
    copy.wait()
    for start in range(0, width, TILE):
        tile = slice(start, start + TILE)
        second = slice(width + start, width + start + TILE)
        stacked = [w_own[:, tile], w_near[:, tile], w_far[:, tile], w_last[:, second]]
        total = dot(attended, jnp.concatenate(stacked, axis=0))
        out[:, tile] = (inputs[:, tile].astype(jnp.float32) + total).astype(jnp.bfloat16)


def finish_grad_kernel(first, count, *refs):
    inputs, cotangent, gain, inverse, own, near, grad_own, far = refs[:8]
    got, (out, held, sem) = refs[8 : 8 + count], refs[-3:]
    row_dot = read_parts(far[:, 2 * HEAD_DIM : EXTRA])
    row_dot = row_dot + read_parts(own[:, 4 * HEAD_DIM :]) + read_parts(near[:, 4 * HEAD_DIM :])
    mean_dot = row_dot / (4 * inputs.shape[1])
    inverse_rms = inverse[...]
    place = 0
    if not first:
        got = (far.at[:, EXTRA:], *got)
    for piece in got:
        for start in range(0, piece.shape[1], TILE):
            tile = slice(first + place, first + place + TILE)
            grad_normed = grad_own[:, tile] + piece[:, start : start + TILE].astype(jnp.float32)
            grad_hat = grad_normed * gain[:, tile].astype(jnp.float32)
            scaled = inputs[:, tile].astype(jnp.float32) * inverse_rms
            change = inverse_rms * (grad_hat - scaled * mean_dot)
            result = cotangent[:, tile].astype(jnp.float32) + change
            held[:, place : place + TILE] = result.astype(jnp.bfloat16)
            place += TILE
    copy = pltpu.make_async_copy(held, out.at[:, pl.ds(first, held.shape[1])], sem)
    copy.start()
    copy.wait()


def finish_grad(name, first, fixed, got, before):
    rows, width = fixed[0].shape
    span = sum(piece.shape[1] for piece in got)
    if not first:
        span += fixed[-1].shape[1] - EXTRA
    count = len(got)
    operands = (*fixed, *got, *before)
    hbm = pl.BlockSpec(memory_space=pltpu.HBM)
    return pl.pallas_call(
        lambda *refs: finish_grad_kernel(first, count, *refs),
        out_shape=shape(jnp.bfloat16, rows, width),
        in_specs=[VMEM] * (len(fixed) + count) + [hbm] * len(before),
        out_specs=hbm,
        scratch_shapes=[pltpu.VMEM((rows, span), jnp.bfloat16), pltpu.SemaphoreType.DMA],
        input_output_aliases={len(operands) - 1: 0} if before else {},
        compiler_params=pltpu.CompilerParams(vmem_limit_bytes=VMEM_LIMIT),
        cost_estimate=pl.CostEstimate(flops=1000, bytes_accessed=1000, transcendentals=0),
        name=name,
    )(*operands)


def move(bucket):
    return lax.all_to_all(bucket, "dp", split_axis=0, concat_axis=0, tiled=True)


def after(array, *others):
    return lax.optimization_barrier((array, *others))[0]


def on_device(
    inputs,
    cotangent,
    norm_gain,
    w_query,
    w_key,
    w_value,
    w_output,
    send_rows,
    receive_slots,
    owner_segments,
):
    rows, width = inputs.shape
    tensor = lax.axis_size("tensor")
    low = jnp.bfloat16
    order = lax.axis_index("tensor").astype(jnp.int32) ^ jnp.arange(4, dtype=jnp.int32)
    gain = norm_gain.reshape(1, width)

    x2 = swap(inputs, 2, tensor)
    c2 = swap(cotangent, 2, tensor)
    gain2 = swap(gain, 2, tensor)
    x1 = swap(inputs, 1, tensor)
    c1 = swap(cotangent, 1, tensor)
    weights = (w_query, w_key, w_value)
    (own_turned, near_turned, output_turned, own_here, far_output, *indices) = prepare(
        order,
        *weights,
        w_output,
        send_rows,
        receive_slots.reshape(1, rows),
        owner_segments.reshape(1, rows),
        width,
    )
    send, receive, segments = indices
    squares, part = begin(
        begin_kernel, "begin", order, inputs, x1, cotangent, c1, output_turned
    )
    x2, c2, gain2, squares, part = lax.optimization_barrier((x2, c2, gain2, squares, part))
    x3 = swap(x2, 1, tensor)
    c3 = swap(c2, 1, tensor)
    gain_own = jnp.concatenate([gain, gain2], axis=0)
    gain_near = swap(gain_own, 1, tensor)
    squares, part = begin(go_on_kernel, "go_on", order, x2, c2, output_turned, squares, part)
    home, inverse_rms, bucket = project(
        order,
        (inputs, x1, x2, x3, c3),
        (gain_own, gain_near),
        (*weights, output_turned),
        squares,
        part,
        send,
    )
    near_turned = swap(after(near_turned, home), 1, tensor)
    far_output = swap(after(far_output, home), 2, tensor)
    back = attend(move(bucket), receive, segments)
    own = bring_home(move(back), send, home)

    near = swap(own, 1, tensor)
    last_output = swap(after(far_output, near), 1, tensor)
    quarter = width // 4
    turn, got = own, []
    for first, span in ((0, 2 * quarter), (2 * quarter, quarter), (3 * quarter, quarter)):
        place = 0 if first else EXTRA
        part = spread(
            "spread_far", width + first, span, place, low, turn, near, own_turned, near_turned
        )
        got.append(swap(part, 2, tensor))
        turn = after(own, part)
    grad_own = spread(
        "spread_own", 0, width, 0, jnp.float32, turn, near, own_turned, near_turned
    )
    far, middle, rest = got
    layer_out = call(
        finish_out_kernel,
        "finish_out",
        shape(low, rows, width),
        (near_turned, inputs, own, near, far, own_here, far_output, last_output),
        scratch=[pltpu.VMEM((HEAD_DIM, width), low), pltpu.SemaphoreType.DMA],
        first=pl.BlockSpec(memory_space=pl.ANY),
    )
    middle = after(middle, layer_out)
    fixed = (inputs, cotangent, gain, inverse_rms, own, near, grad_own, far)
    begun = finish_grad("finish_most", 0, fixed, (middle,), ())
    input_grad = finish_grad("finish_rest", 3 * quarter, fixed, (rest,), (begun,))
    return (layer_out, input_grad)


def solution(mesh):
    return jax.shard_map(
        on_device,
        mesh=mesh,
        in_specs=(
            P("dp", "tensor"),
            P("dp", "tensor"),
            P("tensor"),
            P(None, "tensor"),
            P(None, "tensor"),
            P(None, "tensor"),
            P("tensor", None),
            P("dp", None),
            P("dp"),
            P("dp"),
        ),
        out_specs=(P("dp", "tensor"), P("dp", "tensor")),
        check_vma=False,
    )
```

```python
import math

import jax
import jax.numpy as jnp
from jax import lax
from jax.experimental import pallas as pl
from jax.experimental.pallas import tpu as pltpu
from jax.sharding import PartitionSpec as P

HEAD_DIM = 128
EPSILON = 1e-05
SCALING = 1.0 / math.sqrt(HEAD_DIM)
CONTRACT_LAST = (((1,), (1,)), ((), ()))
CONTRACT_FIRST = (((0,), (0,)), ((), ()))
VMEM_LIMIT = 12 * 1024 * 1024
VMEM = pl.BlockSpec(memory_space=pltpu.VMEM)
SMEM = pl.BlockSpec(memory_space=pltpu.SMEM)
TILE = 512


def dot(left, right, dims=(((1,), (0,)), ((), ()))):
    return lax.dot_general(left, right, dims, preferred_element_type=jnp.float32)


def call(kernel, name, out_shape, operands, scratch=(), first=SMEM, rest=VMEM):
    single = not isinstance(out_shape, (list, tuple))
    shapes = [out_shape] if single else list(out_shape)
    results = pl.pallas_call(
        kernel,
        out_shape=shapes,
        in_specs=[first] + [rest] * (len(operands) - 1),
        out_specs=[VMEM] * len(shapes),
        scratch_shapes=list(scratch),
        compiler_params=pltpu.CompilerParams(vmem_limit_bytes=VMEM_LIMIT),
        cost_estimate=pl.CostEstimate(flops=1000, bytes_accessed=1000, transcendentals=0),
        name=name,
    )(*operands)
    return results[0] if single else results


def shape(dtype, *sizes):
    return jax.ShapeDtypeStruct(sizes, dtype)


def swap(array, mask, count):
    return lax.ppermute(array, "tensor", [(i, i ^ mask) for i in range(count)])


def block_start(order, slot, width):
    return pl.multiple_of(order[slot] * width, width)


def one_hot(places, rows):
    row = lax.broadcasted_iota(jnp.int32, (rows, places.shape[1]), 0)
    return jnp.where(places == row, 1.0, 0.0).astype(jnp.bfloat16)


def prepare_kernel(
    order,
    w_query,
    w_key,
    w_value,
    w_output,
    near_output,
    send,
    receive,
    segments,
    own_turned,
    near_turned,
    here,
    there,
    here_turned,
    there_turned,
    send_out,
    receive_out,
    segments_out,
):
    heads, width = w_output.shape[0], here.shape[1]
    for slot, out, turned in ((0, here, here_turned), (2, there, there_turned)):
        columns = pl.ds(block_start(order, slot, width), width)
        for part, weight in enumerate((w_output, near_output)):
            rows = slice(part * heads, (part + 1) * heads)
            block = weight[:, columns]
            out[rows, :] = block
            turned[:, rows] = block.T
    for source, target in ((send, send_out), (receive, receive_out), (segments, segments_out)):
        target[...] = source[...]
    for out, slots in ((own_turned, (0, 2)), (near_turned, (1, 3))):
        for part, slot in enumerate(slots):
            first = block_start(order, slot, width)
            for start in range(0, width, TILE):
                columns = slice(part * width + start, part * width + start + TILE)
                for place, weight in enumerate((w_query, w_key, w_value)):
                    rows = slice(place * HEAD_DIM, (place + 1) * HEAD_DIM)
                    out[rows, columns] = weight[pl.ds(first + start, TILE), :].T


def prepare(order, w_query, w_key, w_value, w_output, near_output, send, receive, segments, width):
    heads = w_query.shape[1]
    low = jnp.bfloat16
    return call(
        prepare_kernel,
        "prepare",
        [
            *[shape(low, 3 * heads, 2 * width)] * 2,
            *[shape(low, 2 * heads, width)] * 2,
            *[shape(low, width, 2 * heads)] * 2,
            shape(jnp.int32, *send.shape),
            shape(jnp.int32, *receive.shape),
            shape(jnp.int32, *segments.shape),
        ],
        (order, w_query, w_key, w_value, w_output, near_output, send, receive, segments),
    )


def sum_squares(block):
    wide = block[...].astype(jnp.float32)
    return jnp.sum(wide * wide, axis=-1, keepdims=True)


def begin_kernel(x0, x1, c0, here_turned, squares, part):
    squares[...] = sum_squares(x0) + sum_squares(x1)
    part[...] = dot(c0[...], here_turned[...])


def begin(x0, x1, c0, here_turned):
    rows, columns = x0.shape[0], here_turned.shape[1]
    shapes = [shape(jnp.float32, rows, 1), shape(jnp.float32, rows, columns)]
    return call(begin_kernel, "begin", shapes, (x0, x1, c0, here_turned), first=VMEM)


def add_grad_kernel(c2, there_turned, part, own_part, near_part):
    total = part[...] + dot(c2[...], there_turned[...])
    heads = own_part.shape[1]
    own_part[...] = total[:, :heads]
    near_part[...] = total[:, heads:]


def add_grad(c2, there_turned, part):
    shapes = [shape(jnp.float32, part.shape[0], part.shape[1] // 2)] * 2
    return call(add_grad_kernel, "add_grad", shapes, (c2, there_turned, part), first=VMEM)


def add_squares_kernel(x2, squares_in, squares):
    squares[...] = squares_in[...] + sum_squares(x2)


def add_squares(x2, squares):
    out = shape(jnp.float32, *squares.shape)
    return call(add_squares_kernel, "add_squares", out, (x2, squares), first=VMEM)


def project_kernel(
    order,
    x0,
    x1,
    x2,
    x3,
    gain_own,
    gain_near,
    w_query,
    w_key,
    w_value,
    squares,
    own_part,
    got_part,
    send,
    home,
    inverse,
    bucket,
    total,
):
    blocks = (x0, x1, x2, x3)
    width = x0.shape[1]
    mean = (squares[...] + sum_squares(x3)) / (width * len(blocks))
    inverse_rms = lax.rsqrt(mean + EPSILON)
    inverse[...] = inverse_rms
    head_grad = (own_part[...] + got_part[...]).astype(jnp.bfloat16)
    for index, block in enumerate(blocks):
        gain = (gain_own, gain_near)[index % 2][index // 2 : index // 2 + 1, :]
        scaled = block[...].astype(jnp.float32) * inverse_rms
        normed = (scaled * gain.astype(jnp.float32)).astype(jnp.bfloat16)
        here = pl.ds(block_start(order, index, width), width)
        weights = jnp.concatenate([w_query[here, :], w_key[here, :], w_value[here, :]], axis=1)
        product = dot(normed, weights)
        total[...] = total[...] + product if index else product
    rounded = total[...].astype(jnp.bfloat16)
    home[...] = rounded
    chosen = one_hot(send[...], rounded.shape[0])
    split = rounded.shape[1]
    bucket[:, :split] = dot(chosen, rounded, CONTRACT_FIRST).astype(jnp.bfloat16)
    bucket[:, split:] = dot(chosen, head_grad, CONTRACT_FIRST).astype(jnp.bfloat16)


def project(order, blocks, gains, weights, squares, own_part, got_part, send):
    rows = blocks[0].shape[0]
    columns = 3 * HEAD_DIM
    return call(
        project_kernel,
        "project",
        [
            shape(jnp.bfloat16, rows, columns),
            shape(jnp.float32, rows, 1),
            shape(jnp.bfloat16, send.shape[1], columns + HEAD_DIM),
        ],
        (order, *blocks, *gains, *weights, squares, own_part, got_part, send),
        scratch=[pltpu.VMEM((rows, columns), jnp.float32)],
    )


def attend_kernel(moved, receive, segments, back):
    place = one_hot(receive[...], moved.shape[0])
    rows = dot(place, moved[...], CONTRACT_FIRST).astype(jnp.bfloat16)
    queries, key_rows, value_rows, head_grad = (
        rows[:, index * HEAD_DIM : (index + 1) * HEAD_DIM] for index in range(4)
    )
    count = rows.shape[0]
    down = lax.broadcasted_iota(jnp.int32, (count, count), 0)
    across = lax.broadcasted_iota(jnp.int32, (count, count), 1)
    stays = segments[...]
    own_stay = jnp.sum(jnp.where(down == across, stays, 0), axis=1, keepdims=True)
    allowed = (own_stay == stays) & (across <= down)
    scores = jnp.where(allowed, dot(queries, key_rows, CONTRACT_LAST) * SCALING, -1e30)
    raised = jnp.exp(scores - jnp.max(scores, axis=-1, keepdims=True))
    softmax_out = raised / jnp.sum(raised, axis=-1, keepdims=True)
    low_weights = softmax_out.astype(jnp.bfloat16)
    attended = dot(low_weights, value_rows).astype(jnp.bfloat16)
    grad_value = dot(low_weights, head_grad, CONTRACT_FIRST).astype(jnp.bfloat16)
    grad_probs = dot(head_grad, value_rows, CONTRACT_LAST)
    inner = jnp.sum(softmax_out * grad_probs, axis=-1, keepdims=True)
    grad_scores = (softmax_out * (grad_probs - inner) * SCALING).astype(jnp.bfloat16)
    grad_query = dot(grad_scores, key_rows).astype(jnp.bfloat16)
    grad_key = dot(grad_scores, queries, CONTRACT_FIRST).astype(jnp.bfloat16)
    results = jnp.concatenate([grad_query, grad_key, grad_value, attended], axis=1)
    back[...] = dot(place, results).astype(jnp.bfloat16)


def attend(moved, receive, segments):
    out = shape(jnp.bfloat16, *moved.shape)
    return call(attend_kernel, "attend", out, (moved, receive, segments), first=VMEM)


def write_parts(value, out):
    out[...] = jnp.zeros_like(out)
    for place in range(3):
        low = value.astype(jnp.bfloat16)
        out[:, place : place + 1] = low
        value = value - low.astype(jnp.float32)


def read_parts(parts):
    return sum(parts[:, place : place + 1].astype(jnp.float32) for place in (2, 1, 0))


def bring_home_kernel(moved, send, home, grads, extras):
    chosen = one_hot(send[...], grads.shape[0])
    rows = dot(chosen, moved[...])
    split = 3 * HEAD_DIM
    grads[...] = rows[:, :split].astype(jnp.bfloat16)
    extras[:, :HEAD_DIM] = rows[:, split:].astype(jnp.bfloat16)
    product = rows[:, :split] * home[...].astype(jnp.float32)
    row_dot = jnp.sum(product, axis=-1, keepdims=True)
    write_parts(row_dot, extras.at[:, HEAD_DIM:])


def bring_home(moved, send, home):
    rows = home.shape[0]
    shapes = [shape(jnp.bfloat16, rows, 3 * HEAD_DIM), shape(jnp.bfloat16, rows, 2 * HEAD_DIM)]
    return call(bring_home_kernel, "bring_home", shapes, (moved, send, home), first=VMEM)


def spread_kernel(first):
    def kernel(own, near, weights, near_weights, out, held, total, sems):
        span = held.shape[1]
        copies = []
        for index, start in enumerate(range(0, span, TILE)):
            source = near_weights.at[:, pl.ds(first + start, TILE)]
            target = held.at[:, pl.ds(start, TILE)]
            copies.append(pltpu.make_async_copy(source, target, sems.at[index]))
            copies[-1].start()
        own_rows, near_rows = own[...], near[...]
        for start in range(0, span, TILE):
            columns = slice(first + start, first + start + TILE)
            total[:, start : start + TILE] = dot(own_rows, weights[:, columns])
        for index, start in enumerate(range(0, span, TILE)):
            copies[index].wait()
            tile = slice(start, start + TILE)
            result = total[:, tile] + dot(near_rows, held[:, tile])
            out[:, tile] = result.astype(out.dtype)

    return kernel


def spread(name, first, span, dtype, own, near, weights, near_weights):
    rows, depth = own.shape
    return pl.pallas_call(
        spread_kernel(first),
        out_shape=shape(dtype, rows, span),
        in_specs=[VMEM] * 3 + [pl.BlockSpec(memory_space=pl.ANY)],
        out_specs=VMEM,
        scratch_shapes=[
            pltpu.VMEM((depth, span), jnp.bfloat16),
            pltpu.VMEM((rows, span), jnp.float32),
            pltpu.SemaphoreType.DMA((span // TILE,)),
        ],
        compiler_params=pltpu.CompilerParams(vmem_limit_bytes=VMEM_LIMIT),
        cost_estimate=pl.CostEstimate(flops=1000, bytes_accessed=1000, transcendentals=0),
        name=name,
    )(own, near, weights, near_weights)


def finish_out_kernel(inputs, own, near, far, last, here, there, out):
    width = inputs.shape[1]
    chip = jnp.concatenate([own[:, :HEAD_DIM], near[:, :HEAD_DIM]], axis=1)
    other = jnp.concatenate([far[:, :HEAD_DIM], last[:, :HEAD_DIM]], axis=1)
    for start in range(0, width, TILE):
        tile = slice(start, start + TILE)
        total = dot(chip, here[:, tile]) + dot(other, there[:, tile])
        out[:, tile] = (inputs[:, tile].astype(jnp.float32) + total).astype(jnp.bfloat16)


def finish_most_kernel(
    inputs, cotangent, gain, inverse, own, near, far, last, grad_own, got, middle, *outs
):
    out, left, held, sem = outs
    row_dot = sum(read_parts(extras[:, HEAD_DIM:]) for extras in (own, near, far, last))
    mean_dot = row_dot / (4 * inputs.shape[1])
    inverse_rms = inverse[...]
    most = held.shape[1]
    for start in range(0, inputs.shape[1], TILE):
        tile = slice(start, start + TILE)
        grad_normed = grad_own[:, tile]
        if start < got.shape[1]:
            grad_normed = grad_normed + got[:, tile].astype(jnp.float32)
        elif start < most:
            part = slice(start - got.shape[1], start - got.shape[1] + TILE)
            grad_normed = grad_normed + middle[:, part].astype(jnp.float32)
        grad_hat = grad_normed * gain[:, tile].astype(jnp.float32)
        scaled = inputs[:, tile].astype(jnp.float32) * inverse_rms
        change = inverse_rms * (grad_hat - scaled * mean_dot)
        result = cotangent[:, tile].astype(jnp.float32) + change
        if start < most:
            held[:, tile] = result.astype(jnp.bfloat16)
        else:
            left[:, start - most : start - most + TILE] = result
    copy = pltpu.make_async_copy(held, out.at[:, pl.ds(0, most)], sem)
    copy.start()
    copy.wait()


def finish_rest_kernel(gain, inverse, left, rest, before, out, held, sem):
    span = rest.shape[1]
    first = out.shape[1] - span
    for start in range(0, span, TILE):
        tile = slice(start, start + TILE)
        columns = slice(first + start, first + start + TILE)
        grad_hat = rest[:, tile].astype(jnp.float32) * gain[:, columns].astype(jnp.float32)
        held[:, tile] = (left[:, tile] + inverse[...] * grad_hat).astype(jnp.bfloat16)
    copy = pltpu.make_async_copy(held, out.at[:, pl.ds(first, span)], sem)
    copy.start()
    copy.wait()


def finish_grad(inputs, cotangent, gain, inverse, extras, grad_own, got, middle, rest):
    rows, width = inputs.shape
    span = rest.shape[1]
    hbm = pl.BlockSpec(memory_space=pltpu.HBM)
    options = dict(
        compiler_params=pltpu.CompilerParams(vmem_limit_bytes=VMEM_LIMIT),
        cost_estimate=pl.CostEstimate(flops=1000, bytes_accessed=1000, transcendentals=0),
    )
    begun, left = pl.pallas_call(
        finish_most_kernel,
        out_shape=[shape(jnp.bfloat16, rows, width), shape(jnp.float32, rows, span)],
        in_specs=[VMEM] * 11,
        out_specs=[hbm, VMEM],
        scratch_shapes=[pltpu.VMEM((rows, width - span), jnp.bfloat16), pltpu.SemaphoreType.DMA],
        name="finish_most",
        **options,
    )(inputs, cotangent, gain, inverse, *extras, grad_own, got, middle)
    return pl.pallas_call(
        finish_rest_kernel,
        out_shape=shape(jnp.bfloat16, rows, width),
        in_specs=[VMEM] * 4 + [hbm],
        out_specs=hbm,
        scratch_shapes=[pltpu.VMEM((rows, span), jnp.bfloat16), pltpu.SemaphoreType.DMA],
        input_output_aliases={4: 0},
        name="finish_rest",
        **options,
    )(gain, inverse, left, rest, begun)


def move(bucket):
    return lax.all_to_all(bucket, "dp", split_axis=0, concat_axis=0, tiled=True)


def after(array, *others):
    return lax.optimization_barrier((array, *others))[0]


def on_device(
    inputs,
    cotangent,
    norm_gain,
    w_query,
    w_key,
    w_value,
    w_output,
    send_rows,
    receive_slots,
    owner_segments,
):
    rows, width = inputs.shape
    tensor = lax.axis_size("tensor")
    low = jnp.bfloat16
    order = lax.axis_index("tensor").astype(jnp.int32) ^ jnp.arange(4, dtype=jnp.int32)
    gain = norm_gain.reshape(1, width)

    x2 = swap(inputs, 2, tensor)
    c2 = swap(cotangent, 2, tensor)
    gain2 = swap(gain, 2, tensor)
    x1 = swap(inputs, 1, tensor)
    near_output = swap(w_output, 1, tensor)
    weights = (w_query, w_key, w_value)
    own_turned, near_turned, here, there, here_turned, there_turned, *indices = prepare(
        order,
        *weights,
        w_output,
        near_output,
        send_rows,
        receive_slots.reshape(1, rows),
        owner_segments.reshape(1, rows),
        width,
    )
    send, receive, segments = indices
    squares, part = begin(inputs, x1, cotangent, here_turned)

    x2, c2, gain2, squares, part = lax.optimization_barrier((x2, c2, gain2, squares, part))
    x3 = swap(x2, 1, tensor)
    gain_own = jnp.concatenate([gain, gain2], axis=0)
    gain_near = swap(gain_own, 1, tensor)
    own_part, near_part = add_grad(c2, there_turned, part)
    got_part = swap(near_part, 1, tensor)
    squares = add_squares(x2, squares)
    home, inverse_rms, bucket = project(
        order,
        (inputs, x1, x2, x3),
        (gain_own, gain_near),
        weights,
        squares,
        own_part,
        got_part,
        send,
    )
    near_turned = swap(after(near_turned, home), 1, tensor)
    there = swap(after(there, home), 2, tensor)
    back = attend(move(bucket), receive, segments)
    own, own_extras = bring_home(move(back), send, home)

    near = swap(own, 1, tensor)
    far_extras = swap(own_extras, 2, tensor)
    quarter = width // 4
    turn, got = own, []
    for first, span in ((0, 2 * quarter), (2 * quarter, quarter), (3 * quarter, quarter)):
        part = spread("spread_far", width + first, span, low, turn, near, own_turned, near_turned)
        got.append(swap(part if first else after(part, far_extras), 2, tensor))
        turn = after(own, part)
    grad_own = spread("spread_own", 0, width, jnp.float32, turn, near, own_turned, near_turned)
    extras = (own_extras, swap(own_extras, 1, tensor), far_extras, swap(far_extras, 1, tensor))
    layer_out = call(
        finish_out_kernel,
        "finish_out",
        shape(low, rows, width),
        (inputs, *extras, here, there),
        first=VMEM,
    )
    got[1] = after(got[1], layer_out)
    input_grad = finish_grad(inputs, cotangent, gain, inverse_rms, extras, grad_own, *got)
    return (layer_out, input_grad)


def solution(mesh):
    return jax.shard_map(
        on_device,
        mesh=mesh,
        in_specs=(
            P("dp", "tensor"),
            P("dp", "tensor"),
            P("tensor"),
            P(None, "tensor"),
            P(None, "tensor"),
            P(None, "tensor"),
            P("tensor", None),
            P("dp", None),
            P("dp"),
            P("dp"),
        ),
        out_specs=(P("dp", "tensor"), P("dp", "tensor")),
        check_vma=False,
    )
```

```python
import math

import jax
import jax.numpy as jnp
from jax import lax
from jax.experimental import pallas as pl
from jax.experimental.pallas import tpu as pltpu
from jax.sharding import PartitionSpec as P

HEAD_DIM = 128
EPSILON = 1e-05
SCALING = 1.0 / math.sqrt(HEAD_DIM)
CONTRACT_LAST = (((1,), (1,)), ((), ()))
CONTRACT_FIRST = (((0,), (0,)), ((), ()))
VMEM_LIMIT = 6 * 1024 * 1024
VMEM = pl.BlockSpec(memory_space=pltpu.VMEM)
SMEM = pl.BlockSpec(memory_space=pltpu.SMEM)
TILE = 512


def dot(left, right, dims=(((1,), (0,)), ((), ()))):
    return lax.dot_general(left, right, dims, preferred_element_type=jnp.float32)


def call(kernel, name, out_shape, operands, scratch=(), first=SMEM, rest=VMEM):
    single = not isinstance(out_shape, (list, tuple))
    shapes = [out_shape] if single else list(out_shape)
    results = pl.pallas_call(
        kernel,
        out_shape=shapes,
        in_specs=[first] + [rest] * (len(operands) - 1),
        out_specs=[VMEM] * len(shapes),
        scratch_shapes=list(scratch),
        compiler_params=pltpu.CompilerParams(vmem_limit_bytes=VMEM_LIMIT),
        cost_estimate=pl.CostEstimate(flops=1000, bytes_accessed=1000, transcendentals=0),
        name=name,
    )(*operands)
    return results[0] if single else results


def shape(dtype, *sizes):
    return jax.ShapeDtypeStruct(sizes, dtype)


def swap(array, mask, count):
    return lax.ppermute(array, "tensor", [(i, i ^ mask) for i in range(count)])


def block_start(order, slot, width):
    return pl.multiple_of(order[slot] * width, width)


def one_hot(places, rows):
    row = lax.broadcasted_iota(jnp.int32, (rows, places.shape[1]), 0)
    return jnp.where(places == row, 1.0, 0.0).astype(jnp.bfloat16)


def prepare_kernel(
    order,
    w_query,
    w_key,
    w_value,
    w_output,
    near_output,
    send,
    receive,
    segments,
    own_turned,
    near_turned,
    here,
    there,
    here_turned,
    there_turned,
    send_out,
    receive_out,
    segments_out,
):
    heads, width = w_output.shape[0], here.shape[1]
    for slot, out, turned in ((0, here, here_turned), (2, there, there_turned)):
        columns = pl.ds(block_start(order, slot, width), width)
        for part, weight in enumerate((w_output, near_output)):
            rows = slice(part * heads, (part + 1) * heads)
            block = weight[:, columns]
            out[rows, :] = block
            turned[:, rows] = block.T
    for source, target in ((send, send_out), (receive, receive_out), (segments, segments_out)):
        target[...] = source[...]
    for out, slots in ((own_turned, (0, 2)), (near_turned, (1, 3))):
        for part, slot in enumerate(slots):
            first = block_start(order, slot, width)
            for start in range(0, width, TILE):
                columns = slice(part * width + start, part * width + start + TILE)
                for place, weight in enumerate((w_query, w_key, w_value)):
                    rows = slice(place * HEAD_DIM, (place + 1) * HEAD_DIM)
                    out[rows, columns] = weight[pl.ds(first + start, TILE), :].T


def prepare(order, w_query, w_key, w_value, w_output, near_output, send, receive, segments, width):
    heads = w_query.shape[1]
    low = jnp.bfloat16
    return call(
        prepare_kernel,
        "prepare",
        [
            *[shape(low, 3 * heads, 2 * width)] * 2,
            *[shape(low, 2 * heads, width)] * 2,
            *[shape(low, width, 2 * heads)] * 2,
            shape(jnp.int32, *send.shape),
            shape(jnp.int32, *receive.shape),
            shape(jnp.int32, *segments.shape),
        ],
        (order, w_query, w_key, w_value, w_output, near_output, send, receive, segments),
    )


def sum_squares(block):
    wide = block[...].astype(jnp.float32)
    return jnp.sum(wide * wide, axis=-1, keepdims=True)


def begin_kernel(x0, x1, c0, here_turned, squares, part):
    squares[...] = sum_squares(x0) + sum_squares(x1)
    part[...] = dot(c0[...], here_turned[...])


def begin(x0, x1, c0, here_turned):
    rows, columns = x0.shape[0], here_turned.shape[1]
    shapes = [shape(jnp.float32, rows, 1), shape(jnp.float32, rows, columns)]
    return call(begin_kernel, "begin", shapes, (x0, x1, c0, here_turned), first=VMEM)


def add_grad_kernel(c2, there_turned, part, own_part, near_part):
    total = part[...] + dot(c2[...], there_turned[...])
    heads = own_part.shape[1]
    own_part[...] = total[:, :heads]
    near_part[...] = total[:, heads:]


def add_grad(c2, there_turned, part):
    shapes = [shape(jnp.float32, part.shape[0], part.shape[1] // 2)] * 2
    return call(add_grad_kernel, "add_grad", shapes, (c2, there_turned, part), first=VMEM)


def add_squares_kernel(x2, squares_in, squares):
    squares[...] = squares_in[...] + sum_squares(x2)


def add_squares(x2, squares):
    out = shape(jnp.float32, *squares.shape)
    return call(add_squares_kernel, "add_squares", out, (x2, squares), first=VMEM)


def project_kernel(
    order,
    x0,
    x1,
    x2,
    x3,
    gain_own,
    gain_near,
    w_query,
    w_key,
    w_value,
    squares,
    own_part,
    got_part,
    send,
    home,
    inverse,
    bucket,
    total,
):
    blocks = (x0, x1, x2, x3)
    width = x0.shape[1]
    mean = (squares[...] + sum_squares(x3)) / (width * len(blocks))
    inverse_rms = lax.rsqrt(mean + EPSILON)
    inverse[...] = inverse_rms
    head_grad = (own_part[...] + got_part[...]).astype(jnp.bfloat16)
    for index, block in enumerate(blocks):
        gain = (gain_own, gain_near)[index % 2][index // 2 : index // 2 + 1, :]
        scaled = block[...].astype(jnp.float32) * inverse_rms
        normed = (scaled * gain.astype(jnp.float32)).astype(jnp.bfloat16)
        here = pl.ds(block_start(order, index, width), width)
        weights = jnp.concatenate([w_query[here, :], w_key[here, :], w_value[here, :]], axis=1)
        product = dot(normed, weights)
        total[...] = total[...] + product if index else product
    rounded = total[...].astype(jnp.bfloat16)
    home[...] = rounded
    chosen = one_hot(send[...], rounded.shape[0])
    split = rounded.shape[1]
    bucket[:, :split] = dot(chosen, rounded, CONTRACT_FIRST).astype(jnp.bfloat16)
    bucket[:, split:] = dot(chosen, head_grad, CONTRACT_FIRST).astype(jnp.bfloat16)


def project(order, blocks, gains, weights, squares, own_part, got_part, send):
    rows = blocks[0].shape[0]
    columns = 3 * HEAD_DIM
    return call(
        project_kernel,
        "project",
        [
            shape(jnp.bfloat16, rows, columns),
            shape(jnp.float32, rows, 1),
            shape(jnp.bfloat16, send.shape[1], columns + HEAD_DIM),
        ],
        (order, *blocks, *gains, *weights, squares, own_part, got_part, send),
        scratch=[pltpu.VMEM((rows, columns), jnp.float32)],
    )


def attend_kernel(moved, receive, segments, back):
    place = one_hot(receive[...], moved.shape[0])
    rows = dot(place, moved[...], CONTRACT_FIRST).astype(jnp.bfloat16)
    queries, key_rows, value_rows, head_grad = (
        rows[:, index * HEAD_DIM : (index + 1) * HEAD_DIM] for index in range(4)
    )
    count = rows.shape[0]
    down = lax.broadcasted_iota(jnp.int32, (count, count), 0)
    across = lax.broadcasted_iota(jnp.int32, (count, count), 1)
    stays = segments[...]
    own_stay = jnp.sum(jnp.where(down == across, stays, 0), axis=1, keepdims=True)
    allowed = (own_stay == stays) & (across <= down)
    scores = jnp.where(allowed, dot(queries, key_rows, CONTRACT_LAST) * SCALING, -1e30)
    raised = jnp.exp(scores - jnp.max(scores, axis=-1, keepdims=True))
    softmax_out = raised / jnp.sum(raised, axis=-1, keepdims=True)
    low_weights = softmax_out.astype(jnp.bfloat16)
    attended = dot(low_weights, value_rows).astype(jnp.bfloat16)
    grad_value = dot(low_weights, head_grad, CONTRACT_FIRST).astype(jnp.bfloat16)
    grad_probs = dot(head_grad, value_rows, CONTRACT_LAST)
    inner = jnp.sum(softmax_out * grad_probs, axis=-1, keepdims=True)
    grad_scores = (softmax_out * (grad_probs - inner) * SCALING).astype(jnp.bfloat16)
    grad_query = dot(grad_scores, key_rows).astype(jnp.bfloat16)
    grad_key = dot(grad_scores, queries, CONTRACT_FIRST).astype(jnp.bfloat16)
    results = jnp.concatenate([grad_query, grad_key, grad_value, attended], axis=1)
    back[...] = dot(place, results).astype(jnp.bfloat16)


def attend(moved, receive, segments):
    out = shape(jnp.bfloat16, *moved.shape)
    return call(attend_kernel, "attend", out, (moved, receive, segments), first=VMEM)


def write_parts(value, out):
    out[...] = jnp.zeros_like(out)
    for place in range(3):
        low = value.astype(jnp.bfloat16)
        out[:, place : place + 1] = low
        value = value - low.astype(jnp.float32)


def read_parts(parts):
    return sum(parts[:, place : place + 1].astype(jnp.float32) for place in (2, 1, 0))


def bring_home_kernel(moved, send, home, grads, extras):
    chosen = one_hot(send[...], grads.shape[0])
    rows = dot(chosen, moved[...])
    split = 3 * HEAD_DIM
    grads[...] = rows[:, :split].astype(jnp.bfloat16)
    extras[:, :HEAD_DIM] = rows[:, split:].astype(jnp.bfloat16)
    product = rows[:, :split] * home[...].astype(jnp.float32)
    row_dot = jnp.sum(product, axis=-1, keepdims=True)
    write_parts(row_dot, extras.at[:, HEAD_DIM:])


def bring_home(moved, send, home):
    rows = home.shape[0]
    shapes = [shape(jnp.bfloat16, rows, 3 * HEAD_DIM), shape(jnp.bfloat16, rows, 2 * HEAD_DIM)]
    return call(bring_home_kernel, "bring_home", shapes, (moved, send, home), first=VMEM)


def spread_kernel(first):
    def kernel(own, near, weights, near_weights, out, held, total, sems):
        span = held.shape[1]
        copies = []
        for index, start in enumerate(range(0, span, TILE)):
            source = near_weights.at[:, pl.ds(first + start, TILE)]
            target = held.at[:, pl.ds(start, TILE)]
            copies.append(pltpu.make_async_copy(source, target, sems.at[index]))
            copies[-1].start()
        own_rows, near_rows = own[...], near[...]
        for start in range(0, span, TILE):
            columns = slice(first + start, first + start + TILE)
            total[:, start : start + TILE] = dot(own_rows, weights[:, columns])
        for index, start in enumerate(range(0, span, TILE)):
            copies[index].wait()
            tile = slice(start, start + TILE)
            result = total[:, tile] + dot(near_rows, held[:, tile])
            out[:, tile] = result.astype(out.dtype)

    return kernel


def spread(name, first, span, dtype, own, near, weights, near_weights, flops=1000):
    rows, depth = own.shape
    return pl.pallas_call(
        spread_kernel(first),
        out_shape=shape(dtype, rows, span),
        in_specs=[VMEM] * 3 + [pl.BlockSpec(memory_space=pl.ANY)],
        out_specs=VMEM,
        scratch_shapes=[
            pltpu.VMEM((depth, span), jnp.bfloat16),
            pltpu.VMEM((rows, span), jnp.float32),
            pltpu.SemaphoreType.DMA((span // TILE,)),
        ],
        compiler_params=pltpu.CompilerParams(vmem_limit_bytes=VMEM_LIMIT),
        cost_estimate=pl.CostEstimate(flops=flops, bytes_accessed=1000, transcendentals=0),
        name=name,
    )(own, near, weights, near_weights)


def finish_out_kernel(inputs, own, near, far, last, here, there, out):
    width = inputs.shape[1]
    chip = jnp.concatenate([own[:, :HEAD_DIM], near[:, :HEAD_DIM]], axis=1)
    other = jnp.concatenate([far[:, :HEAD_DIM], last[:, :HEAD_DIM]], axis=1)
    for start in range(0, width, TILE):
        tile = slice(start, start + TILE)
        total = dot(chip, here[:, tile]) + dot(other, there[:, tile])
        out[:, tile] = (inputs[:, tile].astype(jnp.float32) + total).astype(jnp.bfloat16)


def finish_most_kernel(
    inputs, cotangent, gain, inverse, own, near, far, last, grad_own, got, middle, *outs
):
    out, left, held, sem = outs
    row_dot = sum(read_parts(extras[:, HEAD_DIM:]) for extras in (own, near, far, last))
    mean_dot = row_dot / (4 * inputs.shape[1])
    inverse_rms = inverse[...]
    most = held.shape[1]
    for start in range(0, inputs.shape[1], TILE):
        tile = slice(start, start + TILE)
        grad_normed = grad_own[:, tile]
        if start < got.shape[1]:
            grad_normed = grad_normed + got[:, tile].astype(jnp.float32)
        elif start < most:
            part = slice(start - got.shape[1], start - got.shape[1] + TILE)
            grad_normed = grad_normed + middle[:, part].astype(jnp.float32)
        grad_hat = grad_normed * gain[:, tile].astype(jnp.float32)
        scaled = inputs[:, tile].astype(jnp.float32) * inverse_rms
        change = inverse_rms * (grad_hat - scaled * mean_dot)
        result = cotangent[:, tile].astype(jnp.float32) + change
        if start < most:
            held[:, tile] = result.astype(jnp.bfloat16)
        else:
            left[:, start - most : start - most + TILE] = result
    copy = pltpu.make_async_copy(held, out.at[:, pl.ds(0, most)], sem)
    copy.start()
    copy.wait()


def finish_rest_kernel(gain, inverse, left, rest, before, out, held, sems):
    span = rest.shape[1]
    first = out.shape[1] - span
    half = span // 2
    copies = []
    for index, start in enumerate(range(0, span, half)):
        tile = slice(start, start + half)
        columns = slice(first + start, first + start + half)
        grad_hat = rest[:, tile].astype(jnp.float32) * gain[:, columns].astype(jnp.float32)
        held[:, tile] = (left[:, tile] + inverse[...] * grad_hat).astype(jnp.bfloat16)
        target = out.at[:, pl.ds(first + start, half)]
        copies.append(
            pltpu.make_async_copy(held.at[:, pl.ds(start, half)], target, sems.at[index])
        )
        copies[-1].start()
    for copy in copies:
        copy.wait()


def finish_grad(inputs, cotangent, gain, inverse, extras, grad_own, got, middle, rest):
    rows, width = inputs.shape
    span = rest.shape[1]
    hbm = pl.BlockSpec(memory_space=pltpu.HBM)
    options = dict(
        compiler_params=pltpu.CompilerParams(vmem_limit_bytes=VMEM_LIMIT),
        cost_estimate=pl.CostEstimate(flops=1000, bytes_accessed=1000, transcendentals=0),
    )
    begun, left = pl.pallas_call(
        finish_most_kernel,
        out_shape=[shape(jnp.bfloat16, rows, width), shape(jnp.float32, rows, span)],
        in_specs=[VMEM] * 11,
        out_specs=[hbm, VMEM],
        scratch_shapes=[pltpu.VMEM((rows, width - span), jnp.bfloat16), pltpu.SemaphoreType.DMA],
        name="finish_most",
        **options,
    )(inputs, cotangent, gain, inverse, *extras, grad_own, got, middle)
    return pl.pallas_call(
        finish_rest_kernel,
        out_shape=shape(jnp.bfloat16, rows, width),
        in_specs=[VMEM] * 4 + [hbm],
        out_specs=hbm,
        scratch_shapes=[pltpu.VMEM((rows, span), jnp.bfloat16), pltpu.SemaphoreType.DMA((2,))],
        input_output_aliases={4: 0},
        name="finish_rest",
        **options,
    )(gain, inverse, left, rest, begun)


def move(bucket):
    return lax.all_to_all(bucket, "dp", split_axis=0, concat_axis=0, tiled=True)


def after(array, *others):
    return lax.optimization_barrier((array, *others))[0]


def on_device(
    inputs,
    cotangent,
    norm_gain,
    w_query,
    w_key,
    w_value,
    w_output,
    send_rows,
    receive_slots,
    owner_segments,
):
    rows, width = inputs.shape
    tensor = lax.axis_size("tensor")
    low = jnp.bfloat16
    order = lax.axis_index("tensor").astype(jnp.int32) ^ jnp.arange(4, dtype=jnp.int32)
    gain = norm_gain.reshape(1, width)

    x2 = swap(inputs, 2, tensor)
    c2 = swap(cotangent, 2, tensor)
    gain2 = swap(gain, 2, tensor)
    x1 = swap(inputs, 1, tensor)
    near_output = swap(w_output, 1, tensor)
    weights = (w_query, w_key, w_value)
    own_turned, near_turned, here, there, here_turned, there_turned, *indices = prepare(
        order,
        *weights,
        w_output,
        near_output,
        send_rows,
        receive_slots.reshape(1, rows),
        owner_segments.reshape(1, rows),
        width,
    )
    send, receive, segments = indices
    squares, part = begin(inputs, x1, cotangent, here_turned)

    x2, c2, gain2, squares, part = lax.optimization_barrier((x2, c2, gain2, squares, part))
    x3 = swap(x2, 1, tensor)
    gain_own = jnp.concatenate([gain, gain2], axis=0)
    gain_near = swap(gain_own, 1, tensor)
    own_part, near_part = add_grad(c2, there_turned, part)
    got_part = swap(near_part, 1, tensor)
    squares = add_squares(x2, squares)
    home, inverse_rms, bucket = project(
        order,
        (inputs, x1, x2, x3),
        (gain_own, gain_near),
        weights,
        squares,
        own_part,
        got_part,
        send,
    )
    near_turned = swap(after(near_turned, home), 1, tensor)
    there = swap(after(there, home), 2, tensor)
    back = attend(move(bucket), receive, segments)
    own, own_extras = bring_home(move(back), send, home)

    near = swap(own, 1, tensor)
    far_extras = swap(own_extras, 2, tensor)
    quarter = width // 4
    turn, got = own, []
    for first, span in ((0, 2 * quarter), (2 * quarter, quarter), (3 * quarter, quarter)):
        flops = 4 * rows * span * width if first else 1000
        sides = (turn, near, own_turned, near_turned)
        part = spread("spread_far", width + first, span, low, *sides, flops=flops)
        got.append(swap(part, 2, tensor))
        turn = after(own, part, far_extras)
    grad_own = spread("spread_own", 0, width, jnp.float32, turn, near, own_turned, near_turned)
    extras = (own_extras, swap(own_extras, 1, tensor), far_extras, swap(far_extras, 1, tensor))
    layer_out = call(
        finish_out_kernel,
        "finish_out",
        shape(low, rows, width),
        (inputs, *extras, here, there),
        first=VMEM,
    )
    got[1] = after(got[1], layer_out)
    input_grad = finish_grad(inputs, cotangent, gain, inverse_rms, extras, grad_own, *got)
    return (layer_out, input_grad)


def solution(mesh):
    return jax.shard_map(
        on_device,
        mesh=mesh,
        in_specs=(
            P("dp", "tensor"),
            P("dp", "tensor"),
            P("tensor"),
            P(None, "tensor"),
            P(None, "tensor"),
            P(None, "tensor"),
            P("tensor", None),
            P("dp", None),
            P("dp"),
            P("dp"),
        ),
        out_specs=(P("dp", "tensor"), P("dp", "tensor")),
        check_vma=False,
    )
```

```python
import math

import jax
import jax.numpy as jnp
from jax import lax
from jax.experimental import pallas as pl
from jax.experimental.pallas import tpu as pltpu
from jax.sharding import PartitionSpec as P

HEAD_DIM = 128
EPSILON = 1e-05
SCALING = 1.0 / math.sqrt(HEAD_DIM)
CONTRACT_LAST = (((1,), (1,)), ((), ()))
CONTRACT_FIRST = (((0,), (0,)), ((), ()))
VMEM_LIMIT = 6 * 1024 * 1024
VMEM = pl.BlockSpec(memory_space=pltpu.VMEM)
SMEM = pl.BlockSpec(memory_space=pltpu.SMEM)
TILE = 512


def dot(left, right, dims=(((1,), (0,)), ((), ()))):
    return lax.dot_general(left, right, dims, preferred_element_type=jnp.float32)


def call(kernel, name, out_shape, operands, scratch=(), first=SMEM, rest=VMEM):
    single = not isinstance(out_shape, (list, tuple))
    shapes = [out_shape] if single else list(out_shape)
    results = pl.pallas_call(
        kernel,
        out_shape=shapes,
        in_specs=[first] + [rest] * (len(operands) - 1),
        out_specs=[VMEM] * len(shapes),
        scratch_shapes=list(scratch),
        compiler_params=pltpu.CompilerParams(vmem_limit_bytes=VMEM_LIMIT),
        cost_estimate=pl.CostEstimate(flops=1000, bytes_accessed=1000, transcendentals=0),
        name=name,
    )(*operands)
    return results[0] if single else results


def shape(dtype, *sizes):
    return jax.ShapeDtypeStruct(sizes, dtype)


def swap(array, mask, count):
    return lax.ppermute(array, "tensor", [(i, i ^ mask) for i in range(count)])


def block_start(order, slot, width):
    return pl.multiple_of(order[slot] * width, width)


def one_hot(places, rows):
    row = lax.broadcasted_iota(jnp.int32, (rows, places.shape[1]), 0)
    return jnp.where(places == row, 1.0, 0.0).astype(jnp.bfloat16)


def prepare_kernel(
    order,
    w_query,
    w_key,
    w_value,
    w_output,
    near_output,
    send,
    receive,
    segments,
    own_turned,
    near_turned,
    here,
    there,
    here_turned,
    there_turned,
    send_out,
    receive_out,
    segments_out,
):
    heads, width = w_output.shape[0], here.shape[1]
    for slot, out, turned in ((0, here, here_turned), (2, there, there_turned)):
        columns = pl.ds(block_start(order, slot, width), width)
        for part, weight in enumerate((w_output, near_output)):
            rows = slice(part * heads, (part + 1) * heads)
            block = weight[:, columns]
            out[rows, :] = block
            turned[:, rows] = block.T
    for source, target in ((send, send_out), (receive, receive_out), (segments, segments_out)):
        target[...] = source[...]
    for out, slots in ((own_turned, (0, 2)), (near_turned, (1, 3))):
        for part, slot in enumerate(slots):
            first = block_start(order, slot, width)
            for start in range(0, width, TILE):
                columns = slice(part * width + start, part * width + start + TILE)
                for place, weight in enumerate((w_query, w_key, w_value)):
                    rows = slice(place * HEAD_DIM, (place + 1) * HEAD_DIM)
                    out[rows, columns] = weight[pl.ds(first + start, TILE), :].T


def prepare(order, w_query, w_key, w_value, w_output, near_output, send, receive, segments, width):
    heads = w_query.shape[1]
    low = jnp.bfloat16
    return call(
        prepare_kernel,
        "prepare",
        [
            *[shape(low, 3 * heads, 2 * width)] * 2,
            *[shape(low, 2 * heads, width)] * 2,
            *[shape(low, width, 2 * heads)] * 2,
            shape(jnp.int32, *send.shape),
            shape(jnp.int32, *receive.shape),
            shape(jnp.int32, *segments.shape),
        ],
        (order, w_query, w_key, w_value, w_output, near_output, send, receive, segments),
    )


def sum_squares(block):
    wide = block[...].astype(jnp.float32)
    return jnp.sum(wide * wide, axis=-1, keepdims=True)


def begin_kernel(x0, x1, c0, here_turned, squares, part):
    squares[...] = sum_squares(x0) + sum_squares(x1)
    part[...] = dot(c0[...], here_turned[...])


def begin(x0, x1, c0, here_turned):
    rows, columns = x0.shape[0], here_turned.shape[1]
    shapes = [shape(jnp.float32, rows, 1), shape(jnp.float32, rows, columns)]
    return call(begin_kernel, "begin", shapes, (x0, x1, c0, here_turned), first=VMEM)


def add_grad_kernel(c2, there_turned, part, own_part, near_part, held, sems):
    copies = []
    for index, start in enumerate(range(0, held.shape[1], TILE)):
        tile = pl.ds(start, TILE)
        copies.append(pltpu.make_async_copy(c2.at[:, tile], held.at[:, tile], sems.at[index]))
        copies[-1].start()
    total = part[...]
    for index, copy in enumerate(copies):
        tile = slice(index * TILE, (index + 1) * TILE)
        copy.wait()
        total = total + dot(held[:, tile], there_turned[tile, :])
    heads = own_part.shape[1]
    own_part[...] = total[:, :heads]
    near_part[...] = total[:, heads:]


def add_grad(c2, there_turned, part):
    rows, width = c2.shape
    return call(
        add_grad_kernel,
        "add_grad",
        [shape(jnp.float32, rows, part.shape[1] // 2)] * 2,
        (c2, there_turned, part),
        scratch=[pltpu.VMEM((rows, width), c2.dtype), pltpu.SemaphoreType.DMA((width // TILE,))],
        first=pl.BlockSpec(memory_space=pl.ANY),
    )


def add_squares_kernel(x2, squares_in, squares):
    squares[...] = squares_in[...] + sum_squares(x2)


def add_squares(x2, squares):
    out = shape(jnp.float32, *squares.shape)
    return call(add_squares_kernel, "add_squares", out, (x2, squares), first=VMEM)


def project_kernel(
    order,
    x0,
    x1,
    x2,
    x3,
    gain_own,
    gain_near,
    w_query,
    w_key,
    w_value,
    squares,
    own_part,
    got_part,
    send,
    home,
    inverse,
    bucket,
    total,
):
    blocks = (x0, x1, x2, x3)
    width = x0.shape[1]
    mean = (squares[...] + sum_squares(x3)) / (width * len(blocks))
    inverse_rms = lax.rsqrt(mean + EPSILON)
    inverse[...] = inverse_rms
    head_grad = (own_part[...] + got_part[...]).astype(jnp.bfloat16)
    for index, block in enumerate(blocks):
        gain = (gain_own, gain_near)[index % 2][index // 2 : index // 2 + 1, :]
        scaled = block[...].astype(jnp.float32) * inverse_rms
        normed = (scaled * gain.astype(jnp.float32)).astype(jnp.bfloat16)
        here = pl.ds(block_start(order, index, width), width)
        weights = jnp.concatenate([w_query[here, :], w_key[here, :], w_value[here, :]], axis=1)
        product = dot(normed, weights)
        total[...] = total[...] + product if index else product
    rounded = total[...].astype(jnp.bfloat16)
    home[...] = rounded
    chosen = one_hot(send[...], rounded.shape[0])
    split = rounded.shape[1]
    bucket[:, :split] = dot(chosen, rounded, CONTRACT_FIRST).astype(jnp.bfloat16)
    bucket[:, split:] = dot(chosen, head_grad, CONTRACT_FIRST).astype(jnp.bfloat16)


def project(order, blocks, gains, weights, squares, own_part, got_part, send):
    rows = blocks[0].shape[0]
    columns = 3 * HEAD_DIM
    return call(
        project_kernel,
        "project",
        [
            shape(jnp.bfloat16, rows, columns),
            shape(jnp.float32, rows, 1),
            shape(jnp.bfloat16, send.shape[1], columns + HEAD_DIM),
        ],
        (order, *blocks, *gains, *weights, squares, own_part, got_part, send),
        scratch=[pltpu.VMEM((rows, columns), jnp.float32)],
    )


def attend_kernel(moved, receive, segments, back):
    place = one_hot(receive[...], moved.shape[0])
    rows = dot(place, moved[...], CONTRACT_FIRST).astype(jnp.bfloat16)
    queries, key_rows, value_rows, head_grad = (
        rows[:, index * HEAD_DIM : (index + 1) * HEAD_DIM] for index in range(4)
    )
    count = rows.shape[0]
    down = lax.broadcasted_iota(jnp.int32, (count, count), 0)
    across = lax.broadcasted_iota(jnp.int32, (count, count), 1)
    stays = segments[...]
    own_stay = jnp.sum(jnp.where(down == across, stays, 0), axis=1, keepdims=True)
    allowed = (own_stay == stays) & (across <= down)
    scores = jnp.where(allowed, dot(queries, key_rows, CONTRACT_LAST) * SCALING, -1e30)
    raised = jnp.exp(scores - jnp.max(scores, axis=-1, keepdims=True))
    softmax_out = raised / jnp.sum(raised, axis=-1, keepdims=True)
    low_weights = softmax_out.astype(jnp.bfloat16)
    attended = dot(low_weights, value_rows).astype(jnp.bfloat16)
    grad_value = dot(low_weights, head_grad, CONTRACT_FIRST).astype(jnp.bfloat16)
    grad_probs = dot(head_grad, value_rows, CONTRACT_LAST)
    inner = jnp.sum(softmax_out * grad_probs, axis=-1, keepdims=True)
    grad_scores = (softmax_out * (grad_probs - inner) * SCALING).astype(jnp.bfloat16)
    grad_query = dot(grad_scores, key_rows).astype(jnp.bfloat16)
    grad_key = dot(grad_scores, queries, CONTRACT_FIRST).astype(jnp.bfloat16)
    results = jnp.concatenate([grad_query, grad_key, grad_value, attended], axis=1)
    back[...] = dot(place, results).astype(jnp.bfloat16)


def attend(moved, receive, segments):
    out = shape(jnp.bfloat16, *moved.shape)
    return call(attend_kernel, "attend", out, (moved, receive, segments), first=VMEM)


def write_parts(value, out):
    out[...] = jnp.zeros_like(out)
    for place in range(3):
        low = value.astype(jnp.bfloat16)
        out[:, place : place + 1] = low
        value = value - low.astype(jnp.float32)


def read_parts(parts):
    return sum(parts[:, place : place + 1].astype(jnp.float32) for place in (2, 1, 0))


def bring_home_kernel(moved, send, home, grads, extras):
    chosen = one_hot(send[...], grads.shape[0])
    rows = dot(chosen, moved[...])
    split = 3 * HEAD_DIM
    grads[...] = rows[:, :split].astype(jnp.bfloat16)
    extras[:, :HEAD_DIM] = rows[:, split:].astype(jnp.bfloat16)
    product = rows[:, :split] * home[...].astype(jnp.float32)
    row_dot = jnp.sum(product, axis=-1, keepdims=True)
    write_parts(row_dot, extras.at[:, HEAD_DIM:])


def bring_home(moved, send, home):
    rows = home.shape[0]
    shapes = [shape(jnp.bfloat16, rows, 3 * HEAD_DIM), shape(jnp.bfloat16, rows, 2 * HEAD_DIM)]
    return call(bring_home_kernel, "bring_home", shapes, (moved, send, home), first=VMEM)


def spread_kernel(first):
    def kernel(own, near, weights, near_weights, out):
        own_rows, near_rows = own[...], near[...]
        for start in range(0, out.shape[1], TILE):
            columns = slice(first + start, first + start + TILE)
            total = dot(own_rows, weights[:, columns]) + dot(near_rows, near_weights[:, columns])
            out[:, start : start + TILE] = total.astype(out.dtype)

    return kernel


def spread(name, first, span, dtype, own, near, weights, near_weights, flops=1000):
    return pl.pallas_call(
        spread_kernel(first),
        out_shape=shape(dtype, own.shape[0], span),
        in_specs=[VMEM] * 4,
        out_specs=VMEM,
        compiler_params=pltpu.CompilerParams(vmem_limit_bytes=VMEM_LIMIT),
        cost_estimate=pl.CostEstimate(flops=flops, bytes_accessed=1000, transcendentals=0),
        name=name,
    )(own, near, weights, near_weights)


def finish_out_kernel(inputs, own, near, far, last, here, there, out):
    width = inputs.shape[1]
    chip = jnp.concatenate([own[:, :HEAD_DIM], near[:, :HEAD_DIM]], axis=1)
    other = jnp.concatenate([far[:, :HEAD_DIM], last[:, :HEAD_DIM]], axis=1)
    for start in range(0, width, TILE):
        tile = slice(start, start + TILE)
        total = dot(chip, here[:, tile]) + dot(other, there[:, tile])
        out[:, tile] = (inputs[:, tile].astype(jnp.float32) + total).astype(jnp.bfloat16)


def finish_most_kernel(
    inputs, cotangent, gain, inverse, own, near, far, last, grad_own, *pieces
):
    *pieces, out, left, held, sem = pieces
    tiles = [
        piece.at[:, start : start + TILE]
        for piece in pieces
        for start in range(0, piece.shape[1], TILE)
    ]
    row_dot = sum(read_parts(extras[:, HEAD_DIM:]) for extras in (own, near, far, last))
    mean_dot = row_dot / (4 * inputs.shape[1])
    inverse_rms = inverse[...]
    most = held.shape[1]
    for start in range(0, inputs.shape[1], TILE):
        tile = slice(start, start + TILE)
        grad_normed = grad_own[:, tile]
        if start < most:
            grad_normed = grad_normed + tiles[start // TILE][...].astype(jnp.float32)
        grad_hat = grad_normed * gain[:, tile].astype(jnp.float32)
        scaled = inputs[:, tile].astype(jnp.float32) * inverse_rms
        change = inverse_rms * (grad_hat - scaled * mean_dot)
        result = cotangent[:, tile].astype(jnp.float32) + change
        if start < most:
            held[:, tile] = result.astype(jnp.bfloat16)
        else:
            left[:, start - most : start - most + TILE] = result
    copy = pltpu.make_async_copy(held, out.at[:, pl.ds(0, most)], sem)
    copy.start()
    copy.wait()


def finish_rest_kernel(gain, inverse, left, rest, before, out, held, sems):
    span = rest.shape[1]
    first = out.shape[1] - span
    half = span // 2
    copies = []
    for index, start in enumerate(range(0, span, half)):
        tile = slice(start, start + half)
        columns = slice(first + start, first + start + half)
        grad_hat = rest[:, tile].astype(jnp.float32) * gain[:, columns].astype(jnp.float32)
        held[:, tile] = (left[:, tile] + inverse[...] * grad_hat).astype(jnp.bfloat16)
        target = out.at[:, pl.ds(first + start, half)]
        copies.append(
            pltpu.make_async_copy(held.at[:, pl.ds(start, half)], target, sems.at[index])
        )
        copies[-1].start()
    for copy in copies:
        copy.wait()


def finish_grad(inputs, cotangent, gain, inverse, extras, grad_own, pieces):
    rows, width = inputs.shape
    *pieces, rest = pieces
    span = rest.shape[1]
    hbm = pl.BlockSpec(memory_space=pltpu.HBM)
    options = dict(
        compiler_params=pltpu.CompilerParams(vmem_limit_bytes=VMEM_LIMIT),
        cost_estimate=pl.CostEstimate(flops=1000, bytes_accessed=1000, transcendentals=0),
    )
    begun, left = pl.pallas_call(
        finish_most_kernel,
        out_shape=[shape(jnp.bfloat16, rows, width), shape(jnp.float32, rows, span)],
        in_specs=[VMEM] * (9 + len(pieces)),
        out_specs=[hbm, VMEM],
        scratch_shapes=[pltpu.VMEM((rows, width - span), jnp.bfloat16), pltpu.SemaphoreType.DMA],
        name="finish_most",
        **options,
    )(inputs, cotangent, gain, inverse, *extras, grad_own, *pieces)
    return pl.pallas_call(
        finish_rest_kernel,
        out_shape=shape(jnp.bfloat16, rows, width),
        in_specs=[VMEM] * 4 + [hbm],
        out_specs=hbm,
        scratch_shapes=[pltpu.VMEM((rows, span), jnp.bfloat16), pltpu.SemaphoreType.DMA((2,))],
        input_output_aliases={4: 0},
        name="finish_rest",
        **options,
    )(gain, inverse, left, rest, begun)


def move(bucket):
    return lax.all_to_all(bucket, "dp", split_axis=0, concat_axis=0, tiled=True)


def after(array, *others):
    return lax.optimization_barrier((array, *others))[0]


def on_device(
    inputs,
    cotangent,
    norm_gain,
    w_query,
    w_key,
    w_value,
    w_output,
    send_rows,
    receive_slots,
    owner_segments,
):
    rows, width = inputs.shape
    tensor = lax.axis_size("tensor")
    low = jnp.bfloat16
    order = lax.axis_index("tensor").astype(jnp.int32) ^ jnp.arange(4, dtype=jnp.int32)
    gain = norm_gain.reshape(1, width)

    x2 = swap(inputs, 2, tensor)
    c2 = swap(cotangent, 2, tensor)
    gain2 = swap(gain, 2, tensor)
    x1 = swap(inputs, 1, tensor)
    near_output = swap(w_output, 1, tensor)
    weights = (w_query, w_key, w_value)
    own_turned, near_turned, here, there, here_turned, there_turned, *indices = prepare(
        order,
        *weights,
        w_output,
        near_output,
        send_rows,
        receive_slots.reshape(1, rows),
        owner_segments.reshape(1, rows),
        width,
    )
    send, receive, segments = indices
    squares, part = begin(inputs, x1, cotangent, here_turned)

    x2, c2, gain2, squares, part = lax.optimization_barrier((x2, c2, gain2, squares, part))
    x3 = swap(x2, 1, tensor)
    gain_own = jnp.concatenate([gain, gain2], axis=0)
    gain_near = swap(gain_own, 1, tensor)
    own_part, near_part = add_grad(c2, there_turned, part)
    got_part = swap(near_part, 1, tensor)
    squares = add_squares(x2, squares)
    home, inverse_rms, bucket = project(
        order,
        (inputs, x1, x2, x3),
        (gain_own, gain_near),
        weights,
        squares,
        own_part,
        got_part,
        send,
    )
    near_turned = swap(after(near_turned, home), 1, tensor)
    there = swap(after(there, home), 2, tensor)
    back = attend(move(bucket), receive, segments)
    own, own_extras = bring_home(move(back), send, home)

    near = swap(own, 1, tensor)
    far_extras = swap(own_extras, 2, tensor)
    quarter = width // 4
    turn, got = own, []
    for first, span in ((0, 2 * quarter), (2 * quarter, quarter), (3 * quarter, quarter)):
        flops = 4 * rows * span * width if first else 1000
        sides = (turn, near, own_turned, near_turned)
        part = spread("spread_far", width + first, span, low, *sides, flops=flops)
        got.append(swap(part, 2, tensor))
        turn = after(own, part, far_extras)
    grad_own = spread("spread_own", 0, width, jnp.float32, turn, near, own_turned, near_turned)
    extras = (own_extras, swap(own_extras, 1, tensor), far_extras, swap(far_extras, 1, tensor))
    layer_out = call(
        finish_out_kernel,
        "finish_out",
        shape(low, rows, width),
        (inputs, *extras, here, there),
        first=VMEM,
    )
    got[1] = after(got[1], layer_out)
    input_grad = finish_grad(inputs, cotangent, gain, inverse_rms, extras, grad_own, got)
    return (layer_out, input_grad)


def solution(mesh):
    return jax.shard_map(
        on_device,
        mesh=mesh,
        in_specs=(
            P("dp", "tensor"),
            P("dp", "tensor"),
            P("tensor"),
            P(None, "tensor"),
            P(None, "tensor"),
            P(None, "tensor"),
            P("tensor", None),
            P("dp", None),
            P("dp"),
            P("dp"),
        ),
        out_specs=(P("dp", "tensor"), P("dp", "tensor")),
        check_vma=False,
    )
```

```python
import math

import jax
import jax.numpy as jnp
from jax import lax
from jax.experimental import pallas as pl
from jax.experimental.pallas import tpu as pltpu
from jax.sharding import PartitionSpec as P

HEAD_DIM = 128
EPSILON = 1e-05
SCALING = 1.0 / math.sqrt(HEAD_DIM)
CONTRACT_LAST = (((1,), (1,)), ((), ()))
CONTRACT_FIRST = (((0,), (0,)), ((), ()))
VMEM_LIMIT = 6 * 1024 * 1024
VMEM = pl.BlockSpec(memory_space=pltpu.VMEM)
SMEM = pl.BlockSpec(memory_space=pltpu.SMEM)
TILE = 512
SQUARES_FLOPS = 10000000000
HOME_FLOPS = 80000000000


def dot(left, right, dims=(((1,), (0,)), ((), ()))):
    return lax.dot_general(left, right, dims, preferred_element_type=jnp.float32)


def call(kernel, name, out_shape, operands, scratch=(), first=SMEM, rest=VMEM, flops=1000):
    single = not isinstance(out_shape, (list, tuple))
    shapes = [out_shape] if single else list(out_shape)
    results = pl.pallas_call(
        kernel,
        out_shape=shapes,
        in_specs=[first] + [rest] * (len(operands) - 1),
        out_specs=[VMEM] * len(shapes),
        scratch_shapes=list(scratch),
        compiler_params=pltpu.CompilerParams(vmem_limit_bytes=VMEM_LIMIT),
        cost_estimate=pl.CostEstimate(flops=flops, bytes_accessed=1000, transcendentals=0),
        name=name,
    )(*operands)
    return results[0] if single else results


def shape(dtype, *sizes):
    return jax.ShapeDtypeStruct(sizes, dtype)


def swap(array, mask, count):
    return lax.ppermute(array, "tensor", [(i, i ^ mask) for i in range(count)])


def block_start(order, slot, width):
    return pl.multiple_of(order[slot] * width, width)


def one_hot(places, rows):
    row = lax.broadcasted_iota(jnp.int32, (rows, places.shape[1]), 0)
    return jnp.where(places == row, 1.0, 0.0).astype(jnp.bfloat16)


def prepare_kernel(
    order,
    w_query,
    w_key,
    w_value,
    w_output,
    near_output,
    send,
    receive,
    segments,
    own_turned,
    near_turned,
    here,
    there,
    here_turned,
    there_turned,
    send_out,
    receive_out,
    segments_out,
):
    heads, width = w_output.shape[0], here.shape[1]
    for slot, out, turned in ((0, here, here_turned), (2, there, there_turned)):
        columns = pl.ds(block_start(order, slot, width), width)
        for part, weight in enumerate((w_output, near_output)):
            rows = slice(part * heads, (part + 1) * heads)
            block = weight[:, columns]
            out[rows, :] = block
            turned[:, rows] = block.T
    for source, target in ((send, send_out), (receive, receive_out), (segments, segments_out)):
        target[...] = source[...]
    for out, slots in ((own_turned, (0, 2)), (near_turned, (1, 3))):
        for part, slot in enumerate(slots):
            first = block_start(order, slot, width)
            for start in range(0, width, TILE):
                columns = slice(part * width + start, part * width + start + TILE)
                for place, weight in enumerate((w_query, w_key, w_value)):
                    rows = slice(place * HEAD_DIM, (place + 1) * HEAD_DIM)
                    out[rows, columns] = weight[pl.ds(first + start, TILE), :].T


def prepare(order, w_query, w_key, w_value, w_output, near_output, send, receive, segments, width):
    heads = w_query.shape[1]
    low = jnp.bfloat16
    return call(
        prepare_kernel,
        "prepare",
        [
            *[shape(low, 3 * heads, 2 * width)] * 2,
            *[shape(low, 2 * heads, width)] * 2,
            *[shape(low, width, 2 * heads)] * 2,
            shape(jnp.int32, *send.shape),
            shape(jnp.int32, *receive.shape),
            shape(jnp.int32, *segments.shape),
        ],
        (order, w_query, w_key, w_value, w_output, near_output, send, receive, segments),
    )


def sum_squares(block):
    wide = block[...].astype(jnp.float32)
    return jnp.sum(wide * wide, axis=-1, keepdims=True)


def begin_kernel(x0, x1, c0, here_turned, squares, part):
    squares[...] = sum_squares(x0) + sum_squares(x1)
    part[...] = dot(c0[...], here_turned[...])


def begin(x0, x1, c0, here_turned):
    rows, columns = x0.shape[0], here_turned.shape[1]
    shapes = [shape(jnp.float32, rows, 1), shape(jnp.float32, rows, columns)]
    return call(begin_kernel, "begin", shapes, (x0, x1, c0, here_turned), first=VMEM)


def add_grad_kernel(c2, there_turned, part, own_part, near_part, held, sems):
    copies = []
    for index, start in enumerate(range(0, held.shape[1], TILE)):
        tile = pl.ds(start, TILE)
        copies.append(pltpu.make_async_copy(c2.at[:, tile], held.at[:, tile], sems.at[index]))
        copies[-1].start()
    total = part[...]
    for index, copy in enumerate(copies):
        tile = slice(index * TILE, (index + 1) * TILE)
        copy.wait()
        total = total + dot(held[:, tile], there_turned[tile, :])
    heads = own_part.shape[1]
    own_part[...] = total[:, :heads]
    near_part[...] = total[:, heads:]


def add_grad(c2, there_turned, part):
    rows, width = c2.shape
    return call(
        add_grad_kernel,
        "add_grad",
        [shape(jnp.float32, rows, part.shape[1] // 2)] * 2,
        (c2, there_turned, part),
        scratch=[pltpu.VMEM((rows, width), c2.dtype), pltpu.SemaphoreType.DMA((width // TILE,))],
        first=pl.BlockSpec(memory_space=pl.ANY),
    )


def add_squares_kernel(x2, squares_in, squares):
    squares[...] = squares_in[...] + sum_squares(x2)


def add_squares(x2, squares):
    out = shape(jnp.float32, *squares.shape)
    operands = (x2, squares)
    return call(
        add_squares_kernel, "add_squares", out, operands, first=VMEM, flops=SQUARES_FLOPS
    )


def project_kernel(
    order,
    x0,
    x1,
    x2,
    x3,
    gain_own,
    gain_near,
    w_query,
    w_key,
    w_value,
    squares,
    home,
    inverse,
    total,
):
    blocks = (x0, x1, x2, x3)
    width = x0.shape[1]
    mean = (squares[...] + sum_squares(x3)) / (width * len(blocks))
    inverse_rms = lax.rsqrt(mean + EPSILON)
    inverse[...] = inverse_rms
    for index, block in enumerate(blocks):
        gain = (gain_own, gain_near)[index % 2][index // 2 : index // 2 + 1, :]
        scaled = block[...].astype(jnp.float32) * inverse_rms
        normed = (scaled * gain.astype(jnp.float32)).astype(jnp.bfloat16)
        here = pl.ds(block_start(order, index, width), width)
        weights = jnp.concatenate([w_query[here, :], w_key[here, :], w_value[here, :]], axis=1)
        product = dot(normed, weights)
        total[...] = total[...] + product if index else product
    home[...] = total[...].astype(jnp.bfloat16)


def project(order, blocks, gains, weights, squares):
    rows = blocks[0].shape[0]
    columns = 3 * HEAD_DIM
    return call(
        project_kernel,
        "project",
        [shape(jnp.bfloat16, rows, columns), shape(jnp.float32, rows, 1)],
        (order, *blocks, *gains, *weights, squares),
        scratch=[pltpu.VMEM((rows, columns), jnp.float32)],
    )


def fill_kernel(home, own_part, got_part, send, bucket):
    head_grad = (own_part[...] + got_part[...]).astype(jnp.bfloat16)
    rows = jnp.concatenate([home[...], head_grad], axis=1)
    chosen = one_hot(send[...], rows.shape[0])
    bucket[...] = dot(chosen, rows, CONTRACT_FIRST).astype(jnp.bfloat16)


def fill(home, own_part, got_part, send):
    out = shape(jnp.bfloat16, send.shape[1], 4 * HEAD_DIM)
    return call(fill_kernel, "fill", out, (home, own_part, got_part, send), first=VMEM)


def attend_kernel(moved, receive, segments, back):
    place = one_hot(receive[...], moved.shape[0])
    rows = dot(place, moved[...], CONTRACT_FIRST).astype(jnp.bfloat16)
    queries, key_rows, value_rows, head_grad = (
        rows[:, index * HEAD_DIM : (index + 1) * HEAD_DIM] for index in range(4)
    )
    count = rows.shape[0]
    down = lax.broadcasted_iota(jnp.int32, (count, count), 0)
    across = lax.broadcasted_iota(jnp.int32, (count, count), 1)
    stays = segments[...]
    own_stay = jnp.sum(jnp.where(down == across, stays, 0), axis=1, keepdims=True)
    allowed = (own_stay == stays) & (across <= down)
    scores = jnp.where(allowed, dot(queries, key_rows, CONTRACT_LAST) * SCALING, -1e30)
    raised = jnp.exp(scores - jnp.max(scores, axis=-1, keepdims=True))
    softmax_out = raised / jnp.sum(raised, axis=-1, keepdims=True)
    low_weights = softmax_out.astype(jnp.bfloat16)
    attended = dot(low_weights, value_rows).astype(jnp.bfloat16)
    grad_value = dot(low_weights, head_grad, CONTRACT_FIRST).astype(jnp.bfloat16)
    grad_probs = dot(head_grad, value_rows, CONTRACT_LAST)
    inner = jnp.sum(softmax_out * grad_probs, axis=-1, keepdims=True)
    grad_scores = (softmax_out * (grad_probs - inner) * SCALING).astype(jnp.bfloat16)
    grad_query = dot(grad_scores, key_rows).astype(jnp.bfloat16)
    grad_key = dot(grad_scores, queries, CONTRACT_FIRST).astype(jnp.bfloat16)
    results = jnp.concatenate([grad_query, grad_key, grad_value, attended], axis=1)
    back[...] = dot(place, results).astype(jnp.bfloat16)


def attend(moved, receive, segments):
    out = shape(jnp.bfloat16, *moved.shape)
    return call(attend_kernel, "attend", out, (moved, receive, segments), first=VMEM)


def write_parts(value, out):
    out[...] = jnp.zeros_like(out)
    for place in range(3):
        low = value.astype(jnp.bfloat16)
        out[:, place : place + 1] = low
        value = value - low.astype(jnp.float32)


def read_parts(parts):
    return sum(parts[:, place : place + 1].astype(jnp.float32) for place in (2, 1, 0))


def bring_home_kernel(moved, send, home, grads, extras):
    chosen = one_hot(send[...], grads.shape[0])
    rows = dot(chosen, moved[...])
    split = 3 * HEAD_DIM
    grads[...] = rows[:, :split].astype(jnp.bfloat16)
    extras[:, :HEAD_DIM] = rows[:, split:].astype(jnp.bfloat16)
    product = rows[:, :split] * home[...].astype(jnp.float32)
    row_dot = jnp.sum(product, axis=-1, keepdims=True)
    write_parts(row_dot, extras.at[:, HEAD_DIM:])


def bring_home(moved, send, home):
    rows = home.shape[0]
    shapes = [shape(jnp.bfloat16, rows, 3 * HEAD_DIM), shape(jnp.bfloat16, rows, 2 * HEAD_DIM)]
    operands = (moved, send, home)
    return call(bring_home_kernel, "bring_home", shapes, operands, first=VMEM, flops=HOME_FLOPS)


def spread_kernel(first):
    def kernel(own, near, weights, near_weights, out):
        own_rows, near_rows = own[...], near[...]
        for start in range(0, out.shape[1], TILE):
            columns = slice(first + start, first + start + TILE)
            total = dot(own_rows, weights[:, columns]) + dot(near_rows, near_weights[:, columns])
            out[:, start : start + TILE] = total.astype(out.dtype)

    return kernel


def spread(name, first, span, dtype, own, near, weights, near_weights, flops=1000):
    return pl.pallas_call(
        spread_kernel(first),
        out_shape=shape(dtype, own.shape[0], span),
        in_specs=[VMEM] * 4,
        out_specs=VMEM,
        compiler_params=pltpu.CompilerParams(vmem_limit_bytes=VMEM_LIMIT),
        cost_estimate=pl.CostEstimate(flops=flops, bytes_accessed=1000, transcendentals=0),
        name=name,
    )(own, near, weights, near_weights)


def finish_out_kernel(inputs, own, near, far, last, here, there, out):
    width = inputs.shape[1]
    chip = jnp.concatenate([own[:, :HEAD_DIM], near[:, :HEAD_DIM]], axis=1)
    other = jnp.concatenate([far[:, :HEAD_DIM], last[:, :HEAD_DIM]], axis=1)
    for start in range(0, width, TILE):
        tile = slice(start, start + TILE)
        total = dot(chip, here[:, tile]) + dot(other, there[:, tile])
        out[:, tile] = (inputs[:, tile].astype(jnp.float32) + total).astype(jnp.bfloat16)


def finish_most_kernel(
    inputs, cotangent, gain, inverse, own, near, far, last, grad_own, *pieces
):
    *pieces, out, left, held, sem = pieces
    tiles = [
        piece.at[:, start : start + TILE]
        for piece in pieces
        for start in range(0, piece.shape[1], TILE)
    ]
    row_dot = sum(read_parts(extras[:, HEAD_DIM:]) for extras in (own, near, far, last))
    mean_dot = row_dot / (4 * inputs.shape[1])
    inverse_rms = inverse[...]
    most = held.shape[1]
    for start in range(0, inputs.shape[1], TILE):
        tile = slice(start, start + TILE)
        grad_normed = grad_own[:, tile]
        if start < most:
            grad_normed = grad_normed + tiles[start // TILE][...].astype(jnp.float32)
        grad_hat = grad_normed * gain[:, tile].astype(jnp.float32)
        scaled = inputs[:, tile].astype(jnp.float32) * inverse_rms
        change = inverse_rms * (grad_hat - scaled * mean_dot)
        result = cotangent[:, tile].astype(jnp.float32) + change
        if start < most:
            held[:, tile] = result.astype(jnp.bfloat16)
        else:
            left[:, start - most : start - most + TILE] = result
    copy = pltpu.make_async_copy(held, out.at[:, pl.ds(0, most)], sem)
    copy.start()
    copy.wait()


def finish_rest_kernel(gain, inverse, left, rest, before, out, held, sems):
    span = rest.shape[1]
    first = out.shape[1] - span
    half = span // 2
    copies = []
    for index, start in enumerate(range(0, span, half)):
        tile = slice(start, start + half)
        columns = slice(first + start, first + start + half)
        grad_hat = rest[:, tile].astype(jnp.float32) * gain[:, columns].astype(jnp.float32)
        held[:, tile] = (left[:, tile] + inverse[...] * grad_hat).astype(jnp.bfloat16)
        target = out.at[:, pl.ds(first + start, half)]
        copies.append(
            pltpu.make_async_copy(held.at[:, pl.ds(start, half)], target, sems.at[index])
        )
        copies[-1].start()
    for copy in copies:
        copy.wait()


def finish_grad(inputs, cotangent, gain, inverse, extras, grad_own, pieces):
    rows, width = inputs.shape
    *pieces, rest = pieces
    span = rest.shape[1]
    hbm = pl.BlockSpec(memory_space=pltpu.HBM)
    options = dict(
        compiler_params=pltpu.CompilerParams(vmem_limit_bytes=VMEM_LIMIT),
        cost_estimate=pl.CostEstimate(flops=1000, bytes_accessed=1000, transcendentals=0),
    )
    begun, left = pl.pallas_call(
        finish_most_kernel,
        out_shape=[shape(jnp.bfloat16, rows, width), shape(jnp.float32, rows, span)],
        in_specs=[VMEM] * (9 + len(pieces)),
        out_specs=[hbm, VMEM],
        scratch_shapes=[pltpu.VMEM((rows, width - span), jnp.bfloat16), pltpu.SemaphoreType.DMA],
        name="finish_most",
        **options,
    )(inputs, cotangent, gain, inverse, *extras, grad_own, *pieces)
    return pl.pallas_call(
        finish_rest_kernel,
        out_shape=shape(jnp.bfloat16, rows, width),
        in_specs=[VMEM] * 4 + [hbm],
        out_specs=hbm,
        scratch_shapes=[pltpu.VMEM((rows, span), jnp.bfloat16), pltpu.SemaphoreType.DMA((2,))],
        input_output_aliases={4: 0},
        name="finish_rest",
        **options,
    )(gain, inverse, left, rest, begun)


def move(bucket):
    return lax.all_to_all(bucket, "dp", split_axis=0, concat_axis=0, tiled=True)


def after(array, *others):
    return lax.optimization_barrier((array, *others))[0]


def on_device(
    inputs,
    cotangent,
    norm_gain,
    w_query,
    w_key,
    w_value,
    w_output,
    send_rows,
    receive_slots,
    owner_segments,
):
    rows, width = inputs.shape
    tensor = lax.axis_size("tensor")
    low = jnp.bfloat16
    order = lax.axis_index("tensor").astype(jnp.int32) ^ jnp.arange(4, dtype=jnp.int32)
    gain = norm_gain.reshape(1, width)

    x2 = swap(inputs, 2, tensor)
    c2 = swap(cotangent, 2, tensor)
    gain2 = swap(gain, 2, tensor)
    x1 = swap(inputs, 1, tensor)
    near_output = swap(w_output, 1, tensor)
    weights = (w_query, w_key, w_value)
    own_turned, near_turned, here, there, here_turned, there_turned, *indices = prepare(
        order,
        *weights,
        w_output,
        near_output,
        send_rows,
        receive_slots.reshape(1, rows),
        owner_segments.reshape(1, rows),
        width,
    )
    send, receive, segments = indices
    squares, part = begin(inputs, x1, cotangent, here_turned)

    x2, c2, gain2, squares, part = lax.optimization_barrier((x2, c2, gain2, squares, part))
    x3 = swap(x2, 1, tensor)
    gain_own = jnp.concatenate([gain, gain2], axis=0)
    gain_near = swap(gain_own, 1, tensor)
    own_part, near_part = add_grad(c2, there_turned, part)
    got_part = swap(near_part, 1, tensor)
    squares = add_squares(x2, after(squares, near_part))
    home, inverse_rms = project(
        order, (inputs, x1, x2, x3), (gain_own, gain_near), weights, squares
    )
    bucket = fill(home, own_part, got_part, send)
    near_turned = swap(after(near_turned, home), 1, tensor)
    there = swap(after(there, near_part), 2, tensor)
    back = attend(move(bucket), receive, segments)
    moved, there = lax.optimization_barrier((move(back), there))
    own, own_extras = bring_home(moved, send, home)

    near = swap(own, 1, tensor)
    far_extras = swap(own_extras, 2, tensor)
    quarter = width // 4
    turn, got = own, []
    for first, span in ((0, 2 * quarter), (2 * quarter, quarter), (3 * quarter, quarter)):
        flops = 4 * rows * span * width if first else 1000
        sides = (turn, near, own_turned, near_turned)
        part = spread("spread_far", width + first, span, low, *sides, flops=flops)
        got.append(swap(part, 2, tensor))
        turn = after(own, part, far_extras)
    grad_own = spread("spread_own", 0, width, jnp.float32, turn, near, own_turned, near_turned)
    extras = (own_extras, swap(own_extras, 1, tensor), far_extras, swap(far_extras, 1, tensor))
    layer_out = call(
        finish_out_kernel,
        "finish_out",
        shape(low, rows, width),
        (inputs, *extras, here, there),
        first=VMEM,
    )
    got[1] = after(got[1], layer_out)
    input_grad = finish_grad(inputs, cotangent, gain, inverse_rms, extras, grad_own, got)
    return (layer_out, input_grad)


def solution(mesh):
    return jax.shard_map(
        on_device,
        mesh=mesh,
        in_specs=(
            P("dp", "tensor"),
            P("dp", "tensor"),
            P("tensor"),
            P(None, "tensor"),
            P(None, "tensor"),
            P(None, "tensor"),
            P("tensor", None),
            P("dp", None),
            P("dp"),
            P("dp"),
        ),
        out_specs=(P("dp", "tensor"), P("dp", "tensor")),
        check_vma=False,
    )
```

```python
import math

import jax
import jax.numpy as jnp
from jax import lax
from jax.experimental import pallas as pl
from jax.experimental.pallas import tpu as pltpu
from jax.sharding import PartitionSpec as P

HEAD_DIM = 128
EPSILON = 1e-05
SCALING = 1.0 / math.sqrt(HEAD_DIM)
CONTRACT_LAST = (((1,), (1,)), ((), ()))
CONTRACT_FIRST = (((0,), (0,)), ((), ()))
VMEM_LIMIT = 6 * 1024 * 1024
VMEM = pl.BlockSpec(memory_space=pltpu.VMEM)
SMEM = pl.BlockSpec(memory_space=pltpu.SMEM)
TILE = 512
SQUARES_FLOPS = 10000000000
HOME_FLOPS = 30000000000


def dot(left, right, dims=(((1,), (0,)), ((), ()))):
    return lax.dot_general(left, right, dims, preferred_element_type=jnp.float32)


def call(kernel, name, out_shape, operands, scratch=(), first=SMEM, rest=VMEM, flops=1000):
    single = not isinstance(out_shape, (list, tuple))
    shapes = [out_shape] if single else list(out_shape)
    results = pl.pallas_call(
        kernel,
        out_shape=shapes,
        in_specs=[first] + [rest] * (len(operands) - 1),
        out_specs=[VMEM] * len(shapes),
        scratch_shapes=list(scratch),
        compiler_params=pltpu.CompilerParams(vmem_limit_bytes=VMEM_LIMIT),
        cost_estimate=pl.CostEstimate(flops=flops, bytes_accessed=1000, transcendentals=0),
        name=name,
    )(*operands)
    return results[0] if single else results


def shape(dtype, *sizes):
    return jax.ShapeDtypeStruct(sizes, dtype)


def swap(array, mask, count):
    return lax.ppermute(array, "tensor", [(i, i ^ mask) for i in range(count)])


def block_start(order, slot, width):
    return pl.multiple_of(order[slot] * width, width)


def one_hot(places, rows):
    row = lax.broadcasted_iota(jnp.int32, (rows, places.shape[1]), 0)
    return jnp.where(places == row, 1.0, 0.0).astype(jnp.bfloat16)


def prepare_kernel(
    order,
    w_query,
    w_key,
    w_value,
    w_output,
    near_output,
    send,
    receive,
    segments,
    own_turned,
    near_turned,
    here,
    there,
    here_turned,
    there_turned,
    send_out,
    receive_out,
    segments_out,
):
    heads, width = w_output.shape[0], here.shape[1]
    for slot, out, turned in ((0, here, here_turned), (2, there, there_turned)):
        columns = pl.ds(block_start(order, slot, width), width)
        for part, weight in enumerate((w_output, near_output)):
            rows = slice(part * heads, (part + 1) * heads)
            block = weight[:, columns]
            out[rows, :] = block
            turned[:, rows] = block.T
    for source, target in ((send, send_out), (receive, receive_out), (segments, segments_out)):
        target[...] = source[...]
    for out, slots in ((own_turned, (0, 2)), (near_turned, (1, 3))):
        for part, slot in enumerate(slots):
            first = block_start(order, slot, width)
            for start in range(0, width, TILE):
                columns = slice(part * width + start, part * width + start + TILE)
                for place, weight in enumerate((w_query, w_key, w_value)):
                    rows = slice(place * HEAD_DIM, (place + 1) * HEAD_DIM)
                    out[rows, columns] = weight[pl.ds(first + start, TILE), :].T


def prepare(order, w_query, w_key, w_value, w_output, near_output, send, receive, segments, width):
    heads = w_query.shape[1]
    low = jnp.bfloat16
    return call(
        prepare_kernel,
        "prepare",
        [
            *[shape(low, 3 * heads, 2 * width)] * 2,
            *[shape(low, 2 * heads, width)] * 2,
            *[shape(low, width, 2 * heads)] * 2,
            shape(jnp.int32, *send.shape),
            shape(jnp.int32, *receive.shape),
            shape(jnp.int32, *segments.shape),
        ],
        (order, w_query, w_key, w_value, w_output, near_output, send, receive, segments),
    )


def sum_squares(block):
    wide = block[...].astype(jnp.float32)
    return jnp.sum(wide * wide, axis=-1, keepdims=True)


def begin_kernel(x0, x1, c0, here_turned, squares, part):
    squares[...] = sum_squares(x0) + sum_squares(x1)
    part[...] = dot(c0[...], here_turned[...])


def begin(x0, x1, c0, here_turned):
    rows, columns = x0.shape[0], here_turned.shape[1]
    shapes = [shape(jnp.float32, rows, 1), shape(jnp.float32, rows, columns)]
    return call(begin_kernel, "begin", shapes, (x0, x1, c0, here_turned), first=VMEM)


def add_grad_kernel(c2, there_turned, part, own_part, near_part, held, sems):
    copies = []
    for index, start in enumerate(range(0, held.shape[1], TILE)):
        tile = pl.ds(start, TILE)
        copies.append(pltpu.make_async_copy(c2.at[:, tile], held.at[:, tile], sems.at[index]))
        copies[-1].start()
    total = part[...]
    for index, copy in enumerate(copies):
        tile = slice(index * TILE, (index + 1) * TILE)
        copy.wait()
        total = total + dot(held[:, tile], there_turned[tile, :])
    heads = own_part.shape[1]
    own_part[...] = total[:, :heads]
    near_part[...] = total[:, heads:]


def add_grad(c2, there_turned, part):
    rows, width = c2.shape
    return call(
        add_grad_kernel,
        "add_grad",
        [shape(jnp.float32, rows, part.shape[1] // 2)] * 2,
        (c2, there_turned, part),
        scratch=[pltpu.VMEM((rows, width), c2.dtype), pltpu.SemaphoreType.DMA((width // TILE,))],
        first=pl.BlockSpec(memory_space=pl.ANY),
    )


def add_squares_kernel(x2, squares_in, squares):
    squares[...] = squares_in[...] + sum_squares(x2)


def add_squares(x2, squares):
    out = shape(jnp.float32, *squares.shape)
    operands = (x2, squares)
    return call(
        add_squares_kernel, "add_squares", out, operands, first=VMEM, flops=SQUARES_FLOPS
    )


def project_kernel(
    order,
    x0,
    x1,
    x2,
    x3,
    gain_own,
    gain_near,
    w_query,
    w_key,
    w_value,
    squares,
    home,
    inverse,
    total,
):
    blocks = (x0, x1, x2, x3)
    width = x0.shape[1]
    mean = (squares[...] + sum_squares(x3)) / (width * len(blocks))
    inverse_rms = lax.rsqrt(mean + EPSILON)
    inverse[...] = inverse_rms
    for index, block in enumerate(blocks):
        gain = (gain_own, gain_near)[index % 2][index // 2 : index // 2 + 1, :]
        scaled = block[...].astype(jnp.float32) * inverse_rms
        normed = (scaled * gain.astype(jnp.float32)).astype(jnp.bfloat16)
        here = pl.ds(block_start(order, index, width), width)
        weights = jnp.concatenate([w_query[here, :], w_key[here, :], w_value[here, :]], axis=1)
        product = dot(normed, weights)
        total[...] = total[...] + product if index else product
    home[...] = total[...].astype(jnp.bfloat16)


def project(order, blocks, gains, weights, squares):
    rows = blocks[0].shape[0]
    columns = 3 * HEAD_DIM
    return call(
        project_kernel,
        "project",
        [shape(jnp.bfloat16, rows, columns), shape(jnp.float32, rows, 1)],
        (order, *blocks, *gains, *weights, squares),
        scratch=[pltpu.VMEM((rows, columns), jnp.float32)],
    )


def fill_kernel(home, own_part, got_part, send, bucket):
    head_grad = (own_part[...] + got_part[...]).astype(jnp.bfloat16)
    rows = jnp.concatenate([home[...], head_grad], axis=1)
    chosen = one_hot(send[...], rows.shape[0])
    bucket[...] = dot(chosen, rows, CONTRACT_FIRST).astype(jnp.bfloat16)


def fill(home, own_part, got_part, send):
    out = shape(jnp.bfloat16, send.shape[1], 4 * HEAD_DIM)
    return call(fill_kernel, "fill", out, (home, own_part, got_part, send), first=VMEM)


def attend_kernel(moved, receive, segments, back):
    place = one_hot(receive[...], moved.shape[0])
    rows = dot(place, moved[...], CONTRACT_FIRST).astype(jnp.bfloat16)
    queries, key_rows, value_rows, head_grad = (
        rows[:, index * HEAD_DIM : (index + 1) * HEAD_DIM] for index in range(4)
    )
    count = rows.shape[0]
    down = lax.broadcasted_iota(jnp.int32, (count, count), 0)
    across = lax.broadcasted_iota(jnp.int32, (count, count), 1)
    stays = segments[...]
    own_stay = jnp.sum(jnp.where(down == across, stays, 0), axis=1, keepdims=True)
    allowed = (own_stay == stays) & (across <= down)
    scores = jnp.where(allowed, dot(queries, key_rows, CONTRACT_LAST) * SCALING, -1e30)
    raised = jnp.exp(scores - jnp.max(scores, axis=-1, keepdims=True))
    softmax_out = raised / jnp.sum(raised, axis=-1, keepdims=True)
    low_weights = softmax_out.astype(jnp.bfloat16)
    attended = dot(low_weights, value_rows).astype(jnp.bfloat16)
    grad_value = dot(low_weights, head_grad, CONTRACT_FIRST).astype(jnp.bfloat16)
    grad_probs = dot(head_grad, value_rows, CONTRACT_LAST)
    inner = jnp.sum(softmax_out * grad_probs, axis=-1, keepdims=True)
    grad_scores = (softmax_out * (grad_probs - inner) * SCALING).astype(jnp.bfloat16)
    grad_query = dot(grad_scores, key_rows).astype(jnp.bfloat16)
    grad_key = dot(grad_scores, queries, CONTRACT_FIRST).astype(jnp.bfloat16)
    results = jnp.concatenate([grad_query, grad_key, grad_value, attended], axis=1)
    back[...] = dot(place, results).astype(jnp.bfloat16)


def attend(moved, receive, segments):
    out = shape(jnp.bfloat16, *moved.shape)
    return call(attend_kernel, "attend", out, (moved, receive, segments), first=VMEM)


def write_parts(value, out):
    out[...] = jnp.zeros_like(out)
    for place in range(3):
        low = value.astype(jnp.bfloat16)
        out[:, place : place + 1] = low
        value = value - low.astype(jnp.float32)


def read_parts(parts):
    return sum(parts[:, place : place + 1].astype(jnp.float32) for place in (2, 1, 0))


def bring_home_kernel(moved, send, home, grads, extras):
    chosen = one_hot(send[...], grads.shape[0])
    rows = dot(chosen, moved[...])
    split = 3 * HEAD_DIM
    grads[...] = rows[:, :split].astype(jnp.bfloat16)
    extras[:, :HEAD_DIM] = rows[:, split:].astype(jnp.bfloat16)
    product = rows[:, :split] * home[...].astype(jnp.float32)
    row_dot = jnp.sum(product, axis=-1, keepdims=True)
    write_parts(row_dot, extras.at[:, HEAD_DIM:])


def bring_home(moved, send, home):
    rows = home.shape[0]
    shapes = [shape(jnp.bfloat16, rows, 3 * HEAD_DIM), shape(jnp.bfloat16, rows, 2 * HEAD_DIM)]
    operands = (moved, send, home)
    return call(bring_home_kernel, "bring_home", shapes, operands, first=VMEM, flops=HOME_FLOPS)


def spread_kernel(first):
    def kernel(own, near, weights, near_weights, out):
        own_rows, near_rows = own[...], near[...]
        for start in range(0, out.shape[1], TILE):
            columns = slice(first + start, first + start + TILE)
            total = dot(own_rows, weights[:, columns]) + dot(near_rows, near_weights[:, columns])
            out[:, start : start + TILE] = total.astype(out.dtype)

    return kernel


def spread(name, first, span, dtype, own, near, weights, near_weights, flops=1000):
    return pl.pallas_call(
        spread_kernel(first),
        out_shape=shape(dtype, own.shape[0], span),
        in_specs=[VMEM] * 4,
        out_specs=VMEM,
        compiler_params=pltpu.CompilerParams(vmem_limit_bytes=VMEM_LIMIT),
        cost_estimate=pl.CostEstimate(flops=flops, bytes_accessed=1000, transcendentals=0),
        name=name,
    )(own, near, weights, near_weights)


def finish_out_kernel(inputs, own, near, far, last, here, there, out):
    width = inputs.shape[1]
    chip = jnp.concatenate([own[:, :HEAD_DIM], near[:, :HEAD_DIM]], axis=1)
    other = jnp.concatenate([far[:, :HEAD_DIM], last[:, :HEAD_DIM]], axis=1)
    for start in range(0, width, TILE):
        tile = slice(start, start + TILE)
        total = dot(chip, here[:, tile]) + dot(other, there[:, tile])
        out[:, tile] = (inputs[:, tile].astype(jnp.float32) + total).astype(jnp.bfloat16)


def finish_most_kernel(
    inputs, cotangent, gain, inverse, own, near, far, last, grad_own, *pieces
):
    *pieces, out, left, held, sem = pieces
    tiles = [
        piece.at[:, start : start + TILE]
        for piece in pieces
        for start in range(0, piece.shape[1], TILE)
    ]
    row_dot = sum(read_parts(extras[:, HEAD_DIM:]) for extras in (own, near, far, last))
    mean_dot = row_dot / (4 * inputs.shape[1])
    inverse_rms = inverse[...]
    most = held.shape[1]
    for start in range(0, inputs.shape[1], TILE):
        tile = slice(start, start + TILE)
        grad_normed = grad_own[:, tile]
        if start < most:
            grad_normed = grad_normed + tiles[start // TILE][...].astype(jnp.float32)
        grad_hat = grad_normed * gain[:, tile].astype(jnp.float32)
        scaled = inputs[:, tile].astype(jnp.float32) * inverse_rms
        change = inverse_rms * (grad_hat - scaled * mean_dot)
        result = cotangent[:, tile].astype(jnp.float32) + change
        if start < most:
            held[:, tile] = result.astype(jnp.bfloat16)
        else:
            left[:, start - most : start - most + TILE] = result
    copy = pltpu.make_async_copy(held, out.at[:, pl.ds(0, most)], sem)
    copy.start()
    copy.wait()


def finish_rest_kernel(gain, inverse, left, rest, before, out, held, sems):
    span = rest.shape[1]
    first = out.shape[1] - span
    half = span // 2
    copies = []
    for index, start in enumerate(range(0, span, half)):
        tile = slice(start, start + half)
        columns = slice(first + start, first + start + half)
        grad_hat = rest[:, tile].astype(jnp.float32) * gain[:, columns].astype(jnp.float32)
        held[:, tile] = (left[:, tile] + inverse[...] * grad_hat).astype(jnp.bfloat16)
        target = out.at[:, pl.ds(first + start, half)]
        copies.append(
            pltpu.make_async_copy(held.at[:, pl.ds(start, half)], target, sems.at[index])
        )
        copies[-1].start()
    for copy in copies:
        copy.wait()


def finish_grad(inputs, cotangent, gain, inverse, extras, grad_own, pieces):
    rows, width = inputs.shape
    *pieces, rest = pieces
    span = rest.shape[1]
    hbm = pl.BlockSpec(memory_space=pltpu.HBM)
    options = dict(
        compiler_params=pltpu.CompilerParams(vmem_limit_bytes=VMEM_LIMIT),
        cost_estimate=pl.CostEstimate(flops=1000, bytes_accessed=1000, transcendentals=0),
    )
    begun, left = pl.pallas_call(
        finish_most_kernel,
        out_shape=[shape(jnp.bfloat16, rows, width), shape(jnp.float32, rows, span)],
        in_specs=[VMEM] * (9 + len(pieces)),
        out_specs=[hbm, VMEM],
        scratch_shapes=[pltpu.VMEM((rows, width - span), jnp.bfloat16), pltpu.SemaphoreType.DMA],
        name="finish_most",
        **options,
    )(inputs, cotangent, gain, inverse, *extras, grad_own, *pieces)
    return pl.pallas_call(
        finish_rest_kernel,
        out_shape=shape(jnp.bfloat16, rows, width),
        in_specs=[VMEM] * 4 + [hbm],
        out_specs=hbm,
        scratch_shapes=[pltpu.VMEM((rows, span), jnp.bfloat16), pltpu.SemaphoreType.DMA((2,))],
        input_output_aliases={4: 0},
        name="finish_rest",
        **options,
    )(gain, inverse, left, rest, begun)


def move(bucket):
    return lax.all_to_all(bucket, "dp", split_axis=0, concat_axis=0, tiled=True)


def after(array, *others):
    return lax.optimization_barrier((array, *others))[0]


def on_device(
    inputs,
    cotangent,
    norm_gain,
    w_query,
    w_key,
    w_value,
    w_output,
    send_rows,
    receive_slots,
    owner_segments,
):
    rows, width = inputs.shape
    tensor = lax.axis_size("tensor")
    low = jnp.bfloat16
    order = lax.axis_index("tensor").astype(jnp.int32) ^ jnp.arange(4, dtype=jnp.int32)
    gain = norm_gain.reshape(1, width)

    x2 = swap(inputs, 2, tensor)
    c2 = swap(cotangent, 2, tensor)
    gain2 = swap(gain, 2, tensor)
    x1 = swap(inputs, 1, tensor)
    near_output = swap(w_output, 1, tensor)
    weights = (w_query, w_key, w_value)
    own_turned, near_turned, here, there, here_turned, there_turned, *indices = prepare(
        order,
        *weights,
        w_output,
        near_output,
        send_rows,
        receive_slots.reshape(1, rows),
        owner_segments.reshape(1, rows),
        width,
    )
    send, receive, segments = indices
    squares, part = begin(inputs, x1, cotangent, here_turned)

    x2, c2, gain2, squares, part = lax.optimization_barrier((x2, c2, gain2, squares, part))
    x3 = swap(x2, 1, tensor)
    gain_own = jnp.concatenate([gain, gain2], axis=0)
    gain_near = swap(gain_own, 1, tensor)
    own_part, near_part = add_grad(c2, there_turned, part)
    got_part = swap(near_part, 1, tensor)
    squares = add_squares(x2, after(squares, near_part))
    home, inverse_rms = project(
        order, (inputs, x1, x2, x3), (gain_own, gain_near), weights, squares
    )
    bucket = fill(home, own_part, got_part, send)
    near_turned = swap(after(near_turned, home), 1, tensor)
    there = swap(after(there, near_part), 2, tensor)
    back = attend(move(bucket), receive, segments)
    moved, there = lax.optimization_barrier((move(back), there))
    own, own_extras = bring_home(moved, send, home)

    near = swap(own, 1, tensor)
    far_extras = swap(own_extras, 2, tensor)
    quarter = width // 4
    turn, got = own, []
    for first, span in ((0, 2 * quarter), (2 * quarter, quarter), (3 * quarter, quarter)):
        flops = 4 * rows * span * width if first else 1000
        sides = (turn, near, own_turned, near_turned)
        part = spread("spread_far", width + first, span, low, *sides, flops=flops)
        got.append(swap(part, 2, tensor))
        turn = after(own, part, far_extras)
    grad_own = spread("spread_own", 0, width, jnp.float32, turn, near, own_turned, near_turned)
    extras = (own_extras, swap(own_extras, 1, tensor), far_extras, swap(far_extras, 1, tensor))
    layer_out = call(
        finish_out_kernel,
        "finish_out",
        shape(low, rows, width),
        (inputs, *extras, here, there),
        first=VMEM,
    )
    got[1] = after(got[1], layer_out)
    input_grad = finish_grad(inputs, cotangent, gain, inverse_rms, extras, grad_own, got)
    return (layer_out, input_grad)


def solution(mesh):
    return jax.shard_map(
        on_device,
        mesh=mesh,
        in_specs=(
            P("dp", "tensor"),
            P("dp", "tensor"),
            P("tensor"),
            P(None, "tensor"),
            P(None, "tensor"),
            P(None, "tensor"),
            P("tensor", None),
            P("dp", None),
            P("dp"),
            P("dp"),
        ),
        out_specs=(P("dp", "tensor"), P("dp", "tensor")),
        check_vma=False,
    )
```

```python
import math

import jax
import jax.numpy as jnp
from jax import lax
from jax.experimental import pallas as pl
from jax.experimental.pallas import tpu as pltpu
from jax.sharding import PartitionSpec as P

HEAD_DIM = 128
EPSILON = 1e-05
SCALING = 1.0 / math.sqrt(HEAD_DIM)
CONTRACT_LAST = (((1,), (1,)), ((), ()))
CONTRACT_FIRST = (((0,), (0,)), ((), ()))
VMEM_LIMIT = 6 * 1024 * 1024
VMEM = pl.BlockSpec(memory_space=pltpu.VMEM)
SMEM = pl.BlockSpec(memory_space=pltpu.SMEM)
TILE = 512
SQUARES_FLOPS = 10000000000
HOME_FLOPS = 24000000000


def dot(left, right, dims=(((1,), (0,)), ((), ()))):
    return lax.dot_general(left, right, dims, preferred_element_type=jnp.float32)


def call(kernel, name, out_shape, operands, scratch=(), first=SMEM, rest=VMEM, flops=1000):
    single = not isinstance(out_shape, (list, tuple))
    shapes = [out_shape] if single else list(out_shape)
    results = pl.pallas_call(
        kernel,
        out_shape=shapes,
        in_specs=[first] + [rest] * (len(operands) - 1),
        out_specs=[VMEM] * len(shapes),
        scratch_shapes=list(scratch),
        compiler_params=pltpu.CompilerParams(vmem_limit_bytes=VMEM_LIMIT),
        cost_estimate=pl.CostEstimate(flops=flops, bytes_accessed=1000, transcendentals=0),
        name=name,
    )(*operands)
    return results[0] if single else results


def shape(dtype, *sizes):
    return jax.ShapeDtypeStruct(sizes, dtype)


def swap(array, mask, count):
    return lax.ppermute(array, "tensor", [(i, i ^ mask) for i in range(count)])


def block_start(order, slot, width):
    return pl.multiple_of(order[slot] * width, width)


def one_hot(places, rows):
    row = lax.broadcasted_iota(jnp.int32, (rows, places.shape[1]), 0)
    return jnp.where(places == row, 1.0, 0.0).astype(jnp.bfloat16)


def prepare_kernel(
    order,
    w_query,
    w_key,
    w_value,
    w_output,
    near_output,
    send,
    receive,
    segments,
    own_turned,
    near_turned,
    here,
    there,
    here_turned,
    there_turned,
    send_out,
    receive_out,
    segments_out,
):
    heads, width = w_output.shape[0], here.shape[1]
    for slot, out, turned in ((0, here, here_turned), (2, there, there_turned)):
        columns = pl.ds(block_start(order, slot, width), width)
        for part, weight in enumerate((w_output, near_output)):
            rows = slice(part * heads, (part + 1) * heads)
            block = weight[:, columns]
            out[rows, :] = block
            turned[:, rows] = block.T
    for source, target in ((send, send_out), (receive, receive_out), (segments, segments_out)):
        target[...] = source[...]
    for out, slots in ((own_turned, (0, 2)), (near_turned, (1, 3))):
        for part, slot in enumerate(slots):
            first = block_start(order, slot, width)
            for start in range(0, width, TILE):
                columns = slice(part * width + start, part * width + start + TILE)
                for place, weight in enumerate((w_query, w_key, w_value)):
                    rows = slice(place * HEAD_DIM, (place + 1) * HEAD_DIM)
                    out[rows, columns] = weight[pl.ds(first + start, TILE), :].T


def prepare(order, w_query, w_key, w_value, w_output, near_output, send, receive, segments, width):
    heads = w_query.shape[1]
    low = jnp.bfloat16
    return call(
        prepare_kernel,
        "prepare",
        [
            *[shape(low, 3 * heads, 2 * width)] * 2,
            *[shape(low, 2 * heads, width)] * 2,
            *[shape(low, width, 2 * heads)] * 2,
            shape(jnp.int32, *send.shape),
            shape(jnp.int32, *receive.shape),
            shape(jnp.int32, *segments.shape),
        ],
        (order, w_query, w_key, w_value, w_output, near_output, send, receive, segments),
    )


def sum_squares(block):
    wide = block[...].astype(jnp.float32)
    return jnp.sum(wide * wide, axis=-1, keepdims=True)


def begin_kernel(x0, x1, c0, here_turned, squares, part):
    squares[...] = sum_squares(x0) + sum_squares(x1)
    part[...] = dot(c0[...], here_turned[...])


def begin(x0, x1, c0, here_turned):
    rows, columns = x0.shape[0], here_turned.shape[1]
    shapes = [shape(jnp.float32, rows, 1), shape(jnp.float32, rows, columns)]
    return call(begin_kernel, "begin", shapes, (x0, x1, c0, here_turned), first=VMEM)


def add_grad_kernel(c2, there_turned, part, own_part, near_part, held, sems):
    copies = []
    for index, start in enumerate(range(0, held.shape[1], TILE)):
        tile = pl.ds(start, TILE)
        copies.append(pltpu.make_async_copy(c2.at[:, tile], held.at[:, tile], sems.at[index]))
        copies[-1].start()
    total = part[...]
    for index, copy in enumerate(copies):
        tile = slice(index * TILE, (index + 1) * TILE)
        copy.wait()
        total = total + dot(held[:, tile], there_turned[tile, :])
    heads = own_part.shape[1]
    own_part[...] = total[:, :heads]
    near_part[...] = total[:, heads:]


def add_grad(c2, there_turned, part):
    rows, width = c2.shape
    return call(
        add_grad_kernel,
        "add_grad",
        [shape(jnp.float32, rows, part.shape[1] // 2)] * 2,
        (c2, there_turned, part),
        scratch=[pltpu.VMEM((rows, width), c2.dtype), pltpu.SemaphoreType.DMA((width // TILE,))],
        first=pl.BlockSpec(memory_space=pl.ANY),
    )


def add_squares_kernel(x2, squares_in, squares):
    squares[...] = squares_in[...] + sum_squares(x2)


def add_squares(x2, squares):
    out = shape(jnp.float32, *squares.shape)
    operands = (x2, squares)
    return call(
        add_squares_kernel, "add_squares", out, operands, first=VMEM, flops=SQUARES_FLOPS
    )


def project_kernel(
    order,
    x0,
    x1,
    x2,
    x3,
    gain_own,
    gain_near,
    w_query,
    w_key,
    w_value,
    squares,
    own_part,
    got_part,
    send,
    home,
    inverse,
    bucket,
    total,
):
    blocks = (x0, x1, x2, x3)
    width = x0.shape[1]
    mean = (squares[...] + sum_squares(x3)) / (width * len(blocks))
    inverse_rms = lax.rsqrt(mean + EPSILON)
    inverse[...] = inverse_rms
    head_grad = (own_part[...] + got_part[...]).astype(jnp.bfloat16)
    for index, block in enumerate(blocks):
        gain = (gain_own, gain_near)[index % 2][index // 2 : index // 2 + 1, :]
        scaled = block[...].astype(jnp.float32) * inverse_rms
        normed = (scaled * gain.astype(jnp.float32)).astype(jnp.bfloat16)
        here = pl.ds(block_start(order, index, width), width)
        weights = jnp.concatenate([w_query[here, :], w_key[here, :], w_value[here, :]], axis=1)
        product = dot(normed, weights)
        total[...] = total[...] + product if index else product
    rounded = total[...].astype(jnp.bfloat16)
    home[...] = rounded
    chosen = one_hot(send[...], rounded.shape[0])
    split = rounded.shape[1]
    bucket[:, :split] = dot(chosen, rounded, CONTRACT_FIRST).astype(jnp.bfloat16)
    bucket[:, split:] = dot(chosen, head_grad, CONTRACT_FIRST).astype(jnp.bfloat16)


def project(order, blocks, gains, weights, squares, own_part, got_part, send):
    rows = blocks[0].shape[0]
    columns = 3 * HEAD_DIM
    return call(
        project_kernel,
        "project",
        [
            shape(jnp.bfloat16, rows, columns),
            shape(jnp.float32, rows, 1),
            shape(jnp.bfloat16, send.shape[1], columns + HEAD_DIM),
        ],
        (order, *blocks, *gains, *weights, squares, own_part, got_part, send),
        scratch=[pltpu.VMEM((rows, columns), jnp.float32)],
    )


def attend_kernel(moved, receive, segments, back):
    place = one_hot(receive[...], moved.shape[0])
    rows = dot(place, moved[...], CONTRACT_FIRST).astype(jnp.bfloat16)
    queries, key_rows, value_rows, head_grad = (
        rows[:, index * HEAD_DIM : (index + 1) * HEAD_DIM] for index in range(4)
    )
    count = rows.shape[0]
    down = lax.broadcasted_iota(jnp.int32, (count, count), 0)
    across = lax.broadcasted_iota(jnp.int32, (count, count), 1)
    stays = segments[...]
    own_stay = jnp.sum(jnp.where(down == across, stays, 0), axis=1, keepdims=True)
    allowed = (own_stay == stays) & (across <= down)
    scores = jnp.where(allowed, dot(queries, key_rows, CONTRACT_LAST) * SCALING, -1e30)
    raised = jnp.exp(scores - jnp.max(scores, axis=-1, keepdims=True))
    softmax_out = raised / jnp.sum(raised, axis=-1, keepdims=True)
    low_weights = softmax_out.astype(jnp.bfloat16)
    attended = dot(low_weights, value_rows).astype(jnp.bfloat16)
    grad_value = dot(low_weights, head_grad, CONTRACT_FIRST).astype(jnp.bfloat16)
    grad_probs = dot(head_grad, value_rows, CONTRACT_LAST)
    inner = jnp.sum(softmax_out * grad_probs, axis=-1, keepdims=True)
    grad_scores = (softmax_out * (grad_probs - inner) * SCALING).astype(jnp.bfloat16)
    grad_query = dot(grad_scores, key_rows).astype(jnp.bfloat16)
    grad_key = dot(grad_scores, queries, CONTRACT_FIRST).astype(jnp.bfloat16)
    results = jnp.concatenate([grad_query, grad_key, grad_value, attended], axis=1)
    back[...] = dot(place, results).astype(jnp.bfloat16)


def attend(moved, receive, segments):
    out = shape(jnp.bfloat16, *moved.shape)
    return call(attend_kernel, "attend", out, (moved, receive, segments), first=VMEM)


def write_parts(value, out):
    out[...] = jnp.zeros_like(out)
    for place in range(3):
        low = value.astype(jnp.bfloat16)
        out[:, place : place + 1] = low
        value = value - low.astype(jnp.float32)


def read_parts(parts):
    return sum(parts[:, place : place + 1].astype(jnp.float32) for place in (2, 1, 0))


def bring_home_kernel(moved, send, home, grads, extras):
    chosen = one_hot(send[...], grads.shape[0])
    rows = dot(chosen, moved[...])
    split = 3 * HEAD_DIM
    grads[...] = rows[:, :split].astype(jnp.bfloat16)
    extras[:, :HEAD_DIM] = rows[:, split:].astype(jnp.bfloat16)
    product = rows[:, :split] * home[...].astype(jnp.float32)
    row_dot = jnp.sum(product, axis=-1, keepdims=True)
    write_parts(row_dot, extras.at[:, HEAD_DIM:])


def bring_home(moved, send, home):
    rows = home.shape[0]
    shapes = [shape(jnp.bfloat16, rows, 3 * HEAD_DIM), shape(jnp.bfloat16, rows, 2 * HEAD_DIM)]
    operands = (moved, send, home)
    return call(bring_home_kernel, "bring_home", shapes, operands, first=VMEM, flops=HOME_FLOPS)


def spread_kernel(first):
    def kernel(own, near, weights, near_weights, out):
        own_rows, near_rows = own[...], near[...]
        for start in range(0, out.shape[1], TILE):
            columns = slice(first + start, first + start + TILE)
            total = dot(own_rows, weights[:, columns]) + dot(near_rows, near_weights[:, columns])
            out[:, start : start + TILE] = total.astype(out.dtype)

    return kernel


def spread(name, first, span, dtype, own, near, weights, near_weights, flops=1000):
    return pl.pallas_call(
        spread_kernel(first),
        out_shape=shape(dtype, own.shape[0], span),
        in_specs=[VMEM] * 4,
        out_specs=VMEM,
        compiler_params=pltpu.CompilerParams(vmem_limit_bytes=VMEM_LIMIT),
        cost_estimate=pl.CostEstimate(flops=flops, bytes_accessed=1000, transcendentals=0),
        name=name,
    )(own, near, weights, near_weights)


def finish_out_kernel(inputs, own, near, far, last, here, there, out):
    width = inputs.shape[1]
    chip = jnp.concatenate([own[:, :HEAD_DIM], near[:, :HEAD_DIM]], axis=1)
    other = jnp.concatenate([far[:, :HEAD_DIM], last[:, :HEAD_DIM]], axis=1)
    for start in range(0, width, TILE):
        tile = slice(start, start + TILE)
        total = dot(chip, here[:, tile]) + dot(other, there[:, tile])
        out[:, tile] = (inputs[:, tile].astype(jnp.float32) + total).astype(jnp.bfloat16)


def finish_most_kernel(
    inputs, cotangent, gain, inverse, own, near, far, last, grad_own, *pieces
):
    *pieces, out, left, held, sem = pieces
    tiles = [
        piece.at[:, start : start + TILE]
        for piece in pieces
        for start in range(0, piece.shape[1], TILE)
    ]
    row_dot = sum(read_parts(extras[:, HEAD_DIM:]) for extras in (own, near, far, last))
    mean_dot = row_dot / (4 * inputs.shape[1])
    inverse_rms = inverse[...]
    most = held.shape[1]
    for start in range(0, inputs.shape[1], TILE):
        tile = slice(start, start + TILE)
        grad_normed = grad_own[:, tile]
        if start < most:
            grad_normed = grad_normed + tiles[start // TILE][...].astype(jnp.float32)
        grad_hat = grad_normed * gain[:, tile].astype(jnp.float32)
        scaled = inputs[:, tile].astype(jnp.float32) * inverse_rms
        change = inverse_rms * (grad_hat - scaled * mean_dot)
        result = cotangent[:, tile].astype(jnp.float32) + change
        if start < most:
            held[:, tile] = result.astype(jnp.bfloat16)
        else:
            left[:, start - most : start - most + TILE] = result
    copy = pltpu.make_async_copy(held, out.at[:, pl.ds(0, most)], sem)
    copy.start()
    copy.wait()


def finish_rest_kernel(gain, inverse, left, rest, before, out, held, sems):
    span = rest.shape[1]
    first = out.shape[1] - span
    half = span // 2
    copies = []
    for index, start in enumerate(range(0, span, half)):
        tile = slice(start, start + half)
        columns = slice(first + start, first + start + half)
        grad_hat = rest[:, tile].astype(jnp.float32) * gain[:, columns].astype(jnp.float32)
        held[:, tile] = (left[:, tile] + inverse[...] * grad_hat).astype(jnp.bfloat16)
        target = out.at[:, pl.ds(first + start, half)]
        copies.append(
            pltpu.make_async_copy(held.at[:, pl.ds(start, half)], target, sems.at[index])
        )
        copies[-1].start()
    for copy in copies:
        copy.wait()


def finish_grad(inputs, cotangent, gain, inverse, extras, grad_own, pieces):
    rows, width = inputs.shape
    *pieces, rest = pieces
    span = rest.shape[1]
    hbm = pl.BlockSpec(memory_space=pltpu.HBM)
    options = dict(
        compiler_params=pltpu.CompilerParams(vmem_limit_bytes=VMEM_LIMIT),
        cost_estimate=pl.CostEstimate(flops=1000, bytes_accessed=1000, transcendentals=0),
    )
    begun, left = pl.pallas_call(
        finish_most_kernel,
        out_shape=[shape(jnp.bfloat16, rows, width), shape(jnp.float32, rows, span)],
        in_specs=[VMEM] * (9 + len(pieces)),
        out_specs=[hbm, VMEM],
        scratch_shapes=[pltpu.VMEM((rows, width - span), jnp.bfloat16), pltpu.SemaphoreType.DMA],
        name="finish_most",
        **options,
    )(inputs, cotangent, gain, inverse, *extras, grad_own, *pieces)
    return pl.pallas_call(
        finish_rest_kernel,
        out_shape=shape(jnp.bfloat16, rows, width),
        in_specs=[VMEM] * 4 + [hbm],
        out_specs=hbm,
        scratch_shapes=[pltpu.VMEM((rows, span), jnp.bfloat16), pltpu.SemaphoreType.DMA((2,))],
        input_output_aliases={4: 0},
        name="finish_rest",
        **options,
    )(gain, inverse, left, rest, begun)


def move(bucket):
    return lax.all_to_all(bucket, "dp", split_axis=0, concat_axis=0, tiled=True)


def after(array, *others):
    return lax.optimization_barrier((array, *others))[0]


def on_device(
    inputs,
    cotangent,
    norm_gain,
    w_query,
    w_key,
    w_value,
    w_output,
    send_rows,
    receive_slots,
    owner_segments,
):
    rows, width = inputs.shape
    tensor = lax.axis_size("tensor")
    low = jnp.bfloat16
    order = lax.axis_index("tensor").astype(jnp.int32) ^ jnp.arange(4, dtype=jnp.int32)
    gain = norm_gain.reshape(1, width)

    x2 = swap(inputs, 2, tensor)
    c2 = swap(cotangent, 2, tensor)
    gain2 = swap(gain, 2, tensor)
    x1 = swap(inputs, 1, tensor)
    near_output = swap(w_output, 1, tensor)
    weights = (w_query, w_key, w_value)
    own_turned, near_turned, here, there, here_turned, there_turned, *indices = prepare(
        order,
        *weights,
        w_output,
        near_output,
        send_rows,
        receive_slots.reshape(1, rows),
        owner_segments.reshape(1, rows),
        width,
    )
    send, receive, segments = indices
    squares, part = begin(inputs, x1, cotangent, here_turned)

    x2, c2, gain2, squares, part = lax.optimization_barrier((x2, c2, gain2, squares, part))
    x3 = swap(x2, 1, tensor)
    gain_own = jnp.concatenate([gain, gain2], axis=0)
    gain_near = swap(gain_own, 1, tensor)
    own_part, near_part = add_grad(c2, there_turned, part)
    got_part = swap(near_part, 1, tensor)
    squares = add_squares(x2, after(squares, near_part))
    home, inverse_rms, bucket = project(
        order,
        (inputs, x1, x2, x3),
        (gain_own, gain_near),
        weights,
        squares,
        own_part,
        got_part,
        send,
    )
    near_turned = swap(after(near_turned, home), 1, tensor)
    there = swap(after(there, near_part), 2, tensor)
    back = attend(move(bucket), receive, segments)
    moved, there = lax.optimization_barrier((move(back), there))
    own, own_extras = bring_home(moved, send, home)

    near = swap(own, 1, tensor)
    far_extras = swap(own_extras, 2, tensor)
    quarter = width // 4
    turn, got = own, []
    for first, span in ((0, 2 * quarter), (2 * quarter, quarter), (3 * quarter, quarter)):
        flops = 4 * rows * span * width if first else 1000
        sides = (turn, near, own_turned, near_turned)
        part = spread("spread_far", width + first, span, low, *sides, flops=flops)
        got.append(swap(part, 2, tensor))
        turn = after(own, part, far_extras)
    grad_own = spread("spread_own", 0, width, jnp.float32, turn, near, own_turned, near_turned)
    extras = (own_extras, swap(own_extras, 1, tensor), far_extras, swap(far_extras, 1, tensor))
    layer_out = call(
        finish_out_kernel,
        "finish_out",
        shape(low, rows, width),
        (inputs, *extras, here, there),
        first=VMEM,
    )
    got[1] = after(got[1], layer_out)
    input_grad = finish_grad(inputs, cotangent, gain, inverse_rms, extras, grad_own, got)
    return (layer_out, input_grad)


def solution(mesh):
    return jax.shard_map(
        on_device,
        mesh=mesh,
        in_specs=(
            P("dp", "tensor"),
            P("dp", "tensor"),
            P("tensor"),
            P(None, "tensor"),
            P(None, "tensor"),
            P(None, "tensor"),
            P("tensor", None),
            P("dp", None),
            P("dp"),
            P("dp"),
        ),
        out_specs=(P("dp", "tensor"), P("dp", "tensor")),
        check_vma=False,
    )
```

```python
import math

import jax
import jax.numpy as jnp
from jax import lax
from jax.experimental import pallas as pl
from jax.experimental.pallas import tpu as pltpu
from jax.sharding import PartitionSpec as P

HEAD_DIM = 128
EPSILON = 1e-05
SCALING = 1.0 / math.sqrt(HEAD_DIM)
CONTRACT_LAST = (((1,), (1,)), ((), ()))
CONTRACT_FIRST = (((0,), (0,)), ((), ()))
VMEM_LIMIT = 3 * 1024 * 1024
VMEM = pl.BlockSpec(memory_space=pltpu.VMEM)
SMEM = pl.BlockSpec(memory_space=pltpu.SMEM)
TILE = 512


def dot(left, right, dims=(((1,), (0,)), ((), ()))):
    return lax.dot_general(left, right, dims, preferred_element_type=jnp.float32)


def call(kernel, name, out_shape, operands, scratch=(), first=SMEM, rest=VMEM):
    single = not isinstance(out_shape, (list, tuple))
    shapes = [out_shape] if single else list(out_shape)
    results = pl.pallas_call(
        kernel,
        out_shape=shapes,
        in_specs=[first] + [rest] * (len(operands) - 1),
        out_specs=[VMEM] * len(shapes),
        scratch_shapes=list(scratch),
        compiler_params=pltpu.CompilerParams(vmem_limit_bytes=VMEM_LIMIT),
        cost_estimate=pl.CostEstimate(flops=1000, bytes_accessed=1000, transcendentals=0),
        name=name,
    )(*operands)
    return results[0] if single else results


def shape(dtype, *sizes):
    return jax.ShapeDtypeStruct(sizes, dtype)


def swap(array, mask, count):
    return lax.ppermute(array, "tensor", [(i, i ^ mask) for i in range(count)])


def block_start(order, slot, width):
    return pl.multiple_of(order[slot] * width, width)


def one_hot(places, rows):
    row = lax.broadcasted_iota(jnp.int32, (rows, places.shape[1]), 0)
    return jnp.where(places == row, 1.0, 0.0).astype(jnp.bfloat16)


def prepare_kernel(
    order,
    w_query,
    w_key,
    w_value,
    w_output,
    near_output,
    send,
    receive,
    segments,
    own_turned,
    near_turned,
    here,
    there,
    there_turned,
    send_out,
    receive_out,
    segments_out,
):
    heads, width = w_output.shape[0], here.shape[1]
    for slot, out, turned in ((0, here, None), (2, there, there_turned)):
        columns = pl.ds(block_start(order, slot, width), width)
        for part, weight in enumerate((w_output, near_output)):
            rows = slice(part * heads, (part + 1) * heads)
            block = weight[:, columns]
            out[rows, :] = block
            if turned is not None:
                turned[:, rows] = block.T
    for source, target in ((send, send_out), (receive, receive_out), (segments, segments_out)):
        target[...] = source[...]
    for out, slots in ((own_turned, (0, 2)), (near_turned, (1, 3))):
        for part, slot in enumerate(slots):
            first = block_start(order, slot, width)
            for start in range(0, width, TILE):
                columns = slice(part * width + start, part * width + start + TILE)
                for place, weight in enumerate((w_query, w_key, w_value)):
                    rows = slice(place * HEAD_DIM, (place + 1) * HEAD_DIM)
                    out[rows, columns] = weight[pl.ds(first + start, TILE), :].T


def prepare(order, w_query, w_key, w_value, w_output, near_output, send, receive, segments, width):
    heads = w_query.shape[1]
    low = jnp.bfloat16
    return call(
        prepare_kernel,
        "prepare",
        [
            *[shape(low, 3 * heads, 2 * width)] * 2,
            *[shape(low, 2 * heads, width)] * 2,
            shape(low, width, 2 * heads),
            shape(jnp.int32, *send.shape),
            shape(jnp.int32, *receive.shape),
            shape(jnp.int32, *segments.shape),
        ],
        (order, w_query, w_key, w_value, w_output, near_output, send, receive, segments),
    )


def sum_squares(block):
    wide = block[...].astype(jnp.float32)
    return jnp.sum(wide * wide, axis=-1, keepdims=True)


def begin_kernel(x0, x1, c0, here, squares, part):
    squares[...] = sum_squares(x0) + sum_squares(x1)
    part[...] = dot(c0[...], here[...], CONTRACT_LAST)


def begin(x0, x1, c0, here):
    rows, columns = x0.shape[0], here.shape[0]
    shapes = [shape(jnp.float32, rows, 1), shape(jnp.float32, rows, columns)]
    return call(begin_kernel, "begin", shapes, (x0, x1, c0, here), first=VMEM)


def add_grad_kernel(c2, there_turned, part, own_part, near_part):
    total = part[...] + dot(c2[...], there_turned[...])
    heads = own_part.shape[1]
    own_part[...] = total[:, :heads]
    near_part[...] = total[:, heads:]


def add_grad(c2, there_turned, part):
    shapes = [shape(jnp.float32, part.shape[0], part.shape[1] // 2)] * 2
    return call(add_grad_kernel, "add_grad", shapes, (c2, there_turned, part), first=VMEM)


def add_squares_kernel(x2, squares_in, squares):
    squares[...] = squares_in[...] + sum_squares(x2)


def add_squares(x2, squares):
    out = shape(jnp.float32, *squares.shape)
    return call(add_squares_kernel, "add_squares", out, (x2, squares), first=VMEM)


def project_kernel(
    order,
    x0,
    x1,
    x2,
    x3,
    gain_own,
    gain_near,
    w_query,
    w_key,
    w_value,
    squares,
    own_part,
    got_part,
    send,
    home,
    inverse,
    bucket,
    total,
):
    blocks = (x0, x1, x2, x3)
    width = x0.shape[1]
    mean = (squares[...] + sum_squares(x3)) / (width * len(blocks))
    inverse_rms = lax.rsqrt(mean + EPSILON)
    inverse[...] = inverse_rms
    head_grad = (own_part[...] + got_part[...]).astype(jnp.bfloat16)
    for index, block in enumerate(blocks):
        gain = (gain_own, gain_near)[index % 2][index // 2 : index // 2 + 1, :]
        scaled = block[...].astype(jnp.float32) * inverse_rms
        normed = (scaled * gain.astype(jnp.float32)).astype(jnp.bfloat16)
        here = pl.ds(block_start(order, index, width), width)
        weights = jnp.concatenate([w_query[here, :], w_key[here, :], w_value[here, :]], axis=1)
        product = dot(normed, weights)
        total[...] = total[...] + product if index else product
    rounded = total[...].astype(jnp.bfloat16)
    home[...] = rounded
    chosen = one_hot(send[...], rounded.shape[0])
    split = rounded.shape[1]
    bucket[:, :split] = dot(chosen, rounded, CONTRACT_FIRST).astype(jnp.bfloat16)
    bucket[:, split:] = dot(chosen, head_grad, CONTRACT_FIRST).astype(jnp.bfloat16)


def project(order, blocks, gains, weights, squares, own_part, got_part, send):
    rows = blocks[0].shape[0]
    columns = 3 * HEAD_DIM
    return call(
        project_kernel,
        "project",
        [
            shape(jnp.bfloat16, rows, columns),
            shape(jnp.float32, rows, 1),
            shape(jnp.bfloat16, send.shape[1], columns + HEAD_DIM),
        ],
        (order, *blocks, *gains, *weights, squares, own_part, got_part, send),
        scratch=[pltpu.VMEM((rows, columns), jnp.float32)],
    )


def attend_kernel(moved, receive, segments, back):
    place = one_hot(receive[...], moved.shape[0])
    rows = dot(place, moved[...], CONTRACT_FIRST).astype(jnp.bfloat16)
    queries, key_rows, value_rows, head_grad = (
        rows[:, index * HEAD_DIM : (index + 1) * HEAD_DIM] for index in range(4)
    )
    count = rows.shape[0]
    down = lax.broadcasted_iota(jnp.int32, (count, count), 0)
    across = lax.broadcasted_iota(jnp.int32, (count, count), 1)
    stays = segments[...]
    own_stay = jnp.sum(jnp.where(down == across, stays, 0), axis=1, keepdims=True)
    allowed = (own_stay == stays) & (across <= down)
    scores = jnp.where(allowed, dot(queries, key_rows, CONTRACT_LAST) * SCALING, -1e30)
    raised = jnp.exp(scores - jnp.max(scores, axis=-1, keepdims=True))
    softmax_out = raised / jnp.sum(raised, axis=-1, keepdims=True)
    low_weights = softmax_out.astype(jnp.bfloat16)
    attended = dot(low_weights, value_rows).astype(jnp.bfloat16)
    grad_value = dot(low_weights, head_grad, CONTRACT_FIRST).astype(jnp.bfloat16)
    grad_probs = dot(head_grad, value_rows, CONTRACT_LAST)
    inner = jnp.sum(softmax_out * grad_probs, axis=-1, keepdims=True)
    grad_scores = (softmax_out * (grad_probs - inner) * SCALING).astype(jnp.bfloat16)
    grad_query = dot(grad_scores, key_rows).astype(jnp.bfloat16)
    grad_key = dot(grad_scores, queries, CONTRACT_FIRST).astype(jnp.bfloat16)
    results = jnp.concatenate([grad_query, grad_key, grad_value, attended], axis=1)
    back[...] = dot(place, results).astype(jnp.bfloat16)


def attend(moved, receive, segments):
    out = shape(jnp.bfloat16, *moved.shape)
    return call(attend_kernel, "attend", out, (moved, receive, segments), first=VMEM)


def write_parts(value, out):
    out[...] = jnp.zeros_like(out)
    for place in range(3):
        low = value.astype(jnp.bfloat16)
        out[:, place : place + 1] = low
        value = value - low.astype(jnp.float32)


def read_parts(parts):
    return sum(parts[:, place : place + 1].astype(jnp.float32) for place in (2, 1, 0))


def bring_home_kernel(moved, send, home, grads, extras):
    chosen = one_hot(send[...], grads.shape[0])
    rows = dot(chosen, moved[...])
    split = 3 * HEAD_DIM
    grads[...] = rows[:, :split].astype(jnp.bfloat16)
    extras[:, :HEAD_DIM] = rows[:, split:].astype(jnp.bfloat16)
    product = rows[:, :split] * home[...].astype(jnp.float32)
    row_dot = jnp.sum(product, axis=-1, keepdims=True)
    write_parts(row_dot, extras.at[:, HEAD_DIM:])


def bring_home(moved, send, home):
    rows = home.shape[0]
    shapes = [shape(jnp.bfloat16, rows, 3 * HEAD_DIM), shape(jnp.bfloat16, rows, 2 * HEAD_DIM)]
    return call(bring_home_kernel, "bring_home", shapes, (moved, send, home), first=VMEM)


def spread_kernel(first):
    def kernel(own, near, weights, near_weights, out):
        own_rows, near_rows = own[...], near[...]
        for start in range(0, out.shape[1], TILE):
            columns = slice(first + start, first + start + TILE)
            total = dot(own_rows, weights[:, columns]) + dot(near_rows, near_weights[:, columns])
            out[:, start : start + TILE] = total.astype(out.dtype)

    return kernel


def spread(name, first, span, dtype, own, near, weights, near_weights, flops=1000):
    return pl.pallas_call(
        spread_kernel(first),
        out_shape=shape(dtype, own.shape[0], span),
        in_specs=[VMEM] * 4,
        out_specs=VMEM,
        compiler_params=pltpu.CompilerParams(vmem_limit_bytes=VMEM_LIMIT),
        cost_estimate=pl.CostEstimate(flops=flops, bytes_accessed=1000, transcendentals=0),
        name=name,
    )(own, near, weights, near_weights)


def finish_out_kernel(inputs, own, near, far, last, here, there, out):
    width = inputs.shape[1]
    chip = jnp.concatenate([own[:, :HEAD_DIM], near[:, :HEAD_DIM]], axis=1)
    other = jnp.concatenate([far[:, :HEAD_DIM], last[:, :HEAD_DIM]], axis=1)
    for start in range(0, width, TILE):
        tile = slice(start, start + TILE)
        total = dot(chip, here[:, tile]) + dot(other, there[:, tile])
        out[:, tile] = (inputs[:, tile].astype(jnp.float32) + total).astype(jnp.bfloat16)


def finish_most_kernel(
    inputs, cotangent, gain, inverse, own, near, far, last, grad_own, *pieces
):
    *pieces, out, left, held, sem = pieces
    tiles = [
        piece.at[:, start : start + TILE]
        for piece in pieces
        for start in range(0, piece.shape[1], TILE)
    ]
    row_dot = sum(read_parts(extras[:, HEAD_DIM:]) for extras in (own, near, far, last))
    mean_dot = row_dot / (4 * inputs.shape[1])
    inverse_rms = inverse[...]
    most = held.shape[1]
    for start in range(0, inputs.shape[1], TILE):
        tile = slice(start, start + TILE)
        grad_normed = grad_own[:, tile]
        if start < most:
            grad_normed = grad_normed + tiles[start // TILE][...].astype(jnp.float32)
        grad_hat = grad_normed * gain[:, tile].astype(jnp.float32)
        scaled = inputs[:, tile].astype(jnp.float32) * inverse_rms
        change = inverse_rms * (grad_hat - scaled * mean_dot)
        result = cotangent[:, tile].astype(jnp.float32) + change
        if start < most:
            held[:, tile] = result.astype(jnp.bfloat16)
        else:
            left[:, start - most : start - most + TILE] = result
    copy = pltpu.make_async_copy(held, out.at[:, pl.ds(0, most)], sem)
    copy.start()
    copy.wait()


def finish_rest_kernel(gain, inverse, left, rest, before, out, held, sems):
    span = rest.shape[1]
    first = out.shape[1] - span
    half = span // 2
    copies = []
    for index, start in enumerate(range(0, span, half)):
        tile = slice(start, start + half)
        columns = slice(first + start, first + start + half)
        grad_hat = rest[:, tile].astype(jnp.float32) * gain[:, columns].astype(jnp.float32)
        held[:, tile] = (left[:, tile] + inverse[...] * grad_hat).astype(jnp.bfloat16)
        target = out.at[:, pl.ds(first + start, half)]
        copies.append(
            pltpu.make_async_copy(held.at[:, pl.ds(start, half)], target, sems.at[index])
        )
        copies[-1].start()
    for copy in copies:
        copy.wait()


def finish_grad(inputs, cotangent, gain, inverse, extras, grad_own, pieces):
    rows, width = inputs.shape
    *pieces, rest = pieces
    span = rest.shape[1]
    hbm = pl.BlockSpec(memory_space=pltpu.HBM)
    options = dict(
        compiler_params=pltpu.CompilerParams(vmem_limit_bytes=VMEM_LIMIT),
        cost_estimate=pl.CostEstimate(flops=1000, bytes_accessed=1000, transcendentals=0),
    )
    begun, left = pl.pallas_call(
        finish_most_kernel,
        out_shape=[shape(jnp.bfloat16, rows, width), shape(jnp.float32, rows, span)],
        in_specs=[VMEM] * (9 + len(pieces)),
        out_specs=[hbm, VMEM],
        scratch_shapes=[pltpu.VMEM((rows, width - span), jnp.bfloat16), pltpu.SemaphoreType.DMA],
        name="finish_most",
        **options,
    )(inputs, cotangent, gain, inverse, *extras, grad_own, *pieces)
    return pl.pallas_call(
        finish_rest_kernel,
        out_shape=shape(jnp.bfloat16, rows, width),
        in_specs=[VMEM] * 4 + [hbm],
        out_specs=hbm,
        scratch_shapes=[pltpu.VMEM((rows, span), jnp.bfloat16), pltpu.SemaphoreType.DMA((2,))],
        input_output_aliases={4: 0},
        name="finish_rest",
        **options,
    )(gain, inverse, left, rest, begun)


def move(bucket):
    return lax.all_to_all(bucket, "dp", split_axis=0, concat_axis=0, tiled=True)


def after(array, *others):
    return lax.optimization_barrier((array, *others))[0]


def on_device(
    inputs,
    cotangent,
    norm_gain,
    w_query,
    w_key,
    w_value,
    w_output,
    send_rows,
    receive_slots,
    owner_segments,
):
    rows, width = inputs.shape
    tensor = lax.axis_size("tensor")
    low = jnp.bfloat16
    order = lax.axis_index("tensor").astype(jnp.int32) ^ jnp.arange(4, dtype=jnp.int32)
    gain = norm_gain.reshape(1, width)

    x2 = swap(inputs, 2, tensor)
    c2 = swap(cotangent, 2, tensor)
    gain2 = swap(gain, 2, tensor)
    x1 = swap(inputs, 1, tensor)
    near_output = swap(w_output, 1, tensor)
    weights = (w_query, w_key, w_value)
    own_turned, near_turned, here, there, there_turned, *indices = prepare(
        order,
        *weights,
        w_output,
        near_output,
        send_rows,
        receive_slots.reshape(1, rows),
        owner_segments.reshape(1, rows),
        width,
    )
    send, receive, segments = indices
    squares, part = begin(inputs, x1, cotangent, here)

    x2, c2, gain2, squares, part = lax.optimization_barrier((x2, c2, gain2, squares, part))
    x3 = swap(x2, 1, tensor)
    gain_own = jnp.concatenate([gain, gain2], axis=0)
    gain_near = swap(gain_own, 1, tensor)
    own_part, near_part = add_grad(c2, there_turned, part)
    got_part = swap(near_part, 1, tensor)
    squares = add_squares(x2, squares)
    home, inverse_rms, bucket = project(
        order,
        (inputs, x1, x2, x3),
        (gain_own, gain_near),
        weights,
        squares,
        own_part,
        got_part,
        send,
    )
    near_turned = swap(after(near_turned, home), 1, tensor)
    there = swap(after(there, home), 2, tensor)
    back = attend(move(bucket), receive, segments)
    own, own_extras = bring_home(move(back), send, home)

    near = swap(own, 1, tensor)
    far_extras = swap(own_extras, 2, tensor)
    quarter = width // 4
    turn, got = own, []
    for first, span in ((0, 2 * quarter), (2 * quarter, quarter), (3 * quarter, quarter)):
        flops = 4 * rows * span * width if first else 1000
        sides = (turn, near, own_turned, near_turned)
        part = spread("spread_far", width + first, span, low, *sides, flops=flops)
        got.append(swap(part, 2, tensor))
        turn = after(own, part, far_extras)
    grad_own = spread("spread_own", 0, width, jnp.float32, turn, near, own_turned, near_turned)
    extras = (own_extras, swap(own_extras, 1, tensor), far_extras, swap(far_extras, 1, tensor))
    layer_out = call(
        finish_out_kernel,
        "finish_out",
        shape(low, rows, width),
        (inputs, *extras, here, there),
        first=VMEM,
    )
    got[1] = after(got[1], layer_out)
    input_grad = finish_grad(inputs, cotangent, gain, inverse_rms, extras, grad_own, got)
    return (layer_out, input_grad)


def solution(mesh):
    return jax.shard_map(
        on_device,
        mesh=mesh,
        in_specs=(
            P("dp", "tensor"),
            P("dp", "tensor"),
            P("tensor"),
            P(None, "tensor"),
            P(None, "tensor"),
            P(None, "tensor"),
            P("tensor", None),
            P("dp", None),
            P("dp"),
            P("dp"),
        ),
        out_specs=(P("dp", "tensor"), P("dp", "tensor")),
        check_vma=False,
    )
```

```python
import math

import jax
import jax.numpy as jnp
from jax import lax
from jax.experimental import pallas as pl
from jax.experimental.pallas import tpu as pltpu
from jax.sharding import PartitionSpec as P

HEAD_DIM = 128
EPSILON = 1e-05
SCALING = 1.0 / math.sqrt(HEAD_DIM)
CONTRACT_LAST = (((1,), (1,)), ((), ()))
CONTRACT_FIRST = (((0,), (0,)), ((), ()))
VMEM_LIMIT = 3 * 1024 * 1024
VMEM = pl.BlockSpec(memory_space=pltpu.VMEM)
SMEM = pl.BlockSpec(memory_space=pltpu.SMEM)
TILE = 512


def dot(left, right, dims=(((1,), (0,)), ((), ()))):
    return lax.dot_general(left, right, dims, preferred_element_type=jnp.float32)


def call(kernel, name, out_shape, operands, scratch=(), first=SMEM, rest=VMEM):
    single = not isinstance(out_shape, (list, tuple))
    shapes = [out_shape] if single else list(out_shape)
    results = pl.pallas_call(
        kernel,
        out_shape=shapes,
        in_specs=[first] + [rest] * (len(operands) - 1),
        out_specs=[VMEM] * len(shapes),
        scratch_shapes=list(scratch),
        compiler_params=pltpu.CompilerParams(vmem_limit_bytes=VMEM_LIMIT),
        cost_estimate=pl.CostEstimate(flops=1000, bytes_accessed=1000, transcendentals=0),
        name=name,
    )(*operands)
    return results[0] if single else results


def shape(dtype, *sizes):
    return jax.ShapeDtypeStruct(sizes, dtype)


def swap(array, mask, count):
    return lax.ppermute(array, "tensor", [(i, i ^ mask) for i in range(count)])


def block_start(order, slot, width):
    return pl.multiple_of(order[slot] * width, width)


def one_hot(places, rows):
    row = lax.broadcasted_iota(jnp.int32, (rows, places.shape[1]), 0)
    return jnp.where(places == row, 1.0, 0.0).astype(jnp.bfloat16)


def prepare_kernel(
    order,
    w_query,
    w_key,
    w_value,
    w_output,
    near_output,
    send,
    receive,
    segments,
    own_turned,
    near_turned,
    here,
    there,
    there_turned,
    send_out,
    receive_out,
    segments_out,
):
    heads, width = w_output.shape[0], here.shape[1]
    for slot, out, turned in ((0, here, None), (2, there, there_turned)):
        columns = pl.ds(block_start(order, slot, width), width)
        for part, weight in enumerate((w_output, near_output)):
            rows = slice(part * heads, (part + 1) * heads)
            block = weight[:, columns]
            out[rows, :] = block
            if turned is not None:
                turned[:, rows] = block.T
    for source, target in ((send, send_out), (receive, receive_out), (segments, segments_out)):
        target[...] = source[...]
    for out, slots in ((own_turned, (0, 2)), (near_turned, (1, 3))):
        for part, slot in enumerate(slots):
            first = block_start(order, slot, width)
            for start in range(0, width, TILE):
                columns = slice(part * width + start, part * width + start + TILE)
                for place, weight in enumerate((w_query, w_key, w_value)):
                    rows = slice(place * HEAD_DIM, (place + 1) * HEAD_DIM)
                    out[rows, columns] = weight[pl.ds(first + start, TILE), :].T


def prepare(order, w_query, w_key, w_value, w_output, near_output, send, receive, segments, width):
    heads = w_query.shape[1]
    low = jnp.bfloat16
    return call(
        prepare_kernel,
        "prepare",
        [
            *[shape(low, 3 * heads, 2 * width)] * 2,
            *[shape(low, 2 * heads, width)] * 2,
            shape(low, width, 2 * heads),
            shape(jnp.int32, *send.shape),
            shape(jnp.int32, *receive.shape),
            shape(jnp.int32, *segments.shape),
        ],
        (order, w_query, w_key, w_value, w_output, near_output, send, receive, segments),
    )


def sum_squares(block):
    wide = block[...].astype(jnp.float32)
    return jnp.sum(wide * wide, axis=-1, keepdims=True)


def begin_kernel(x0, x1, c0, here, squares, part):
    squares[...] = sum_squares(x0) + sum_squares(x1)
    part[...] = dot(c0[...], here[...], CONTRACT_LAST)


def begin(x0, x1, c0, here):
    rows, columns = x0.shape[0], here.shape[0]
    shapes = [shape(jnp.float32, rows, 1), shape(jnp.float32, rows, columns)]
    return call(begin_kernel, "begin", shapes, (x0, x1, c0, here), first=VMEM)


def add_grad_kernel(half):
    def kernel(c2, there_turned, part, total):
        heads = total.shape[1]
        columns = slice(half * heads, (half + 1) * heads)
        total[...] = part[:, columns] + dot(c2[...], there_turned[:, columns])

    return kernel


def add_grad(half, c2, there_turned, part):
    out = shape(jnp.float32, part.shape[0], part.shape[1] // 2)
    return call(add_grad_kernel(half), "add_grad", out, (c2, there_turned, part), first=VMEM)


def add_squares_kernel(x2, squares_in, squares):
    squares[...] = squares_in[...] + sum_squares(x2)


def add_squares(x2, squares):
    out = shape(jnp.float32, *squares.shape)
    return call(add_squares_kernel, "add_squares", out, (x2, squares), first=VMEM)


def project_kernel(
    order,
    x0,
    x1,
    x2,
    x3,
    gain_chip,
    gain_far,
    w_query,
    w_key,
    w_value,
    squares,
    own_part,
    got_part,
    send,
    home,
    inverse,
    bucket,
    total,
):
    blocks = (x0, x1, x2, x3)
    width = x0.shape[1]
    mean = (squares[...] + sum_squares(x3)) / (width * len(blocks))
    inverse_rms = lax.rsqrt(mean + EPSILON)
    inverse[...] = inverse_rms
    head_grad = (own_part[...] + got_part[...]).astype(jnp.bfloat16)
    for index, block in enumerate(blocks):
        gain = (gain_chip, gain_far)[index // 2][index % 2 : index % 2 + 1, :]
        scaled = block[...].astype(jnp.float32) * inverse_rms
        normed = (scaled * gain.astype(jnp.float32)).astype(jnp.bfloat16)
        here = pl.ds(block_start(order, index, width), width)
        weights = jnp.concatenate([w_query[here, :], w_key[here, :], w_value[here, :]], axis=1)
        product = dot(normed, weights)
        total[...] = total[...] + product if index else product
    rounded = total[...].astype(jnp.bfloat16)
    home[...] = rounded
    chosen = one_hot(send[...], rounded.shape[0])
    split = rounded.shape[1]
    bucket[:, :split] = dot(chosen, rounded, CONTRACT_FIRST).astype(jnp.bfloat16)
    bucket[:, split:] = dot(chosen, head_grad, CONTRACT_FIRST).astype(jnp.bfloat16)


def project(order, blocks, gains, weights, squares, own_part, got_part, send):
    rows = blocks[0].shape[0]
    columns = 3 * HEAD_DIM
    return call(
        project_kernel,
        "project",
        [
            shape(jnp.bfloat16, rows, columns),
            shape(jnp.float32, rows, 1),
            shape(jnp.bfloat16, send.shape[1], columns + HEAD_DIM),
        ],
        (order, *blocks, *gains, *weights, squares, own_part, got_part, send),
        scratch=[pltpu.VMEM((rows, columns), jnp.float32)],
    )


def attend_kernel(moved, receive, segments, back):
    place = one_hot(receive[...], moved.shape[0])
    rows = dot(place, moved[...], CONTRACT_FIRST).astype(jnp.bfloat16)
    queries, key_rows, value_rows, head_grad = (
        rows[:, index * HEAD_DIM : (index + 1) * HEAD_DIM] for index in range(4)
    )
    count = rows.shape[0]
    down = lax.broadcasted_iota(jnp.int32, (count, count), 0)
    across = lax.broadcasted_iota(jnp.int32, (count, count), 1)
    stays = segments[...]
    own_stay = jnp.sum(jnp.where(down == across, stays, 0), axis=1, keepdims=True)
    allowed = (own_stay == stays) & (across <= down)
    scores = jnp.where(allowed, dot(queries, key_rows, CONTRACT_LAST) * SCALING, -1e30)
    raised = jnp.exp(scores - jnp.max(scores, axis=-1, keepdims=True))
    softmax_out = raised / jnp.sum(raised, axis=-1, keepdims=True)
    low_weights = softmax_out.astype(jnp.bfloat16)
    attended = dot(low_weights, value_rows).astype(jnp.bfloat16)
    grad_value = dot(low_weights, head_grad, CONTRACT_FIRST).astype(jnp.bfloat16)
    grad_probs = dot(head_grad, value_rows, CONTRACT_LAST)
    inner = jnp.sum(softmax_out * grad_probs, axis=-1, keepdims=True)
    grad_scores = (softmax_out * (grad_probs - inner) * SCALING).astype(jnp.bfloat16)
    grad_query = dot(grad_scores, key_rows).astype(jnp.bfloat16)
    grad_key = dot(grad_scores, queries, CONTRACT_FIRST).astype(jnp.bfloat16)
    results = jnp.concatenate([grad_query, grad_key, grad_value, attended], axis=1)
    back[...] = dot(place, results).astype(jnp.bfloat16)


def attend(moved, receive, segments):
    out = shape(jnp.bfloat16, *moved.shape)
    return call(attend_kernel, "attend", out, (moved, receive, segments), first=VMEM)


def write_parts(value, out):
    out[...] = jnp.zeros_like(out)
    for place in range(3):
        low = value.astype(jnp.bfloat16)
        out[:, place : place + 1] = low
        value = value - low.astype(jnp.float32)


def read_parts(parts):
    return sum(parts[:, place : place + 1].astype(jnp.float32) for place in (2, 1, 0))


def bring_home_kernel(moved, send, home, grads, extras):
    chosen = one_hot(send[...], grads.shape[0])
    rows = dot(chosen, moved[...])
    split = 3 * HEAD_DIM
    grads[...] = rows[:, :split].astype(jnp.bfloat16)
    extras[:, :HEAD_DIM] = rows[:, split:].astype(jnp.bfloat16)
    product = rows[:, :split] * home[...].astype(jnp.float32)
    row_dot = jnp.sum(product, axis=-1, keepdims=True)
    write_parts(row_dot, extras.at[:, HEAD_DIM:])


def bring_home(moved, send, home):
    rows = home.shape[0]
    shapes = [shape(jnp.bfloat16, rows, 3 * HEAD_DIM), shape(jnp.bfloat16, rows, 2 * HEAD_DIM)]
    return call(bring_home_kernel, "bring_home", shapes, (moved, send, home), first=VMEM)


def spread_kernel(first):
    def kernel(own, near, weights, near_weights, out):
        own_rows, near_rows = own[...], near[...]
        for start in range(0, out.shape[1], TILE):
            columns = slice(first + start, first + start + TILE)
            total = dot(own_rows, weights[:, columns]) + dot(near_rows, near_weights[:, columns])
            out[:, start : start + TILE] = total.astype(out.dtype)

    return kernel


def spread(name, first, span, dtype, own, near, weights, near_weights, flops=1000):
    return pl.pallas_call(
        spread_kernel(first),
        out_shape=shape(dtype, own.shape[0], span),
        in_specs=[VMEM] * 4,
        out_specs=VMEM,
        compiler_params=pltpu.CompilerParams(vmem_limit_bytes=VMEM_LIMIT),
        cost_estimate=pl.CostEstimate(flops=flops, bytes_accessed=1000, transcendentals=0),
        name=name,
    )(own, near, weights, near_weights)


def finish_out_kernel(inputs, own, near, far, last, here, there, out):
    width = inputs.shape[1]
    chip = jnp.concatenate([own[:, :HEAD_DIM], near[:, :HEAD_DIM]], axis=1)
    other = jnp.concatenate([far[:, :HEAD_DIM], last[:, :HEAD_DIM]], axis=1)
    for start in range(0, width, TILE):
        tile = slice(start, start + TILE)
        total = dot(chip, here[:, tile]) + dot(other, there[:, tile])
        out[:, tile] = (inputs[:, tile].astype(jnp.float32) + total).astype(jnp.bfloat16)


def finish_most_kernel(
    inputs, cotangent, gain, inverse, own, near, far, last, grad_own, *pieces
):
    *pieces, out, left, held, sem = pieces
    tiles = [
        piece.at[:, start : start + TILE]
        for piece in pieces
        for start in range(0, piece.shape[1], TILE)
    ]
    row_dot = sum(read_parts(extras[:, HEAD_DIM:]) for extras in (own, near, far, last))
    mean_dot = row_dot / (4 * inputs.shape[1])
    inverse_rms = inverse[...]
    most = held.shape[1]
    for start in range(0, inputs.shape[1], TILE):
        tile = slice(start, start + TILE)
        grad_normed = grad_own[:, tile]
        if start < most:
            grad_normed = grad_normed + tiles[start // TILE][...].astype(jnp.float32)
        grad_hat = grad_normed * gain[:, tile].astype(jnp.float32)
        scaled = inputs[:, tile].astype(jnp.float32) * inverse_rms
        change = inverse_rms * (grad_hat - scaled * mean_dot)
        result = cotangent[:, tile].astype(jnp.float32) + change
        if start < most:
            held[:, tile] = result.astype(jnp.bfloat16)
        else:
            left[:, start - most : start - most + TILE] = result
    copy = pltpu.make_async_copy(held, out.at[:, pl.ds(0, most)], sem)
    copy.start()
    copy.wait()


def finish_rest_kernel(gain, inverse, left, rest, before, out, held, sems):
    span = rest.shape[1]
    first = out.shape[1] - span
    half = span // 2
    copies = []
    for index, start in enumerate(range(0, span, half)):
        tile = slice(start, start + half)
        columns = slice(first + start, first + start + half)
        grad_hat = rest[:, tile].astype(jnp.float32) * gain[:, columns].astype(jnp.float32)
        held[:, tile] = (left[:, tile] + inverse[...] * grad_hat).astype(jnp.bfloat16)
        target = out.at[:, pl.ds(first + start, half)]
        copies.append(
            pltpu.make_async_copy(held.at[:, pl.ds(start, half)], target, sems.at[index])
        )
        copies[-1].start()
    for copy in copies:
        copy.wait()


def finish_grad(inputs, cotangent, gain, inverse, extras, grad_own, pieces):
    rows, width = inputs.shape
    *pieces, rest = pieces
    span = rest.shape[1]
    hbm = pl.BlockSpec(memory_space=pltpu.HBM)
    options = dict(
        compiler_params=pltpu.CompilerParams(vmem_limit_bytes=VMEM_LIMIT),
        cost_estimate=pl.CostEstimate(flops=1000, bytes_accessed=1000, transcendentals=0),
    )
    begun, left = pl.pallas_call(
        finish_most_kernel,
        out_shape=[shape(jnp.bfloat16, rows, width), shape(jnp.float32, rows, span)],
        in_specs=[VMEM] * (9 + len(pieces)),
        out_specs=[hbm, VMEM],
        scratch_shapes=[pltpu.VMEM((rows, width - span), jnp.bfloat16), pltpu.SemaphoreType.DMA],
        name="finish_most",
        **options,
    )(inputs, cotangent, gain, inverse, *extras, grad_own, *pieces)
    return pl.pallas_call(
        finish_rest_kernel,
        out_shape=shape(jnp.bfloat16, rows, width),
        in_specs=[VMEM] * 4 + [hbm],
        out_specs=hbm,
        scratch_shapes=[pltpu.VMEM((rows, span), jnp.bfloat16), pltpu.SemaphoreType.DMA((2,))],
        input_output_aliases={4: 0},
        name="finish_rest",
        **options,
    )(gain, inverse, left, rest, begun)


def move(bucket):
    return lax.all_to_all(bucket, "dp", split_axis=0, concat_axis=0, tiled=True)


def after(array, *others):
    return lax.optimization_barrier((array, *others))[0]


def on_device(
    inputs,
    cotangent,
    norm_gain,
    w_query,
    w_key,
    w_value,
    w_output,
    send_rows,
    receive_slots,
    owner_segments,
):
    rows, width = inputs.shape
    tensor = lax.axis_size("tensor")
    low = jnp.bfloat16
    order = lax.axis_index("tensor").astype(jnp.int32) ^ jnp.arange(4, dtype=jnp.int32)
    gain = norm_gain.reshape(1, width)

    x2 = swap(inputs, 2, tensor)
    c2 = swap(cotangent, 2, tensor)
    gain_chip = jnp.concatenate([gain, swap(gain, 1, tensor)], axis=0)
    gain_far = swap(gain_chip, 2, tensor)
    x1 = swap(inputs, 1, tensor)
    near_output = swap(w_output, 1, tensor)
    weights = (w_query, w_key, w_value)
    own_turned, near_turned, here, there, there_turned, *indices = prepare(
        order,
        *weights,
        w_output,
        near_output,
        send_rows,
        receive_slots.reshape(1, rows),
        owner_segments.reshape(1, rows),
        width,
    )
    send, receive, segments = indices
    squares, part = begin(inputs, x1, cotangent, here)

    x2, c2, gain_far, squares, part = lax.optimization_barrier((x2, c2, gain_far, squares, part))
    x3 = swap(x2, 1, tensor)
    near_part = add_grad(1, c2, there_turned, part)
    got_part = swap(near_part, 1, tensor)
    own_part = add_grad(0, c2, there_turned, after(part, near_part))
    squares = add_squares(x2, squares)
    home, inverse_rms, bucket = project(
        order,
        (inputs, x1, x2, x3),
        (gain_chip, gain_far),
        weights,
        squares,
        own_part,
        got_part,
        send,
    )
    near_turned = swap(after(near_turned, home), 1, tensor)
    there = swap(after(there, home), 2, tensor)
    back = attend(move(bucket), receive, segments)
    own, own_extras = bring_home(move(back), send, home)

    near = swap(own, 1, tensor)
    far_extras = swap(own_extras, 2, tensor)
    quarter = width // 4
    turn, got = own, []
    for first, span in ((0, 2 * quarter), (2 * quarter, quarter), (3 * quarter, quarter)):
        flops = 4 * rows * span * width if first else 1000
        sides = (turn, near, own_turned, near_turned)
        part = spread("spread_far", width + first, span, low, *sides, flops=flops)
        got.append(swap(part, 2, tensor))
        turn = after(own, part, far_extras)
    grad_own = spread("spread_own", 0, width, jnp.float32, turn, near, own_turned, near_turned)
    extras = (own_extras, swap(own_extras, 1, tensor), far_extras, swap(far_extras, 1, tensor))
    layer_out = call(
        finish_out_kernel,
        "finish_out",
        shape(low, rows, width),
        (inputs, *extras, here, there),
        first=VMEM,
    )
    got[1] = after(got[1], layer_out)
    input_grad = finish_grad(inputs, cotangent, gain, inverse_rms, extras, grad_own, got)
    return (layer_out, input_grad)


def solution(mesh):
    return jax.shard_map(
        on_device,
        mesh=mesh,
        in_specs=(
            P("dp", "tensor"),
            P("dp", "tensor"),
            P("tensor"),
            P(None, "tensor"),
            P(None, "tensor"),
            P(None, "tensor"),
            P("tensor", None),
            P("dp", None),
            P("dp"),
            P("dp"),
        ),
        out_specs=(P("dp", "tensor"), P("dp", "tensor")),
        check_vma=False,
    )
```

```python
import math

import jax
import jax.numpy as jnp
from jax import lax
from jax.experimental import pallas as pl
from jax.experimental.pallas import tpu as pltpu
from jax.sharding import PartitionSpec as P

HEAD_DIM = 128
EPSILON = 1e-05
SCALING = 1.0 / math.sqrt(HEAD_DIM)
CONTRACT_LAST = (((1,), (1,)), ((), ()))
CONTRACT_FIRST = (((0,), (0,)), ((), ()))
VMEM_LIMIT = 3 * 1024 * 1024
VMEM = pl.BlockSpec(memory_space=pltpu.VMEM)
SMEM = pl.BlockSpec(memory_space=pltpu.SMEM)
TILE = 512
SQUARES_FLOPS = 4000000000
HOME_FLOPS = 24000000000


def dot(left, right, dims=(((1,), (0,)), ((), ()))):
    return lax.dot_general(left, right, dims, preferred_element_type=jnp.float32)


def call(kernel, name, out_shape, operands, scratch=(), first=SMEM, rest=VMEM, flops=1000):
    single = not isinstance(out_shape, (list, tuple))
    shapes = [out_shape] if single else list(out_shape)
    results = pl.pallas_call(
        kernel,
        out_shape=shapes,
        in_specs=[first] + [rest] * (len(operands) - 1),
        out_specs=[VMEM] * len(shapes),
        scratch_shapes=list(scratch),
        compiler_params=pltpu.CompilerParams(vmem_limit_bytes=VMEM_LIMIT),
        cost_estimate=pl.CostEstimate(flops=flops, bytes_accessed=1000, transcendentals=0),
        name=name,
    )(*operands)
    return results[0] if single else results


def shape(dtype, *sizes):
    return jax.ShapeDtypeStruct(sizes, dtype)


def swap(array, mask, count):
    return lax.ppermute(array, "tensor", [(i, i ^ mask) for i in range(count)])


def block_start(order, slot, width):
    return pl.multiple_of(order[slot] * width, width)


def one_hot(places, rows):
    row = lax.broadcasted_iota(jnp.int32, (rows, places.shape[1]), 0)
    return jnp.where(places == row, 1.0, 0.0).astype(jnp.bfloat16)


def prepare_kernel(
    order,
    w_query,
    w_key,
    w_value,
    w_output,
    near_output,
    send,
    receive,
    segments,
    own_turned,
    near_turned,
    here,
    there,
    there_turned,
    send_out,
    receive_out,
    segments_out,
):
    heads, width = w_output.shape[0], here.shape[1]
    for slot, out, turned in ((0, here, None), (2, there, there_turned)):
        columns = pl.ds(block_start(order, slot, width), width)
        for part, weight in enumerate((w_output, near_output)):
            rows = slice(part * heads, (part + 1) * heads)
            block = weight[:, columns]
            out[rows, :] = block
            if turned is not None:
                turned[:, rows] = block.T
    for source, target in ((send, send_out), (receive, receive_out), (segments, segments_out)):
        target[...] = source[...]
    for out, slots in ((own_turned, (0, 2)), (near_turned, (1, 3))):
        for part, slot in enumerate(slots):
            first = block_start(order, slot, width)
            for start in range(0, width, TILE):
                columns = slice(part * width + start, part * width + start + TILE)
                for place, weight in enumerate((w_query, w_key, w_value)):
                    rows = slice(place * HEAD_DIM, (place + 1) * HEAD_DIM)
                    out[rows, columns] = weight[pl.ds(first + start, TILE), :].T


def prepare(order, w_query, w_key, w_value, w_output, near_output, send, receive, segments, width):
    heads = w_query.shape[1]
    low = jnp.bfloat16
    return call(
        prepare_kernel,
        "prepare",
        [
            *[shape(low, 3 * heads, 2 * width)] * 2,
            *[shape(low, 2 * heads, width)] * 2,
            shape(low, width, 2 * heads),
            shape(jnp.int32, *send.shape),
            shape(jnp.int32, *receive.shape),
            shape(jnp.int32, *segments.shape),
        ],
        (order, w_query, w_key, w_value, w_output, near_output, send, receive, segments),
    )


def sum_squares(block):
    wide = block[...].astype(jnp.float32)
    return jnp.sum(wide * wide, axis=-1, keepdims=True)


def begin_kernel(x0, x1, c0, here, squares, part):
    squares[...] = sum_squares(x0) + sum_squares(x1)
    part[...] = dot(c0[...], here[...], CONTRACT_LAST)


def begin(x0, x1, c0, here):
    rows, columns = x0.shape[0], here.shape[0]
    shapes = [shape(jnp.float32, rows, 1), shape(jnp.float32, rows, columns)]
    return call(begin_kernel, "begin", shapes, (x0, x1, c0, here), first=VMEM)


def add_grad_kernel(half):
    def kernel(c2, there_turned, part, total):
        heads = total.shape[1]
        columns = slice(half * heads, (half + 1) * heads)
        total[...] = part[:, columns] + dot(c2[...], there_turned[:, columns])

    return kernel


def add_grad(half, c2, there_turned, part):
    out = shape(jnp.float32, part.shape[0], part.shape[1] // 2)
    return call(add_grad_kernel(half), "add_grad", out, (c2, there_turned, part), first=VMEM)


def add_squares_kernel(x2, squares_in, squares):
    squares[...] = squares_in[...] + sum_squares(x2)


def add_squares(x2, squares):
    out = shape(jnp.float32, *squares.shape)
    operands = (x2, squares)
    return call(
        add_squares_kernel, "add_squares", out, operands, first=VMEM, flops=SQUARES_FLOPS
    )


def project_kernel(
    order,
    x0,
    x1,
    x2,
    x3,
    gain_chip,
    gain_far,
    w_query,
    w_key,
    w_value,
    squares,
    own_part,
    got_part,
    send,
    home,
    inverse,
    bucket,
    total,
):
    blocks = (x0, x1, x2, x3)
    width = x0.shape[1]
    mean = (squares[...] + sum_squares(x3)) / (width * len(blocks))
    inverse_rms = lax.rsqrt(mean + EPSILON)
    inverse[...] = inverse_rms
    head_grad = (own_part[...] + got_part[...]).astype(jnp.bfloat16)
    for index, block in enumerate(blocks):
        gain = (gain_chip, gain_far)[index // 2][index % 2 : index % 2 + 1, :]
        scaled = block[...].astype(jnp.float32) * inverse_rms
        normed = (scaled * gain.astype(jnp.float32)).astype(jnp.bfloat16)
        here = pl.ds(block_start(order, index, width), width)
        weights = jnp.concatenate([w_query[here, :], w_key[here, :], w_value[here, :]], axis=1)
        product = dot(normed, weights)
        total[...] = total[...] + product if index else product
    rounded = total[...].astype(jnp.bfloat16)
    home[...] = rounded
    chosen = one_hot(send[...], rounded.shape[0])
    split = rounded.shape[1]
    bucket[:, :split] = dot(chosen, rounded, CONTRACT_FIRST).astype(jnp.bfloat16)
    bucket[:, split:] = dot(chosen, head_grad, CONTRACT_FIRST).astype(jnp.bfloat16)


def project(order, blocks, gains, weights, squares, own_part, got_part, send):
    rows = blocks[0].shape[0]
    columns = 3 * HEAD_DIM
    return call(
        project_kernel,
        "project",
        [
            shape(jnp.bfloat16, rows, columns),
            shape(jnp.float32, rows, 1),
            shape(jnp.bfloat16, send.shape[1], columns + HEAD_DIM),
        ],
        (order, *blocks, *gains, *weights, squares, own_part, got_part, send),
        scratch=[pltpu.VMEM((rows, columns), jnp.float32)],
    )


def attend_kernel(moved, receive, segments, back):
    place = one_hot(receive[...], moved.shape[0])
    rows = dot(place, moved[...], CONTRACT_FIRST).astype(jnp.bfloat16)
    queries, key_rows, value_rows, head_grad = (
        rows[:, index * HEAD_DIM : (index + 1) * HEAD_DIM] for index in range(4)
    )
    count = rows.shape[0]
    down = lax.broadcasted_iota(jnp.int32, (count, count), 0)
    across = lax.broadcasted_iota(jnp.int32, (count, count), 1)
    stays = segments[...]
    own_stay = jnp.sum(jnp.where(down == across, stays, 0), axis=1, keepdims=True)
    allowed = (own_stay == stays) & (across <= down)
    scores = jnp.where(allowed, dot(queries, key_rows, CONTRACT_LAST) * SCALING, -1e30)
    raised = jnp.exp(scores - jnp.max(scores, axis=-1, keepdims=True))
    softmax_out = raised / jnp.sum(raised, axis=-1, keepdims=True)
    low_weights = softmax_out.astype(jnp.bfloat16)
    attended = dot(low_weights, value_rows).astype(jnp.bfloat16)
    grad_value = dot(low_weights, head_grad, CONTRACT_FIRST).astype(jnp.bfloat16)
    grad_probs = dot(head_grad, value_rows, CONTRACT_LAST)
    inner = jnp.sum(softmax_out * grad_probs, axis=-1, keepdims=True)
    grad_scores = (softmax_out * (grad_probs - inner) * SCALING).astype(jnp.bfloat16)
    grad_query = dot(grad_scores, key_rows).astype(jnp.bfloat16)
    grad_key = dot(grad_scores, queries, CONTRACT_FIRST).astype(jnp.bfloat16)
    results = jnp.concatenate([grad_query, grad_key, grad_value, attended], axis=1)
    back[...] = dot(place, results).astype(jnp.bfloat16)


def attend(moved, receive, segments):
    out = shape(jnp.bfloat16, *moved.shape)
    return call(attend_kernel, "attend", out, (moved, receive, segments), first=VMEM)


def write_parts(value, out):
    out[...] = jnp.zeros_like(out)
    for place in range(3):
        low = value.astype(jnp.bfloat16)
        out[:, place : place + 1] = low
        value = value - low.astype(jnp.float32)


def read_parts(parts):
    return sum(parts[:, place : place + 1].astype(jnp.float32) for place in (2, 1, 0))


def bring_home_kernel(moved, send, home, grads, extras):
    chosen = one_hot(send[...], grads.shape[0])
    rows = dot(chosen, moved[...])
    split = 3 * HEAD_DIM
    grads[...] = rows[:, :split].astype(jnp.bfloat16)
    extras[:, :HEAD_DIM] = rows[:, split:].astype(jnp.bfloat16)
    product = rows[:, :split] * home[...].astype(jnp.float32)
    row_dot = jnp.sum(product, axis=-1, keepdims=True)
    write_parts(row_dot, extras.at[:, HEAD_DIM:])


def bring_home(moved, send, home):
    rows = home.shape[0]
    shapes = [shape(jnp.bfloat16, rows, 3 * HEAD_DIM), shape(jnp.bfloat16, rows, 2 * HEAD_DIM)]
    operands = (moved, send, home)
    return call(bring_home_kernel, "bring_home", shapes, operands, first=VMEM, flops=HOME_FLOPS)


def spread_kernel(first):
    def kernel(own, near, weights, near_weights, out):
        own_rows, near_rows = own[...], near[...]
        for start in range(0, out.shape[1], TILE):
            columns = slice(first + start, first + start + TILE)
            total = dot(own_rows, weights[:, columns]) + dot(near_rows, near_weights[:, columns])
            out[:, start : start + TILE] = total.astype(out.dtype)

    return kernel


def spread(name, first, span, dtype, own, near, weights, near_weights, flops=1000):
    return pl.pallas_call(
        spread_kernel(first),
        out_shape=shape(dtype, own.shape[0], span),
        in_specs=[VMEM] * 4,
        out_specs=VMEM,
        compiler_params=pltpu.CompilerParams(vmem_limit_bytes=VMEM_LIMIT),
        cost_estimate=pl.CostEstimate(flops=flops, bytes_accessed=1000, transcendentals=0),
        name=name,
    )(own, near, weights, near_weights)


def finish_out_kernel(inputs, own, near, far, last, here, there, out):
    width = inputs.shape[1]
    chip = jnp.concatenate([own[:, :HEAD_DIM], near[:, :HEAD_DIM]], axis=1)
    other = jnp.concatenate([far[:, :HEAD_DIM], last[:, :HEAD_DIM]], axis=1)
    for start in range(0, width, TILE):
        tile = slice(start, start + TILE)
        total = dot(chip, here[:, tile]) + dot(other, there[:, tile])
        out[:, tile] = (inputs[:, tile].astype(jnp.float32) + total).astype(jnp.bfloat16)


def finish_most_kernel(
    inputs, cotangent, gain, inverse, own, near, far, last, grad_own, *pieces
):
    *pieces, out, left, held, sem = pieces
    tiles = [
        piece.at[:, start : start + TILE]
        for piece in pieces
        for start in range(0, piece.shape[1], TILE)
    ]
    row_dot = sum(read_parts(extras[:, HEAD_DIM:]) for extras in (own, near, far, last))
    mean_dot = row_dot / (4 * inputs.shape[1])
    inverse_rms = inverse[...]
    most = held.shape[1]
    for start in range(0, inputs.shape[1], TILE):
        tile = slice(start, start + TILE)
        grad_normed = grad_own[:, tile]
        if start < most:
            grad_normed = grad_normed + tiles[start // TILE][...].astype(jnp.float32)
        grad_hat = grad_normed * gain[:, tile].astype(jnp.float32)
        scaled = inputs[:, tile].astype(jnp.float32) * inverse_rms
        change = inverse_rms * (grad_hat - scaled * mean_dot)
        result = cotangent[:, tile].astype(jnp.float32) + change
        if start < most:
            held[:, tile] = result.astype(jnp.bfloat16)
        else:
            left[:, start - most : start - most + TILE] = result
    copy = pltpu.make_async_copy(held, out.at[:, pl.ds(0, most)], sem)
    copy.start()
    copy.wait()


def finish_rest_kernel(gain, inverse, left, rest, before, out, held, sems):
    span = rest.shape[1]
    first = out.shape[1] - span
    half = span // 2
    copies = []
    for index, start in enumerate(range(0, span, half)):
        tile = slice(start, start + half)
        columns = slice(first + start, first + start + half)
        grad_hat = rest[:, tile].astype(jnp.float32) * gain[:, columns].astype(jnp.float32)
        held[:, tile] = (left[:, tile] + inverse[...] * grad_hat).astype(jnp.bfloat16)
        target = out.at[:, pl.ds(first + start, half)]
        copies.append(
            pltpu.make_async_copy(held.at[:, pl.ds(start, half)], target, sems.at[index])
        )
        copies[-1].start()
    for copy in copies:
        copy.wait()


def finish_grad(inputs, cotangent, gain, inverse, extras, grad_own, pieces):
    rows, width = inputs.shape
    *pieces, rest = pieces
    span = rest.shape[1]
    hbm = pl.BlockSpec(memory_space=pltpu.HBM)
    options = dict(
        compiler_params=pltpu.CompilerParams(vmem_limit_bytes=VMEM_LIMIT),
        cost_estimate=pl.CostEstimate(flops=1000, bytes_accessed=1000, transcendentals=0),
    )
    begun, left = pl.pallas_call(
        finish_most_kernel,
        out_shape=[shape(jnp.bfloat16, rows, width), shape(jnp.float32, rows, span)],
        in_specs=[VMEM] * (9 + len(pieces)),
        out_specs=[hbm, VMEM],
        scratch_shapes=[pltpu.VMEM((rows, width - span), jnp.bfloat16), pltpu.SemaphoreType.DMA],
        name="finish_most",
        **options,
    )(inputs, cotangent, gain, inverse, *extras, grad_own, *pieces)
    return pl.pallas_call(
        finish_rest_kernel,
        out_shape=shape(jnp.bfloat16, rows, width),
        in_specs=[VMEM] * 4 + [hbm],
        out_specs=hbm,
        scratch_shapes=[pltpu.VMEM((rows, span), jnp.bfloat16), pltpu.SemaphoreType.DMA((2,))],
        input_output_aliases={4: 0},
        name="finish_rest",
        **options,
    )(gain, inverse, left, rest, begun)


def move(bucket):
    return lax.all_to_all(bucket, "dp", split_axis=0, concat_axis=0, tiled=True)


def after(array, *others):
    return lax.optimization_barrier((array, *others))[0]


def on_device(
    inputs,
    cotangent,
    norm_gain,
    w_query,
    w_key,
    w_value,
    w_output,
    send_rows,
    receive_slots,
    owner_segments,
):
    rows, width = inputs.shape
    tensor = lax.axis_size("tensor")
    low = jnp.bfloat16
    order = lax.axis_index("tensor").astype(jnp.int32) ^ jnp.arange(4, dtype=jnp.int32)
    gain = norm_gain.reshape(1, width)

    x2 = swap(inputs, 2, tensor)
    c2 = swap(cotangent, 2, tensor)
    gain_chip = jnp.concatenate([gain, swap(gain, 1, tensor)], axis=0)
    gain_far = swap(gain_chip, 2, tensor)
    x1 = swap(inputs, 1, tensor)
    near_output = swap(w_output, 1, tensor)
    weights = (w_query, w_key, w_value)
    own_turned, near_turned, here, there, there_turned, *indices = prepare(
        order,
        *weights,
        w_output,
        near_output,
        send_rows,
        receive_slots.reshape(1, rows),
        owner_segments.reshape(1, rows),
        width,
    )
    send, receive, segments = indices
    squares, part = begin(inputs, x1, cotangent, here)

    x2, c2, gain_far, squares, part = lax.optimization_barrier((x2, c2, gain_far, squares, part))
    x3 = swap(x2, 1, tensor)
    near_part = add_grad(1, c2, there_turned, part)
    got_part = swap(near_part, 1, tensor)
    own_part = add_grad(0, c2, there_turned, after(part, near_part))
    squares = add_squares(x2, after(squares, near_part, own_part))
    home, inverse_rms, bucket = project(
        order,
        (inputs, x1, x2, x3),
        (gain_chip, gain_far),
        weights,
        squares,
        own_part,
        got_part,
        send,
    )
    near_turned = swap(after(near_turned, home), 1, tensor)
    there = swap(after(there, near_part), 2, tensor)
    back = attend(move(bucket), receive, segments)
    moved, there = lax.optimization_barrier((move(back), there))
    own, own_extras = bring_home(moved, send, home)

    near = swap(own, 1, tensor)
    far_extras = swap(own_extras, 2, tensor)
    quarter = width // 4
    turn, got = own, []
    for first, span in ((0, 2 * quarter), (2 * quarter, quarter), (3 * quarter, quarter)):
        flops = 4 * rows * span * width if first else 1000
        sides = (turn, near, own_turned, near_turned)
        part = spread("spread_far", width + first, span, low, *sides, flops=flops)
        got.append(swap(part, 2, tensor))
        turn = after(own, part, far_extras)
    grad_own = spread("spread_own", 0, width, jnp.float32, turn, near, own_turned, near_turned)
    extras = (own_extras, swap(own_extras, 1, tensor), far_extras, swap(far_extras, 1, tensor))
    layer_out = call(
        finish_out_kernel,
        "finish_out",
        shape(low, rows, width),
        (inputs, *extras, here, there),
        first=VMEM,
    )
    got[1] = after(got[1], layer_out)
    input_grad = finish_grad(inputs, cotangent, gain, inverse_rms, extras, grad_own, got)
    return (layer_out, input_grad)


def solution(mesh):
    return jax.shard_map(
        on_device,
        mesh=mesh,
        in_specs=(
            P("dp", "tensor"),
            P("dp", "tensor"),
            P("tensor"),
            P(None, "tensor"),
            P(None, "tensor"),
            P(None, "tensor"),
            P("tensor", None),
            P("dp", None),
            P("dp"),
            P("dp"),
        ),
        out_specs=(P("dp", "tensor"), P("dp", "tensor")),
        check_vma=False,
    )
```

```python
import math

import jax
import jax.numpy as jnp
from jax import lax
from jax.experimental import pallas as pl
from jax.experimental.pallas import tpu as pltpu
from jax.sharding import PartitionSpec as P

HEAD_DIM = 128
EPSILON = 1e-05
SCALING = 1.0 / math.sqrt(HEAD_DIM)
CONTRACT_LAST = (((1,), (1,)), ((), ()))
CONTRACT_FIRST = (((0,), (0,)), ((), ()))
VMEM_LIMIT = 3 * 1024 * 1024
VMEM = pl.BlockSpec(memory_space=pltpu.VMEM)
SMEM = pl.BlockSpec(memory_space=pltpu.SMEM)
TILE = 512
OWN_FLOPS = 4000000000
HOME_FLOPS = 24000000000


def dot(left, right, dims=(((1,), (0,)), ((), ()))):
    return lax.dot_general(left, right, dims, preferred_element_type=jnp.float32)


def call(kernel, name, out_shape, operands, scratch=(), first=SMEM, rest=VMEM, flops=1000):
    single = not isinstance(out_shape, (list, tuple))
    shapes = [out_shape] if single else list(out_shape)
    results = pl.pallas_call(
        kernel,
        out_shape=shapes,
        in_specs=[first] + [rest] * (len(operands) - 1),
        out_specs=[VMEM] * len(shapes),
        scratch_shapes=list(scratch),
        compiler_params=pltpu.CompilerParams(vmem_limit_bytes=VMEM_LIMIT),
        cost_estimate=pl.CostEstimate(flops=flops, bytes_accessed=1000, transcendentals=0),
        name=name,
    )(*operands)
    return results[0] if single else results


def shape(dtype, *sizes):
    return jax.ShapeDtypeStruct(sizes, dtype)


def swap(array, mask, count):
    return lax.ppermute(array, "tensor", [(i, i ^ mask) for i in range(count)])


def block_start(order, slot, width):
    return pl.multiple_of(order[slot] * width, width)


def one_hot(places, rows):
    row = lax.broadcasted_iota(jnp.int32, (rows, places.shape[1]), 0)
    return jnp.where(places == row, 1.0, 0.0).astype(jnp.bfloat16)


def prepare_kernel(
    order,
    w_query,
    w_key,
    w_value,
    w_output,
    near_output,
    send,
    receive,
    segments,
    own_turned,
    near_turned,
    here,
    there,
    there_turned,
    send_out,
    receive_out,
    segments_out,
):
    heads, width = w_output.shape[0], here.shape[1]
    for slot, out, turned in ((0, here, None), (2, there, there_turned)):
        columns = pl.ds(block_start(order, slot, width), width)
        for part, weight in enumerate((w_output, near_output)):
            rows = slice(part * heads, (part + 1) * heads)
            block = weight[:, columns]
            out[rows, :] = block
            if turned is not None:
                turned[:, rows] = block.T
    for source, target in ((send, send_out), (receive, receive_out), (segments, segments_out)):
        target[...] = source[...]
    for out, slots in ((own_turned, (0, 2)), (near_turned, (1, 3))):
        for part, slot in enumerate(slots):
            first = block_start(order, slot, width)
            for start in range(0, width, TILE):
                columns = slice(part * width + start, part * width + start + TILE)
                for place, weight in enumerate((w_query, w_key, w_value)):
                    rows = slice(place * HEAD_DIM, (place + 1) * HEAD_DIM)
                    out[rows, columns] = weight[pl.ds(first + start, TILE), :].T


def prepare(order, w_query, w_key, w_value, w_output, near_output, send, receive, segments, width):
    heads = w_query.shape[1]
    low = jnp.bfloat16
    return call(
        prepare_kernel,
        "prepare",
        [
            *[shape(low, 3 * heads, 2 * width)] * 2,
            *[shape(low, 2 * heads, width)] * 2,
            shape(low, width, 2 * heads),
            shape(jnp.int32, *send.shape),
            shape(jnp.int32, *receive.shape),
            shape(jnp.int32, *segments.shape),
        ],
        (order, w_query, w_key, w_value, w_output, near_output, send, receive, segments),
    )


def sum_squares(block):
    wide = block[...].astype(jnp.float32)
    return jnp.sum(wide * wide, axis=-1, keepdims=True)


def begin_kernel(x0, x1, c0, here, squares, part):
    squares[...] = sum_squares(x0) + sum_squares(x1)
    part[...] = dot(c0[...], here[...], CONTRACT_LAST)


def begin(x0, x1, c0, here):
    rows, columns = x0.shape[0], here.shape[0]
    shapes = [shape(jnp.float32, rows, 1), shape(jnp.float32, rows, columns)]
    return call(begin_kernel, "begin", shapes, (x0, x1, c0, here), first=VMEM)


def add_grad_kernel(half):
    def kernel(c2, there_turned, part, total):
        heads = total.shape[1]
        columns = slice(half * heads, (half + 1) * heads)
        total[...] = part[:, columns] + dot(c2[...], there_turned[:, columns])

    return kernel


def add_grad(half, c2, there_turned, part):
    out = shape(jnp.float32, part.shape[0], part.shape[1] // 2)
    flops = 1000 if half else OWN_FLOPS
    operands = (c2, there_turned, part)
    return call(add_grad_kernel(half), "add_grad", out, operands, first=VMEM, flops=flops)


def project_kernel(
    order,
    x0,
    x1,
    x2,
    x3,
    gain_chip,
    gain_far,
    w_query,
    w_key,
    w_value,
    squares,
    own_part,
    got_part,
    send,
    home,
    inverse,
    bucket,
    total,
):
    blocks = (x0, x1, x2, x3)
    width = x0.shape[1]
    mean = (squares[...] + sum_squares(x2) + sum_squares(x3)) / (width * len(blocks))
    inverse_rms = lax.rsqrt(mean + EPSILON)
    inverse[...] = inverse_rms
    head_grad = (own_part[...] + got_part[...]).astype(jnp.bfloat16)
    for index, block in enumerate(blocks):
        gain = (gain_chip, gain_far)[index // 2][index % 2 : index % 2 + 1, :]
        scaled = block[...].astype(jnp.float32) * inverse_rms
        normed = (scaled * gain.astype(jnp.float32)).astype(jnp.bfloat16)
        here = pl.ds(block_start(order, index, width), width)
        weights = jnp.concatenate([w_query[here, :], w_key[here, :], w_value[here, :]], axis=1)
        product = dot(normed, weights)
        total[...] = total[...] + product if index else product
    rounded = total[...].astype(jnp.bfloat16)
    home[...] = rounded
    chosen = one_hot(send[...], rounded.shape[0])
    split = rounded.shape[1]
    bucket[:, :split] = dot(chosen, rounded, CONTRACT_FIRST).astype(jnp.bfloat16)
    bucket[:, split:] = dot(chosen, head_grad, CONTRACT_FIRST).astype(jnp.bfloat16)


def project(order, blocks, gains, weights, squares, own_part, got_part, send):
    rows = blocks[0].shape[0]
    columns = 3 * HEAD_DIM
    return call(
        project_kernel,
        "project",
        [
            shape(jnp.bfloat16, rows, columns),
            shape(jnp.float32, rows, 1),
            shape(jnp.bfloat16, send.shape[1], columns + HEAD_DIM),
        ],
        (order, *blocks, *gains, *weights, squares, own_part, got_part, send),
        scratch=[pltpu.VMEM((rows, columns), jnp.float32)],
    )


def attend_kernel(moved, receive, segments, back):
    place = one_hot(receive[...], moved.shape[0])
    rows = dot(place, moved[...], CONTRACT_FIRST).astype(jnp.bfloat16)
    queries, key_rows, value_rows, head_grad = (
        rows[:, index * HEAD_DIM : (index + 1) * HEAD_DIM] for index in range(4)
    )
    count = rows.shape[0]
    down = lax.broadcasted_iota(jnp.int32, (count, count), 0)
    across = lax.broadcasted_iota(jnp.int32, (count, count), 1)
    stays = segments[...]
    own_stay = jnp.sum(jnp.where(down == across, stays, 0), axis=1, keepdims=True)
    allowed = (own_stay == stays) & (across <= down)
    scores = jnp.where(allowed, dot(queries, key_rows, CONTRACT_LAST) * SCALING, -1e30)
    raised = jnp.exp(scores - jnp.max(scores, axis=-1, keepdims=True))
    softmax_out = raised / jnp.sum(raised, axis=-1, keepdims=True)
    low_weights = softmax_out.astype(jnp.bfloat16)
    attended = dot(low_weights, value_rows).astype(jnp.bfloat16)
    grad_value = dot(low_weights, head_grad, CONTRACT_FIRST).astype(jnp.bfloat16)
    grad_probs = dot(head_grad, value_rows, CONTRACT_LAST)
    inner = jnp.sum(softmax_out * grad_probs, axis=-1, keepdims=True)
    grad_scores = (softmax_out * (grad_probs - inner) * SCALING).astype(jnp.bfloat16)
    grad_query = dot(grad_scores, key_rows).astype(jnp.bfloat16)
    grad_key = dot(grad_scores, queries, CONTRACT_FIRST).astype(jnp.bfloat16)
    results = jnp.concatenate([grad_query, grad_key, grad_value, attended], axis=1)
    back[...] = dot(place, results).astype(jnp.bfloat16)


def attend(moved, receive, segments):
    out = shape(jnp.bfloat16, *moved.shape)
    return call(attend_kernel, "attend", out, (moved, receive, segments), first=VMEM)


def write_parts(value, out):
    out[...] = jnp.zeros_like(out)
    for place in range(3):
        low = value.astype(jnp.bfloat16)
        out[:, place : place + 1] = low
        value = value - low.astype(jnp.float32)


def read_parts(parts):
    return sum(parts[:, place : place + 1].astype(jnp.float32) for place in (2, 1, 0))


def bring_home_kernel(moved, send, home, grads, extras):
    chosen = one_hot(send[...], grads.shape[0])
    rows = dot(chosen, moved[...])
    split = 3 * HEAD_DIM
    grads[...] = rows[:, :split].astype(jnp.bfloat16)
    extras[:, :HEAD_DIM] = rows[:, split:].astype(jnp.bfloat16)
    product = rows[:, :split] * home[...].astype(jnp.float32)
    row_dot = jnp.sum(product, axis=-1, keepdims=True)
    write_parts(row_dot, extras.at[:, HEAD_DIM:])


def bring_home(moved, send, home):
    rows = home.shape[0]
    shapes = [shape(jnp.bfloat16, rows, 3 * HEAD_DIM), shape(jnp.bfloat16, rows, 2 * HEAD_DIM)]
    operands = (moved, send, home)
    return call(bring_home_kernel, "bring_home", shapes, operands, first=VMEM, flops=HOME_FLOPS)


def spread_kernel(first):
    def kernel(own, near, weights, near_weights, out):
        own_rows, near_rows = own[...], near[...]
        for start in range(0, out.shape[1], TILE):
            columns = slice(first + start, first + start + TILE)
            total = dot(own_rows, weights[:, columns]) + dot(near_rows, near_weights[:, columns])
            out[:, start : start + TILE] = total.astype(out.dtype)

    return kernel


def spread(name, first, span, dtype, own, near, weights, near_weights, flops=1000):
    return pl.pallas_call(
        spread_kernel(first),
        out_shape=shape(dtype, own.shape[0], span),
        in_specs=[VMEM] * 4,
        out_specs=VMEM,
        compiler_params=pltpu.CompilerParams(vmem_limit_bytes=VMEM_LIMIT),
        cost_estimate=pl.CostEstimate(flops=flops, bytes_accessed=1000, transcendentals=0),
        name=name,
    )(own, near, weights, near_weights)


def finish_out_kernel(inputs, own, near, far, last, here, there, out):
    width = inputs.shape[1]
    chip = jnp.concatenate([own[:, :HEAD_DIM], near[:, :HEAD_DIM]], axis=1)
    other = jnp.concatenate([far[:, :HEAD_DIM], last[:, :HEAD_DIM]], axis=1)
    for start in range(0, width, TILE):
        tile = slice(start, start + TILE)
        total = dot(chip, here[:, tile]) + dot(other, there[:, tile])
        out[:, tile] = (inputs[:, tile].astype(jnp.float32) + total).astype(jnp.bfloat16)


def finish_most_kernel(
    inputs, cotangent, gain, inverse, own, near, far, last, grad_own, *pieces
):
    *pieces, out, left, held, sem = pieces
    tiles = [
        piece.at[:, start : start + TILE]
        for piece in pieces
        for start in range(0, piece.shape[1], TILE)
    ]
    row_dot = sum(read_parts(extras[:, HEAD_DIM:]) for extras in (own, near, far, last))
    mean_dot = row_dot / (4 * inputs.shape[1])
    inverse_rms = inverse[...]
    most = held.shape[1]
    for start in range(0, inputs.shape[1], TILE):
        tile = slice(start, start + TILE)
        grad_normed = grad_own[:, tile]
        if start < most:
            grad_normed = grad_normed + tiles[start // TILE][...].astype(jnp.float32)
        grad_hat = grad_normed * gain[:, tile].astype(jnp.float32)
        scaled = inputs[:, tile].astype(jnp.float32) * inverse_rms
        change = inverse_rms * (grad_hat - scaled * mean_dot)
        result = cotangent[:, tile].astype(jnp.float32) + change
        if start < most:
            held[:, tile] = result.astype(jnp.bfloat16)
        else:
            left[:, start - most : start - most + TILE] = result
    copy = pltpu.make_async_copy(held, out.at[:, pl.ds(0, most)], sem)
    copy.start()
    copy.wait()


def finish_rest_kernel(gain, inverse, left, rest, before, out, held, sems):
    span = rest.shape[1]
    first = out.shape[1] - span
    half = span // 2
    copies = []
    for index, start in enumerate(range(0, span, half)):
        tile = slice(start, start + half)
        columns = slice(first + start, first + start + half)
        grad_hat = rest[:, tile].astype(jnp.float32) * gain[:, columns].astype(jnp.float32)
        held[:, tile] = (left[:, tile] + inverse[...] * grad_hat).astype(jnp.bfloat16)
        target = out.at[:, pl.ds(first + start, half)]
        copies.append(
            pltpu.make_async_copy(held.at[:, pl.ds(start, half)], target, sems.at[index])
        )
        copies[-1].start()
    for copy in copies:
        copy.wait()


def finish_grad(inputs, cotangent, gain, inverse, extras, grad_own, pieces):
    rows, width = inputs.shape
    *pieces, rest = pieces
    span = rest.shape[1]
    hbm = pl.BlockSpec(memory_space=pltpu.HBM)
    options = dict(
        compiler_params=pltpu.CompilerParams(vmem_limit_bytes=VMEM_LIMIT),
        cost_estimate=pl.CostEstimate(flops=1000, bytes_accessed=1000, transcendentals=0),
    )
    begun, left = pl.pallas_call(
        finish_most_kernel,
        out_shape=[shape(jnp.bfloat16, rows, width), shape(jnp.float32, rows, span)],
        in_specs=[VMEM] * (9 + len(pieces)),
        out_specs=[hbm, VMEM],
        scratch_shapes=[pltpu.VMEM((rows, width - span), jnp.bfloat16), pltpu.SemaphoreType.DMA],
        name="finish_most",
        **options,
    )(inputs, cotangent, gain, inverse, *extras, grad_own, *pieces)
    return pl.pallas_call(
        finish_rest_kernel,
        out_shape=shape(jnp.bfloat16, rows, width),
        in_specs=[VMEM] * 4 + [hbm],
        out_specs=hbm,
        scratch_shapes=[pltpu.VMEM((rows, span), jnp.bfloat16), pltpu.SemaphoreType.DMA((2,))],
        input_output_aliases={4: 0},
        name="finish_rest",
        **options,
    )(gain, inverse, left, rest, begun)


def move(bucket):
    return lax.all_to_all(bucket, "dp", split_axis=0, concat_axis=0, tiled=True)


def after(array, *others):
    return lax.optimization_barrier((array, *others))[0]


def on_device(
    inputs,
    cotangent,
    norm_gain,
    w_query,
    w_key,
    w_value,
    w_output,
    send_rows,
    receive_slots,
    owner_segments,
):
    rows, width = inputs.shape
    tensor = lax.axis_size("tensor")
    low = jnp.bfloat16
    order = lax.axis_index("tensor").astype(jnp.int32) ^ jnp.arange(4, dtype=jnp.int32)
    gain = norm_gain.reshape(1, width)

    x2 = swap(inputs, 2, tensor)
    c2 = swap(cotangent, 2, tensor)
    gain_chip = jnp.concatenate([gain, swap(gain, 1, tensor)], axis=0)
    gain_far = swap(gain_chip, 2, tensor)
    x1 = swap(inputs, 1, tensor)
    near_output = swap(w_output, 1, tensor)
    weights = (w_query, w_key, w_value)
    own_turned, near_turned, here, there, there_turned, *indices = prepare(
        order,
        *weights,
        w_output,
        near_output,
        send_rows,
        receive_slots.reshape(1, rows),
        owner_segments.reshape(1, rows),
        width,
    )
    send, receive, segments = indices
    squares, part = begin(inputs, x1, cotangent, here)

    x2, c2, gain_far, squares, part = lax.optimization_barrier((x2, c2, gain_far, squares, part))
    x3 = swap(x2, 1, tensor)
    near_part = add_grad(1, c2, there_turned, part)
    got_part = swap(near_part, 1, tensor)
    own_part = add_grad(0, c2, there_turned, after(part, near_part))
    squares = after(squares, own_part)
    home, inverse_rms, bucket = project(
        order,
        (inputs, x1, x2, x3),
        (gain_chip, gain_far),
        weights,
        squares,
        own_part,
        got_part,
        send,
    )
    near_turned = swap(after(near_turned, home), 1, tensor)
    there = swap(after(there, near_part), 2, tensor)
    back = attend(move(bucket), receive, segments)
    moved, there = lax.optimization_barrier((move(back), there))
    own, own_extras = bring_home(moved, send, home)

    near = swap(own, 1, tensor)
    far_extras = swap(own_extras, 2, tensor)
    quarter = width // 4
    turn, got = own, []
    for first, span in ((0, 2 * quarter), (2 * quarter, quarter), (3 * quarter, quarter)):
        flops = 4 * rows * span * width if first else 1000
        sides = (turn, near, own_turned, near_turned)
        part = spread("spread_far", width + first, span, low, *sides, flops=flops)
        got.append(swap(part, 2, tensor))
        turn = after(own, part, far_extras)
    grad_own = spread("spread_own", 0, width, jnp.float32, turn, near, own_turned, near_turned)
    extras = (own_extras, swap(own_extras, 1, tensor), far_extras, swap(far_extras, 1, tensor))
    layer_out = call(
        finish_out_kernel,
        "finish_out",
        shape(low, rows, width),
        (inputs, *extras, here, there),
        first=VMEM,
    )
    got[1] = after(got[1], layer_out)
    input_grad = finish_grad(inputs, cotangent, gain, inverse_rms, extras, grad_own, got)
    return (layer_out, input_grad)


def solution(mesh):
    return jax.shard_map(
        on_device,
        mesh=mesh,
        in_specs=(
            P("dp", "tensor"),
            P("dp", "tensor"),
            P("tensor"),
            P(None, "tensor"),
            P(None, "tensor"),
            P(None, "tensor"),
            P("tensor", None),
            P("dp", None),
            P("dp"),
            P("dp"),
        ),
        out_specs=(P("dp", "tensor"), P("dp", "tensor")),
        check_vma=False,
    )
```

```python
import math

import jax
import jax.numpy as jnp
from jax import lax
from jax.experimental import pallas as pl
from jax.experimental.pallas import tpu as pltpu
from jax.sharding import PartitionSpec as P

HEAD_DIM = 128
EPSILON = 1e-05
SCALING = 1.0 / math.sqrt(HEAD_DIM)
CONTRACT_LAST = (((1,), (1,)), ((), ()))
CONTRACT_FIRST = (((0,), (0,)), ((), ()))
VMEM_LIMIT = 5 * 1024 * 1024
VMEM = pl.BlockSpec(memory_space=pltpu.VMEM)
SMEM = pl.BlockSpec(memory_space=pltpu.SMEM)
TILE = 512
SQUARES_FLOPS = 4000000000
HOME_FLOPS = 24000000000


def dot(left, right, dims=(((1,), (0,)), ((), ()))):
    return lax.dot_general(left, right, dims, preferred_element_type=jnp.float32)


def call(kernel, name, out_shape, operands, scratch=(), first=SMEM, rest=VMEM, flops=1000):
    single = not isinstance(out_shape, (list, tuple))
    shapes = [out_shape] if single else list(out_shape)
    results = pl.pallas_call(
        kernel,
        out_shape=shapes,
        in_specs=[first] + [rest] * (len(operands) - 1),
        out_specs=[VMEM] * len(shapes),
        scratch_shapes=list(scratch),
        compiler_params=pltpu.CompilerParams(vmem_limit_bytes=VMEM_LIMIT),
        cost_estimate=pl.CostEstimate(flops=flops, bytes_accessed=1000, transcendentals=0),
        name=name,
    )(*operands)
    return results[0] if single else results


def shape(dtype, *sizes):
    return jax.ShapeDtypeStruct(sizes, dtype)


def swap(array, mask, count):
    return lax.ppermute(array, "tensor", [(i, i ^ mask) for i in range(count)])


def block_start(order, slot, width):
    return pl.multiple_of(order[slot] * width, width)


def one_hot(places, rows):
    row = lax.broadcasted_iota(jnp.int32, (rows, places.shape[1]), 0)
    return jnp.where(places == row, 1.0, 0.0).astype(jnp.bfloat16)


def prepare_kernel(
    order,
    w_query,
    w_key,
    w_value,
    w_output,
    near_output,
    send,
    receive,
    segments,
    own_turned,
    near_turned,
    here,
    there,
    there_turned,
    send_out,
    receive_out,
    segments_out,
):
    heads, width = w_output.shape[0], here.shape[1]
    for slot, out, turned in ((0, here, None), (2, there, there_turned)):
        columns = pl.ds(block_start(order, slot, width), width)
        for part, weight in enumerate((w_output, near_output)):
            rows = slice(part * heads, (part + 1) * heads)
            block = weight[:, columns]
            out[rows, :] = block
            if turned is not None:
                turned[:, rows] = block.T
    for source, target in ((send, send_out), (receive, receive_out), (segments, segments_out)):
        target[...] = source[...]
    for out, slots in ((own_turned, (0, 2)), (near_turned, (1, 3))):
        for part, slot in enumerate(slots):
            first = block_start(order, slot, width)
            for start in range(0, width, TILE):
                columns = slice(part * width + start, part * width + start + TILE)
                for place, weight in enumerate((w_query, w_key, w_value)):
                    rows = slice(place * HEAD_DIM, (place + 1) * HEAD_DIM)
                    out[rows, columns] = weight[pl.ds(first + start, TILE), :].T


def prepare(order, w_query, w_key, w_value, w_output, near_output, send, receive, segments, width):
    heads = w_query.shape[1]
    low = jnp.bfloat16
    return call(
        prepare_kernel,
        "prepare",
        [
            *[shape(low, 3 * heads, 2 * width)] * 2,
            *[shape(low, 2 * heads, width)] * 2,
            shape(low, width, 2 * heads),
            shape(jnp.int32, *send.shape),
            shape(jnp.int32, *receive.shape),
            shape(jnp.int32, *segments.shape),
        ],
        (order, w_query, w_key, w_value, w_output, near_output, send, receive, segments),
    )


def sum_squares(block):
    wide = block[...].astype(jnp.float32)
    return jnp.sum(wide * wide, axis=-1, keepdims=True)


def begin_kernel(x0, x1, c0, here, squares, part):
    squares[...] = sum_squares(x0) + sum_squares(x1)
    part[...] = dot(c0[...], here[...], CONTRACT_LAST)


def begin(x0, x1, c0, here):
    rows, columns = x0.shape[0], here.shape[0]
    shapes = [shape(jnp.float32, rows, 1), shape(jnp.float32, rows, columns)]
    return call(begin_kernel, "begin", shapes, (x0, x1, c0, here), first=VMEM)


def add_grad_kernel(half):
    def kernel(c2, there_turned, part, total):
        heads = total.shape[1]
        columns = slice(half * heads, (half + 1) * heads)
        total[...] = part[:, columns] + dot(c2[...], there_turned[:, columns])

    return kernel


def add_grad(half, c2, there_turned, part):
    out = shape(jnp.float32, part.shape[0], part.shape[1] // 2)
    return call(add_grad_kernel(half), "add_grad", out, (c2, there_turned, part), first=VMEM)


def add_squares_kernel(x2, squares_in, squares):
    squares[...] = squares_in[...] + sum_squares(x2)


def add_squares(x2, squares):
    out = shape(jnp.float32, *squares.shape)
    operands = (x2, squares)
    return call(
        add_squares_kernel, "add_squares", out, operands, first=VMEM, flops=SQUARES_FLOPS
    )


def project_kernel(
    order,
    x0,
    x1,
    x2,
    x3,
    gain_chip,
    gain_far,
    w_query,
    w_key,
    w_value,
    squares,
    own_part,
    got_part,
    send,
    home,
    inverse,
    bucket,
    total,
):
    blocks = (x0, x1, x2, x3)
    width = x0.shape[1]
    mean = (squares[...] + sum_squares(x3)) / (width * len(blocks))
    inverse_rms = lax.rsqrt(mean + EPSILON)
    inverse[...] = inverse_rms
    head_grad = (own_part[...] + got_part[...]).astype(jnp.bfloat16)
    for index, block in enumerate(blocks):
        gain = (gain_chip, gain_far)[index // 2][index % 2 : index % 2 + 1, :]
        scaled = block[...].astype(jnp.float32) * inverse_rms
        normed = (scaled * gain.astype(jnp.float32)).astype(jnp.bfloat16)
        here = pl.ds(block_start(order, index, width), width)
        weights = jnp.concatenate([w_query[here, :], w_key[here, :], w_value[here, :]], axis=1)
        product = dot(normed, weights)
        total[...] = total[...] + product if index else product
    rounded = total[...].astype(jnp.bfloat16)
    home[...] = rounded
    chosen = one_hot(send[...], rounded.shape[0])
    split = rounded.shape[1]
    bucket[:, :split] = dot(chosen, rounded, CONTRACT_FIRST).astype(jnp.bfloat16)
    bucket[:, split:] = dot(chosen, head_grad, CONTRACT_FIRST).astype(jnp.bfloat16)


def project(order, blocks, gains, weights, squares, own_part, got_part, send):
    rows = blocks[0].shape[0]
    columns = 3 * HEAD_DIM
    return call(
        project_kernel,
        "project",
        [
            shape(jnp.bfloat16, rows, columns),
            shape(jnp.float32, rows, 1),
            shape(jnp.bfloat16, send.shape[1], columns + HEAD_DIM),
        ],
        (order, *blocks, *gains, *weights, squares, own_part, got_part, send),
        scratch=[pltpu.VMEM((rows, columns), jnp.float32)],
    )


def attend_kernel(moved, receive, segments, back):
    place = one_hot(receive[...], moved.shape[0])
    rows = dot(place, moved[...], CONTRACT_FIRST).astype(jnp.bfloat16)
    queries, key_rows, value_rows, head_grad = (
        rows[:, index * HEAD_DIM : (index + 1) * HEAD_DIM] for index in range(4)
    )
    count = rows.shape[0]
    down = lax.broadcasted_iota(jnp.int32, (count, count), 0)
    across = lax.broadcasted_iota(jnp.int32, (count, count), 1)
    stays = segments[...]
    own_stay = jnp.sum(jnp.where(down == across, stays, 0), axis=1, keepdims=True)
    allowed = (own_stay == stays) & (across <= down)
    scores = jnp.where(allowed, dot(queries, key_rows, CONTRACT_LAST) * SCALING, -1e30)
    raised = jnp.exp(scores - jnp.max(scores, axis=-1, keepdims=True))
    softmax_out = raised / jnp.sum(raised, axis=-1, keepdims=True)
    low_weights = softmax_out.astype(jnp.bfloat16)
    attended = dot(low_weights, value_rows).astype(jnp.bfloat16)
    grad_value = dot(low_weights, head_grad, CONTRACT_FIRST).astype(jnp.bfloat16)
    grad_probs = dot(head_grad, value_rows, CONTRACT_LAST)
    inner = jnp.sum(softmax_out * grad_probs, axis=-1, keepdims=True)
    grad_scores = (softmax_out * (grad_probs - inner) * SCALING).astype(jnp.bfloat16)
    grad_query = dot(grad_scores, key_rows).astype(jnp.bfloat16)
    grad_key = dot(grad_scores, queries, CONTRACT_FIRST).astype(jnp.bfloat16)
    results = jnp.concatenate([grad_query, grad_key, grad_value, attended], axis=1)
    back[...] = dot(place, results).astype(jnp.bfloat16)


def attend(moved, receive, segments):
    out = shape(jnp.bfloat16, *moved.shape)
    return call(attend_kernel, "attend", out, (moved, receive, segments), first=VMEM)


def write_parts(value, out):
    out[...] = jnp.zeros_like(out)
    for place in range(3):
        low = value.astype(jnp.bfloat16)
        out[:, place : place + 1] = low
        value = value - low.astype(jnp.float32)


def read_parts(parts):
    return sum(parts[:, place : place + 1].astype(jnp.float32) for place in (2, 1, 0))


def bring_home_kernel(moved, send, home, grads, extras):
    chosen = one_hot(send[...], grads.shape[0])
    rows = dot(chosen, moved[...])
    split = 3 * HEAD_DIM
    grads[...] = rows[:, :split].astype(jnp.bfloat16)
    extras[:, :HEAD_DIM] = rows[:, split:].astype(jnp.bfloat16)
    product = rows[:, :split] * home[...].astype(jnp.float32)
    row_dot = jnp.sum(product, axis=-1, keepdims=True)
    write_parts(row_dot, extras.at[:, HEAD_DIM:])


def bring_home(moved, send, home):
    rows = home.shape[0]
    shapes = [shape(jnp.bfloat16, rows, 3 * HEAD_DIM), shape(jnp.bfloat16, rows, 2 * HEAD_DIM)]
    operands = (moved, send, home)
    return call(bring_home_kernel, "bring_home", shapes, operands, first=VMEM, flops=HOME_FLOPS)


def spread_kernel(first):
    def kernel(own, near, weights, near_weights, out):
        own_rows, near_rows = own[...], near[...]
        for start in range(0, out.shape[1], TILE):
            columns = slice(first + start, first + start + TILE)
            total = dot(own_rows, weights[:, columns]) + dot(near_rows, near_weights[:, columns])
            out[:, start : start + TILE] = total.astype(out.dtype)

    return kernel


def spread(name, first, span, dtype, own, near, weights, near_weights, flops=1000):
    return pl.pallas_call(
        spread_kernel(first),
        out_shape=shape(dtype, own.shape[0], span),
        in_specs=[VMEM] * 4,
        out_specs=VMEM,
        compiler_params=pltpu.CompilerParams(vmem_limit_bytes=VMEM_LIMIT),
        cost_estimate=pl.CostEstimate(flops=flops, bytes_accessed=1000, transcendentals=0),
        name=name,
    )(own, near, weights, near_weights)


def finish_out_kernel(inputs, own, near, far, last, here, there, out):
    width = inputs.shape[1]
    chip = jnp.concatenate([own[:, :HEAD_DIM], near[:, :HEAD_DIM]], axis=1)
    other = jnp.concatenate([far[:, :HEAD_DIM], last[:, :HEAD_DIM]], axis=1)
    for start in range(0, width, TILE):
        tile = slice(start, start + TILE)
        total = dot(chip, here[:, tile]) + dot(other, there[:, tile])
        out[:, tile] = (inputs[:, tile].astype(jnp.float32) + total).astype(jnp.bfloat16)


def finish_most_kernel(
    inputs, cotangent, gain, inverse, own, near, far, last, grad_own, *pieces
):
    *pieces, out, left, held, sem = pieces
    tiles = [
        piece.at[:, start : start + TILE]
        for piece in pieces
        for start in range(0, piece.shape[1], TILE)
    ]
    row_dot = sum(read_parts(extras[:, HEAD_DIM:]) for extras in (own, near, far, last))
    mean_dot = row_dot / (4 * inputs.shape[1])
    inverse_rms = inverse[...]
    most = held.shape[1]
    for start in range(0, inputs.shape[1], TILE):
        tile = slice(start, start + TILE)
        grad_normed = grad_own[:, tile]
        if start < most:
            grad_normed = grad_normed + tiles[start // TILE][...].astype(jnp.float32)
        grad_hat = grad_normed * gain[:, tile].astype(jnp.float32)
        scaled = inputs[:, tile].astype(jnp.float32) * inverse_rms
        change = inverse_rms * (grad_hat - scaled * mean_dot)
        result = cotangent[:, tile].astype(jnp.float32) + change
        if start < most:
            held[:, tile] = result.astype(jnp.bfloat16)
        else:
            left[:, start - most : start - most + TILE] = result
    copy = pltpu.make_async_copy(held, out.at[:, pl.ds(0, most)], sem)
    copy.start()
    copy.wait()


def finish_rest_kernel(gain, inverse, left, rest, before, out, held, sems):
    span = rest.shape[1]
    first = out.shape[1] - span
    half = span // 2
    copies = []
    for index, start in enumerate(range(0, span, half)):
        tile = slice(start, start + half)
        columns = slice(first + start, first + start + half)
        grad_hat = rest[:, tile].astype(jnp.float32) * gain[:, columns].astype(jnp.float32)
        held[:, tile] = (left[:, tile] + inverse[...] * grad_hat).astype(jnp.bfloat16)
        target = out.at[:, pl.ds(first + start, half)]
        copies.append(
            pltpu.make_async_copy(held.at[:, pl.ds(start, half)], target, sems.at[index])
        )
        copies[-1].start()
    for copy in copies:
        copy.wait()


def finish_grad(inputs, cotangent, gain, inverse, extras, grad_own, pieces):
    rows, width = inputs.shape
    *pieces, rest = pieces
    span = rest.shape[1]
    hbm = pl.BlockSpec(memory_space=pltpu.HBM)
    options = dict(
        compiler_params=pltpu.CompilerParams(vmem_limit_bytes=VMEM_LIMIT),
        cost_estimate=pl.CostEstimate(flops=1000, bytes_accessed=1000, transcendentals=0),
    )
    begun, left = pl.pallas_call(
        finish_most_kernel,
        out_shape=[shape(jnp.bfloat16, rows, width), shape(jnp.float32, rows, span)],
        in_specs=[VMEM] * (9 + len(pieces)),
        out_specs=[hbm, VMEM],
        scratch_shapes=[pltpu.VMEM((rows, width - span), jnp.bfloat16), pltpu.SemaphoreType.DMA],
        name="finish_most",
        **options,
    )(inputs, cotangent, gain, inverse, *extras, grad_own, *pieces)
    return pl.pallas_call(
        finish_rest_kernel,
        out_shape=shape(jnp.bfloat16, rows, width),
        in_specs=[VMEM] * 4 + [hbm],
        out_specs=hbm,
        scratch_shapes=[pltpu.VMEM((rows, span), jnp.bfloat16), pltpu.SemaphoreType.DMA((2,))],
        input_output_aliases={4: 0},
        name="finish_rest",
        **options,
    )(gain, inverse, left, rest, begun)


def move(bucket):
    return lax.all_to_all(bucket, "dp", split_axis=0, concat_axis=0, tiled=True)


def after(array, *others):
    return lax.optimization_barrier((array, *others))[0]


def on_device(
    inputs,
    cotangent,
    norm_gain,
    w_query,
    w_key,
    w_value,
    w_output,
    send_rows,
    receive_slots,
    owner_segments,
):
    rows, width = inputs.shape
    tensor = lax.axis_size("tensor")
    low = jnp.bfloat16
    order = lax.axis_index("tensor").astype(jnp.int32) ^ jnp.arange(4, dtype=jnp.int32)
    gain = norm_gain.reshape(1, width)

    x2 = swap(inputs, 2, tensor)
    c2 = swap(cotangent, 2, tensor)
    gain_chip = jnp.concatenate([gain, swap(gain, 1, tensor)], axis=0)
    gain_far = swap(gain_chip, 2, tensor)
    x1 = swap(inputs, 1, tensor)
    near_output = swap(w_output, 1, tensor)
    weights = (w_query, w_key, w_value)
    own_turned, near_turned, here, there, there_turned, *indices = prepare(
        order,
        *weights,
        w_output,
        near_output,
        send_rows,
        receive_slots.reshape(1, rows),
        owner_segments.reshape(1, rows),
        width,
    )
    send, receive, segments = indices
    squares, part = begin(inputs, x1, cotangent, here)

    x2, c2, gain_far, squares, part = lax.optimization_barrier((x2, c2, gain_far, squares, part))
    x3 = swap(x2, 1, tensor)
    near_part = add_grad(1, c2, there_turned, part)
    got_part = swap(near_part, 1, tensor)
    own_part = add_grad(0, c2, there_turned, after(part, near_part))
    squares = add_squares(x2, after(squares, near_part, own_part))
    home, inverse_rms, bucket = project(
        order,
        (inputs, x1, x2, x3),
        (gain_chip, gain_far),
        weights,
        squares,
        own_part,
        got_part,
        send,
    )
    near_turned = swap(after(near_turned, home), 1, tensor)
    there = swap(after(there, near_part), 2, tensor)
    back = attend(move(bucket), receive, segments)
    moved, there = lax.optimization_barrier((move(back), there))
    own, own_extras = bring_home(moved, send, home)

    near = swap(own, 1, tensor)
    far_extras = swap(own_extras, 2, tensor)
    quarter = width // 4
    turn, got = own, []
    for first, span in ((0, 2 * quarter), (2 * quarter, quarter), (3 * quarter, quarter)):
        flops = 4 * rows * span * width if first else 1000
        sides = (turn, near, own_turned, near_turned)
        part = spread("spread_far", width + first, span, low, *sides, flops=flops)
        got.append(swap(part, 2, tensor))
        turn = after(own, part, far_extras)
    grad_own = spread("spread_own", 0, width, jnp.float32, turn, near, own_turned, near_turned)
    extras = (own_extras, swap(own_extras, 1, tensor), far_extras, swap(far_extras, 1, tensor))
    layer_out = call(
        finish_out_kernel,
        "finish_out",
        shape(low, rows, width),
        (inputs, *extras, here, there),
        first=VMEM,
    )
    got[1] = after(got[1], layer_out)
    input_grad = finish_grad(inputs, cotangent, gain, inverse_rms, extras, grad_own, got)
    return (layer_out, input_grad)


def solution(mesh):
    return jax.shard_map(
        on_device,
        mesh=mesh,
        in_specs=(
            P("dp", "tensor"),
            P("dp", "tensor"),
            P("tensor"),
            P(None, "tensor"),
            P(None, "tensor"),
            P(None, "tensor"),
            P("tensor", None),
            P("dp", None),
            P("dp"),
            P("dp"),
        ),
        out_specs=(P("dp", "tensor"), P("dp", "tensor")),
        check_vma=False,
    )
```

```python
import math

import jax
import jax.numpy as jnp
from jax import lax
from jax.experimental import pallas as pl
from jax.experimental.pallas import tpu as pltpu
from jax.sharding import PartitionSpec as P

HEAD_DIM = 128
EPSILON = 1e-05
SCALING = 1.0 / math.sqrt(HEAD_DIM)
CONTRACT_LAST = (((1,), (1,)), ((), ()))
CONTRACT_FIRST = (((0,), (0,)), ((), ()))
VMEM_LIMIT = 3 * 1024 * 1024
VMEM = pl.BlockSpec(memory_space=pltpu.VMEM)
SMEM = pl.BlockSpec(memory_space=pltpu.SMEM)
TILE = 512
SQUARES_FLOPS = 4000000000
HOME_FLOPS = 24000000000


def dot(left, right, dims=(((1,), (0,)), ((), ()))):
    return lax.dot_general(left, right, dims, preferred_element_type=jnp.float32)


def call(kernel, name, out_shape, operands, scratch=(), first=SMEM, rest=VMEM, flops=1000):
    single = not isinstance(out_shape, (list, tuple))
    shapes = [out_shape] if single else list(out_shape)
    results = pl.pallas_call(
        kernel,
        out_shape=shapes,
        in_specs=[first] + [rest] * (len(operands) - 1),
        out_specs=[VMEM] * len(shapes),
        scratch_shapes=list(scratch),
        compiler_params=pltpu.CompilerParams(vmem_limit_bytes=VMEM_LIMIT),
        cost_estimate=pl.CostEstimate(flops=flops, bytes_accessed=1000, transcendentals=0),
        name=name,
    )(*operands)
    return results[0] if single else results


def shape(dtype, *sizes):
    return jax.ShapeDtypeStruct(sizes, dtype)


def swap(array, mask, count):
    return lax.ppermute(array, "tensor", [(i, i ^ mask) for i in range(count)])


def block_start(order, slot, width):
    return pl.multiple_of(order[slot] * width, width)


def one_hot(places, rows):
    row = lax.broadcasted_iota(jnp.int32, (rows, places.shape[1]), 0)
    return jnp.where(places == row, 1.0, 0.0).astype(jnp.bfloat16)


def prepare_kernel(
    order,
    w_query,
    w_key,
    w_value,
    w_output,
    near_output,
    send,
    receive,
    segments,
    own_turned,
    near_turned,
    here,
    there,
    there_turned,
    send_out,
    receive_out,
    segments_out,
):
    heads, width = w_output.shape[0], here.shape[1]
    for slot, out, turned in ((0, here, None), (2, there, there_turned)):
        columns = pl.ds(block_start(order, slot, width), width)
        for part, weight in enumerate((w_output, near_output)):
            rows = slice(part * heads, (part + 1) * heads)
            block = weight[:, columns]
            out[rows, :] = block
            if turned is not None:
                turned[:, rows] = block.T
    for source, target in ((send, send_out), (receive, receive_out), (segments, segments_out)):
        target[...] = source[...]
    for out, slots in ((own_turned, (0, 2)), (near_turned, (1, 3))):
        for part, slot in enumerate(slots):
            first = block_start(order, slot, width)
            for start in range(0, width, TILE):
                columns = slice(part * width + start, part * width + start + TILE)
                for place, weight in enumerate((w_query, w_key, w_value)):
                    rows = slice(place * HEAD_DIM, (place + 1) * HEAD_DIM)
                    out[rows, columns] = weight[pl.ds(first + start, TILE), :].T


def prepare(order, w_query, w_key, w_value, w_output, near_output, send, receive, segments, width):
    heads = w_query.shape[1]
    low = jnp.bfloat16
    return call(
        prepare_kernel,
        "prepare",
        [
            *[shape(low, 3 * heads, 2 * width)] * 2,
            *[shape(low, 2 * heads, width)] * 2,
            shape(low, width, 2 * heads),
            shape(jnp.int32, *send.shape),
            shape(jnp.int32, *receive.shape),
            shape(jnp.int32, *segments.shape),
        ],
        (order, w_query, w_key, w_value, w_output, near_output, send, receive, segments),
    )


def sum_squares(block):
    wide = block[...].astype(jnp.float32)
    return jnp.sum(wide * wide, axis=-1, keepdims=True)


def begin_kernel(x0, x1, c0, here, squares, part, x1_out):
    x1_out[...] = x1[...]
    squares[...] = sum_squares(x0) + sum_squares(x1)
    part[...] = dot(c0[...], here[...], CONTRACT_LAST)


def begin(x0, x1, c0, here):
    rows, columns = x0.shape[0], here.shape[0]
    shapes = [
        shape(jnp.float32, rows, 1),
        shape(jnp.float32, rows, columns),
        shape(x1.dtype, *x1.shape),
    ]
    return call(begin_kernel, "begin", shapes, (x0, x1, c0, here), first=VMEM)


def add_grad_kernel(half):
    def kernel(c2, there_turned, part, total):
        heads = total.shape[1]
        columns = slice(half * heads, (half + 1) * heads)
        total[...] = part[:, columns] + dot(c2[...], there_turned[:, columns])

    return kernel


def add_grad(half, c2, there_turned, part):
    out = shape(jnp.float32, part.shape[0], part.shape[1] // 2)
    return call(add_grad_kernel(half), "add_grad", out, (c2, there_turned, part), first=VMEM)


def add_squares_kernel(x2, squares_in, squares):
    squares[...] = squares_in[...] + sum_squares(x2)


def add_squares(x2, squares):
    out = shape(jnp.float32, *squares.shape)
    operands = (x2, squares)
    return call(
        add_squares_kernel, "add_squares", out, operands, first=VMEM, flops=SQUARES_FLOPS
    )


def project_kernel(
    order,
    x0,
    x1,
    x2,
    x3,
    gain_chip,
    gain_far,
    w_query,
    w_key,
    w_value,
    squares,
    own_part,
    got_part,
    send,
    home,
    inverse,
    bucket,
    total,
):
    blocks = (x0, x1, x2, x3)
    width = x0.shape[1]
    mean = (squares[...] + sum_squares(x3)) / (width * len(blocks))
    inverse_rms = lax.rsqrt(mean + EPSILON)
    inverse[...] = inverse_rms
    head_grad = (own_part[...] + got_part[...]).astype(jnp.bfloat16)
    for index, block in enumerate(blocks):
        gain = (gain_chip, gain_far)[index // 2][index % 2 : index % 2 + 1, :]
        scaled = block[...].astype(jnp.float32) * inverse_rms
        normed = (scaled * gain.astype(jnp.float32)).astype(jnp.bfloat16)
        here = pl.ds(block_start(order, index, width), width)
        weights = jnp.concatenate([w_query[here, :], w_key[here, :], w_value[here, :]], axis=1)
        product = dot(normed, weights)
        total[...] = total[...] + product if index else product
    rounded = total[...].astype(jnp.bfloat16)
    home[...] = rounded
    chosen = one_hot(send[...], rounded.shape[0])
    split = rounded.shape[1]
    bucket[:, :split] = dot(chosen, rounded, CONTRACT_FIRST).astype(jnp.bfloat16)
    bucket[:, split:] = dot(chosen, head_grad, CONTRACT_FIRST).astype(jnp.bfloat16)


def project(order, blocks, gains, weights, squares, own_part, got_part, send):
    rows = blocks[0].shape[0]
    columns = 3 * HEAD_DIM
    return call(
        project_kernel,
        "project",
        [
            shape(jnp.bfloat16, rows, columns),
            shape(jnp.float32, rows, 1),
            shape(jnp.bfloat16, send.shape[1], columns + HEAD_DIM),
        ],
        (order, *blocks, *gains, *weights, squares, own_part, got_part, send),
        scratch=[pltpu.VMEM((rows, columns), jnp.float32)],
    )


def attend_kernel(moved, receive, segments, back):
    place = one_hot(receive[...], moved.shape[0])
    rows = dot(place, moved[...], CONTRACT_FIRST).astype(jnp.bfloat16)
    queries, key_rows, value_rows, head_grad = (
        rows[:, index * HEAD_DIM : (index + 1) * HEAD_DIM] for index in range(4)
    )
    count = rows.shape[0]
    down = lax.broadcasted_iota(jnp.int32, (count, count), 0)
    across = lax.broadcasted_iota(jnp.int32, (count, count), 1)
    stays = segments[...]
    own_stay = jnp.sum(jnp.where(down == across, stays, 0), axis=1, keepdims=True)
    allowed = (own_stay == stays) & (across <= down)
    scores = jnp.where(allowed, dot(queries, key_rows, CONTRACT_LAST) * SCALING, -1e30)
    raised = jnp.exp(scores - jnp.max(scores, axis=-1, keepdims=True))
    softmax_out = raised / jnp.sum(raised, axis=-1, keepdims=True)
    low_weights = softmax_out.astype(jnp.bfloat16)
    attended = dot(low_weights, value_rows).astype(jnp.bfloat16)
    grad_value = dot(low_weights, head_grad, CONTRACT_FIRST).astype(jnp.bfloat16)
    grad_probs = dot(head_grad, value_rows, CONTRACT_LAST)
    inner = jnp.sum(softmax_out * grad_probs, axis=-1, keepdims=True)
    grad_scores = (softmax_out * (grad_probs - inner) * SCALING).astype(jnp.bfloat16)
    grad_query = dot(grad_scores, key_rows).astype(jnp.bfloat16)
    grad_key = dot(grad_scores, queries, CONTRACT_FIRST).astype(jnp.bfloat16)
    results = jnp.concatenate([grad_query, grad_key, grad_value, attended], axis=1)
    back[...] = dot(place, results).astype(jnp.bfloat16)


def attend(moved, receive, segments):
    out = shape(jnp.bfloat16, *moved.shape)
    return call(attend_kernel, "attend", out, (moved, receive, segments), first=VMEM)


def write_parts(value, out):
    out[...] = jnp.zeros_like(out)
    for place in range(3):
        low = value.astype(jnp.bfloat16)
        out[:, place : place + 1] = low
        value = value - low.astype(jnp.float32)


def read_parts(parts):
    return sum(parts[:, place : place + 1].astype(jnp.float32) for place in (2, 1, 0))


def bring_home_kernel(moved, send, home, grads, extras):
    chosen = one_hot(send[...], grads.shape[0])
    rows = dot(chosen, moved[...])
    split = 3 * HEAD_DIM
    grads[...] = rows[:, :split].astype(jnp.bfloat16)
    extras[:, :HEAD_DIM] = rows[:, split:].astype(jnp.bfloat16)
    product = rows[:, :split] * home[...].astype(jnp.float32)
    row_dot = jnp.sum(product, axis=-1, keepdims=True)
    write_parts(row_dot, extras.at[:, HEAD_DIM:])


def bring_home(moved, send, home):
    rows = home.shape[0]
    shapes = [shape(jnp.bfloat16, rows, 3 * HEAD_DIM), shape(jnp.bfloat16, rows, 2 * HEAD_DIM)]
    operands = (moved, send, home)
    return call(bring_home_kernel, "bring_home", shapes, operands, first=VMEM, flops=HOME_FLOPS)


def spread_kernel(first):
    def kernel(own, near, weights, near_weights, out):
        own_rows, near_rows = own[...], near[...]
        for start in range(0, out.shape[1], TILE):
            columns = slice(first + start, first + start + TILE)
            total = dot(own_rows, weights[:, columns]) + dot(near_rows, near_weights[:, columns])
            out[:, start : start + TILE] = total.astype(out.dtype)

    return kernel


def spread(name, first, span, dtype, own, near, weights, near_weights, flops=1000):
    return pl.pallas_call(
        spread_kernel(first),
        out_shape=shape(dtype, own.shape[0], span),
        in_specs=[VMEM] * 4,
        out_specs=VMEM,
        compiler_params=pltpu.CompilerParams(vmem_limit_bytes=VMEM_LIMIT),
        cost_estimate=pl.CostEstimate(flops=flops, bytes_accessed=1000, transcendentals=0),
        name=name,
    )(own, near, weights, near_weights)


def finish_out_kernel(inputs, own, near, far, last, here, there, out):
    width = inputs.shape[1]
    chip = jnp.concatenate([own[:, :HEAD_DIM], near[:, :HEAD_DIM]], axis=1)
    other = jnp.concatenate([far[:, :HEAD_DIM], last[:, :HEAD_DIM]], axis=1)
    for start in range(0, width, TILE):
        tile = slice(start, start + TILE)
        total = dot(chip, here[:, tile]) + dot(other, there[:, tile])
        out[:, tile] = (inputs[:, tile].astype(jnp.float32) + total).astype(jnp.bfloat16)


def finish_most_kernel(
    inputs, cotangent, gain, inverse, own, near, far, last, grad_own, *pieces
):
    *pieces, out, left, held, sem = pieces
    tiles = [
        piece.at[:, start : start + TILE]
        for piece in pieces
        for start in range(0, piece.shape[1], TILE)
    ]
    row_dot = sum(read_parts(extras[:, HEAD_DIM:]) for extras in (own, near, far, last))
    mean_dot = row_dot / (4 * inputs.shape[1])
    inverse_rms = inverse[...]
    most = held.shape[1]
    for start in range(0, inputs.shape[1], TILE):
        tile = slice(start, start + TILE)
        grad_normed = grad_own[:, tile]
        if start < most:
            grad_normed = grad_normed + tiles[start // TILE][...].astype(jnp.float32)
        grad_hat = grad_normed * gain[:, tile].astype(jnp.float32)
        scaled = inputs[:, tile].astype(jnp.float32) * inverse_rms
        change = inverse_rms * (grad_hat - scaled * mean_dot)
        result = cotangent[:, tile].astype(jnp.float32) + change
        if start < most:
            held[:, tile] = result.astype(jnp.bfloat16)
        else:
            left[:, start - most : start - most + TILE] = result
    copy = pltpu.make_async_copy(held, out.at[:, pl.ds(0, most)], sem)
    copy.start()
    copy.wait()


def finish_rest_kernel(gain, inverse, left, rest, before, out, held, sems):
    span = rest.shape[1]
    first = out.shape[1] - span
    half = span // 2
    copies = []
    for index, start in enumerate(range(0, span, half)):
        tile = slice(start, start + half)
        columns = slice(first + start, first + start + half)
        grad_hat = rest[:, tile].astype(jnp.float32) * gain[:, columns].astype(jnp.float32)
        held[:, tile] = (left[:, tile] + inverse[...] * grad_hat).astype(jnp.bfloat16)
        target = out.at[:, pl.ds(first + start, half)]
        copies.append(
            pltpu.make_async_copy(held.at[:, pl.ds(start, half)], target, sems.at[index])
        )
        copies[-1].start()
    for copy in copies:
        copy.wait()


def finish_grad(inputs, cotangent, gain, inverse, extras, grad_own, pieces):
    rows, width = inputs.shape
    *pieces, rest = pieces
    span = rest.shape[1]
    hbm = pl.BlockSpec(memory_space=pltpu.HBM)
    options = dict(
        compiler_params=pltpu.CompilerParams(vmem_limit_bytes=VMEM_LIMIT),
        cost_estimate=pl.CostEstimate(flops=1000, bytes_accessed=1000, transcendentals=0),
    )
    begun, left = pl.pallas_call(
        finish_most_kernel,
        out_shape=[shape(jnp.bfloat16, rows, width), shape(jnp.float32, rows, span)],
        in_specs=[VMEM] * (9 + len(pieces)),
        out_specs=[hbm, VMEM],
        scratch_shapes=[pltpu.VMEM((rows, width - span), jnp.bfloat16), pltpu.SemaphoreType.DMA],
        name="finish_most",
        **options,
    )(inputs, cotangent, gain, inverse, *extras, grad_own, *pieces)
    return pl.pallas_call(
        finish_rest_kernel,
        out_shape=shape(jnp.bfloat16, rows, width),
        in_specs=[VMEM] * 4 + [hbm],
        out_specs=hbm,
        scratch_shapes=[pltpu.VMEM((rows, span), jnp.bfloat16), pltpu.SemaphoreType.DMA((2,))],
        input_output_aliases={4: 0},
        name="finish_rest",
        **options,
    )(gain, inverse, left, rest, begun)


def move(bucket):
    return lax.all_to_all(bucket, "dp", split_axis=0, concat_axis=0, tiled=True)


def after(array, *others):
    return lax.optimization_barrier((array, *others))[0]


def on_device(
    inputs,
    cotangent,
    norm_gain,
    w_query,
    w_key,
    w_value,
    w_output,
    send_rows,
    receive_slots,
    owner_segments,
):
    rows, width = inputs.shape
    tensor = lax.axis_size("tensor")
    low = jnp.bfloat16
    order = lax.axis_index("tensor").astype(jnp.int32) ^ jnp.arange(4, dtype=jnp.int32)
    gain = norm_gain.reshape(1, width)

    x2 = swap(inputs, 2, tensor)
    c2 = swap(cotangent, 2, tensor)
    gain_chip = jnp.concatenate([gain, swap(gain, 1, tensor)], axis=0)
    gain_far = swap(gain_chip, 2, tensor)
    x1 = swap(inputs, 1, tensor)
    near_output = swap(w_output, 1, tensor)
    weights = (w_query, w_key, w_value)
    own_turned, near_turned, here, there, there_turned, *indices = prepare(
        order,
        *weights,
        w_output,
        near_output,
        send_rows,
        receive_slots.reshape(1, rows),
        owner_segments.reshape(1, rows),
        width,
    )
    send, receive, segments = indices
    squares, part, x1 = begin(inputs, x1, cotangent, here)

    x2, c2, gain_far, squares, part = lax.optimization_barrier((x2, c2, gain_far, squares, part))
    x3 = swap(x2, 1, tensor)
    near_part = add_grad(1, c2, there_turned, part)
    got_part = swap(near_part, 1, tensor)
    own_part = add_grad(0, c2, there_turned, after(part, near_part))
    squares = add_squares(x2, after(squares, near_part, own_part))
    home, inverse_rms, bucket = project(
        order,
        (inputs, x1, x2, x3),
        (gain_chip, gain_far),
        weights,
        squares,
        own_part,
        got_part,
        send,
    )
    near_turned = swap(after(near_turned, home), 1, tensor)
    there = swap(after(there, near_part), 2, tensor)
    back = attend(move(bucket), receive, segments)
    moved, there = lax.optimization_barrier((move(back), there))
    own, own_extras = bring_home(moved, send, home)

    near = swap(own, 1, tensor)
    far_extras = swap(own_extras, 2, tensor)
    quarter = width // 4
    turn, got = own, []
    for first, span in ((0, 2 * quarter), (2 * quarter, quarter), (3 * quarter, quarter)):
        flops = 4 * rows * span * width if first else 1000
        sides = (turn, near, own_turned, near_turned)
        part = spread("spread_far", width + first, span, low, *sides, flops=flops)
        got.append(swap(part, 2, tensor))
        turn = after(own, part, far_extras)
    grad_own = spread("spread_own", 0, width, jnp.float32, turn, near, own_turned, near_turned)
    extras = (own_extras, swap(own_extras, 1, tensor), far_extras, swap(far_extras, 1, tensor))
    layer_out = call(
        finish_out_kernel,
        "finish_out",
        shape(low, rows, width),
        (inputs, *extras, here, there),
        first=VMEM,
    )
    got[1] = after(got[1], layer_out)
    input_grad = finish_grad(inputs, cotangent, gain, inverse_rms, extras, grad_own, got)
    return (layer_out, input_grad)


def solution(mesh):
    return jax.shard_map(
        on_device,
        mesh=mesh,
        in_specs=(
            P("dp", "tensor"),
            P("dp", "tensor"),
            P("tensor"),
            P(None, "tensor"),
            P(None, "tensor"),
            P(None, "tensor"),
            P("tensor", None),
            P("dp", None),
            P("dp"),
            P("dp"),
        ),
        out_specs=(P("dp", "tensor"), P("dp", "tensor")),
        check_vma=False,
    )
```

```python
import math

import jax
import jax.numpy as jnp
from jax import lax
from jax.experimental import pallas as pl
from jax.experimental.pallas import tpu as pltpu
from jax.sharding import PartitionSpec as P

HEAD_DIM = 128
EPSILON = 1e-05
SCALING = 1.0 / math.sqrt(HEAD_DIM)
CONTRACT_LAST = (((1,), (1,)), ((), ()))
CONTRACT_FIRST = (((0,), (0,)), ((), ()))
VMEM_LIMIT = 3 * 1024 * 1024
VMEM = pl.BlockSpec(memory_space=pltpu.VMEM)
SMEM = pl.BlockSpec(memory_space=pltpu.SMEM)
TILE = 512


def dot(left, right, dims=(((1,), (0,)), ((), ()))):
    return lax.dot_general(left, right, dims, preferred_element_type=jnp.float32)


def call(kernel, name, out_shape, operands, scratch=(), first=SMEM, rest=VMEM):
    single = not isinstance(out_shape, (list, tuple))
    shapes = [out_shape] if single else list(out_shape)
    results = pl.pallas_call(
        kernel,
        out_shape=shapes,
        in_specs=[first] + [rest] * (len(operands) - 1),
        out_specs=[VMEM] * len(shapes),
        scratch_shapes=list(scratch),
        compiler_params=pltpu.CompilerParams(vmem_limit_bytes=VMEM_LIMIT),
        cost_estimate=pl.CostEstimate(flops=1000, bytes_accessed=1000, transcendentals=0),
        name=name,
    )(*operands)
    return results[0] if single else results


def shape(dtype, *sizes):
    return jax.ShapeDtypeStruct(sizes, dtype)


def swap(array, mask, count):
    return lax.ppermute(array, "tensor", [(i, i ^ mask) for i in range(count)])


def block_start(order, slot, width):
    return pl.multiple_of(order[slot] * width, width)


def one_hot(places, rows):
    row = lax.broadcasted_iota(jnp.int32, (rows, places.shape[1]), 0)
    return jnp.where(places == row, 1.0, 0.0).astype(jnp.bfloat16)


def slot_mask(receive, stays, slots):
    place = one_hot(receive, slots).astype(jnp.float32)
    down = lax.broadcasted_iota(jnp.int32, (slots, slots), 0)
    across = lax.broadcasted_iota(jnp.int32, (slots, slots), 1)
    position = lax.broadcasted_iota(jnp.int32, receive.shape, 1)
    both = []
    for values in (stays, position):
        column = jnp.sum(place * values.astype(jnp.float32), axis=1, keepdims=True)
        both.append((column, jnp.sum(jnp.where(down == across, column, 0.0), axis=0, keepdims=True)))
    (stay_down, stay_across), (place_down, place_across) = both
    allowed = (stay_down == stay_across) & (place_across <= place_down)
    return jnp.where(allowed, 1.0, 0.0)


def prepare_kernel(
    order,
    w_query,
    w_key,
    w_value,
    w_output,
    near_output,
    send,
    receive,
    segments,
    own_turned,
    near_turned,
    here,
    there,
    there_turned,
    send_out,
    receive_out,
    segments_out,
    mask_out,
):
    heads, width = w_output.shape[0], here.shape[1]
    mask_out[...] = slot_mask(receive[...], segments[...], mask_out.shape[0])
    for slot, out, turned in ((0, here, None), (2, there, there_turned)):
        columns = pl.ds(block_start(order, slot, width), width)
        for part, weight in enumerate((w_output, near_output)):
            rows = slice(part * heads, (part + 1) * heads)
            block = weight[:, columns]
            out[rows, :] = block
            if turned is not None:
                turned[:, rows] = block.T
    for source, target in ((send, send_out), (receive, receive_out), (segments, segments_out)):
        target[...] = source[...]
    for out, slots in ((own_turned, (0, 2)), (near_turned, (1, 3))):
        for part, slot in enumerate(slots):
            first = block_start(order, slot, width)
            for start in range(0, width, TILE):
                columns = slice(part * width + start, part * width + start + TILE)
                for place, weight in enumerate((w_query, w_key, w_value)):
                    rows = slice(place * HEAD_DIM, (place + 1) * HEAD_DIM)
                    out[rows, columns] = weight[pl.ds(first + start, TILE), :].T


def prepare(order, w_query, w_key, w_value, w_output, near_output, send, receive, segments, width):
    heads = w_query.shape[1]
    low = jnp.bfloat16
    return call(
        prepare_kernel,
        "prepare",
        [
            *[shape(low, 3 * heads, 2 * width)] * 2,
            *[shape(low, 2 * heads, width)] * 2,
            shape(low, width, 2 * heads),
            shape(jnp.int32, *send.shape),
            shape(jnp.int32, *receive.shape),
            shape(jnp.int32, *segments.shape),
            shape(jnp.float32, send.shape[1], send.shape[1]),
        ],
        (order, w_query, w_key, w_value, w_output, near_output, send, receive, segments),
    )


def sum_squares(block):
    wide = block[...].astype(jnp.float32)
    return jnp.sum(wide * wide, axis=-1, keepdims=True)


def begin_kernel(x0, x1, c0, here, squares, part):
    squares[...] = sum_squares(x0) + sum_squares(x1)
    part[...] = dot(c0[...], here[...], CONTRACT_LAST)


def begin(x0, x1, c0, here):
    rows, columns = x0.shape[0], here.shape[0]
    shapes = [shape(jnp.float32, rows, 1), shape(jnp.float32, rows, columns)]
    return call(begin_kernel, "begin", shapes, (x0, x1, c0, here), first=VMEM)


def add_grad_kernel(half):
    def kernel(c2, there_turned, part, total):
        heads = total.shape[1]
        columns = slice(half * heads, (half + 1) * heads)
        total[...] = part[:, columns] + dot(c2[...], there_turned[:, columns])

    return kernel


def add_grad(half, c2, there_turned, part):
    out = shape(jnp.float32, part.shape[0], part.shape[1] // 2)
    return call(add_grad_kernel(half), "add_grad", out, (c2, there_turned, part), first=VMEM)


def add_squares_kernel(x2, squares_in, squares):
    squares[...] = squares_in[...] + sum_squares(x2)


def add_squares(x2, squares):
    out = shape(jnp.float32, *squares.shape)
    return call(add_squares_kernel, "add_squares", out, (x2, squares), first=VMEM)


def project_kernel(
    order,
    x0,
    x1,
    x2,
    x3,
    gain_chip,
    gain_far,
    w_query,
    w_key,
    w_value,
    squares,
    own_part,
    got_part,
    send,
    home,
    inverse,
    bucket,
    total,
):
    blocks = (x0, x1, x2, x3)
    width = x0.shape[1]
    mean = (squares[...] + sum_squares(x3)) / (width * len(blocks))
    inverse_rms = lax.rsqrt(mean + EPSILON)
    inverse[...] = inverse_rms
    head_grad = (own_part[...] + got_part[...]).astype(jnp.bfloat16)
    for index, block in enumerate(blocks):
        gain = (gain_chip, gain_far)[index // 2][index % 2 : index % 2 + 1, :]
        scaled = block[...].astype(jnp.float32) * inverse_rms
        normed = (scaled * gain.astype(jnp.float32)).astype(jnp.bfloat16)
        here = pl.ds(block_start(order, index, width), width)
        weights = jnp.concatenate([w_query[here, :], w_key[here, :], w_value[here, :]], axis=1)
        product = dot(normed, weights)
        total[...] = total[...] + product if index else product
    rounded = total[...].astype(jnp.bfloat16)
    home[...] = rounded
    chosen = one_hot(send[...], rounded.shape[0])
    split = rounded.shape[1]
    bucket[:, :split] = dot(chosen, rounded, CONTRACT_FIRST).astype(jnp.bfloat16)
    bucket[:, split:] = dot(chosen, head_grad, CONTRACT_FIRST).astype(jnp.bfloat16)


def project(order, blocks, gains, weights, squares, own_part, got_part, send):
    rows = blocks[0].shape[0]
    columns = 3 * HEAD_DIM
    return call(
        project_kernel,
        "project",
        [
            shape(jnp.bfloat16, rows, columns),
            shape(jnp.float32, rows, 1),
            shape(jnp.bfloat16, send.shape[1], columns + HEAD_DIM),
        ],
        (order, *blocks, *gains, *weights, squares, own_part, got_part, send),
        scratch=[pltpu.VMEM((rows, columns), jnp.float32)],
    )


def attend_kernel(moved, mask, back):
    back[...] = attention(moved[...], mask[...] > 0.5)


def attend_sparse_kernel(moved, receive, segments, back):
    place = one_hot(receive[...], moved.shape[0])
    rows = dot(place, moved[...], CONTRACT_FIRST).astype(jnp.bfloat16)
    count = rows.shape[0]
    down = lax.broadcasted_iota(jnp.int32, (count, count), 0)
    across = lax.broadcasted_iota(jnp.int32, (count, count), 1)
    stays = segments[...]
    own_stay = jnp.sum(jnp.where(down == across, stays, 0), axis=1, keepdims=True)
    results = attention(rows, (own_stay == stays) & (across <= down))
    back[...] = dot(place, results).astype(jnp.bfloat16)


def attention(rows, allowed):
    queries, key_rows, value_rows, head_grad = (
        rows[:, index * HEAD_DIM : (index + 1) * HEAD_DIM] for index in range(4)
    )
    scores = jnp.where(allowed, dot(queries, key_rows, CONTRACT_LAST) * SCALING, -1e30)
    raised = jnp.exp(scores - jnp.max(scores, axis=-1, keepdims=True))
    softmax_out = raised / jnp.sum(raised, axis=-1, keepdims=True)
    low_weights = softmax_out.astype(jnp.bfloat16)
    attended = dot(low_weights, value_rows).astype(jnp.bfloat16)
    grad_value = dot(low_weights, head_grad, CONTRACT_FIRST).astype(jnp.bfloat16)
    grad_probs = dot(head_grad, value_rows, CONTRACT_LAST)
    inner = jnp.sum(softmax_out * grad_probs, axis=-1, keepdims=True)
    grad_scores = (softmax_out * (grad_probs - inner) * SCALING).astype(jnp.bfloat16)
    grad_query = dot(grad_scores, key_rows).astype(jnp.bfloat16)
    grad_key = dot(grad_scores, queries, CONTRACT_FIRST).astype(jnp.bfloat16)
    return jnp.concatenate([grad_query, grad_key, grad_value, attended], axis=1)


def attend(moved, receive, segments, mask):
    out = shape(jnp.bfloat16, *moved.shape)
    if moved.shape[0] == receive.shape[1]:
        return call(attend_kernel, "attend", out, (moved, mask), first=VMEM)
    return call(attend_sparse_kernel, "attend", out, (moved, receive, segments), first=VMEM)


def write_parts(value, out):
    out[...] = jnp.zeros_like(out)
    for place in range(3):
        low = value.astype(jnp.bfloat16)
        out[:, place : place + 1] = low
        value = value - low.astype(jnp.float32)


def read_parts(parts):
    return sum(parts[:, place : place + 1].astype(jnp.float32) for place in (2, 1, 0))


def bring_home_kernel(moved, send, home, grads, extras):
    chosen = one_hot(send[...], grads.shape[0])
    rows = dot(chosen, moved[...])
    split = 3 * HEAD_DIM
    grads[...] = rows[:, :split].astype(jnp.bfloat16)
    extras[:, :HEAD_DIM] = rows[:, split:].astype(jnp.bfloat16)
    product = rows[:, :split] * home[...].astype(jnp.float32)
    row_dot = jnp.sum(product, axis=-1, keepdims=True)
    write_parts(row_dot, extras.at[:, HEAD_DIM:])


def bring_home(moved, send, home):
    rows = home.shape[0]
    shapes = [shape(jnp.bfloat16, rows, 3 * HEAD_DIM), shape(jnp.bfloat16, rows, 2 * HEAD_DIM)]
    return call(bring_home_kernel, "bring_home", shapes, (moved, send, home), first=VMEM)


def spread_kernel(first):
    def kernel(own, near, weights, near_weights, out):
        own_rows, near_rows = own[...], near[...]
        for start in range(0, out.shape[1], TILE):
            columns = slice(first + start, first + start + TILE)
            total = dot(own_rows, weights[:, columns]) + dot(near_rows, near_weights[:, columns])
            out[:, start : start + TILE] = total.astype(out.dtype)

    return kernel


def spread(name, first, span, dtype, own, near, weights, near_weights, flops=1000):
    return pl.pallas_call(
        spread_kernel(first),
        out_shape=shape(dtype, own.shape[0], span),
        in_specs=[VMEM] * 4,
        out_specs=VMEM,
        compiler_params=pltpu.CompilerParams(vmem_limit_bytes=VMEM_LIMIT),
        cost_estimate=pl.CostEstimate(flops=flops, bytes_accessed=1000, transcendentals=0),
        name=name,
    )(own, near, weights, near_weights)


def finish_out_kernel(inputs, own, near, far, last, here, there, out):
    width = inputs.shape[1]
    chip = jnp.concatenate([own[:, :HEAD_DIM], near[:, :HEAD_DIM]], axis=1)
    other = jnp.concatenate([far[:, :HEAD_DIM], last[:, :HEAD_DIM]], axis=1)
    for start in range(0, width, TILE):
        tile = slice(start, start + TILE)
        total = dot(chip, here[:, tile]) + dot(other, there[:, tile])
        out[:, tile] = (inputs[:, tile].astype(jnp.float32) + total).astype(jnp.bfloat16)


def finish_most_kernel(
    inputs, cotangent, gain, inverse, own, near, far, last, grad_own, *pieces
):
    *pieces, out, left, held, sem = pieces
    tiles = [
        piece.at[:, start : start + TILE]
        for piece in pieces
        for start in range(0, piece.shape[1], TILE)
    ]
    row_dot = sum(read_parts(extras[:, HEAD_DIM:]) for extras in (own, near, far, last))
    mean_dot = row_dot / (4 * inputs.shape[1])
    inverse_rms = inverse[...]
    most = held.shape[1]
    for start in range(0, inputs.shape[1], TILE):
        tile = slice(start, start + TILE)
        grad_normed = grad_own[:, tile]
        if start < most:
            grad_normed = grad_normed + tiles[start // TILE][...].astype(jnp.float32)
        grad_hat = grad_normed * gain[:, tile].astype(jnp.float32)
        scaled = inputs[:, tile].astype(jnp.float32) * inverse_rms
        change = inverse_rms * (grad_hat - scaled * mean_dot)
        result = cotangent[:, tile].astype(jnp.float32) + change
        if start < most:
            held[:, tile] = result.astype(jnp.bfloat16)
        else:
            left[:, start - most : start - most + TILE] = result
    copy = pltpu.make_async_copy(held, out.at[:, pl.ds(0, most)], sem)
    copy.start()
    copy.wait()


def finish_rest_kernel(gain, inverse, left, rest, before, out, held, sems):
    span = rest.shape[1]
    first = out.shape[1] - span
    half = span // 2
    copies = []
    for index, start in enumerate(range(0, span, half)):
        tile = slice(start, start + half)
        columns = slice(first + start, first + start + half)
        grad_hat = rest[:, tile].astype(jnp.float32) * gain[:, columns].astype(jnp.float32)
        held[:, tile] = (left[:, tile] + inverse[...] * grad_hat).astype(jnp.bfloat16)
        target = out.at[:, pl.ds(first + start, half)]
        copies.append(
            pltpu.make_async_copy(held.at[:, pl.ds(start, half)], target, sems.at[index])
        )
        copies[-1].start()
    for copy in copies:
        copy.wait()


def finish_grad(inputs, cotangent, gain, inverse, extras, grad_own, pieces):
    rows, width = inputs.shape
    *pieces, rest = pieces
    span = rest.shape[1]
    hbm = pl.BlockSpec(memory_space=pltpu.HBM)
    options = dict(
        compiler_params=pltpu.CompilerParams(vmem_limit_bytes=VMEM_LIMIT),
        cost_estimate=pl.CostEstimate(flops=1000, bytes_accessed=1000, transcendentals=0),
    )
    begun, left = pl.pallas_call(
        finish_most_kernel,
        out_shape=[shape(jnp.bfloat16, rows, width), shape(jnp.float32, rows, span)],
        in_specs=[VMEM] * (9 + len(pieces)),
        out_specs=[hbm, VMEM],
        scratch_shapes=[pltpu.VMEM((rows, width - span), jnp.bfloat16), pltpu.SemaphoreType.DMA],
        name="finish_most",
        **options,
    )(inputs, cotangent, gain, inverse, *extras, grad_own, *pieces)
    return pl.pallas_call(
        finish_rest_kernel,
        out_shape=shape(jnp.bfloat16, rows, width),
        in_specs=[VMEM] * 4 + [hbm],
        out_specs=hbm,
        scratch_shapes=[pltpu.VMEM((rows, span), jnp.bfloat16), pltpu.SemaphoreType.DMA((2,))],
        input_output_aliases={4: 0},
        name="finish_rest",
        **options,
    )(gain, inverse, left, rest, begun)


def move(bucket):
    return lax.all_to_all(bucket, "dp", split_axis=0, concat_axis=0, tiled=True)


def after(array, *others):
    return lax.optimization_barrier((array, *others))[0]


def on_device(
    inputs,
    cotangent,
    norm_gain,
    w_query,
    w_key,
    w_value,
    w_output,
    send_rows,
    receive_slots,
    owner_segments,
):
    rows, width = inputs.shape
    tensor = lax.axis_size("tensor")
    low = jnp.bfloat16
    order = lax.axis_index("tensor").astype(jnp.int32) ^ jnp.arange(4, dtype=jnp.int32)
    gain = norm_gain.reshape(1, width)

    x2 = swap(inputs, 2, tensor)
    c2 = swap(cotangent, 2, tensor)
    gain_chip = jnp.concatenate([gain, swap(gain, 1, tensor)], axis=0)
    gain_far = swap(gain_chip, 2, tensor)
    x1 = swap(inputs, 1, tensor)
    near_output = swap(w_output, 1, tensor)
    weights = (w_query, w_key, w_value)
    own_turned, near_turned, here, there, there_turned, *indices = prepare(
        order,
        *weights,
        w_output,
        near_output,
        send_rows,
        receive_slots.reshape(1, rows),
        owner_segments.reshape(1, rows),
        width,
    )
    send, receive, segments, mask = indices
    squares, part = begin(inputs, x1, cotangent, here)

    x2, c2, gain_far, squares, part = lax.optimization_barrier((x2, c2, gain_far, squares, part))
    x3 = swap(x2, 1, tensor)
    near_part = add_grad(1, c2, there_turned, part)
    got_part = swap(near_part, 1, tensor)
    own_part = add_grad(0, c2, there_turned, after(part, near_part))
    squares = add_squares(x2, squares)
    home, inverse_rms, bucket = project(
        order,
        (inputs, x1, x2, x3),
        (gain_chip, gain_far),
        weights,
        squares,
        own_part,
        got_part,
        send,
    )
    near_turned = swap(after(near_turned, home), 1, tensor)
    there = swap(after(there, home), 2, tensor)
    back = attend(move(bucket), receive, segments, mask)
    own, own_extras = bring_home(move(back), send, home)

    near = swap(own, 1, tensor)
    far_extras = swap(own_extras, 2, tensor)
    quarter = width // 4
    turn, got = own, []
    for first, span in ((0, 2 * quarter), (2 * quarter, quarter), (3 * quarter, quarter)):
        flops = 4 * rows * span * width if first else 1000
        sides = (turn, near, own_turned, near_turned)
        part = spread("spread_far", width + first, span, low, *sides, flops=flops)
        got.append(swap(part, 2, tensor))
        turn = after(own, part, far_extras)
    grad_own = spread("spread_own", 0, width, jnp.float32, turn, near, own_turned, near_turned)
    extras = (own_extras, swap(own_extras, 1, tensor), far_extras, swap(far_extras, 1, tensor))
    layer_out = call(
        finish_out_kernel,
        "finish_out",
        shape(low, rows, width),
        (inputs, *extras, here, there),
        first=VMEM,
    )
    got[1] = after(got[1], layer_out)
    input_grad = finish_grad(inputs, cotangent, gain, inverse_rms, extras, grad_own, got)
    return (layer_out, input_grad)


def solution(mesh):
    return jax.shard_map(
        on_device,
        mesh=mesh,
        in_specs=(
            P("dp", "tensor"),
            P("dp", "tensor"),
            P("tensor"),
            P(None, "tensor"),
            P(None, "tensor"),
            P(None, "tensor"),
            P("tensor", None),
            P("dp", None),
            P("dp"),
            P("dp"),
        ),
        out_specs=(P("dp", "tensor"), P("dp", "tensor")),
        check_vma=False,
    )
```

```python
import math

import jax
import jax.numpy as jnp
from jax import lax
from jax.experimental import pallas as pl
from jax.experimental.pallas import tpu as pltpu
from jax.sharding import PartitionSpec as P

HEAD_DIM = 128
EPSILON = 1e-05
SCALING = 1.0 / math.sqrt(HEAD_DIM)
CONTRACT_LAST = (((1,), (1,)), ((), ()))
CONTRACT_FIRST = (((0,), (0,)), ((), ()))
VMEM_LIMIT = 3 * 1024 * 1024
VMEM = pl.BlockSpec(memory_space=pltpu.VMEM)
SMEM = pl.BlockSpec(memory_space=pltpu.SMEM)
TILE = 512
SQUARES_FLOPS = 4000000000
HOME_FLOPS = 24000000000


def dot(left, right, dims=(((1,), (0,)), ((), ()))):
    return lax.dot_general(left, right, dims, preferred_element_type=jnp.float32)


def call(kernel, name, out_shape, operands, scratch=(), first=SMEM, rest=VMEM, flops=1000):
    single = not isinstance(out_shape, (list, tuple))
    shapes = [out_shape] if single else list(out_shape)
    results = pl.pallas_call(
        kernel,
        out_shape=shapes,
        in_specs=[first] + [rest] * (len(operands) - 1),
        out_specs=[VMEM] * len(shapes),
        scratch_shapes=list(scratch),
        compiler_params=pltpu.CompilerParams(vmem_limit_bytes=VMEM_LIMIT),
        cost_estimate=pl.CostEstimate(flops=flops, bytes_accessed=1000, transcendentals=0),
        name=name,
    )(*operands)
    return results[0] if single else results


def shape(dtype, *sizes):
    return jax.ShapeDtypeStruct(sizes, dtype)


def swap(array, mask, count):
    return lax.ppermute(array, "tensor", [(i, i ^ mask) for i in range(count)])


def block_start(order, slot, width):
    return pl.multiple_of(order[slot] * width, width)


def one_hot(places, rows):
    row = lax.broadcasted_iota(jnp.int32, (rows, places.shape[1]), 0)
    return jnp.where(places == row, 1.0, 0.0).astype(jnp.bfloat16)


def slot_mask(receive, stays, slots):
    place = one_hot(receive, slots).astype(jnp.float32)
    down = lax.broadcasted_iota(jnp.int32, (slots, slots), 0)
    across = lax.broadcasted_iota(jnp.int32, (slots, slots), 1)
    position = lax.broadcasted_iota(jnp.int32, receive.shape, 1)
    both = []
    for values in (stays, position):
        column = jnp.sum(place * values.astype(jnp.float32), axis=1, keepdims=True)
        both.append((column, jnp.sum(jnp.where(down == across, column, 0.0), axis=0, keepdims=True)))
    (stay_down, stay_across), (place_down, place_across) = both
    allowed = (stay_down == stay_across) & (place_across <= place_down)
    return jnp.where(allowed, 1.0, 0.0)


def prepare_kernel(
    order,
    w_query,
    w_key,
    w_value,
    w_output,
    near_output,
    send,
    receive,
    segments,
    own_turned,
    near_turned,
    here,
    there,
    there_turned,
    send_out,
    receive_out,
    segments_out,
    mask_out,
):
    heads, width = w_output.shape[0], here.shape[1]
    mask_out[...] = slot_mask(receive[...], segments[...], mask_out.shape[0])
    for slot, out, turned in ((0, here, None), (2, there, there_turned)):
        columns = pl.ds(block_start(order, slot, width), width)
        for part, weight in enumerate((w_output, near_output)):
            rows = slice(part * heads, (part + 1) * heads)
            block = weight[:, columns]
            out[rows, :] = block
            if turned is not None:
                turned[:, rows] = block.T
    for source, target in ((send, send_out), (receive, receive_out), (segments, segments_out)):
        target[...] = source[...]
    for out, slots in ((own_turned, (0, 2)), (near_turned, (1, 3))):
        for part, slot in enumerate(slots):
            first = block_start(order, slot, width)
            for start in range(0, width, TILE):
                columns = slice(part * width + start, part * width + start + TILE)
                for place, weight in enumerate((w_query, w_key, w_value)):
                    rows = slice(place * HEAD_DIM, (place + 1) * HEAD_DIM)
                    out[rows, columns] = weight[pl.ds(first + start, TILE), :].T


def prepare(order, w_query, w_key, w_value, w_output, near_output, send, receive, segments, width):
    heads = w_query.shape[1]
    low = jnp.bfloat16
    return call(
        prepare_kernel,
        "prepare",
        [
            *[shape(low, 3 * heads, 2 * width)] * 2,
            *[shape(low, 2 * heads, width)] * 2,
            shape(low, width, 2 * heads),
            shape(jnp.int32, *send.shape),
            shape(jnp.int32, *receive.shape),
            shape(jnp.int32, *segments.shape),
            shape(jnp.float32, send.shape[1], send.shape[1]),
        ],
        (order, w_query, w_key, w_value, w_output, near_output, send, receive, segments),
    )


def sum_squares(block):
    wide = block[...].astype(jnp.float32)
    return jnp.sum(wide * wide, axis=-1, keepdims=True)


def begin_kernel(x0, x1, c0, here, squares, part, x1_out):
    x1_out[...] = x1[...]
    squares[...] = sum_squares(x0) + sum_squares(x1)
    part[...] = dot(c0[...], here[...], CONTRACT_LAST)


def begin(x0, x1, c0, here):
    rows, columns = x0.shape[0], here.shape[0]
    shapes = [
        shape(jnp.float32, rows, 1),
        shape(jnp.float32, rows, columns),
        shape(x1.dtype, *x1.shape),
    ]
    return call(begin_kernel, "begin", shapes, (x0, x1, c0, here), first=VMEM)


def add_grad_kernel(half):
    def kernel(c2, there_turned, part, total):
        heads = total.shape[1]
        columns = slice(half * heads, (half + 1) * heads)
        total[...] = part[:, columns] + dot(c2[...], there_turned[:, columns])

    return kernel


def add_grad(half, c2, there_turned, part):
    out = shape(jnp.float32, part.shape[0], part.shape[1] // 2)
    return call(add_grad_kernel(half), "add_grad", out, (c2, there_turned, part), first=VMEM)


def add_squares_kernel(x2, squares_in, squares):
    squares[...] = squares_in[...] + sum_squares(x2)


def add_squares(x2, squares):
    out = shape(jnp.float32, *squares.shape)
    operands = (x2, squares)
    return call(
        add_squares_kernel, "add_squares", out, operands, first=VMEM, flops=SQUARES_FLOPS
    )


def project_kernel(
    order,
    x0,
    x1,
    x2,
    x3,
    gain_chip,
    gain_far,
    w_query,
    w_key,
    w_value,
    squares,
    own_part,
    got_part,
    send,
    home,
    inverse,
    bucket,
    total,
):
    blocks = (x0, x1, x2, x3)
    width = x0.shape[1]
    mean = (squares[...] + sum_squares(x3)) / (width * len(blocks))
    inverse_rms = lax.rsqrt(mean + EPSILON)
    inverse[...] = inverse_rms
    head_grad = (own_part[...] + got_part[...]).astype(jnp.bfloat16)
    for index, block in enumerate(blocks):
        gain = (gain_chip, gain_far)[index // 2][index % 2 : index % 2 + 1, :]
        scaled = block[...].astype(jnp.float32) * inverse_rms
        normed = (scaled * gain.astype(jnp.float32)).astype(jnp.bfloat16)
        here = pl.ds(block_start(order, index, width), width)
        weights = jnp.concatenate([w_query[here, :], w_key[here, :], w_value[here, :]], axis=1)
        product = dot(normed, weights)
        total[...] = total[...] + product if index else product
    rounded = total[...].astype(jnp.bfloat16)
    home[...] = rounded
    chosen = one_hot(send[...], rounded.shape[0])
    split = rounded.shape[1]
    bucket[:, :split] = dot(chosen, rounded, CONTRACT_FIRST).astype(jnp.bfloat16)
    bucket[:, split:] = dot(chosen, head_grad, CONTRACT_FIRST).astype(jnp.bfloat16)


def project(order, blocks, gains, weights, squares, own_part, got_part, send):
    rows = blocks[0].shape[0]
    columns = 3 * HEAD_DIM
    return call(
        project_kernel,
        "project",
        [
            shape(jnp.bfloat16, rows, columns),
            shape(jnp.float32, rows, 1),
            shape(jnp.bfloat16, send.shape[1], columns + HEAD_DIM),
        ],
        (order, *blocks, *gains, *weights, squares, own_part, got_part, send),
        scratch=[pltpu.VMEM((rows, columns), jnp.float32)],
    )


def attend_kernel(moved, mask, back):
    back[...] = attention(moved[...], mask[...] > 0.5)


def attend_sparse_kernel(moved, receive, segments, back):
    place = one_hot(receive[...], moved.shape[0])
    rows = dot(place, moved[...], CONTRACT_FIRST).astype(jnp.bfloat16)
    count = rows.shape[0]
    down = lax.broadcasted_iota(jnp.int32, (count, count), 0)
    across = lax.broadcasted_iota(jnp.int32, (count, count), 1)
    stays = segments[...]
    own_stay = jnp.sum(jnp.where(down == across, stays, 0), axis=1, keepdims=True)
    results = attention(rows, (own_stay == stays) & (across <= down))
    back[...] = dot(place, results).astype(jnp.bfloat16)


def attention(rows, allowed):
    queries, key_rows, value_rows, head_grad = (
        rows[:, index * HEAD_DIM : (index + 1) * HEAD_DIM] for index in range(4)
    )
    scores = jnp.where(allowed, dot(queries, key_rows, CONTRACT_LAST) * SCALING, -1e30)
    raised = jnp.exp(scores - jnp.max(scores, axis=-1, keepdims=True))
    softmax_out = raised / jnp.sum(raised, axis=-1, keepdims=True)
    low_weights = softmax_out.astype(jnp.bfloat16)
    attended = dot(low_weights, value_rows).astype(jnp.bfloat16)
    grad_value = dot(low_weights, head_grad, CONTRACT_FIRST).astype(jnp.bfloat16)
    grad_probs = dot(head_grad, value_rows, CONTRACT_LAST)
    inner = jnp.sum(softmax_out * grad_probs, axis=-1, keepdims=True)
    grad_scores = (softmax_out * (grad_probs - inner) * SCALING).astype(jnp.bfloat16)
    grad_query = dot(grad_scores, key_rows).astype(jnp.bfloat16)
    grad_key = dot(grad_scores, queries, CONTRACT_FIRST).astype(jnp.bfloat16)
    return jnp.concatenate([grad_query, grad_key, grad_value, attended], axis=1)


def attend(moved, receive, segments, mask):
    out = shape(jnp.bfloat16, *moved.shape)
    if moved.shape[0] == receive.shape[1]:
        return call(attend_kernel, "attend", out, (moved, mask), first=VMEM)
    return call(attend_sparse_kernel, "attend", out, (moved, receive, segments), first=VMEM)


def write_parts(value, out):
    out[...] = jnp.zeros_like(out)
    for place in range(3):
        low = value.astype(jnp.bfloat16)
        out[:, place : place + 1] = low
        value = value - low.astype(jnp.float32)


def read_parts(parts):
    return sum(parts[:, place : place + 1].astype(jnp.float32) for place in (2, 1, 0))


def bring_home_kernel(moved, send, home, grads, extras):
    chosen = one_hot(send[...], grads.shape[0])
    rows = dot(chosen, moved[...])
    split = 3 * HEAD_DIM
    grads[...] = rows[:, :split].astype(jnp.bfloat16)
    extras[:, :HEAD_DIM] = rows[:, split:].astype(jnp.bfloat16)
    product = rows[:, :split] * home[...].astype(jnp.float32)
    row_dot = jnp.sum(product, axis=-1, keepdims=True)
    write_parts(row_dot, extras.at[:, HEAD_DIM:])


def bring_home(moved, send, home):
    rows = home.shape[0]
    shapes = [shape(jnp.bfloat16, rows, 3 * HEAD_DIM), shape(jnp.bfloat16, rows, 2 * HEAD_DIM)]
    operands = (moved, send, home)
    return call(bring_home_kernel, "bring_home", shapes, operands, first=VMEM, flops=HOME_FLOPS)


def spread_kernel(first):
    def kernel(own, near, weights, near_weights, out):
        own_rows, near_rows = own[...], near[...]
        for start in range(0, out.shape[1], TILE):
            columns = slice(first + start, first + start + TILE)
            total = dot(own_rows, weights[:, columns]) + dot(near_rows, near_weights[:, columns])
            out[:, start : start + TILE] = total.astype(out.dtype)

    return kernel


def spread(name, first, span, dtype, own, near, weights, near_weights, flops=1000):
    return pl.pallas_call(
        spread_kernel(first),
        out_shape=shape(dtype, own.shape[0], span),
        in_specs=[VMEM] * 4,
        out_specs=VMEM,
        compiler_params=pltpu.CompilerParams(vmem_limit_bytes=VMEM_LIMIT),
        cost_estimate=pl.CostEstimate(flops=flops, bytes_accessed=1000, transcendentals=0),
        name=name,
    )(own, near, weights, near_weights)


def finish_out_kernel(inputs, own, near, far, last, here, there, out):
    width = inputs.shape[1]
    chip = jnp.concatenate([own[:, :HEAD_DIM], near[:, :HEAD_DIM]], axis=1)
    other = jnp.concatenate([far[:, :HEAD_DIM], last[:, :HEAD_DIM]], axis=1)
    for start in range(0, width, TILE):
        tile = slice(start, start + TILE)
        total = dot(chip, here[:, tile]) + dot(other, there[:, tile])
        out[:, tile] = (inputs[:, tile].astype(jnp.float32) + total).astype(jnp.bfloat16)


def finish_most_kernel(
    inputs, cotangent, gain, inverse, own, near, far, last, grad_own, *pieces
):
    *pieces, out, left, held, sem = pieces
    tiles = [
        piece.at[:, start : start + TILE]
        for piece in pieces
        for start in range(0, piece.shape[1], TILE)
    ]
    row_dot = sum(read_parts(extras[:, HEAD_DIM:]) for extras in (own, near, far, last))
    mean_dot = row_dot / (4 * inputs.shape[1])
    inverse_rms = inverse[...]
    most = held.shape[1]
    for start in range(0, inputs.shape[1], TILE):
        tile = slice(start, start + TILE)
        grad_normed = grad_own[:, tile]
        if start < most:
            grad_normed = grad_normed + tiles[start // TILE][...].astype(jnp.float32)
        grad_hat = grad_normed * gain[:, tile].astype(jnp.float32)
        scaled = inputs[:, tile].astype(jnp.float32) * inverse_rms
        change = inverse_rms * (grad_hat - scaled * mean_dot)
        result = cotangent[:, tile].astype(jnp.float32) + change
        if start < most:
            held[:, tile] = result.astype(jnp.bfloat16)
        else:
            left[:, start - most : start - most + TILE] = result
    copy = pltpu.make_async_copy(held, out.at[:, pl.ds(0, most)], sem)
    copy.start()
    copy.wait()


def finish_rest_kernel(gain, inverse, left, rest, before, out, held, sems):
    span = rest.shape[1]
    first = out.shape[1] - span
    half = span // 2
    copies = []
    for index, start in enumerate(range(0, span, half)):
        tile = slice(start, start + half)
        columns = slice(first + start, first + start + half)
        grad_hat = rest[:, tile].astype(jnp.float32) * gain[:, columns].astype(jnp.float32)
        held[:, tile] = (left[:, tile] + inverse[...] * grad_hat).astype(jnp.bfloat16)
        target = out.at[:, pl.ds(first + start, half)]
        copies.append(
            pltpu.make_async_copy(held.at[:, pl.ds(start, half)], target, sems.at[index])
        )
        copies[-1].start()
    for copy in copies:
        copy.wait()


def finish_grad(inputs, cotangent, gain, inverse, extras, grad_own, pieces):
    rows, width = inputs.shape
    *pieces, rest = pieces
    span = rest.shape[1]
    hbm = pl.BlockSpec(memory_space=pltpu.HBM)
    options = dict(
        compiler_params=pltpu.CompilerParams(vmem_limit_bytes=VMEM_LIMIT),
        cost_estimate=pl.CostEstimate(flops=1000, bytes_accessed=1000, transcendentals=0),
    )
    begun, left = pl.pallas_call(
        finish_most_kernel,
        out_shape=[shape(jnp.bfloat16, rows, width), shape(jnp.float32, rows, span)],
        in_specs=[VMEM] * (9 + len(pieces)),
        out_specs=[hbm, VMEM],
        scratch_shapes=[pltpu.VMEM((rows, width - span), jnp.bfloat16), pltpu.SemaphoreType.DMA],
        name="finish_most",
        **options,
    )(inputs, cotangent, gain, inverse, *extras, grad_own, *pieces)
    return pl.pallas_call(
        finish_rest_kernel,
        out_shape=shape(jnp.bfloat16, rows, width),
        in_specs=[VMEM] * 4 + [hbm],
        out_specs=hbm,
        scratch_shapes=[pltpu.VMEM((rows, span), jnp.bfloat16), pltpu.SemaphoreType.DMA((2,))],
        input_output_aliases={4: 0},
        name="finish_rest",
        **options,
    )(gain, inverse, left, rest, begun)


def move(bucket):
    return lax.all_to_all(bucket, "dp", split_axis=0, concat_axis=0, tiled=True)


def after(array, *others):
    return lax.optimization_barrier((array, *others))[0]


def on_device(
    inputs,
    cotangent,
    norm_gain,
    w_query,
    w_key,
    w_value,
    w_output,
    send_rows,
    receive_slots,
    owner_segments,
):
    rows, width = inputs.shape
    tensor = lax.axis_size("tensor")
    low = jnp.bfloat16
    order = lax.axis_index("tensor").astype(jnp.int32) ^ jnp.arange(4, dtype=jnp.int32)
    gain = norm_gain.reshape(1, width)

    x2 = swap(inputs, 2, tensor)
    c2 = swap(cotangent, 2, tensor)
    gain_chip = jnp.concatenate([gain, swap(gain, 1, tensor)], axis=0)
    gain_far = swap(gain_chip, 2, tensor)
    x1 = swap(inputs, 1, tensor)
    near_output = swap(w_output, 1, tensor)
    weights = (w_query, w_key, w_value)
    own_turned, near_turned, here, there, there_turned, *indices = prepare(
        order,
        *weights,
        w_output,
        near_output,
        send_rows,
        receive_slots.reshape(1, rows),
        owner_segments.reshape(1, rows),
        width,
    )
    send, receive, segments, mask = indices
    squares, part, x1 = begin(inputs, x1, cotangent, here)

    x2, c2, gain_far, squares, part = lax.optimization_barrier((x2, c2, gain_far, squares, part))
    x3 = swap(x2, 1, tensor)
    near_part = add_grad(1, c2, there_turned, part)
    got_part = swap(near_part, 1, tensor)
    own_part = add_grad(0, c2, there_turned, after(part, near_part))
    squares = add_squares(x2, after(squares, near_part, own_part))
    home, inverse_rms, bucket = project(
        order,
        (inputs, x1, x2, x3),
        (gain_chip, gain_far),
        weights,
        squares,
        own_part,
        got_part,
        send,
    )
    near_turned = swap(after(near_turned, home), 1, tensor)
    there = swap(after(there, near_part), 2, tensor)
    back = attend(move(bucket), receive, segments, mask)
    moved, there = lax.optimization_barrier((move(back), there))
    own, own_extras = bring_home(moved, send, home)

    near = swap(own, 1, tensor)
    far_extras = swap(own_extras, 2, tensor)
    quarter = width // 4
    turn, got = own, []
    for first, span in ((0, 2 * quarter), (2 * quarter, quarter), (3 * quarter, quarter)):
        flops = 4 * rows * span * width if first else 1000
        sides = (turn, near, own_turned, near_turned)
        part = spread("spread_far", width + first, span, low, *sides, flops=flops)
        got.append(swap(part, 2, tensor))
        turn = after(own, part, far_extras)
    grad_own = spread("spread_own", 0, width, jnp.float32, turn, near, own_turned, near_turned)
    extras = (own_extras, swap(own_extras, 1, tensor), far_extras, swap(far_extras, 1, tensor))
    layer_out = call(
        finish_out_kernel,
        "finish_out",
        shape(low, rows, width),
        (inputs, *extras, here, there),
        first=VMEM,
    )
    got[1] = after(got[1], layer_out)
    input_grad = finish_grad(inputs, cotangent, gain, inverse_rms, extras, grad_own, got)
    return (layer_out, input_grad)


def solution(mesh):
    return jax.shard_map(
        on_device,
        mesh=mesh,
        in_specs=(
            P("dp", "tensor"),
            P("dp", "tensor"),
            P("tensor"),
            P(None, "tensor"),
            P(None, "tensor"),
            P(None, "tensor"),
            P("tensor", None),
            P("dp", None),
            P("dp"),
            P("dp"),
        ),
        out_specs=(P("dp", "tensor"), P("dp", "tensor")),
        check_vma=False,
    )
```

```python
import math

import jax
import jax.numpy as jnp
from jax import lax
from jax.experimental import pallas as pl
from jax.experimental.pallas import tpu as pltpu
from jax.sharding import PartitionSpec as P

HEAD_DIM = 128
EPSILON = 1e-05
SCALING = 1.0 / math.sqrt(HEAD_DIM)
CONTRACT_LAST = (((1,), (1,)), ((), ()))
CONTRACT_FIRST = (((0,), (0,)), ((), ()))
VMEM_LIMIT = 3 * 1024 * 1024
VMEM = pl.BlockSpec(memory_space=pltpu.VMEM)
SMEM = pl.BlockSpec(memory_space=pltpu.SMEM)
TILE = 512


def dot(left, right, dims=(((1,), (0,)), ((), ()))):
    return lax.dot_general(left, right, dims, preferred_element_type=jnp.float32)


def call(kernel, name, out_shape, operands, scratch=(), first=SMEM, rest=VMEM):
    single = not isinstance(out_shape, (list, tuple))
    shapes = [out_shape] if single else list(out_shape)
    results = pl.pallas_call(
        kernel,
        out_shape=shapes,
        in_specs=[first] + [rest] * (len(operands) - 1),
        out_specs=[VMEM] * len(shapes),
        scratch_shapes=list(scratch),
        compiler_params=pltpu.CompilerParams(vmem_limit_bytes=VMEM_LIMIT),
        cost_estimate=pl.CostEstimate(flops=1000, bytes_accessed=1000, transcendentals=0),
        name=name,
    )(*operands)
    return results[0] if single else results


def shape(dtype, *sizes):
    return jax.ShapeDtypeStruct(sizes, dtype)


def swap(array, mask, count):
    return lax.ppermute(array, "tensor", [(i, i ^ mask) for i in range(count)])


def block_start(order, slot, width):
    return pl.multiple_of(order[slot] * width, width)


def one_hot(places, rows):
    row = lax.broadcasted_iota(jnp.int32, (rows, places.shape[1]), 0)
    return jnp.where(places == row, 1.0, 0.0).astype(jnp.bfloat16)


def slot_mask(receive, stays, slots):
    place = one_hot(receive, slots).astype(jnp.float32)
    down = lax.broadcasted_iota(jnp.int32, (slots, slots), 0)
    across = lax.broadcasted_iota(jnp.int32, (slots, slots), 1)
    position = lax.broadcasted_iota(jnp.int32, receive.shape, 1)
    both = []
    for values in (stays, position):
        column = jnp.sum(place * values.astype(jnp.float32), axis=1, keepdims=True)
        both.append((column, jnp.sum(jnp.where(down == across, column, 0.0), axis=0, keepdims=True)))
    (stay_down, stay_across), (place_down, place_across) = both
    allowed = (stay_down == stay_across) & (place_across <= place_down)
    return jnp.where(allowed, 1.0, 0.0)


def prepare_kernel(
    order,
    w_query,
    w_key,
    w_value,
    w_output,
    near_output,
    send,
    receive,
    segments,
    own_turned,
    near_turned,
    here,
    there,
    there_turned,
    send_out,
    receive_out,
    segments_out,
    mask_out,
):
    heads, width = w_output.shape[0], here.shape[1]
    mask_out[...] = slot_mask(receive[...], segments[...], mask_out.shape[0])
    for slot, out, turned in ((0, here, None), (2, there, there_turned)):
        columns = pl.ds(block_start(order, slot, width), width)
        for part, weight in enumerate((w_output, near_output)):
            rows = slice(part * heads, (part + 1) * heads)
            block = weight[:, columns]
            out[rows, :] = block
            if turned is not None:
                turned[:, rows] = block.T
    for source, target in ((send, send_out), (receive, receive_out), (segments, segments_out)):
        target[...] = source[...]
    for out, slots in ((own_turned, (0, 2)), (near_turned, (1, 3))):
        for part, slot in enumerate(slots):
            first = block_start(order, slot, width)
            for start in range(0, width, TILE):
                columns = slice(part * width + start, part * width + start + TILE)
                for place, weight in enumerate((w_query, w_key, w_value)):
                    rows = slice(place * HEAD_DIM, (place + 1) * HEAD_DIM)
                    out[rows, columns] = weight[pl.ds(first + start, TILE), :].T


def prepare(order, w_query, w_key, w_value, w_output, near_output, send, receive, segments, width):
    heads = w_query.shape[1]
    low = jnp.bfloat16
    return call(
        prepare_kernel,
        "prepare",
        [
            *[shape(low, 3 * heads, 2 * width)] * 2,
            *[shape(low, 2 * heads, width)] * 2,
            shape(low, width, 2 * heads),
            shape(jnp.int32, *send.shape),
            shape(jnp.int32, *receive.shape),
            shape(jnp.int32, *segments.shape),
            shape(jnp.float32, send.shape[1], send.shape[1]),
        ],
        (order, w_query, w_key, w_value, w_output, near_output, send, receive, segments),
    )


def sum_squares(block):
    wide = block[...].astype(jnp.float32)
    return jnp.sum(wide * wide, axis=-1, keepdims=True)


def begin_kernel(x0, x1, c0, here, squares, part):
    squares[...] = sum_squares(x0) + sum_squares(x1)
    part[...] = dot(c0[...], here[...], CONTRACT_LAST)


def begin(x0, x1, c0, here):
    rows, columns = x0.shape[0], here.shape[0]
    shapes = [shape(jnp.float32, rows, 1), shape(jnp.float32, rows, columns)]
    return call(begin_kernel, "begin", shapes, (x0, x1, c0, here), first=VMEM)


def add_grad_kernel(half):
    def kernel(c2, there_turned, part, total):
        heads = total.shape[1]
        columns = slice(half * heads, (half + 1) * heads)
        total[...] = part[:, columns] + dot(c2[...], there_turned[:, columns])

    return kernel


def add_grad(half, c2, there_turned, part):
    out = shape(jnp.float32, part.shape[0], part.shape[1] // 2)
    return call(add_grad_kernel(half), "add_grad", out, (c2, there_turned, part), first=VMEM)


def add_squares_kernel(x2, squares_in, squares):
    squares[...] = squares_in[...] + sum_squares(x2)


def add_squares(x2, squares):
    out = shape(jnp.float32, *squares.shape)
    return call(add_squares_kernel, "add_squares", out, (x2, squares), first=VMEM)


def project_kernel(
    order,
    x0,
    x1,
    x2,
    x3,
    gain_chip,
    gain_far,
    w_query,
    w_key,
    w_value,
    squares,
    own_part,
    got_part,
    send,
    home,
    inverse,
    bucket,
    total,
):
    blocks = (x0, x1, x2, x3)
    width = x0.shape[1]
    mean = (squares[...] + sum_squares(x3)) / (width * len(blocks))
    inverse_rms = lax.rsqrt(mean + EPSILON)
    inverse[...] = inverse_rms
    head_grad = (own_part[...] + got_part[...]).astype(jnp.bfloat16)
    for index, block in enumerate(blocks):
        gain = (gain_chip, gain_far)[index // 2][index % 2 : index % 2 + 1, :]
        scaled = block[...].astype(jnp.float32) * inverse_rms
        normed = (scaled * gain.astype(jnp.float32)).astype(jnp.bfloat16)
        here = pl.ds(block_start(order, index, width), width)
        weights = jnp.concatenate([w_query[here, :], w_key[here, :], w_value[here, :]], axis=1)
        product = dot(normed, weights)
        total[...] = total[...] + product if index else product
    rounded = total[...].astype(jnp.bfloat16)
    home[...] = rounded
    chosen = one_hot(send[...], rounded.shape[0])
    split = rounded.shape[1]
    bucket[:, :split] = dot(chosen, rounded, CONTRACT_FIRST).astype(jnp.bfloat16)
    bucket[:, split:] = dot(chosen, head_grad, CONTRACT_FIRST).astype(jnp.bfloat16)


def project(order, blocks, gains, weights, squares, own_part, got_part, send):
    rows = blocks[0].shape[0]
    columns = 3 * HEAD_DIM
    return call(
        project_kernel,
        "project",
        [
            shape(jnp.bfloat16, rows, columns),
            shape(jnp.float32, rows, 1),
            shape(jnp.bfloat16, send.shape[1], columns + HEAD_DIM),
        ],
        (order, *blocks, *gains, *weights, squares, own_part, got_part, send),
        scratch=[pltpu.VMEM((rows, columns), jnp.float32)],
    )


def attend_kernel(moved, mask, back):
    back[...] = attention(moved[...], mask[...] > 0.5)


def attend_sparse_kernel(moved, receive, segments, back):
    place = one_hot(receive[...], moved.shape[0])
    rows = dot(place, moved[...], CONTRACT_FIRST).astype(jnp.bfloat16)
    count = rows.shape[0]
    down = lax.broadcasted_iota(jnp.int32, (count, count), 0)
    across = lax.broadcasted_iota(jnp.int32, (count, count), 1)
    stays = segments[...]
    own_stay = jnp.sum(jnp.where(down == across, stays, 0), axis=1, keepdims=True)
    results = attention(rows, (own_stay == stays) & (across <= down))
    back[...] = dot(place, results).astype(jnp.bfloat16)


def attention(rows, allowed):
    queries, key_rows, value_rows, head_grad = (
        rows[:, index * HEAD_DIM : (index + 1) * HEAD_DIM] for index in range(4)
    )
    scores = jnp.where(allowed, dot(queries, key_rows, CONTRACT_LAST) * SCALING, -1e30)
    raised = jnp.exp(scores - jnp.max(scores, axis=-1, keepdims=True))
    softmax_out = raised / jnp.sum(raised, axis=-1, keepdims=True)
    low_weights = softmax_out.astype(jnp.bfloat16)
    attended = dot(low_weights, value_rows).astype(jnp.bfloat16)
    grad_value = dot(low_weights, head_grad, CONTRACT_FIRST).astype(jnp.bfloat16)
    grad_probs = dot(head_grad, value_rows, CONTRACT_LAST)
    inner = jnp.sum(softmax_out * grad_probs, axis=-1, keepdims=True)
    grad_scores = (softmax_out * (grad_probs - inner) * SCALING).astype(jnp.bfloat16)
    grad_query = dot(grad_scores, key_rows).astype(jnp.bfloat16)
    grad_key = dot(grad_scores, queries, CONTRACT_FIRST).astype(jnp.bfloat16)
    return jnp.concatenate([grad_query, grad_key, grad_value, attended], axis=1)


def attend(moved, receive, segments, mask):
    out = shape(jnp.bfloat16, *moved.shape)
    if moved.shape[0] == receive.shape[1]:
        return call(attend_kernel, "attend", out, (moved, mask), first=VMEM)
    return call(attend_sparse_kernel, "attend", out, (moved, receive, segments), first=VMEM)


def write_parts(value, out):
    out[...] = jnp.zeros_like(out)
    for place in range(3):
        low = value.astype(jnp.bfloat16)
        out[:, place : place + 1] = low
        value = value - low.astype(jnp.float32)


def read_parts(parts):
    return sum(parts[:, place : place + 1].astype(jnp.float32) for place in (2, 1, 0))


def bring_home_kernel(moved, send, home, grads, extras):
    chosen = one_hot(send[...], grads.shape[0])
    rows = dot(chosen, moved[...])
    split = 3 * HEAD_DIM
    grads[...] = rows[:, :split].astype(jnp.bfloat16)
    extras[:, :HEAD_DIM] = rows[:, split:].astype(jnp.bfloat16)
    product = rows[:, :split] * home[...].astype(jnp.float32)
    row_dot = jnp.sum(product, axis=-1, keepdims=True)
    write_parts(row_dot, extras.at[:, HEAD_DIM:])


def bring_home(moved, send, home):
    rows = home.shape[0]
    shapes = [shape(jnp.bfloat16, rows, 3 * HEAD_DIM), shape(jnp.bfloat16, rows, 2 * HEAD_DIM)]
    return call(bring_home_kernel, "bring_home", shapes, (moved, send, home), first=VMEM)


def spread_kernel(first):
    def kernel(own, near, weights, near_weights, out):
        both_rows = jnp.concatenate([own[...], near[...]], axis=1)
        for start in range(0, out.shape[1], TILE):
            columns = slice(first + start, first + start + TILE)
            both = jnp.concatenate([weights[:, columns], near_weights[:, columns]], axis=0)
            total = dot(both_rows, both)
            out[:, start : start + TILE] = total.astype(out.dtype)

    return kernel


def spread(name, first, span, dtype, own, near, weights, near_weights, flops=1000):
    return pl.pallas_call(
        spread_kernel(first),
        out_shape=shape(dtype, own.shape[0], span),
        in_specs=[VMEM] * 4,
        out_specs=VMEM,
        compiler_params=pltpu.CompilerParams(vmem_limit_bytes=VMEM_LIMIT),
        cost_estimate=pl.CostEstimate(flops=flops, bytes_accessed=1000, transcendentals=0),
        name=name,
    )(own, near, weights, near_weights)


def finish_out_kernel(inputs, own, near, far, last, here, there, out):
    width = inputs.shape[1]
    chip = jnp.concatenate([own[:, :HEAD_DIM], near[:, :HEAD_DIM]], axis=1)
    other = jnp.concatenate([far[:, :HEAD_DIM], last[:, :HEAD_DIM]], axis=1)
    for start in range(0, width, TILE):
        tile = slice(start, start + TILE)
        total = dot(chip, here[:, tile]) + dot(other, there[:, tile])
        out[:, tile] = (inputs[:, tile].astype(jnp.float32) + total).astype(jnp.bfloat16)


def finish_most_kernel(
    inputs, cotangent, gain, inverse, own, near, far, last, grad_own, *pieces
):
    *pieces, out, left, held, sem = pieces
    tiles = [
        piece.at[:, start : start + TILE]
        for piece in pieces
        for start in range(0, piece.shape[1], TILE)
    ]
    row_dot = sum(read_parts(extras[:, HEAD_DIM:]) for extras in (own, near, far, last))
    mean_dot = row_dot / (4 * inputs.shape[1])
    inverse_rms = inverse[...]
    most = held.shape[1]
    for start in range(0, inputs.shape[1], TILE):
        tile = slice(start, start + TILE)
        grad_normed = grad_own[:, tile]
        if start < most:
            grad_normed = grad_normed + tiles[start // TILE][...].astype(jnp.float32)
        grad_hat = grad_normed * gain[:, tile].astype(jnp.float32)
        scaled = inputs[:, tile].astype(jnp.float32) * inverse_rms
        change = inverse_rms * (grad_hat - scaled * mean_dot)
        result = cotangent[:, tile].astype(jnp.float32) + change
        if start < most:
            held[:, tile] = result.astype(jnp.bfloat16)
        else:
            left[:, start - most : start - most + TILE] = result
    copy = pltpu.make_async_copy(held, out.at[:, pl.ds(0, most)], sem)
    copy.start()
    copy.wait()


def finish_rest_kernel(gain, inverse, left, rest, before, out, held, sems):
    span = rest.shape[1]
    first = out.shape[1] - span
    half = span // 2
    copies = []
    for index, start in enumerate(range(0, span, half)):
        tile = slice(start, start + half)
        columns = slice(first + start, first + start + half)
        grad_hat = rest[:, tile].astype(jnp.float32) * gain[:, columns].astype(jnp.float32)
        held[:, tile] = (left[:, tile] + inverse[...] * grad_hat).astype(jnp.bfloat16)
        target = out.at[:, pl.ds(first + start, half)]
        copies.append(
            pltpu.make_async_copy(held.at[:, pl.ds(start, half)], target, sems.at[index])
        )
        copies[-1].start()
    for copy in copies:
        copy.wait()


def finish_grad(inputs, cotangent, gain, inverse, extras, grad_own, pieces):
    rows, width = inputs.shape
    *pieces, rest = pieces
    span = rest.shape[1]
    hbm = pl.BlockSpec(memory_space=pltpu.HBM)
    options = dict(
        compiler_params=pltpu.CompilerParams(vmem_limit_bytes=VMEM_LIMIT),
        cost_estimate=pl.CostEstimate(flops=1000, bytes_accessed=1000, transcendentals=0),
    )
    begun, left = pl.pallas_call(
        finish_most_kernel,
        out_shape=[shape(jnp.bfloat16, rows, width), shape(jnp.float32, rows, span)],
        in_specs=[VMEM] * (9 + len(pieces)),
        out_specs=[hbm, VMEM],
        scratch_shapes=[pltpu.VMEM((rows, width - span), jnp.bfloat16), pltpu.SemaphoreType.DMA],
        name="finish_most",
        **options,
    )(inputs, cotangent, gain, inverse, *extras, grad_own, *pieces)
    return pl.pallas_call(
        finish_rest_kernel,
        out_shape=shape(jnp.bfloat16, rows, width),
        in_specs=[VMEM] * 4 + [hbm],
        out_specs=hbm,
        scratch_shapes=[pltpu.VMEM((rows, span), jnp.bfloat16), pltpu.SemaphoreType.DMA((2,))],
        input_output_aliases={4: 0},
        name="finish_rest",
        **options,
    )(gain, inverse, left, rest, begun)


def move(bucket):
    return lax.all_to_all(bucket, "dp", split_axis=0, concat_axis=0, tiled=True)


def after(array, *others):
    return lax.optimization_barrier((array, *others))[0]


def on_device(
    inputs,
    cotangent,
    norm_gain,
    w_query,
    w_key,
    w_value,
    w_output,
    send_rows,
    receive_slots,
    owner_segments,
):
    rows, width = inputs.shape
    tensor = lax.axis_size("tensor")
    low = jnp.bfloat16
    order = lax.axis_index("tensor").astype(jnp.int32) ^ jnp.arange(4, dtype=jnp.int32)
    gain = norm_gain.reshape(1, width)

    x2 = swap(inputs, 2, tensor)
    c2 = swap(cotangent, 2, tensor)
    gain_chip = jnp.concatenate([gain, swap(gain, 1, tensor)], axis=0)
    gain_far = swap(gain_chip, 2, tensor)
    x1 = swap(inputs, 1, tensor)
    near_output = swap(w_output, 1, tensor)
    weights = (w_query, w_key, w_value)
    own_turned, near_turned, here, there, there_turned, *indices = prepare(
        order,
        *weights,
        w_output,
        near_output,
        send_rows,
        receive_slots.reshape(1, rows),
        owner_segments.reshape(1, rows),
        width,
    )
    send, receive, segments, mask = indices
    squares, part = begin(inputs, x1, cotangent, here)

    x2, c2, gain_far, squares, part = lax.optimization_barrier((x2, c2, gain_far, squares, part))
    x3 = swap(x2, 1, tensor)
    near_part = add_grad(1, c2, there_turned, part)
    got_part = swap(near_part, 1, tensor)
    own_part = add_grad(0, c2, there_turned, after(part, near_part))
    squares = add_squares(x2, squares)
    home, inverse_rms, bucket = project(
        order,
        (inputs, x1, x2, x3),
        (gain_chip, gain_far),
        weights,
        squares,
        own_part,
        got_part,
        send,
    )
    near_turned = swap(after(near_turned, home), 1, tensor)
    there = swap(after(there, home), 2, tensor)
    back = attend(move(bucket), receive, segments, mask)
    own, own_extras = bring_home(move(back), send, home)

    near = swap(own, 1, tensor)
    far_extras = swap(own_extras, 2, tensor)
    quarter = width // 4
    turn, got = own, []
    for first, span in ((0, 2 * quarter), (2 * quarter, quarter), (3 * quarter, quarter)):
        flops = 4 * rows * span * width if first else 1000
        sides = (turn, near, own_turned, near_turned)
        part = spread("spread_far", width + first, span, low, *sides, flops=flops)
        got.append(swap(part, 2, tensor))
        turn = after(own, part, far_extras)
    grad_own = spread("spread_own", 0, width, jnp.float32, turn, near, own_turned, near_turned)
    extras = (own_extras, swap(own_extras, 1, tensor), far_extras, swap(far_extras, 1, tensor))
    layer_out = call(
        finish_out_kernel,
        "finish_out",
        shape(low, rows, width),
        (inputs, *extras, here, there),
        first=VMEM,
    )
    got[1] = after(got[1], layer_out)
    input_grad = finish_grad(inputs, cotangent, gain, inverse_rms, extras, grad_own, got)
    return (layer_out, input_grad)


def solution(mesh):
    return jax.shard_map(
        on_device,
        mesh=mesh,
        in_specs=(
            P("dp", "tensor"),
            P("dp", "tensor"),
            P("tensor"),
            P(None, "tensor"),
            P(None, "tensor"),
            P(None, "tensor"),
            P("tensor", None),
            P("dp", None),
            P("dp"),
            P("dp"),
        ),
        out_specs=(P("dp", "tensor"), P("dp", "tensor")),
        check_vma=False,
    )
```

```python
import math

import jax
import jax.numpy as jnp
from jax import lax
from jax.experimental import pallas as pl
from jax.experimental.pallas import tpu as pltpu
from jax.sharding import PartitionSpec as P

HEAD_DIM = 128
EPSILON = 1e-05
SCALING = 1.0 / math.sqrt(HEAD_DIM)
CONTRACT_LAST = (((1,), (1,)), ((), ()))
CONTRACT_FIRST = (((0,), (0,)), ((), ()))
VMEM_LIMIT = 3 * 1024 * 1024
VMEM = pl.BlockSpec(memory_space=pltpu.VMEM)
SMEM = pl.BlockSpec(memory_space=pltpu.SMEM)
TILE = 512


def dot(left, right, dims=(((1,), (0,)), ((), ()))):
    return lax.dot_general(left, right, dims, preferred_element_type=jnp.float32)


def call(kernel, name, out_shape, operands, scratch=(), first=SMEM, rest=VMEM):
    single = not isinstance(out_shape, (list, tuple))
    shapes = [out_shape] if single else list(out_shape)
    results = pl.pallas_call(
        kernel,
        out_shape=shapes,
        in_specs=[first] + [rest] * (len(operands) - 1),
        out_specs=[VMEM] * len(shapes),
        scratch_shapes=list(scratch),
        compiler_params=pltpu.CompilerParams(vmem_limit_bytes=VMEM_LIMIT),
        cost_estimate=pl.CostEstimate(flops=1000, bytes_accessed=1000, transcendentals=0),
        name=name,
    )(*operands)
    return results[0] if single else results


def shape(dtype, *sizes):
    return jax.ShapeDtypeStruct(sizes, dtype)


def swap(array, mask, count):
    return lax.ppermute(array, "tensor", [(i, i ^ mask) for i in range(count)])


def block_start(order, slot, width):
    return pl.multiple_of(order[slot] * width, width)


def one_hot(places, rows):
    row = lax.broadcasted_iota(jnp.int32, (rows, places.shape[1]), 0)
    return jnp.where(places == row, 1.0, 0.0).astype(jnp.bfloat16)


def slot_mask(receive, stays, slots):
    place = one_hot(receive, slots).astype(jnp.float32)
    down = lax.broadcasted_iota(jnp.int32, (slots, slots), 0)
    across = lax.broadcasted_iota(jnp.int32, (slots, slots), 1)
    position = lax.broadcasted_iota(jnp.int32, receive.shape, 1)
    both = []
    for values in (stays, position):
        column = jnp.sum(place * values.astype(jnp.float32), axis=1, keepdims=True)
        both.append((column, jnp.sum(jnp.where(down == across, column, 0.0), axis=0, keepdims=True)))
    (stay_down, stay_across), (place_down, place_across) = both
    allowed = (stay_down == stay_across) & (place_across <= place_down)
    return jnp.where(allowed, 1.0, 0.0)


def prepare_kernel(
    order,
    w_query,
    w_key,
    w_value,
    w_output,
    near_output,
    send,
    receive,
    segments,
    own_turned,
    near_turned,
    here,
    there,
    there_turned,
    send_out,
    receive_out,
    segments_out,
    mask_out,
):
    heads, width = w_output.shape[0], here.shape[1]
    mask_out[...] = slot_mask(receive[...], segments[...], mask_out.shape[0])
    for slot, out, turned in ((0, here, None), (2, there, there_turned)):
        columns = pl.ds(block_start(order, slot, width), width)
        for part, weight in enumerate((w_output, near_output)):
            rows = slice(part * heads, (part + 1) * heads)
            block = weight[:, columns]
            out[rows, :] = block
            if turned is not None:
                turned[:, rows] = block.T
    for source, target in ((send, send_out), (receive, receive_out), (segments, segments_out)):
        target[...] = source[...]
    for out, slots in ((own_turned, (0, 2)), (near_turned, (1, 3))):
        for part, slot in enumerate(slots):
            first = block_start(order, slot, width)
            for start in range(0, width, TILE):
                columns = slice(part * width + start, part * width + start + TILE)
                for place, weight in enumerate((w_query, w_key, w_value)):
                    rows = slice(place * HEAD_DIM, (place + 1) * HEAD_DIM)
                    out[rows, columns] = weight[pl.ds(first + start, TILE), :].T


def prepare(order, w_query, w_key, w_value, w_output, near_output, send, receive, segments, width):
    heads = w_query.shape[1]
    low = jnp.bfloat16
    return call(
        prepare_kernel,
        "prepare",
        [
            *[shape(low, 3 * heads, 2 * width)] * 2,
            *[shape(low, 2 * heads, width)] * 2,
            shape(low, width, 2 * heads),
            shape(jnp.int32, *send.shape),
            shape(jnp.int32, *receive.shape),
            shape(jnp.int32, *segments.shape),
            shape(jnp.float32, send.shape[1], send.shape[1]),
        ],
        (order, w_query, w_key, w_value, w_output, near_output, send, receive, segments),
    )


def sum_squares(block):
    wide = block[...].astype(jnp.float32)
    return jnp.sum(wide * wide, axis=-1, keepdims=True)


def begin_kernel(x0, x1, c0, here, squares, part):
    squares[...] = sum_squares(x0) + sum_squares(x1)
    part[...] = dot(c0[...], here[...], CONTRACT_LAST)


def begin(x0, x1, c0, here):
    rows, columns = x0.shape[0], here.shape[0]
    shapes = [shape(jnp.float32, rows, 1), shape(jnp.float32, rows, columns)]
    return call(begin_kernel, "begin", shapes, (x0, x1, c0, here), first=VMEM)


def add_grad_kernel(half):
    def kernel(c2, there_turned, part, total):
        heads = total.shape[1]
        columns = slice(half * heads, (half + 1) * heads)
        total[...] = part[:, columns] + dot(c2[...], there_turned[:, columns])

    return kernel


def add_grad(half, c2, there_turned, part):
    out = shape(jnp.float32, part.shape[0], part.shape[1] // 2)
    return call(add_grad_kernel(half), "add_grad", out, (c2, there_turned, part), first=VMEM)


def add_squares_kernel(x2, squares_in, squares):
    squares[...] = squares_in[...] + sum_squares(x2)


def add_squares(x2, squares):
    out = shape(jnp.float32, *squares.shape)
    return call(add_squares_kernel, "add_squares", out, (x2, squares), first=VMEM)


def project_kernel(
    order,
    x0,
    x1,
    x2,
    x3,
    gain_chip,
    gain_far,
    w_query,
    w_key,
    w_value,
    squares,
    own_part,
    got_part,
    send,
    home,
    inverse,
    bucket,
    total,
):
    blocks = (x0, x1, x2, x3)
    width = x0.shape[1]
    mean = (squares[...] + sum_squares(x3)) / (width * len(blocks))
    inverse_rms = lax.rsqrt(mean + EPSILON)
    inverse[...] = inverse_rms
    head_grad = (own_part[...] + got_part[...]).astype(jnp.bfloat16)
    for index, block in enumerate(blocks):
        gain = (gain_chip, gain_far)[index // 2][index % 2 : index % 2 + 1, :]
        scaled = block[...].astype(jnp.float32) * inverse_rms
        normed = (scaled * gain.astype(jnp.float32)).astype(jnp.bfloat16)
        here = pl.ds(block_start(order, index, width), width)
        weights = jnp.concatenate([w_query[here, :], w_key[here, :], w_value[here, :]], axis=1)
        product = dot(normed, weights)
        total[...] = total[...] + product if index else product
    rounded = total[...].astype(jnp.bfloat16)
    home[...] = rounded
    chosen = one_hot(send[...], rounded.shape[0])
    split = rounded.shape[1]
    bucket[:, :split] = dot(chosen, rounded, CONTRACT_FIRST).astype(jnp.bfloat16)
    bucket[:, split:] = dot(chosen, head_grad, CONTRACT_FIRST).astype(jnp.bfloat16)


def project(order, blocks, gains, weights, squares, own_part, got_part, send):
    rows = blocks[0].shape[0]
    columns = 3 * HEAD_DIM
    return call(
        project_kernel,
        "project",
        [
            shape(jnp.bfloat16, rows, columns),
            shape(jnp.float32, rows, 1),
            shape(jnp.bfloat16, send.shape[1], columns + HEAD_DIM),
        ],
        (order, *blocks, *gains, *weights, squares, own_part, got_part, send),
        scratch=[pltpu.VMEM((rows, columns), jnp.float32)],
    )


def attend_kernel(moved, mask, back):
    back[...] = attention(moved[...], mask[...] > 0.5)


def attend_sparse_kernel(moved, receive, segments, back):
    place = one_hot(receive[...], moved.shape[0])
    rows = dot(place, moved[...], CONTRACT_FIRST).astype(jnp.bfloat16)
    count = rows.shape[0]
    down = lax.broadcasted_iota(jnp.int32, (count, count), 0)
    across = lax.broadcasted_iota(jnp.int32, (count, count), 1)
    stays = segments[...]
    own_stay = jnp.sum(jnp.where(down == across, stays, 0), axis=1, keepdims=True)
    results = attention(rows, (own_stay == stays) & (across <= down))
    back[...] = dot(place, results).astype(jnp.bfloat16)


def attention(rows, allowed):
    queries, key_rows, value_rows, head_grad = (
        rows[:, index * HEAD_DIM : (index + 1) * HEAD_DIM] for index in range(4)
    )
    scores = jnp.where(allowed, dot(queries, key_rows, CONTRACT_LAST) * SCALING, -1e30)
    raised = jnp.exp(scores - jnp.max(scores, axis=-1, keepdims=True))
    softmax_out = raised / jnp.sum(raised, axis=-1, keepdims=True)
    low_weights = softmax_out.astype(jnp.bfloat16)
    attended = dot(low_weights, value_rows).astype(jnp.bfloat16)
    grad_value = dot(low_weights, head_grad, CONTRACT_FIRST).astype(jnp.bfloat16)
    grad_probs = dot(head_grad, value_rows, CONTRACT_LAST)
    inner = jnp.sum(softmax_out * grad_probs, axis=-1, keepdims=True)
    grad_scores = (softmax_out * (grad_probs - inner) * SCALING).astype(jnp.bfloat16)
    grad_query = dot(grad_scores, key_rows).astype(jnp.bfloat16)
    grad_key = dot(grad_scores, queries, CONTRACT_FIRST).astype(jnp.bfloat16)
    return jnp.concatenate([grad_query, grad_key, grad_value, attended], axis=1)


def attend(moved, receive, segments, mask):
    out = shape(jnp.bfloat16, *moved.shape)
    if moved.shape[0] == receive.shape[1]:
        return call(attend_kernel, "attend", out, (moved, mask), first=VMEM)
    return call(attend_sparse_kernel, "attend", out, (moved, receive, segments), first=VMEM)


def write_parts(value, out):
    out[...] = jnp.zeros_like(out)
    for place in range(3):
        low = value.astype(jnp.bfloat16)
        out[:, place : place + 1] = low
        value = value - low.astype(jnp.float32)


def read_parts(parts):
    return sum(parts[:, place : place + 1].astype(jnp.float32) for place in (2, 1, 0))


def bring_home_kernel(moved, send, home, grads, extras):
    chosen = one_hot(send[...], grads.shape[0])
    rows = dot(chosen, moved[...])
    split = 3 * HEAD_DIM
    grads[...] = rows[:, :split].astype(jnp.bfloat16)
    extras[:, :HEAD_DIM] = rows[:, split:].astype(jnp.bfloat16)
    product = rows[:, :split] * home[...].astype(jnp.float32)
    row_dot = jnp.sum(product, axis=-1, keepdims=True)
    write_parts(row_dot, extras.at[:, HEAD_DIM:])


def bring_home(moved, send, home):
    rows = home.shape[0]
    shapes = [shape(jnp.bfloat16, rows, 3 * HEAD_DIM), shape(jnp.bfloat16, rows, 2 * HEAD_DIM)]
    return call(bring_home_kernel, "bring_home", shapes, (moved, send, home), first=VMEM)


def spread_kernel(first):
    def kernel(own, near, weights, near_weights, out):
        own_rows, near_rows = own[...], near[...]
        for start in range(0, out.shape[1], TILE):
            columns = slice(first + start, first + start + TILE)
            total = dot(own_rows, weights[:, columns]) + dot(near_rows, near_weights[:, columns])
            out[:, start : start + TILE] = total.astype(out.dtype)

    return kernel


def spread(name, first, span, dtype, own, near, weights, near_weights, flops=1000):
    return pl.pallas_call(
        spread_kernel(first),
        out_shape=shape(dtype, own.shape[0], span),
        in_specs=[VMEM] * 4,
        out_specs=VMEM,
        compiler_params=pltpu.CompilerParams(vmem_limit_bytes=VMEM_LIMIT),
        cost_estimate=pl.CostEstimate(flops=flops, bytes_accessed=1000, transcendentals=0),
        name=name,
    )(own, near, weights, near_weights)


def finish_out_kernel(inputs, own, near, far, last, here, there, out):
    width = inputs.shape[1]
    chip = jnp.concatenate([own[:, :HEAD_DIM], near[:, :HEAD_DIM]], axis=1)
    other = jnp.concatenate([far[:, :HEAD_DIM], last[:, :HEAD_DIM]], axis=1)
    for start in range(0, width, TILE):
        tile = slice(start, start + TILE)
        total = dot(chip, here[:, tile]) + dot(other, there[:, tile])
        out[:, tile] = (inputs[:, tile].astype(jnp.float32) + total).astype(jnp.bfloat16)


def finish_most_kernel(
    inputs, cotangent, gain, inverse, own, near, far, last, grad_own, *pieces
):
    *pieces, out, left, held, sem = pieces
    tiles = [
        piece.at[:, start : start + TILE]
        for piece in pieces
        for start in range(0, piece.shape[1], TILE)
    ]
    row_dot = sum(read_parts(extras[:, HEAD_DIM:]) for extras in (own, near, far, last))
    mean_dot = row_dot / (4 * inputs.shape[1])
    inverse_rms = inverse[...]
    most = held.shape[1]
    for start in range(0, inputs.shape[1], TILE):
        tile = slice(start, start + TILE)
        grad_normed = grad_own[:, tile]
        if start < most:
            grad_normed = grad_normed + tiles[start // TILE][...].astype(jnp.float32)
        grad_hat = grad_normed * gain[:, tile].astype(jnp.float32)
        scaled = inputs[:, tile].astype(jnp.float32) * inverse_rms
        change = inverse_rms * (grad_hat - scaled * mean_dot)
        result = cotangent[:, tile].astype(jnp.float32) + change
        if start < most:
            held[:, tile] = result.astype(jnp.bfloat16)
        else:
            left[:, start - most : start - most + TILE] = result
    copy = pltpu.make_async_copy(held, out.at[:, pl.ds(0, most)], sem)
    copy.start()
    copy.wait()


def finish_rest_kernel(gain, inverse, left, rest, before, out, held, sems):
    span = rest.shape[1]
    first = out.shape[1] - span
    half = span // 2
    copies = []
    for index, start in enumerate(range(0, span, half)):
        tile = slice(start, start + half)
        columns = slice(first + start, first + start + half)
        grad_hat = rest[:, tile].astype(jnp.float32) * gain[:, columns].astype(jnp.float32)
        held[:, tile] = (left[:, tile] + inverse[...] * grad_hat).astype(jnp.bfloat16)
        target = out.at[:, pl.ds(first + start, half)]
        copies.append(
            pltpu.make_async_copy(held.at[:, pl.ds(start, half)], target, sems.at[index])
        )
        copies[-1].start()
    for copy in copies:
        copy.wait()


def finish_grad(inputs, cotangent, gain, inverse, extras, grad_own, pieces):
    rows, width = inputs.shape
    *pieces, rest = pieces
    span = rest.shape[1]
    hbm = pl.BlockSpec(memory_space=pltpu.HBM)
    options = dict(
        compiler_params=pltpu.CompilerParams(vmem_limit_bytes=VMEM_LIMIT),
        cost_estimate=pl.CostEstimate(flops=1000, bytes_accessed=1000, transcendentals=0),
    )
    begun, left = pl.pallas_call(
        finish_most_kernel,
        out_shape=[shape(jnp.bfloat16, rows, width), shape(jnp.float32, rows, span)],
        in_specs=[VMEM] * (9 + len(pieces)),
        out_specs=[hbm, VMEM],
        scratch_shapes=[pltpu.VMEM((rows, width - span), jnp.bfloat16), pltpu.SemaphoreType.DMA],
        name="finish_most",
        **options,
    )(inputs, cotangent, gain, inverse, *extras, grad_own, *pieces)
    return pl.pallas_call(
        finish_rest_kernel,
        out_shape=shape(jnp.bfloat16, rows, width),
        in_specs=[VMEM] * 4 + [hbm],
        out_specs=hbm,
        scratch_shapes=[pltpu.VMEM((rows, span), jnp.bfloat16), pltpu.SemaphoreType.DMA((2,))],
        input_output_aliases={4: 0},
        name="finish_rest",
        **options,
    )(gain, inverse, left, rest, begun)


def move(bucket):
    return lax.all_to_all(bucket, "dp", split_axis=0, concat_axis=0, tiled=True)


def after(array, *others):
    return lax.optimization_barrier((array, *others))[0]


def on_device(
    inputs,
    cotangent,
    norm_gain,
    w_query,
    w_key,
    w_value,
    w_output,
    send_rows,
    receive_slots,
    owner_segments,
):
    rows, width = inputs.shape
    tensor = lax.axis_size("tensor")
    low = jnp.bfloat16
    order = lax.axis_index("tensor").astype(jnp.int32) ^ jnp.arange(4, dtype=jnp.int32)
    gain = norm_gain.reshape(1, width)

    x2 = swap(inputs, 2, tensor)
    c2 = swap(cotangent, 2, tensor)
    gain_chip = jnp.concatenate([gain, swap(gain, 1, tensor)], axis=0)
    gain_far = swap(gain_chip, 2, tensor)
    x1 = swap(inputs, 1, tensor)
    near_output = swap(w_output, 1, tensor)
    weights = (w_query, w_key, w_value)
    own_turned, near_turned, here, there, there_turned, *indices = prepare(
        order,
        *weights,
        w_output,
        near_output,
        send_rows,
        receive_slots.reshape(1, rows),
        owner_segments.reshape(1, rows),
        width,
    )
    send, receive, segments, mask = indices
    squares, part = begin(inputs, x1, cotangent, here)

    x2, c2, gain_far, squares, part = lax.optimization_barrier((x2, c2, gain_far, squares, part))
    x3 = swap(x2, 1, tensor)
    near_part = add_grad(1, c2, there_turned, part)
    got_part = swap(near_part, 1, tensor)
    own_part = add_grad(0, c2, there_turned, after(part, near_part))
    squares = add_squares(x2, squares)
    home, inverse_rms, bucket = project(
        order,
        (inputs, x1, x2, x3),
        (gain_chip, gain_far),
        weights,
        squares,
        own_part,
        got_part,
        send,
    )
    near_turned = swap(after(near_turned, home), 1, tensor)
    there = swap(after(there, home), 2, tensor)
    back = attend(move(bucket), receive, segments, mask)
    own, own_extras = bring_home(move(back), send, home)

    near = swap(own, 1, tensor)
    far_extras = swap(own_extras, 2, tensor)
    quarter = width // 4
    turn, got = own, []
    for first, span in ((0, 2 * quarter), (2 * quarter, 2 * quarter)):
        flops = 4 * rows * span * width if first else 1000
        sides = (turn, near, own_turned, near_turned)
        part = spread("spread_far", width + first, span, low, *sides, flops=flops)
        got.append(swap(part, 2, tensor))
        turn = after(own, part, far_extras)
    grad_own = spread("spread_own", 0, width, jnp.float32, turn, near, own_turned, near_turned)
    extras = (own_extras, swap(own_extras, 1, tensor), far_extras, swap(far_extras, 1, tensor))
    layer_out = call(
        finish_out_kernel,
        "finish_out",
        shape(low, rows, width),
        (inputs, *extras, here, there),
        first=VMEM,
    )
    got[1] = after(got[1], layer_out)
    input_grad = finish_grad(inputs, cotangent, gain, inverse_rms, extras, grad_own, got)
    return (layer_out, input_grad)


def solution(mesh):
    return jax.shard_map(
        on_device,
        mesh=mesh,
        in_specs=(
            P("dp", "tensor"),
            P("dp", "tensor"),
            P("tensor"),
            P(None, "tensor"),
            P(None, "tensor"),
            P(None, "tensor"),
            P("tensor", None),
            P("dp", None),
            P("dp"),
            P("dp"),
        ),
        out_specs=(P("dp", "tensor"), P("dp", "tensor")),
        check_vma=False,
    )
```
